32 devices in a mesh: grp: 2 (over core), seq: 8 (over z, y), mdl: 2 (over x).
Axes of the slice: x: 2, y: 2, z: 4, core: 2. Of those that a mesh axis runs over, the one named last changes fastest.
Arguments:
- signal: bfloat16 [2, 1024, 1536], P(None, 'seq', 'mdl'), may hold values from -6 to 6
- mask_token: bfloat16 [1536], P('mdl'), may hold values from -6 to 6
- keep: int32 [2, 256], P(None, 'seq'), may hold values 0 or 1
- target_shard: int32 [2, 256], P(None, 'seq'), may hold values from 0 to 7, as said below
- enc_weight: bfloat16 [2, 3, 1536, 1536], P('grp', None, 'seq', 'mdl'), may hold values from -0.5 to 0.5
- pred_weight: bfloat16 [1536, 1536], P(None, 'mdl'), may hold values from -0.15625 to 0.15625
Outputs:
- block_loss: float32 [8, 128], P('seq', 'grp')
The draws below stay inside these ranges and needn't reach their ends.
Inputs may be any that keep to these rules, and one draw needn't show every extreme that they name: `target_shard`: among the blocks of one position range of 128 tokens, all sequences together, at most 16 name the same shard; one shard is named by exactly 16 blocks of every range.
All inputs are finite; a program needn't handle non-finite values. No bound on the sum of `keep` on one device may be relied on, other than what follows from the above.
Results may differ from the reference program's by a relative error of at most 0.0015.
Values may be sent and summed in bfloat16 or wider, within the bound.
No kernel may reach another device: no remote copies, remote signals or barrier semaphores. Data moves between devices by JAX's collectives and lax.ppermute only.
A program may use at most 64 MiB of HBM per device.

```python
import math
import jax
import jax.numpy as jnp
from jax import lax

D = 1536
HD = 128
HEADS = 12
WIN = 64
MBLK = 4
LEN_DEV = 128
SEQS = 2
LENGTH = 1024
NBLK_SEQ = 256
BLK_DEV = 64
SHARDS = 8
CAP = 16
SLOTS = 128


def draw_signal(key, part):
    full_shape = (SEQS, LENGTH, D)
    values = jax.random.normal(key, full_shape, jnp.float32)
    return jnp.clip(values, -6.0, 6.0).astype(jnp.bfloat16)


def draw_enc_weight(key, part):
    spread = D ** (-0.5)
    normal_part = jax.random.normal(key, (2, 3, D, D), jnp.float32)
    return jnp.clip(normal_part * spread, -0.5, 0.5).astype(jnp.bfloat16)


def draw_target_shard(key, part):
    hot_shard = jax.random.randint(jax.random.fold_in(key, 7), (), 0, SHARDS)

    def one_source(source_key):
        shuffled = jax.random.permutation(source_key, CAP * (SHARDS - 1))
        others = shuffled % (SHARDS - 1)
        others = jnp.where(others >= hot_shard, others + 1, others)
        chosen = jnp.concatenate([jnp.full((CAP,), hot_shard, jnp.int32), others[:BLK_DEV - CAP].astype(jnp.int32)])
        return jax.random.permutation(jax.random.fold_in(source_key, 1), chosen)
    source_keys = jax.random.split(jax.random.fold_in(key, 11), SHARDS)
    assigned = jax.vmap(one_source)(source_keys)
    assigned = assigned.reshape(SHARDS, SEQS, BLK_DEV // SEQS).transpose(1, 0, 2).reshape(SEQS, NBLK_SEQ)
    return assigned.astype(jnp.int32)


def set_ends(values, stream_key, least, high):
    spot = [jax.random.randint(jax.random.fold_in(stream_key, axis), (), 0, length) for axis, length in enumerate(values.shape)]
    longest = values.shape.index(max(values.shape))
    neighbour = spot[:longest] + [(spot[longest] + 1) % values.shape[longest]] + spot[longest + 1:]
    return values.at[tuple(spot)].set(least).at[tuple(neighbour)].set(high)


def steps_of(stream_key, dims, pieces, least, high):
    loudness = 1.0
    for position, blocks in pieces:
        steps = jax.random.uniform(jax.random.fold_in(jax.random.fold_in(stream_key, 6), position), (blocks,), jnp.float32, least / len(pieces), high / len(pieces))
        loudness = loudness * jnp.repeat(jnp.exp(steps), dims[position] // blocks).reshape((-1,) + (1,) * (len(dims) - 1 - position))
    return loudness


def gaussian(own_key, shape, scale, limit, pieces=(), kind=jnp.bfloat16):
    gain = steps_of(own_key, shape, pieces, -0.22, 0.18) if pieces else 1.0
    values = jax.random.normal(own_key, shape, jnp.float32) * scale * gain
    return jnp.minimum(jnp.maximum(values, -limit), limit).astype(kind)


def setup_inputs(seed: int = 0) -> dict:
    key_list = jax.random.split(jax.random.key(seed), 7)
    return {
        "signal": draw_signal(jax.random.fold_in(key_list[6], 71), 0),
        "mask_token": gaussian(key_list[1], (D,), 1.0, 6.0, ((0, 2),)),
        "keep": set_ends((jax.random.randint(key_list[2], (SEQS, NBLK_SEQ), 0, 4) < 1).astype(jnp.int32), jax.random.fold_in(key_list[2], 1), 0, 1),
        "target_shard": draw_target_shard(jax.random.fold_in(key_list[6], 71), 0),
        "enc_weight": draw_enc_weight(jax.random.fold_in(key_list[6], 71), 0),
        "pred_weight": gaussian(key_list[5], (D, D), D ** -0.5, 0.15625, ((1, 2),)),
    }


def encode(inputs, weight):
    queries = jnp.dot(inputs, weight[0], preferred_element_type=jnp.float32).astype(jnp.bfloat16)
    key_rows = jnp.dot(inputs, weight[1], preferred_element_type=jnp.float32).astype(jnp.bfloat16)
    value_rows = jnp.dot(inputs, weight[2], preferred_element_type=jnp.float32).astype(jnp.bfloat16)
    nblocks = LENGTH // LEN_DEV
    span = LEN_DEV + 2 * WIN
    padded_keys = jnp.pad(key_rows, ((WIN, WIN), (0, 0)))
    padded_values = jnp.pad(value_rows, ((WIN, WIN), (0, 0)))
    window = (jnp.arange(nblocks) * LEN_DEV)[:, None] + jnp.arange(span)[None, :]
    key_blocks = padded_keys[window].reshape(nblocks, span, HEADS, HD).astype(jnp.float32)
    value_blocks = padded_values[window].reshape(nblocks, span, HEADS, HD).astype(jnp.float32)
    query_blocks = queries.reshape(nblocks, LEN_DEV, HEADS, HD).astype(jnp.float32)
    scores = jnp.einsum('nahd,nbhd->nhab', query_blocks, key_blocks) * (1.0 / math.sqrt(HD))
    query_pos = (jnp.arange(nblocks) * LEN_DEV)[:, None] + jnp.arange(LEN_DEV)[None, :]
    key_pos = (jnp.arange(nblocks) * LEN_DEV - WIN)[:, None] + jnp.arange(span)[None, :]
    in_window = (jnp.abs(query_pos[:, :, None] - key_pos[:, None, :]) <= WIN) & (key_pos[:, None, :] >= 0) & (key_pos[:, None, :] < LENGTH)
    scores = jnp.where(in_window[:, None], scores, -jnp.inf)
    row_peak = lax.optimization_barrier(jnp.max(scores, axis=-1, keepdims=True))
    exp_scores = jnp.exp(scores - row_peak)
    attention = (exp_scores / lax.optimization_barrier(jnp.sum(exp_scores, axis=-1, keepdims=True))).astype(jnp.bfloat16)
    attended = jnp.einsum('nhab,nbhd->nahd', attention.astype(jnp.float32), value_blocks)
    return attended.astype(jnp.bfloat16).reshape(LENGTH, D)

def reference(signal, mask_token, keep, target_shard, enc_weight, pred_weight):
    kept_rows = jnp.repeat(keep, MBLK, axis=1)[:, :, None]
    context_input = jnp.where(kept_rows == 1, signal, mask_token[None, None, :])
    context = lax.map(lambda inputs: encode(inputs, enc_weight[0]), context_input)
    target = lax.map(lambda inputs: encode(inputs, enc_weight[1]), signal)

    def block_error(paired):
        context_seq, target_seq = paired
        predicted = jnp.dot(context_seq, pred_weight, preferred_element_type=jnp.float32)
        residue = predicted - target_seq.astype(jnp.float32)
        return lax.optimization_barrier(jnp.sum((residue * residue).reshape(NBLK_SEQ, MBLK * D), axis=1)) / (MBLK * D)
    errors = lax.map(block_error, (context, target))
    errors = errors * (keep == 0).astype(jnp.float32)
    per_range = LEN_DEV // MBLK
    error_src = errors.reshape(SEQS, SHARDS, per_range).transpose(1, 0, 2).reshape(SHARDS, BLK_DEV)
    shard_src = target_shard.reshape(SEQS, SHARDS, per_range).transpose(1, 0, 2).reshape(SHARDS, BLK_DEV)
    order_ids = jnp.arange(BLK_DEV)
    earlier = (shard_src[:, :, None] == shard_src[:, None, :]) & (order_ids[:, None] < order_ids[None, :])[None]
    slot_rank = lax.optimization_barrier(jnp.sum(earlier.astype(jnp.int32), axis=1))
    slot_index = shard_src * CAP + slot_rank
    onehot = slot_index[:, :, None] == jnp.arange(SLOTS)[None, None, :]
    placed = lax.optimization_barrier(jnp.sum(jnp.where(onehot, error_src[:, :, None], 0.0), axis=1))
    return placed.reshape(SHARDS, SHARDS, CAP).transpose(1, 0, 2).reshape(SHARDS, SLOTS)
```

```python
import functools
import math

import jax
import jax.numpy as jnp
from jax import lax
from jax.experimental import pallas as pl
from jax.experimental.pallas import tpu as pltpu
from jax.sharding import PartitionSpec as P

HD = 128
WIN = 64
AXES = ("grp", "seq", "mdl")


def padded(x, sides, width):
    for axis, dim in sides:
        count, length = (lax.axis_size(axis), x.shape[dim])
        up = [(i, (i + 1) % count) for i in range(count - 1)]
        down = [(j, i) for i, j in up]
        last = lax.slice_in_dim(x, length - width, length, axis=dim)
        leading = lax.slice_in_dim(x, 0, width, axis=dim)
        before = lax.ppermute(last, axis, up)
        after = lax.ppermute(leading, axis, down)
        x = jnp.concatenate([before, x, after], axis=dim)
    return x


def predict(context, target, live_flags, pred_weight, divisor):
    flat_rows = context.reshape(-1, context.shape[-1])
    wide_rows = lax.all_gather(flat_rows, "mdl", axis=1, tiled=True)
    predicted = jnp.dot(wide_rows, pred_weight, preferred_element_type=jnp.float32)
    residue = predicted - target.reshape(flat_rows.shape).astype(jnp.float32)
    partial_sums = jnp.sum((residue * residue).reshape(live_flags.shape[0], -1), axis=1)
    summed = lax.psum(partial_sums, "mdl")
    return summed / divisor * live_flags


def local(signal, mask_token, keep, target_shard, enc_weight, pred_weight):
    group_index = lax.axis_index("grp")
    seq_index = lax.axis_index("seq")
    shards = lax.axis_size("seq")
    sequences, length, half_width = signal.shape
    per_range = keep.shape[1]
    block_len = length // per_range
    kept_rows = jnp.repeat(keep, block_len, axis=1)[:, :, None]
    masked_in = jnp.where(kept_rows == 1, signal, mask_token[None, None, :])
    source = jnp.where(group_index == 0, masked_in, signal)
    wide_in = lax.all_gather(source, "mdl", axis=2, tiled=True)
    full_width = wide_in.shape[2]
    flat_in = wide_in.reshape(-1, full_width)
    span = length + 2 * WIN
    weight_all = lax.all_gather(enc_weight, "seq", axis=2, tiled=True)[0]
    queries = jnp.dot(flat_in, weight_all[0], preferred_element_type=jnp.float32).astype(
        jnp.bfloat16
    )
    pair_made = jnp.einsum(
        "nd,cde->cne", flat_in, weight_all[1:], preferred_element_type=jnp.float32
    ).astype(jnp.bfloat16)
    own_pairs = pair_made.reshape(2, sequences, length, half_width)
    pair_rows = padded(own_pairs, (("seq", 2),), WIN)
    head_count = half_width // HD
    query_heads = queries.reshape(sequences, length, head_count, HD)
    key_heads = pair_rows[0].reshape(sequences, span, head_count, HD)
    value_heads = pair_rows[1].reshape(sequences, span, head_count, HD)
    query_pos = seq_index * length + jnp.arange(length)
    key_pos = seq_index * length - WIN + jnp.arange(span)
    total_len = length * shards
    in_window = (
        (jnp.abs(query_pos[:, None] - key_pos[None, :]) <= WIN)
        & (key_pos[None, :] >= 0)
        & (key_pos[None, :] < total_len)
    )
    scores = jnp.einsum(
        "sahd,sbhd->shab", query_heads, key_heads, preferred_element_type=jnp.float32
    ) * (1.0 / math.sqrt(HD))
    scores = jnp.where(in_window[None, None], scores, -jnp.inf)
    row_peak = jnp.max(scores, axis=-1, keepdims=True)
    exp_scores = jnp.exp(scores - row_peak)
    attention = (exp_scores / jnp.sum(exp_scores, axis=-1, keepdims=True)).astype(jnp.bfloat16)
    attended = jnp.einsum(
        "shab,sbhd->sahd", attention, value_heads, preferred_element_type=jnp.float32
    ).astype(jnp.bfloat16)
    latent = attended.reshape(sequences * per_range, block_len, half_width)
    blocks_here = latent.shape[0]
    capacity = max(2, 2 * blocks_here // shards)
    slot_count = shards * capacity
    shard_of = target_shard.reshape(-1)
    masked_flag = (keep.reshape(-1) == 0).astype(jnp.float32)
    order_ids = jnp.arange(blocks_here)
    earlier = (shard_of[:, None] == shard_of[None, :]) & (order_ids[:, None] < order_ids[None, :])
    slot_rank = jnp.sum(earlier.astype(jnp.int32), axis=0)
    slot_index = shard_of * capacity + slot_rank
    onehot = slot_index[None, :] == jnp.arange(slot_count)[:, None]
    divisor = float(block_len * full_width)
    halves = lax.all_to_all(latent[None], "grp", split_axis=1, concat_axis=0, tiled=True)
    half_count = blocks_here // 2
    first_block = group_index * half_count
    own_flags = lax.dynamic_slice_in_dim(masked_flag, first_block, half_count)
    losses = predict(halves[0], halves[1], own_flags, pred_weight, divisor)
    spread = lax.dynamic_update_slice_in_dim(
        jnp.zeros((blocks_here,), jnp.float32), losses, first_block, 0
    )
    slotted = jnp.sum(jnp.where(onehot, spread[None, :], 0.0), axis=1).reshape(shards, capacity)
    arrived = lax.all_to_all(slotted, "seq", split_axis=0, concat_axis=0, tiled=True)
    result = lax.psum_scatter(arrived, "grp", scatter_dimension=0, tiled=True)
    return result.reshape(1, -1)


def move(x, target):
    pairs = []
    for c in range(2):
        for s in range(8):
            for m in range(2):
                c2, z2, y2, m2 = target(c, s // 2, s % 2, m)
                pairs.append(((c * 8 + s) * 2 + m, (c2 * 8 + 2 * z2 + y2) * 2 + m2))
    return lax.ppermute(x, AXES, pairs)


def encode_kernel(
    where_ref, flag_ref, mask_ref, x_own, x_across, x_near, x_near_across, halo_ref,
    w0, w1, w2, w3, w4, w5, w6, w7,
    out_ref, x_buf, w_buf, q_buf, k_buf, v_buf, sems,
):
    core, z, y, m = (where_ref[i] for i in range(4))
    half = x_own.shape[-1]
    rows = x_own.shape[1]
    depth = w0.shape[1]
    wide = w0.shape[2]
    own_rows = 4 * rows
    copies = []
    side = lax.rem(z, 2)
    for piece, near, across in (
        (x_own, 0, 0), (x_across, 0, 1), (x_near, 1, 0), (x_near_across, 1, 1)
    ):
        first = WIN + 2 * rows * (side if near == 0 else 1 - side)
        lane = half * (m if across == 0 else 1 - m)
        for part in range(2):
            copies.append((
                piece.at[part],
                x_buf.at[
                    pl.ds(pl.multiple_of(first + part * rows, 64), rows),
                    pl.ds(pl.multiple_of(lane, 128), half),
                ],
            ))
    halo_first = pl.multiple_of((1 - core) * (WIN + own_rows), 64)
    empty_first = pl.multiple_of(core * (WIN + own_rows), 64)
    for across in range(2):
        lane = half * (m if across == 0 else 1 - m)
        copies.append((
            halo_ref.at[across],
            x_buf.at[pl.ds(halo_first, WIN), pl.ds(pl.multiple_of(lane, 128), half)],
        ))
    t = lax.rem(z, 2)
    for index, piece in enumerate((w0, w1, w2, w3, w4, w5, w6, w7)):
        turned, crossed, other = index // 4, (index // 2) % 2, index % 2
        pos_z = 2 * (t if turned == 0 else 1 - t) + (core if other == 0 else 1 - core)
        pos = 2 * pos_z + (y if crossed == 0 else 1 - y)
        copies.append((
            piece, w_buf.at[:, pl.ds(pl.multiple_of(pos * depth, 64), depth), :]
        ))
    started = []
    for index, (source, target) in enumerate(copies):
        copy = pltpu.make_async_copy(source, target, sems.at[index])
        copy.start()
        started.append(copy)
    x_buf[pl.ds(empty_first, WIN), :] = jnp.zeros((WIN, 2 * half), x_buf.dtype)
    for copy in started:
        copy.wait()
    mask_row = mask_ref[...].astype(jnp.float32)
    span = x_buf.shape[0]
    for r in range(span // 128):
        x = x_buf[r * 128:(r + 1) * 128, :].astype(jnp.float32)
        flags = flag_ref[r * 128:(r + 1) * 128, :]
        x_buf[r * 128:(r + 1) * 128, :] = jnp.where(flags == 1, x, mask_row).astype(x_buf.dtype)
    x = x_buf[...]
    q_buf[...] = jnp.dot(
        x[WIN:WIN + own_rows], w_buf[0], preferred_element_type=jnp.float32
    ).astype(q_buf.dtype)
    k_buf[...] = jnp.dot(x, w_buf[1], preferred_element_type=jnp.float32).astype(k_buf.dtype)
    v_buf[...] = jnp.dot(x, w_buf[2], preferred_element_type=jnp.float32).astype(v_buf.dtype)
    keys = rows + 2 * WIN
    a = lax.broadcasted_iota(jnp.int32, (rows, keys), 0)
    b = lax.broadcasted_iota(jnp.int32, (rows, keys), 1)
    band = (b >= a) & (b <= a + 2 * WIN)
    for j in range(4):
        admitted = band
        if j == 0:
            admitted = admitted & (b >= WIN * (1 - core))
        if j == 3:
            admitted = admitted & (b < keys - WIN * core)
        for h in range(wide // HD):
            lanes = slice(h * HD, (h + 1) * HD)
            scores = lax.dot_general(
                q_buf[j * rows:(j + 1) * rows, lanes],
                k_buf[j * rows:j * rows + keys, lanes],
                (((1,), (1,)), ((), ())),
                preferred_element_type=jnp.float32,
            ) * (1.0 / math.sqrt(HD))
            scores = jnp.where(admitted, scores, -jnp.inf)
            peak = jnp.max(scores, axis=-1, keepdims=True)
            exps = jnp.exp(scores - peak)
            attention = (exps / jnp.sum(exps, axis=-1, keepdims=True)).astype(jnp.bfloat16)
            out_ref[j, :, lanes] = jnp.dot(
                attention,
                v_buf[j * rows:j * rows + keys, lanes],
                preferred_element_type=jnp.float32,
            ).astype(out_ref.dtype)


def predict_kernel(where_ref, lat_ref, across_ref, weight_ref, out_ref):
    m = where_ref[3]
    wide = lat_ref.shape[2]
    predicted = None
    for t in range(2):
        for across in range(2):
            first = (m if across == 0 else 1 - m) * 2 * wide + t * wide
            source = lat_ref[t] if across == 0 else across_ref[t]
            term = jnp.dot(
                source,
                weight_ref[pl.ds(pl.multiple_of(first, 128), wide), :],
                preferred_element_type=jnp.float32,
            )
            predicted = term if predicted is None else predicted + term
    total = None
    for t in range(2):
        residue = predicted[:, t * wide:(t + 1) * wide] - lat_ref[2 + t].astype(jnp.float32)
        for i in range(wide // 128):
            piece = residue[:, i * 128:(i + 1) * 128]
            total = piece * piece if total is None else total + piece * piece
    out_ref[...] = jnp.sum(total.T, axis=0, keepdims=True)


def local_lines(signal, mask_token, keep, target_shard, enc_weight, pred_weight):
    core = lax.axis_index("grp")
    s = lax.axis_index("seq")
    m = lax.axis_index("mdl")
    z, y = s // 2, s % 2
    where = jnp.stack([core, z, y, m]).astype(jnp.int32)
    sequences, length, half = signal.shape
    per_range = keep.shape[1]
    block_len = length // per_range
    depth = enc_weight.shape[2]
    wide = half // 2

    def chunk(t):
        return lax.dynamic_slice(enc_weight, (0, 0, 0, t * wide), (1, 3, depth, wide))[0]

    near_w = move(chunk(z // 2), lambda c, z, y, m: (z % 2, z // 2 + 2 * c, y, m))
    far_w = move(chunk(1 - z // 2), lambda c, z, y, m: (z % 2, 1 - z // 2 + 2 * c, y, m))

    def flip_y(c, z, y, m):
        return (c, z, 1 - y, m)

    def flip_core(c, z, y, m):
        return (1 - c, z, y, m)

    def flip_x(c, z, y, m):
        return (c, z, y, 1 - m)

    def flip_z(c, z, y, m):
        return (c, z + 1 - 2 * (z % 2), y, m)

    def across_z(c, z, y, m):
        if z // 2 == c:
            return (c, (z + 2) % 4, y, m)
        return (1 - c, z, y, m)

    mine = lax.dynamic_index_in_dim(signal, y, 0, keepdims=False)
    given = lax.dynamic_index_in_dim(signal, 1 - y, 0, keepdims=False)
    got = move(given, flip_y)
    both = jnp.where(y == 0, jnp.stack([mine, got]), jnp.stack([got, mine]))
    x_own = move(both, across_z)
    x_across = move(x_own, flip_x)
    x_near = move(x_own, flip_z)
    x_near_across = move(x_near, flip_x)
    odd = z % 2 == 1

    def edge(first, second):
        low = jnp.where(odd, first[1, length - WIN:], second[1, length - WIN:])
        high = jnp.where(odd, second[0, :WIN], first[0, :WIN])
        return jnp.where(core == 0, low, high)

    halo = move(jnp.stack([edge(x_own, x_near), edge(x_across, x_near_across)]), flip_core)
    near_y = move(near_w, flip_y)
    near_c = move(near_w, flip_core)
    near_yc = move(near_y, flip_core)
    far_y = move(far_w, flip_y)
    far_c = move(far_w, flip_core)
    far_yc = move(far_y, flip_core)

    small = lax.all_gather(jnp.stack([keep, target_shard]), "seq", axis=0)
    mask_other = move(mask_token, flip_x)
    mask_row = jnp.where(
        m == 0,
        jnp.concatenate([mask_token, mask_other]),
        jnp.concatenate([mask_other, mask_token]),
    )[None, :]
    keep_rows = lax.dynamic_index_in_dim(small[:, 0], y, 1, keepdims=False).reshape(-1)
    keep_rows = jnp.pad(jnp.repeat(keep_rows, block_len), (WIN, WIN), constant_values=1)
    span = 4 * length + 2 * WIN
    keep_rows = lax.dynamic_slice_in_dim(keep_rows, core * 4 * length, span)
    flags = jnp.where(z // 2 == 1, 1, keep_rows)[:, None]

    vmem = pl.BlockSpec(memory_space=pltpu.VMEM)
    smem = pl.BlockSpec(memory_space=pltpu.SMEM)
    anywhere = pl.BlockSpec(memory_space=pl.ANY)
    latent = pl.pallas_call(
        encode_kernel,
        out_shape=jax.ShapeDtypeStruct((4, length, wide), jnp.bfloat16),
        in_specs=[smem, vmem, vmem] + [anywhere] * 13,
        out_specs=vmem,
        scratch_shapes=[
            pltpu.VMEM((span, 2 * half), jnp.bfloat16),
            pltpu.VMEM((3, 2 * half, wide), jnp.bfloat16),
            pltpu.VMEM((4 * length, wide), jnp.bfloat16),
            pltpu.VMEM((span, wide), jnp.bfloat16),
            pltpu.VMEM((span, wide), jnp.bfloat16),
            pltpu.SemaphoreType.DMA((18,)),
        ],
        compiler_params=pltpu.CompilerParams(vmem_limit_bytes=40 * 2**20),
    )(
        where, flags, mask_row, x_own, x_across, x_near, x_near_across, halo,
        near_w, near_c, near_y, near_yc, far_w, far_c, far_y, far_yc,
    )
    lines = [[2 * i + j for i in range(4)] for j in range(2)]
    latents = lax.all_to_all(
        latent, "seq", split_axis=0, concat_axis=0, tiled=True, axis_index_groups=lines
    )
    across = move(latents[:2], flip_x)
    row_errors = pl.pallas_call(
        predict_kernel,
        out_shape=jax.ShapeDtypeStruct((1, length), jnp.float32),
        in_specs=[smem, vmem, vmem, vmem],
        out_specs=vmem,
        compiler_params=pltpu.CompilerParams(vmem_limit_bytes=40 * 2**20),
    )(where, latents, across, pred_weight)
    gathered = lax.all_gather(row_errors, ("seq", "mdl"), axis=0, tiled=True)

    here = lax.dynamic_slice_in_dim(small, 4 * core, 4, 0)
    shard_of = here[:, 1].reshape(4, -1)
    hidden = here[:, 0].reshape(4, -1) == 0
    blocks = shard_of.shape[1]
    order_ids = jnp.arange(blocks)
    match = shard_of == s
    earlier = match[:, :, None] & (order_ids[:, None] < order_ids[None, :])[None]
    rank = jnp.sum(earlier.astype(jnp.int32), axis=1)
    capacity = max(2, 2 * blocks // 8)
    chosen = jnp.where(match & hidden, rank, -1)
    hot = chosen[:, None, :] == jnp.arange(capacity)[None, :, None]
    hot = jnp.repeat(hot, block_len, axis=2).reshape(4, capacity, sequences, 1, length)
    terms = jnp.where(hot, gathered.reshape(4, 1, sequences, 2, length), 0.0)
    return jnp.sum(terms, axis=(2, 3, 4)).reshape(1, -1) / float(block_len * 2 * half)


def solution(mesh):
    placed = (
        P(None, "seq", "mdl"),
        P("mdl"),
        P(None, "seq"),
        P(None, "seq"),
        P("grp", None, "seq", "mdl"),
        P(None, "mdl"),
    )
    plan = local_lines if mesh.shape["seq"] == 8 else local
    return jax.shard_map(
        plan, mesh=mesh, in_specs=placed, out_specs=P("seq", "grp"), check_vma=False
    )
```

```python
import functools
import math

import jax
import jax.numpy as jnp
from jax import lax
from jax.experimental import pallas as pl
from jax.experimental.pallas import tpu as pltpu
from jax.sharding import PartitionSpec as P

HD = 128
WIN = 64
AXES = ("grp", "seq", "mdl")


def padded(x, sides, width):
    for axis, dim in sides:
        count, length = (lax.axis_size(axis), x.shape[dim])
        up = [(i, (i + 1) % count) for i in range(count - 1)]
        down = [(j, i) for i, j in up]
        last = lax.slice_in_dim(x, length - width, length, axis=dim)
        leading = lax.slice_in_dim(x, 0, width, axis=dim)
        before = lax.ppermute(last, axis, up)
        after = lax.ppermute(leading, axis, down)
        x = jnp.concatenate([before, x, after], axis=dim)
    return x


def predict(context, target, live_flags, pred_weight, divisor):
    flat_rows = context.reshape(-1, context.shape[-1])
    wide_rows = lax.all_gather(flat_rows, "mdl", axis=1, tiled=True)
    predicted = jnp.dot(wide_rows, pred_weight, preferred_element_type=jnp.float32)
    residue = predicted - target.reshape(flat_rows.shape).astype(jnp.float32)
    partial_sums = jnp.sum((residue * residue).reshape(live_flags.shape[0], -1), axis=1)
    summed = lax.psum(partial_sums, "mdl")
    return summed / divisor * live_flags


def local(signal, mask_token, keep, target_shard, enc_weight, pred_weight):
    group_index = lax.axis_index("grp")
    seq_index = lax.axis_index("seq")
    shards = lax.axis_size("seq")
    sequences, length, half_width = signal.shape
    per_range = keep.shape[1]
    block_len = length // per_range
    kept_rows = jnp.repeat(keep, block_len, axis=1)[:, :, None]
    masked_in = jnp.where(kept_rows == 1, signal, mask_token[None, None, :])
    source = jnp.where(group_index == 0, masked_in, signal)
    wide_in = lax.all_gather(source, "mdl", axis=2, tiled=True)
    full_width = wide_in.shape[2]
    flat_in = wide_in.reshape(-1, full_width)
    span = length + 2 * WIN
    weight_all = lax.all_gather(enc_weight, "seq", axis=2, tiled=True)[0]
    queries = jnp.dot(flat_in, weight_all[0], preferred_element_type=jnp.float32).astype(
        jnp.bfloat16
    )
    pair_made = jnp.einsum(
        "nd,cde->cne", flat_in, weight_all[1:], preferred_element_type=jnp.float32
    ).astype(jnp.bfloat16)
    own_pairs = pair_made.reshape(2, sequences, length, half_width)
    pair_rows = padded(own_pairs, (("seq", 2),), WIN)
    head_count = half_width // HD
    query_heads = queries.reshape(sequences, length, head_count, HD)
    key_heads = pair_rows[0].reshape(sequences, span, head_count, HD)
    value_heads = pair_rows[1].reshape(sequences, span, head_count, HD)
    query_pos = seq_index * length + jnp.arange(length)
    key_pos = seq_index * length - WIN + jnp.arange(span)
    total_len = length * shards
    in_window = (
        (jnp.abs(query_pos[:, None] - key_pos[None, :]) <= WIN)
        & (key_pos[None, :] >= 0)
        & (key_pos[None, :] < total_len)
    )
    scores = jnp.einsum(
        "sahd,sbhd->shab", query_heads, key_heads, preferred_element_type=jnp.float32
    ) * (1.0 / math.sqrt(HD))
    scores = jnp.where(in_window[None, None], scores, -jnp.inf)
    row_peak = jnp.max(scores, axis=-1, keepdims=True)
    exp_scores = jnp.exp(scores - row_peak)
    attention = (exp_scores / jnp.sum(exp_scores, axis=-1, keepdims=True)).astype(jnp.bfloat16)
    attended = jnp.einsum(
        "shab,sbhd->sahd", attention, value_heads, preferred_element_type=jnp.float32
    ).astype(jnp.bfloat16)
    latent = attended.reshape(sequences * per_range, block_len, half_width)
    blocks_here = latent.shape[0]
    capacity = max(2, 2 * blocks_here // shards)
    slot_count = shards * capacity
    shard_of = target_shard.reshape(-1)
    masked_flag = (keep.reshape(-1) == 0).astype(jnp.float32)
    order_ids = jnp.arange(blocks_here)
    earlier = (shard_of[:, None] == shard_of[None, :]) & (order_ids[:, None] < order_ids[None, :])
    slot_rank = jnp.sum(earlier.astype(jnp.int32), axis=0)
    slot_index = shard_of * capacity + slot_rank
    onehot = slot_index[None, :] == jnp.arange(slot_count)[:, None]
    divisor = float(block_len * full_width)
    halves = lax.all_to_all(latent[None], "grp", split_axis=1, concat_axis=0, tiled=True)
    half_count = blocks_here // 2
    first_block = group_index * half_count
    own_flags = lax.dynamic_slice_in_dim(masked_flag, first_block, half_count)
    losses = predict(halves[0], halves[1], own_flags, pred_weight, divisor)
    spread = lax.dynamic_update_slice_in_dim(
        jnp.zeros((blocks_here,), jnp.float32), losses, first_block, 0
    )
    slotted = jnp.sum(jnp.where(onehot, spread[None, :], 0.0), axis=1).reshape(shards, capacity)
    arrived = lax.all_to_all(slotted, "seq", split_axis=0, concat_axis=0, tiled=True)
    result = lax.psum_scatter(arrived, "grp", scatter_dimension=0, tiled=True)
    return result.reshape(1, -1)


def move(x, target):
    pairs = []
    for c in range(2):
        for s in range(8):
            for m in range(2):
                c2, z2, y2, m2 = target(c, s // 2, s % 2, m)
                pairs.append(((c * 8 + s) * 2 + m, (c2 * 8 + 2 * z2 + y2) * 2 + m2))
    return lax.ppermute(x, AXES, pairs)


def encode_kernel(
    where_ref, x_own, x_across, x_near, x_near_across, halo_ref,
    w0, w1, w2, w3, w4, w5, w6, w7,
    out_ref, x_buf, w_buf, q_buf, k_buf, v_buf, sems,
):
    core, z, y, m = (where_ref[i] for i in range(4))
    half = x_own.shape[-1]
    rows = x_own.shape[1]
    depth = w0.shape[1]
    wide = w0.shape[2]
    own_rows = 4 * rows
    copies = []
    side = lax.rem(z, 2)
    for piece, near, across in (
        (x_own, 0, 0), (x_across, 0, 1), (x_near, 1, 0), (x_near_across, 1, 1)
    ):
        first = WIN + 2 * rows * (side if near == 0 else 1 - side)
        lane = half * (m if across == 0 else 1 - m)
        for part in range(2):
            copies.append((
                piece.at[part],
                x_buf.at[
                    pl.ds(pl.multiple_of(first + (y if part == 0 else 1 - y) * rows, 64), rows),
                    pl.ds(pl.multiple_of(lane, 128), half),
                ],
            ))
    halo_first = pl.multiple_of((1 - core) * (WIN + own_rows), 64)
    empty_first = pl.multiple_of(core * (WIN + own_rows), 64)
    for across in range(2):
        lane = half * (m if across == 0 else 1 - m)
        copies.append((
            halo_ref.at[across],
            x_buf.at[pl.ds(halo_first, WIN), pl.ds(pl.multiple_of(lane, 128), half)],
        ))
    t = lax.rem(z, 2)
    for index, piece in enumerate((w0, w1, w2, w3, w4, w5, w6, w7)):
        turned, crossed, other = index // 4, (index // 2) % 2, index % 2
        pos_z = 2 * (t if turned == 0 else 1 - t) + (core if other == 0 else 1 - core)
        pos = 2 * pos_z + (y if crossed == 0 else 1 - y)
        copies.append((
            piece, w_buf.at[:, pl.ds(pl.multiple_of(pos * depth, 64), depth), :]
        ))
    started = []
    for index, (source, target) in enumerate(copies):
        copy = pltpu.make_async_copy(source, target, sems.at[index])
        copy.start()
        started.append(copy)
    x_buf[pl.ds(empty_first, WIN), :] = jnp.zeros((WIN, 2 * half), x_buf.dtype)
    for copy in started:
        copy.wait()
    x = x_buf[...]
    q_buf[...] = jnp.dot(
        x[WIN:WIN + own_rows], w_buf[0], preferred_element_type=jnp.float32
    ).astype(q_buf.dtype)
    k_buf[...] = jnp.dot(x, w_buf[1], preferred_element_type=jnp.float32).astype(k_buf.dtype)
    v_buf[...] = jnp.dot(x, w_buf[2], preferred_element_type=jnp.float32).astype(v_buf.dtype)
    keys = rows + 2 * WIN
    a = lax.broadcasted_iota(jnp.int32, (rows, keys), 0)
    b = lax.broadcasted_iota(jnp.int32, (rows, keys), 1)
    band = (b >= a) & (b <= a + 2 * WIN)
    for j in range(4):
        admitted = band
        if j == 0:
            admitted = admitted & (b >= WIN * (1 - core))
        if j == 3:
            admitted = admitted & (b < keys - WIN * core)
        for h in range(wide // HD):
            lanes = slice(h * HD, (h + 1) * HD)
            scores = lax.dot_general(
                q_buf[j * rows:(j + 1) * rows, lanes],
                k_buf[j * rows:j * rows + keys, lanes],
                (((1,), (1,)), ((), ())),
                preferred_element_type=jnp.float32,
            ) * (1.0 / math.sqrt(HD))
            scores = jnp.where(admitted, scores, -jnp.inf)
            peak = jnp.max(scores, axis=-1, keepdims=True)
            exps = jnp.exp(scores - peak)
            attention = (exps / jnp.sum(exps, axis=-1, keepdims=True)).astype(jnp.bfloat16)
            out_ref[j, :, lanes] = jnp.dot(
                attention,
                v_buf[j * rows:j * rows + keys, lanes],
                preferred_element_type=jnp.float32,
            ).astype(out_ref.dtype)


def predict_kernel(where_ref, slot_ref, lat_ref, across_ref, weight_ref, out_ref):
    m = where_ref[3]
    wide = lat_ref.shape[2]
    predicted = None
    for t in range(2):
        for across in range(2):
            first = (m if across == 0 else 1 - m) * 2 * wide + t * wide
            source = lat_ref[t] if across == 0 else across_ref[t]
            term = jnp.dot(
                source,
                weight_ref[pl.ds(pl.multiple_of(first, 128), wide), :],
                preferred_element_type=jnp.float32,
            )
            predicted = term if predicted is None else predicted + term
    total = None
    for t in range(2):
        residue = predicted[:, t * wide:(t + 1) * wide] - lat_ref[2 + t].astype(jnp.float32)
        for i in range(wide // 128):
            piece = residue[:, i * 128:(i + 1) * 128]
            total = piece * piece if total is None else total + piece * piece
    row_errors = jnp.sum(total, axis=1, keepdims=True)
    rows, slots = total.shape[0], out_ref.shape[2]
    chosen = slot_ref[...] == lax.broadcasted_iota(jnp.int32, (rows, slots), 1)
    routed = jnp.sum(jnp.where(chosen, row_errors, 0.0), axis=0, keepdims=True)
    for i in range(out_ref.shape[0]):
        out_ref[i] = routed


def local_lines(signal, mask_token, keep, target_shard, enc_weight, pred_weight):
    core = lax.axis_index("grp")
    s = lax.axis_index("seq")
    m = lax.axis_index("mdl")
    z, y = s // 2, s % 2
    where = jnp.stack([core, z, y, m]).astype(jnp.int32)
    sequences, length, half = signal.shape
    per_range = keep.shape[1]
    block_len = length // per_range
    depth = enc_weight.shape[2]
    wide = half // 2

    def chunk(t):
        return lax.dynamic_slice(enc_weight, (0, 0, 0, t * wide), (1, 3, depth, wide))[0]

    near_w = move(chunk(z // 2), lambda c, z, y, m: (z % 2, z // 2 + 2 * c, y, m))
    far_w = move(chunk(1 - z // 2), lambda c, z, y, m: (z % 2, 1 - z // 2 + 2 * c, y, m))

    def flip_y(c, z, y, m):
        return (c, z, 1 - y, m)

    def flip_core(c, z, y, m):
        return (1 - c, z, y, m)

    def flip_x(c, z, y, m):
        return (c, z, y, 1 - m)

    def flip_z(c, z, y, m):
        return (c, z + 1 - 2 * (z % 2), y, m)

    def across_z(c, z, y, m):
        if z // 2 == c:
            return (c, (z + 2) % 4, y, m)
        return (1 - c, z, y, m)

    def across_zy(c, z, y, m):
        c, z, y, m = across_z(c, z, y, m)
        return (c, z, 1 - y, m)

    to_context = jnp.where(z // 2 == core, z // 2 == 1, z // 2 == 0)
    shown = (jnp.repeat(keep, block_len, axis=1) == 1) | ~to_context
    source = jnp.where(shown[:, :, None], signal, mask_token[None, None, :])
    mine = lax.dynamic_index_in_dim(source, y, 0, keepdims=False)
    given = lax.dynamic_index_in_dim(source, 1 - y, 0, keepdims=False)
    x_own = jnp.stack([move(mine, across_z), move(given, across_zy)])
    x_across = move(x_own, flip_x)
    x_near = move(x_own, flip_z)
    x_near_across = move(x_near, flip_x)

    def edge(own, near):
        found = jnp.where(z % 2 == 1 - core, own, near)
        part = jnp.where(core == 0, 1 - y, y)
        first = jnp.where(core == 0, length - WIN, 0)
        return lax.dynamic_slice(found, (part, first, 0), (1, WIN, half))[0]

    halo = move(jnp.stack([edge(x_own, x_near), edge(x_across, x_near_across)]), flip_core)
    near_y = move(near_w, flip_y)
    near_c = move(near_w, flip_core)
    near_yc = move(near_y, flip_core)
    far_y = move(far_w, flip_y)
    far_c = move(far_w, flip_core)
    far_yc = move(far_y, flip_core)

    routing = move(
        jnp.stack([keep, target_shard]), lambda c, z, y, m: ((2 * z + y) // 4, (2 * z + y) % 4, c, m)
    )
    hidden = lax.dynamic_index_in_dim(routing[0], y, 0, keepdims=False) == 0
    shard_of = routing[1].reshape(-1)
    blocks = shard_of.shape[0]
    capacity = max(2, 2 * blocks // 8)
    order_ids = jnp.arange(blocks)
    earlier = (shard_of[:, None] == shard_of[None, :]) & (order_ids[:, None] < order_ids[None, :])
    slot = shard_of * capacity + jnp.sum(earlier.astype(jnp.int32), axis=0)
    slot = lax.dynamic_index_in_dim(slot.reshape(sequences, -1), y, 0, keepdims=False)
    slot = jnp.repeat(jnp.where(hidden, slot, -1), block_len)[:, None]
    span = 4 * length + 2 * WIN

    vmem = pl.BlockSpec(memory_space=pltpu.VMEM)
    smem = pl.BlockSpec(memory_space=pltpu.SMEM)
    anywhere = pl.BlockSpec(memory_space=pl.ANY)
    latent = pl.pallas_call(
        encode_kernel,
        out_shape=jax.ShapeDtypeStruct((4, length, wide), jnp.bfloat16),
        in_specs=[smem] + [anywhere] * 13,
        out_specs=vmem,
        scratch_shapes=[
            pltpu.VMEM((span, 2 * half), jnp.bfloat16),
            pltpu.VMEM((3, 2 * half, wide), jnp.bfloat16),
            pltpu.VMEM((4 * length, wide), jnp.bfloat16),
            pltpu.VMEM((span, wide), jnp.bfloat16),
            pltpu.VMEM((span, wide), jnp.bfloat16),
            pltpu.SemaphoreType.DMA((18,)),
        ],
        compiler_params=pltpu.CompilerParams(vmem_limit_bytes=40 * 2**20),
    )(
        where, x_own, x_across, x_near, x_near_across, halo,
        near_w, near_c, near_y, near_yc, far_w, far_c, far_y, far_yc,
    )
    lines = [[2 * i + j for i in range(4)] for j in range(2)]
    latents = lax.all_to_all(
        latent, "seq", split_axis=0, concat_axis=0, tiled=True, axis_index_groups=lines
    )
    across = move(latents[:2], flip_x)
    routed = pl.pallas_call(
        predict_kernel,
        out_shape=jax.ShapeDtypeStruct((16, 1, 8 * capacity), jnp.float32),
        in_specs=[smem, vmem, vmem, vmem, vmem],
        out_specs=vmem,
        compiler_params=pltpu.CompilerParams(vmem_limit_bytes=40 * 2**20),
    )(where, slot, latents, across, pred_weight)
    arrived = lax.all_to_all(routed, ("seq", "mdl"), split_axis=0, concat_axis=0, tiled=True)
    mine = lax.dynamic_slice_in_dim(arrived[:, 0], capacity * s, capacity, 1)
    summed = jnp.sum(mine.reshape(4, 4, capacity), axis=1)
    return summed.reshape(1, -1) / float(block_len * 2 * half)


def solution(mesh):
    placed = (
        P(None, "seq", "mdl"),
        P("mdl"),
        P(None, "seq"),
        P(None, "seq"),
        P("grp", None, "seq", "mdl"),
        P(None, "mdl"),
    )
    plan = local_lines if mesh.shape["seq"] == 8 else local
    return jax.shard_map(
        plan, mesh=mesh, in_specs=placed, out_specs=P("seq", "grp"), check_vma=False
    )
```

```python
import functools
import math

import jax
import jax.numpy as jnp
from jax import lax
from jax.experimental import pallas as pl
from jax.experimental.pallas import tpu as pltpu
from jax.sharding import PartitionSpec as P

HD = 128
WIN = 64
AXES = ("grp", "seq", "mdl")
PIECES = 12


def padded(x, sides, width):
    for axis, dim in sides:
        count, length = (lax.axis_size(axis), x.shape[dim])
        up = [(i, (i + 1) % count) for i in range(count - 1)]
        down = [(j, i) for i, j in up]
        last = lax.slice_in_dim(x, length - width, length, axis=dim)
        leading = lax.slice_in_dim(x, 0, width, axis=dim)
        before = lax.ppermute(last, axis, up)
        after = lax.ppermute(leading, axis, down)
        x = jnp.concatenate([before, x, after], axis=dim)
    return x


def predict(context, target, live_flags, pred_weight, divisor):
    flat_rows = context.reshape(-1, context.shape[-1])
    wide_rows = lax.all_gather(flat_rows, "mdl", axis=1, tiled=True)
    predicted = jnp.dot(wide_rows, pred_weight, preferred_element_type=jnp.float32)
    residue = predicted - target.reshape(flat_rows.shape).astype(jnp.float32)
    partial_sums = jnp.sum((residue * residue).reshape(live_flags.shape[0], -1), axis=1)
    summed = lax.psum(partial_sums, "mdl")
    return summed / divisor * live_flags


def local(signal, mask_token, keep, target_shard, enc_weight, pred_weight):
    group_index = lax.axis_index("grp")
    seq_index = lax.axis_index("seq")
    shards = lax.axis_size("seq")
    sequences, length, half_width = signal.shape
    per_range = keep.shape[1]
    block_len = length // per_range
    kept_rows = jnp.repeat(keep, block_len, axis=1)[:, :, None]
    masked_in = jnp.where(kept_rows == 1, signal, mask_token[None, None, :])
    source = jnp.where(group_index == 0, masked_in, signal)
    wide_in = lax.all_gather(source, "mdl", axis=2, tiled=True)
    full_width = wide_in.shape[2]
    flat_in = wide_in.reshape(-1, full_width)
    span = length + 2 * WIN
    weight_all = lax.all_gather(enc_weight, "seq", axis=2, tiled=True)[0]
    queries = jnp.dot(flat_in, weight_all[0], preferred_element_type=jnp.float32).astype(
        jnp.bfloat16
    )
    pair_made = jnp.einsum(
        "nd,cde->cne", flat_in, weight_all[1:], preferred_element_type=jnp.float32
    ).astype(jnp.bfloat16)
    own_pairs = pair_made.reshape(2, sequences, length, half_width)
    pair_rows = padded(own_pairs, (("seq", 2),), WIN)
    head_count = half_width // HD
    query_heads = queries.reshape(sequences, length, head_count, HD)
    key_heads = pair_rows[0].reshape(sequences, span, head_count, HD)
    value_heads = pair_rows[1].reshape(sequences, span, head_count, HD)
    query_pos = seq_index * length + jnp.arange(length)
    key_pos = seq_index * length - WIN + jnp.arange(span)
    total_len = length * shards
    in_window = (
        (jnp.abs(query_pos[:, None] - key_pos[None, :]) <= WIN)
        & (key_pos[None, :] >= 0)
        & (key_pos[None, :] < total_len)
    )
    scores = jnp.einsum(
        "sahd,sbhd->shab", query_heads, key_heads, preferred_element_type=jnp.float32
    ) * (1.0 / math.sqrt(HD))
    scores = jnp.where(in_window[None, None], scores, -jnp.inf)
    row_peak = jnp.max(scores, axis=-1, keepdims=True)
    exp_scores = jnp.exp(scores - row_peak)
    attention = (exp_scores / jnp.sum(exp_scores, axis=-1, keepdims=True)).astype(jnp.bfloat16)
    attended = jnp.einsum(
        "shab,sbhd->sahd", attention, value_heads, preferred_element_type=jnp.float32
    ).astype(jnp.bfloat16)
    latent = attended.reshape(sequences * per_range, block_len, half_width)
    blocks_here = latent.shape[0]
    capacity = max(2, 2 * blocks_here // shards)
    slot_count = shards * capacity
    shard_of = target_shard.reshape(-1)
    masked_flag = (keep.reshape(-1) == 0).astype(jnp.float32)
    order_ids = jnp.arange(blocks_here)
    earlier = (shard_of[:, None] == shard_of[None, :]) & (order_ids[:, None] < order_ids[None, :])
    slot_rank = jnp.sum(earlier.astype(jnp.int32), axis=0)
    slot_index = shard_of * capacity + slot_rank
    onehot = slot_index[None, :] == jnp.arange(slot_count)[:, None]
    divisor = float(block_len * full_width)
    halves = lax.all_to_all(latent[None], "grp", split_axis=1, concat_axis=0, tiled=True)
    half_count = blocks_here // 2
    first_block = group_index * half_count
    own_flags = lax.dynamic_slice_in_dim(masked_flag, first_block, half_count)
    losses = predict(halves[0], halves[1], own_flags, pred_weight, divisor)
    spread = lax.dynamic_update_slice_in_dim(
        jnp.zeros((blocks_here,), jnp.float32), losses, first_block, 0
    )
    slotted = jnp.sum(jnp.where(onehot, spread[None, :], 0.0), axis=1).reshape(shards, capacity)
    arrived = lax.all_to_all(slotted, "seq", split_axis=0, concat_axis=0, tiled=True)
    result = lax.psum_scatter(arrived, "grp", scatter_dimension=0, tiled=True)
    return result.reshape(1, -1)


def move(x, target):
    pairs = []
    for c in range(2):
        for s in range(8):
            for m in range(2):
                c2, z2, y2, m2 = target(c, s // 2, s % 2, m)
                pairs.append(((c * 8 + s) * 2 + m, (c2 * 8 + 2 * z2 + y2) * 2 + m2))
    return lax.ppermute(x, AXES, pairs)


def encode_kernel(where_ref, x_own, x_across, x_near, x_near_across, halo_ref, *refs):
    pieces = refs[:PIECES]
    out_ref, x_buf, w_buf, q_buf, k_buf, v_buf, sems = refs[PIECES:]
    core, z, y, m = (where_ref[i] for i in range(4))
    half = x_own.shape[-1]
    rows = x_own.shape[1]
    depth = pieces[0].shape[1]
    wide = pieces[0].shape[2]
    own_rows = 4 * rows
    copies = []
    side = lax.rem(z, 2)
    for piece, near, across in (
        (x_own, 0, 0), (x_across, 0, 1), (x_near, 1, 0), (x_near_across, 1, 1)
    ):
        first = WIN + 2 * rows * (side if near == 0 else 1 - side)
        lane = half * (m if across == 0 else 1 - m)
        for part in range(2):
            copies.append((
                piece.at[part],
                x_buf.at[
                    pl.ds(pl.multiple_of(first + (y if part == 0 else 1 - y) * rows, 64), rows),
                    pl.ds(pl.multiple_of(lane, 128), half),
                ],
            ))
    halo_first = pl.multiple_of((1 - core) * (WIN + own_rows), 64)
    empty_first = pl.multiple_of(core * (WIN + own_rows), 64)
    for across in range(2):
        lane = half * (m if across == 0 else 1 - m)
        copies.append((
            halo_ref.at[across],
            x_buf.at[pl.ds(halo_first, WIN), pl.ds(pl.multiple_of(lane, 128), half)],
        ))
    t = lax.rem(z, 2)
    for index, piece in enumerate(pieces):
        crossed, other = (index // 2) % 2, index % 2
        pos_z = 2 * (t if index < 4 else 1 - t) + (core if other == 0 else 1 - core)
        pos = 2 * pos_z + (y if crossed == 0 else 1 - y)
        first = pos * depth + (piece.shape[1] if index >= 8 else 0)
        copies.append((
            piece, w_buf.at[:, pl.ds(pl.multiple_of(first, 32), piece.shape[1]), :]
        ))
    started = []
    for index, (source, target) in enumerate(copies):
        copy = pltpu.make_async_copy(source, target, sems.at[index])
        copy.start()
        started.append(copy)
    x_buf[pl.ds(empty_first, WIN), :] = jnp.zeros((WIN, 2 * half), x_buf.dtype)
    for copy in started:
        copy.wait()
    x = x_buf[...]
    q_buf[...] = jnp.dot(
        x[WIN:WIN + own_rows], w_buf[0], preferred_element_type=jnp.float32
    ).astype(q_buf.dtype)
    k_buf[...] = jnp.dot(x, w_buf[1], preferred_element_type=jnp.float32).astype(k_buf.dtype)
    v_buf[...] = jnp.dot(x, w_buf[2], preferred_element_type=jnp.float32).astype(v_buf.dtype)
    keys = rows + 2 * WIN
    a = lax.broadcasted_iota(jnp.int32, (rows, keys), 0)
    b = lax.broadcasted_iota(jnp.int32, (rows, keys), 1)
    band = (b >= a) & (b <= a + 2 * WIN)
    for j in range(4):
        admitted = band
        if j == 0:
            admitted = admitted & (b >= WIN * (1 - core))
        if j == 3:
            admitted = admitted & (b < keys - WIN * core)
        for h in range(wide // HD):
            lanes = slice(h * HD, (h + 1) * HD)
            scores = lax.dot_general(
                q_buf[j * rows:(j + 1) * rows, lanes],
                k_buf[j * rows:j * rows + keys, lanes],
                (((1,), (1,)), ((), ())),
                preferred_element_type=jnp.float32,
            ) * (1.0 / math.sqrt(HD))
            scores = jnp.where(admitted, scores, -jnp.inf)
            peak = jnp.max(scores, axis=-1, keepdims=True)
            exps = jnp.exp(scores - peak)
            attention = (exps / jnp.sum(exps, axis=-1, keepdims=True)).astype(jnp.bfloat16)
            out_ref[j, :, lanes] = jnp.dot(
                attention,
                v_buf[j * rows:j * rows + keys, lanes],
                preferred_element_type=jnp.float32,
            ).astype(out_ref.dtype)


def predict_kernel(where_ref, slot_ref, lat_ref, own_ref, e0, e1, l0, l1, out_ref):
    core, m = where_ref[0], where_ref[3]
    wide = lat_ref.shape[2]
    lent = ((e0, e1), (l0, l1))
    total = None
    for side in range(2):
        predicted = None
        for t in range(2):
            for x in range(2):
                if side == 0:
                    source = lat_ref[2 * t + x]
                    weight = own_ref[(2 * x + t) * wide:(2 * x + t + 1) * wide, :]
                else:
                    source = lat_ref[2 * t + (core if x == 0 else 1 - core)]
                    weight = lent[t][x][...]
                term = jnp.dot(source, weight, preferred_element_type=jnp.float32)
                predicted = term if predicted is None else predicted + term
        for t in range(2):
            target = lat_ref[4 + 2 * t + (m if side == 0 else 1 - m)].astype(jnp.float32)
            residue = predicted[:, t * wide:(t + 1) * wide] - target
            for i in range(wide // 128):
                piece = residue[:, i * 128:(i + 1) * 128]
                total = piece * piece if total is None else total + piece * piece
    row_errors = jnp.sum(total, axis=1, keepdims=True)
    rows, slots = total.shape[0], out_ref.shape[2]
    chosen = slot_ref[...] == lax.broadcasted_iota(jnp.int32, (rows, slots), 1)
    routed = jnp.sum(jnp.where(chosen, row_errors, 0.0), axis=0, keepdims=True)
    for i in range(out_ref.shape[0]):
        out_ref[i] = routed


def local_lines(signal, mask_token, keep, target_shard, enc_weight, pred_weight):
    core = lax.axis_index("grp")
    s = lax.axis_index("seq")
    m = lax.axis_index("mdl")
    z, y = s // 2, s % 2
    where = jnp.stack([core, z, y, m]).astype(jnp.int32)
    sequences, length, half = signal.shape
    per_range = keep.shape[1]
    block_len = length // per_range
    depth = enc_weight.shape[2]
    wide = half // 2

    def chunk(t, first, count):
        part = lax.dynamic_slice(
            enc_weight, (0, 0, first, t * wide), (1, 3, count, wide)
        )
        return part[0]

    def to_near(c, z, y, m):
        return (z % 2, z // 2 + 2 * c, y, m)

    def to_far(c, z, y, m):
        return (z % 2, 1 - z // 2 + 2 * c, y, m)

    def flip_y(c, z, y, m):
        return (c, z, 1 - y, m)

    def flip_core(c, z, y, m):
        return (1 - c, z, y, m)

    def flip_x(c, z, y, m):
        return (c, z, y, 1 - m)

    def flip_z(c, z, y, m):
        return (c, z + 1 - 2 * (z % 2), y, m)

    def across_z(c, z, y, m):
        if z // 2 == c:
            return (c, (z + 2) % 4, y, m)
        return (1 - c, z, y, m)

    def across_zy(c, z, y, m):
        c, z, y, m = across_z(c, z, y, m)
        return (c, z, 1 - y, m)

    near = chunk(z // 2, 0, depth)
    signal, near = lax.optimization_barrier((signal, near))
    near_w = move(near, to_near)
    to_context = jnp.where(z // 2 == core, z // 2 == 1, z // 2 == 0)
    shown = (jnp.repeat(keep, block_len, axis=1) == 1) | ~to_context
    source = jnp.where(shown[:, :, None], signal, mask_token[None, None, :])
    mine = lax.dynamic_index_in_dim(source, y, 0, keepdims=False)
    given = lax.dynamic_index_in_dim(source, 1 - y, 0, keepdims=False)
    x_own = jnp.stack([move(mine, across_z), move(given, across_zy)])

    lent = lax.dynamic_slice_in_dim(pred_weight, core * half, half, 0)
    cut = half // 2
    weight_early = move(lent[:cut], flip_x)
    weight_early_c = move(weight_early, flip_core)

    routing = move(
        jnp.stack([keep, target_shard]), lambda c, z, y, m: ((2 * z + y) // 4, (2 * z + y) % 4, c, m)
    )
    hidden = lax.dynamic_index_in_dim(routing[0], y, 0, keepdims=False) == 0
    shard_of = routing[1].reshape(-1)
    blocks = shard_of.shape[0]
    capacity = max(2, 2 * blocks // 8)
    order_ids = jnp.arange(blocks)
    earlier = (shard_of[:, None] == shard_of[None, :]) & (order_ids[:, None] < order_ids[None, :])
    slot = shard_of * capacity + jnp.sum(earlier.astype(jnp.int32), axis=0)
    slot = lax.dynamic_index_in_dim(slot.reshape(sequences, -1), y, 0, keepdims=False)
    slot = jnp.where(hidden, slot, -1)
    slot = lax.dynamic_slice_in_dim(slot, m * (per_range // 2), per_range // 2)
    slot = jnp.repeat(slot, block_len)[:, None]

    far_first, x_own = lax.optimization_barrier((chunk(1 - z // 2, 0, depth // 2), x_own))
    far_first = move(far_first, to_far)
    x_near = move(x_own, flip_z)
    x_across = move(x_own, flip_x)
    far_last, near_w = lax.optimization_barrier(
        (chunk(1 - z // 2, depth // 2, depth // 2), near_w)
    )
    far_last = move(far_last, to_far)
    x_near_across = move(x_near, flip_x)
    late, x_near_across = lax.optimization_barrier((lent[cut:], x_near_across))
    weight_late = move(late, flip_x)
    weight_late_c = move(weight_late, flip_core)

    def edge(own, near):
        found = jnp.where(z % 2 == 1 - core, own, near)
        part = jnp.where(core == 0, 1 - y, y)
        first = jnp.where(core == 0, length - WIN, 0)
        return lax.dynamic_slice(found, (part, first, 0), (1, WIN, half))[0]

    halo = move(jnp.stack([edge(x_own, x_near), edge(x_across, x_near_across)]), flip_core)
    pieces = []
    for piece in (near_w, far_first, far_last):
        piece_y = move(piece, flip_y)
        pieces += [piece, move(piece, flip_core), piece_y, move(piece_y, flip_core)]
    halo, slot = lax.optimization_barrier((halo, slot))
    span = 4 * length + 2 * WIN

    vmem = pl.BlockSpec(memory_space=pltpu.VMEM)
    smem = pl.BlockSpec(memory_space=pltpu.SMEM)
    anywhere = pl.BlockSpec(memory_space=pl.ANY)
    latent = pl.pallas_call(
        encode_kernel,
        out_shape=jax.ShapeDtypeStruct((4, length, wide), jnp.bfloat16),
        in_specs=[smem] + [anywhere] * (5 + PIECES),
        out_specs=vmem,
        scratch_shapes=[
            pltpu.VMEM((span, 2 * half), jnp.bfloat16),
            pltpu.VMEM((3, 2 * half, wide), jnp.bfloat16),
            pltpu.VMEM((4 * length, wide), jnp.bfloat16),
            pltpu.VMEM((span, wide), jnp.bfloat16),
            pltpu.VMEM((span, wide), jnp.bfloat16),
            pltpu.SemaphoreType.DMA((10 + PIECES,)),
        ],
        compiler_params=pltpu.CompilerParams(vmem_limit_bytes=40 * 2**20),
    )(where, x_own, x_across, x_near, x_near_across, halo, *pieces)
    lines = [[4 * i + 2 * j + k for i in range(4) for k in range(2)] for j in range(2)]
    latents = lax.all_to_all(
        latent.reshape(8, length // 2, wide), ("seq", "mdl"),
        split_axis=0, concat_axis=0, tiled=True, axis_index_groups=lines,
    )
    routed = pl.pallas_call(
        predict_kernel,
        out_shape=jax.ShapeDtypeStruct((16, 1, 8 * capacity), jnp.float32),
        in_specs=[smem] + [vmem] * 7,
        out_specs=vmem,
        compiler_params=pltpu.CompilerParams(vmem_limit_bytes=40 * 2**20),
    )(
        where, slot, latents, pred_weight,
        weight_early, weight_early_c, weight_late, weight_late_c,
    )
    arrived = lax.all_to_all(routed, ("seq", "mdl"), split_axis=0, concat_axis=0, tiled=True)
    mine = lax.dynamic_slice_in_dim(arrived[:, 0], capacity * s, capacity, 1)
    summed = jnp.sum(mine.reshape(4, 4, capacity), axis=1)
    return summed.reshape(1, -1) / float(block_len * 2 * half)


def solution(mesh):
    placed = (
        P(None, "seq", "mdl"),
        P("mdl"),
        P(None, "seq"),
        P(None, "seq"),
        P("grp", None, "seq", "mdl"),
        P(None, "mdl"),
    )
    plan = local_lines if mesh.shape["seq"] == 8 else local
    return jax.shard_map(
        plan, mesh=mesh, in_specs=placed, out_specs=P("seq", "grp"), check_vma=False
    )
```

```python
import functools
import math

import jax
import jax.numpy as jnp
from jax import lax
from jax.experimental import pallas as pl
from jax.experimental.pallas import tpu as pltpu
from jax.sharding import PartitionSpec as P

HD = 128
WIN = 64
AXES = ("grp", "seq", "mdl")
PIECES = 8


def padded(x, sides, width):
    for axis, dim in sides:
        count, length = (lax.axis_size(axis), x.shape[dim])
        up = [(i, (i + 1) % count) for i in range(count - 1)]
        down = [(j, i) for i, j in up]
        last = lax.slice_in_dim(x, length - width, length, axis=dim)
        leading = lax.slice_in_dim(x, 0, width, axis=dim)
        before = lax.ppermute(last, axis, up)
        after = lax.ppermute(leading, axis, down)
        x = jnp.concatenate([before, x, after], axis=dim)
    return x


def predict(context, target, live_flags, pred_weight, divisor):
    flat_rows = context.reshape(-1, context.shape[-1])
    wide_rows = lax.all_gather(flat_rows, "mdl", axis=1, tiled=True)
    predicted = jnp.dot(wide_rows, pred_weight, preferred_element_type=jnp.float32)
    residue = predicted - target.reshape(flat_rows.shape).astype(jnp.float32)
    partial_sums = jnp.sum((residue * residue).reshape(live_flags.shape[0], -1), axis=1)
    summed = lax.psum(partial_sums, "mdl")
    return summed / divisor * live_flags


def local(signal, mask_token, keep, target_shard, enc_weight, pred_weight):
    group_index = lax.axis_index("grp")
    seq_index = lax.axis_index("seq")
    shards = lax.axis_size("seq")
    sequences, length, half_width = signal.shape
    per_range = keep.shape[1]
    block_len = length // per_range
    kept_rows = jnp.repeat(keep, block_len, axis=1)[:, :, None]
    masked_in = jnp.where(kept_rows == 1, signal, mask_token[None, None, :])
    source = jnp.where(group_index == 0, masked_in, signal)
    wide_in = lax.all_gather(source, "mdl", axis=2, tiled=True)
    full_width = wide_in.shape[2]
    flat_in = wide_in.reshape(-1, full_width)
    span = length + 2 * WIN
    weight_all = lax.all_gather(enc_weight, "seq", axis=2, tiled=True)[0]
    queries = jnp.dot(flat_in, weight_all[0], preferred_element_type=jnp.float32).astype(
        jnp.bfloat16
    )
    pair_made = jnp.einsum(
        "nd,cde->cne", flat_in, weight_all[1:], preferred_element_type=jnp.float32
    ).astype(jnp.bfloat16)
    own_pairs = pair_made.reshape(2, sequences, length, half_width)
    pair_rows = padded(own_pairs, (("seq", 2),), WIN)
    head_count = half_width // HD
    query_heads = queries.reshape(sequences, length, head_count, HD)
    key_heads = pair_rows[0].reshape(sequences, span, head_count, HD)
    value_heads = pair_rows[1].reshape(sequences, span, head_count, HD)
    query_pos = seq_index * length + jnp.arange(length)
    key_pos = seq_index * length - WIN + jnp.arange(span)
    total_len = length * shards
    in_window = (
        (jnp.abs(query_pos[:, None] - key_pos[None, :]) <= WIN)
        & (key_pos[None, :] >= 0)
        & (key_pos[None, :] < total_len)
    )
    scores = jnp.einsum(
        "sahd,sbhd->shab", query_heads, key_heads, preferred_element_type=jnp.float32
    ) * (1.0 / math.sqrt(HD))
    scores = jnp.where(in_window[None, None], scores, -jnp.inf)
    row_peak = jnp.max(scores, axis=-1, keepdims=True)
    exp_scores = jnp.exp(scores - row_peak)
    attention = (exp_scores / jnp.sum(exp_scores, axis=-1, keepdims=True)).astype(jnp.bfloat16)
    attended = jnp.einsum(
        "shab,sbhd->sahd", attention, value_heads, preferred_element_type=jnp.float32
    ).astype(jnp.bfloat16)
    latent = attended.reshape(sequences * per_range, block_len, half_width)
    blocks_here = latent.shape[0]
    capacity = max(2, 2 * blocks_here // shards)
    slot_count = shards * capacity
    shard_of = target_shard.reshape(-1)
    masked_flag = (keep.reshape(-1) == 0).astype(jnp.float32)
    order_ids = jnp.arange(blocks_here)
    earlier = (shard_of[:, None] == shard_of[None, :]) & (order_ids[:, None] < order_ids[None, :])
    slot_rank = jnp.sum(earlier.astype(jnp.int32), axis=0)
    slot_index = shard_of * capacity + slot_rank
    onehot = slot_index[None, :] == jnp.arange(slot_count)[:, None]
    divisor = float(block_len * full_width)
    halves = lax.all_to_all(latent[None], "grp", split_axis=1, concat_axis=0, tiled=True)
    half_count = blocks_here // 2
    first_block = group_index * half_count
    own_flags = lax.dynamic_slice_in_dim(masked_flag, first_block, half_count)
    losses = predict(halves[0], halves[1], own_flags, pred_weight, divisor)
    spread = lax.dynamic_update_slice_in_dim(
        jnp.zeros((blocks_here,), jnp.float32), losses, first_block, 0
    )
    slotted = jnp.sum(jnp.where(onehot, spread[None, :], 0.0), axis=1).reshape(shards, capacity)
    arrived = lax.all_to_all(slotted, "seq", split_axis=0, concat_axis=0, tiled=True)
    result = lax.psum_scatter(arrived, "grp", scatter_dimension=0, tiled=True)
    return result.reshape(1, -1)


def move(x, target):
    pairs = []
    for c in range(2):
        for s in range(8):
            for m in range(2):
                c2, z2, y2, m2 = target(c, s // 2, s % 2, m)
                pairs.append(((c * 8 + s) * 2 + m, (c2 * 8 + 2 * z2 + y2) * 2 + m2))
    return lax.ppermute(x, AXES, pairs)


def places():
    s = lax.axis_index("seq")
    return lax.axis_index("grp"), s // 2, lax.rem(s, 2), lax.axis_index("mdl")


def prepare_kernel(
    signal_ref, token_ref, keep_ref, weight_ref, pred_ref,
    mine_ref, given_ref, near_ref, far_ref, early_ref, late_ref, sems,
):
    core, z, y, m = places()
    wide = near_ref.shape[2]
    cut = early_ref.shape[0]
    t = lax.rem(z, 2)
    copies = []
    for index, (target, chosen) in enumerate(((near_ref, t), (far_ref, 1 - t))):
        lanes = pl.ds(pl.multiple_of(chosen * wide, 128), wide)
        copies.append((weight_ref.at[0, :, :, lanes], target))
    for index, target in enumerate((early_ref, late_ref)):
        first = pl.multiple_of((2 * core + index) * cut, 128)
        copies.append((pred_ref.at[pl.ds(first, cut), :], target))
    copies = [
        pltpu.make_async_copy(source, target, sems.at[index])
        for index, (source, target) in enumerate(copies)
    ]
    for copy in copies:
        copy.start()
    length = signal_ref.shape[1]
    blocks = keep_ref.shape[1]
    block_len = length // blocks
    row = lax.broadcasted_iota(jnp.int32, (length, blocks), 0)
    first = lax.broadcasted_iota(jnp.int32, (length, blocks), 1) * block_len
    covers = (row >= first) & (row < first + block_len)
    token = token_ref[...].astype(jnp.float32)
    for target, chosen in ((mine_ref, y), (given_ref, 1 - y)):
        kept = jnp.where(covers, keep_ref[pl.ds(chosen, 1), :], 0)
        kept = jnp.sum(kept, axis=1, keepdims=True) + core
        rows = signal_ref[chosen].astype(jnp.float32)
        target[...] = jnp.where(kept > 0, rows, token).astype(target.dtype)
    for copy in copies:
        copy.wait()


def encode_kernel(x_own, x_across, x_near, x_near_across, halo_ref, *refs):
    pieces = refs[:PIECES]
    out_ref, x_buf, w_buf, q_buf, k_buf, v_buf, sems = refs[PIECES:]
    core, z, y, m = places()
    half = x_own.shape[-1]
    rows = x_own.shape[1]
    depth = pieces[0].shape[1]
    wide = pieces[0].shape[2]
    own_rows = 4 * rows
    copies = []
    side = lax.rem(z, 2)
    for piece, near, across in (
        (x_own, 0, 0), (x_across, 0, 1), (x_near, 1, 0), (x_near_across, 1, 1)
    ):
        first = WIN + 2 * rows * (side if near == 0 else 1 - side)
        lane = half * (m if across == 0 else 1 - m)
        for part in range(2):
            copies.append((
                piece.at[part],
                x_buf.at[
                    pl.ds(pl.multiple_of(first + (y if part == 0 else 1 - y) * rows, 64), rows),
                    pl.ds(pl.multiple_of(lane, 128), half),
                ],
            ))
    halo_first = pl.multiple_of((1 - core) * (WIN + own_rows), 64)
    empty_first = pl.multiple_of(core * (WIN + own_rows), 64)
    for across in range(2):
        lane = half * (m if across == 0 else 1 - m)
        copies.append((
            halo_ref.at[across],
            x_buf.at[pl.ds(halo_first, WIN), pl.ds(pl.multiple_of(lane, 128), half)],
        ))
    t = lax.rem(z, 2)
    for index, piece in enumerate(pieces):
        crossed, other = (index // 2) % 2, index % 2
        pos_z = 2 * (core if other == 0 else 1 - core) + (t if index < 4 else 1 - t)
        pos = 2 * pos_z + (y if crossed == 0 else 1 - y)
        copies.append((
            piece, w_buf.at[:, pl.ds(pl.multiple_of(pos * depth, 64), depth), :]
        ))
    started = []
    for index, (source, target) in enumerate(copies):
        copy = pltpu.make_async_copy(source, target, sems.at[index])
        copy.start()
        started.append(copy)
    x_buf[pl.ds(empty_first, WIN), :] = jnp.zeros((WIN, 2 * half), x_buf.dtype)
    for copy in started:
        copy.wait()
    x = x_buf[...]
    q_buf[...] = jnp.dot(
        x[WIN:WIN + own_rows], w_buf[0], preferred_element_type=jnp.float32
    ).astype(q_buf.dtype)
    k_buf[...] = jnp.dot(x, w_buf[1], preferred_element_type=jnp.float32).astype(k_buf.dtype)
    v_buf[...] = jnp.dot(x, w_buf[2], preferred_element_type=jnp.float32).astype(v_buf.dtype)
    keys = rows + 2 * WIN
    a = lax.broadcasted_iota(jnp.int32, (rows, keys), 0)
    b = lax.broadcasted_iota(jnp.int32, (rows, keys), 1)
    band = (b >= a) & (b <= a + 2 * WIN)
    for j in range(4):
        admitted = band
        if j == 0:
            admitted = admitted & (b >= WIN * (1 - core))
        if j == 3:
            admitted = admitted & (b < keys - WIN * core)
        for h in range(wide // HD):
            lanes = slice(h * HD, (h + 1) * HD)
            scores = lax.dot_general(
                q_buf[j * rows:(j + 1) * rows, lanes],
                k_buf[j * rows:j * rows + keys, lanes],
                (((1,), (1,)), ((), ())),
                preferred_element_type=jnp.float32,
            ) * (1.0 / math.sqrt(HD))
            scores = jnp.where(admitted, scores, -jnp.inf)
            peak = jnp.max(scores, axis=-1, keepdims=True)
            exps = jnp.exp(scores - peak)
            attention = (exps / jnp.sum(exps, axis=-1, keepdims=True)).astype(jnp.bfloat16)
            out_ref[j, :, lanes] = jnp.dot(
                attention,
                v_buf[j * rows:j * rows + keys, lanes],
                preferred_element_type=jnp.float32,
            ).astype(out_ref.dtype)


def predict_kernel(slot_ref, lat_ref, own_ref, e0, e1, l0, l1, out_ref):
    core, _, _, m = places()
    wide = lat_ref.shape[2]
    lent = ((e0, e1), (l0, l1))
    total = None
    for side in range(2):
        predicted = None
        for t in range(2):
            for x in range(2):
                if side == 0:
                    source = lat_ref[2 * t + x]
                    weight = own_ref[(2 * x + t) * wide:(2 * x + t + 1) * wide, :]
                else:
                    source = lat_ref[2 * t + (core if x == 0 else 1 - core)]
                    weight = lent[t][x][...]
                term = jnp.dot(source, weight, preferred_element_type=jnp.float32)
                predicted = term if predicted is None else predicted + term
        for t in range(2):
            target = lat_ref[4 + 2 * t + (m if side == 0 else 1 - m)].astype(jnp.float32)
            residue = predicted[:, t * wide:(t + 1) * wide] - target
            for i in range(wide // 128):
                piece = residue[:, i * 128:(i + 1) * 128]
                total = piece * piece if total is None else total + piece * piece
    row_errors = jnp.sum(total, axis=1, keepdims=True)
    rows, slots = total.shape[0], out_ref.shape[2]
    chosen = slot_ref[...] == lax.broadcasted_iota(jnp.int32, (rows, slots), 1)
    routed = jnp.sum(jnp.where(chosen, row_errors, 0.0), axis=0, keepdims=True)
    for i in range(out_ref.shape[0]):
        out_ref[i] = routed


def local_lines(signal, mask_token, keep, target_shard, enc_weight, pred_weight):
    core = lax.axis_index("grp")
    s = lax.axis_index("seq")
    m = lax.axis_index("mdl")
    z, y = s // 2, s % 2
    sequences, length, half = signal.shape
    per_range = keep.shape[1]
    block_len = length // per_range
    depth = enc_weight.shape[2]
    wide = half // 2

    vmem = pl.BlockSpec(memory_space=pltpu.VMEM)
    anywhere = pl.BlockSpec(memory_space=pl.ANY)

    def to_line(c, z, y, m):
        return (z // 2, z % 2 + 2 * c, y, m)

    def to_far(c, z, y, m):
        return (z // 2, 1 - z % 2 + 2 * c, y, m)

    def to_line_y(c, z, y, m):
        return (z // 2, z % 2 + 2 * c, 1 - y, m)

    def flip_y(c, z, y, m):
        return (c, z, 1 - y, m)

    def flip_core(c, z, y, m):
        return (1 - c, z, y, m)

    def flip_x(c, z, y, m):
        return (c, z, y, 1 - m)

    def flip_z(c, z, y, m):
        return (c, z + 1 - 2 * (z % 2), y, m)

    cut = half // 2
    mine, given, near, far, early, late = pl.pallas_call(
        prepare_kernel,
        out_shape=[jax.ShapeDtypeStruct(shape, jnp.bfloat16) for shape in (
            (length, half), (length, half), (3, depth, wide), (3, depth, wide),
            (cut, half), (cut, half),
        )],
        in_specs=[vmem, vmem, vmem, anywhere, anywhere],
        out_specs=[vmem, vmem] + [anywhere] * 4,
        scratch_shapes=[pltpu.SemaphoreType.DMA((4,))],
        compiler_params=pltpu.CompilerParams(vmem_limit_bytes=56 * 2**20),
    )(signal, mask_token[None, :], keep, enc_weight, pred_weight)
    near_w = move(near, to_line)
    x_own = jnp.stack([move(mine, to_line), move(given, to_line_y)])
    weight_early = move(early, flip_x)
    far, _ = lax.optimization_barrier((far, near_w))
    far_w = move(far, to_far)
    x_near = move(x_own, flip_z)
    x_across = move(x_own, flip_x)
    near_y_source, weight_early = lax.optimization_barrier((near_w, weight_early))
    weight_early_c = move(weight_early, flip_core)
    near_y = move(near_y_source, flip_y)
    far_y_source, _ = lax.optimization_barrier((far_w, x_across))
    far_y = move(far_y_source, flip_y)

    routing = move(
        jnp.stack([keep, target_shard]), lambda c, z, y, m: ((2 * z + y) // 4, (2 * z + y) % 4, c, m)
    )
    x_near_source, routing = lax.optimization_barrier((x_near, routing))
    x_near_across = move(x_near_source, flip_x)
    late, _ = lax.optimization_barrier((late, x_near_across))
    weight_late = move(late, flip_x)
    weight_late_c = move(weight_late, flip_core)
    hidden = lax.dynamic_index_in_dim(routing[0], y, 0, keepdims=False) == 0
    shard_of = routing[1].reshape(-1)
    blocks = shard_of.shape[0]
    capacity = max(2, 2 * blocks // 8)
    order_ids = jnp.arange(blocks)
    earlier = (shard_of[:, None] == shard_of[None, :]) & (order_ids[:, None] < order_ids[None, :])
    slot = shard_of * capacity + jnp.sum(earlier.astype(jnp.int32), axis=0)
    slot = lax.dynamic_index_in_dim(slot.reshape(sequences, -1), y, 0, keepdims=False)
    slot = jnp.where(hidden, slot, -1)
    slot = lax.dynamic_slice_in_dim(slot, m * (per_range // 2), per_range // 2)
    slot = jnp.repeat(slot, block_len)[:, None]

    def edge(own, near):
        found = jnp.where(z % 2 == 1 - core, own, near)
        part = jnp.where(core == 0, 1 - y, y)
        first = jnp.where(core == 0, length - WIN, 0)
        return lax.dynamic_slice(found, (part, first, 0), (1, WIN, half))[0]

    halo = move(jnp.stack([edge(x_own, x_near), edge(x_across, x_near_across)]), flip_core)
    pieces = []
    for piece in (near_w, near_y, far_w, far_y):
        pieces += [piece, move(piece, flip_core)]
    span = 4 * length + 2 * WIN

    latent = pl.pallas_call(
        encode_kernel,
        out_shape=jax.ShapeDtypeStruct((4, length, wide), jnp.bfloat16),
        in_specs=[anywhere] * (5 + PIECES),
        out_specs=vmem,
        scratch_shapes=[
            pltpu.VMEM((span, 2 * half), jnp.bfloat16),
            pltpu.VMEM((3, 2 * half, wide), jnp.bfloat16),
            pltpu.VMEM((4 * length, wide), jnp.bfloat16),
            pltpu.VMEM((span, wide), jnp.bfloat16),
            pltpu.VMEM((span, wide), jnp.bfloat16),
            pltpu.SemaphoreType.DMA((10 + PIECES,)),
        ],
        compiler_params=pltpu.CompilerParams(vmem_limit_bytes=56 * 2**20),
    )(x_own, x_across, x_near, x_near_across, halo, *pieces)
    lines = [[4 * i + 2 * j + k for i in range(4) for k in range(2)] for j in range(2)]
    latents = lax.all_to_all(
        latent.reshape(8, length // 2, wide), ("seq", "mdl"),
        split_axis=0, concat_axis=0, tiled=True, axis_index_groups=lines,
    )
    routed = pl.pallas_call(
        predict_kernel,
        out_shape=jax.ShapeDtypeStruct((16, 1, 8 * capacity), jnp.float32),
        in_specs=[vmem] * 7,
        out_specs=vmem,
        compiler_params=pltpu.CompilerParams(vmem_limit_bytes=56 * 2**20),
    )(
        slot, latents, pred_weight,
        weight_early, weight_early_c, weight_late, weight_late_c,
    )
    arrived = lax.all_to_all(routed, ("seq", "mdl"), split_axis=0, concat_axis=0, tiled=True)
    mine = lax.dynamic_slice_in_dim(arrived[:, 0], capacity * s, capacity, 1)
    summed = jnp.sum(mine.reshape(4, 4, capacity), axis=1)
    return summed.reshape(1, -1) / float(block_len * 2 * half)


def solution(mesh):
    placed = (
        P(None, "seq", "mdl"),
        P("mdl"),
        P(None, "seq"),
        P(None, "seq"),
        P("grp", None, "seq", "mdl"),
        P(None, "mdl"),
    )
    plan = local_lines if mesh.shape["seq"] == 8 else local
    return jax.shard_map(
        plan, mesh=mesh, in_specs=placed, out_specs=P("seq", "grp"), check_vma=False
    )
```

```python
import functools
import math

import jax
import jax.numpy as jnp
from jax import lax
from jax.experimental import pallas as pl
from jax.experimental.pallas import tpu as pltpu
from jax.sharding import PartitionSpec as P

HD = 128
WIN = 64
AXES = ("grp", "seq", "mdl")
PIECES = 8


def padded(x, sides, width):
    for axis, dim in sides:
        count, length = (lax.axis_size(axis), x.shape[dim])
        up = [(i, (i + 1) % count) for i in range(count - 1)]
        down = [(j, i) for i, j in up]
        last = lax.slice_in_dim(x, length - width, length, axis=dim)
        leading = lax.slice_in_dim(x, 0, width, axis=dim)
        before = lax.ppermute(last, axis, up)
        after = lax.ppermute(leading, axis, down)
        x = jnp.concatenate([before, x, after], axis=dim)
    return x


def predict(context, target, live_flags, pred_weight, divisor):
    flat_rows = context.reshape(-1, context.shape[-1])
    wide_rows = lax.all_gather(flat_rows, "mdl", axis=1, tiled=True)
    predicted = jnp.dot(wide_rows, pred_weight, preferred_element_type=jnp.float32)
    residue = predicted - target.reshape(flat_rows.shape).astype(jnp.float32)
    partial_sums = jnp.sum((residue * residue).reshape(live_flags.shape[0], -1), axis=1)
    summed = lax.psum(partial_sums, "mdl")
    return summed / divisor * live_flags


def local(signal, mask_token, keep, target_shard, enc_weight, pred_weight):
    group_index = lax.axis_index("grp")
    seq_index = lax.axis_index("seq")
    shards = lax.axis_size("seq")
    sequences, length, half_width = signal.shape
    per_range = keep.shape[1]
    block_len = length // per_range
    kept_rows = jnp.repeat(keep, block_len, axis=1)[:, :, None]
    masked_in = jnp.where(kept_rows == 1, signal, mask_token[None, None, :])
    source = jnp.where(group_index == 0, masked_in, signal)
    wide_in = lax.all_gather(source, "mdl", axis=2, tiled=True)
    full_width = wide_in.shape[2]
    flat_in = wide_in.reshape(-1, full_width)
    span = length + 2 * WIN
    weight_all = lax.all_gather(enc_weight, "seq", axis=2, tiled=True)[0]
    queries = jnp.dot(flat_in, weight_all[0], preferred_element_type=jnp.float32).astype(
        jnp.bfloat16
    )
    pair_made = jnp.einsum(
        "nd,cde->cne", flat_in, weight_all[1:], preferred_element_type=jnp.float32
    ).astype(jnp.bfloat16)
    own_pairs = pair_made.reshape(2, sequences, length, half_width)
    pair_rows = padded(own_pairs, (("seq", 2),), WIN)
    head_count = half_width // HD
    query_heads = queries.reshape(sequences, length, head_count, HD)
    key_heads = pair_rows[0].reshape(sequences, span, head_count, HD)
    value_heads = pair_rows[1].reshape(sequences, span, head_count, HD)
    query_pos = seq_index * length + jnp.arange(length)
    key_pos = seq_index * length - WIN + jnp.arange(span)
    total_len = length * shards
    in_window = (
        (jnp.abs(query_pos[:, None] - key_pos[None, :]) <= WIN)
        & (key_pos[None, :] >= 0)
        & (key_pos[None, :] < total_len)
    )
    scores = jnp.einsum(
        "sahd,sbhd->shab", query_heads, key_heads, preferred_element_type=jnp.float32
    ) * (1.0 / math.sqrt(HD))
    scores = jnp.where(in_window[None, None], scores, -jnp.inf)
    row_peak = jnp.max(scores, axis=-1, keepdims=True)
    exp_scores = jnp.exp(scores - row_peak)
    attention = (exp_scores / jnp.sum(exp_scores, axis=-1, keepdims=True)).astype(jnp.bfloat16)
    attended = jnp.einsum(
        "shab,sbhd->sahd", attention, value_heads, preferred_element_type=jnp.float32
    ).astype(jnp.bfloat16)
    latent = attended.reshape(sequences * per_range, block_len, half_width)
    blocks_here = latent.shape[0]
    capacity = max(2, 2 * blocks_here // shards)
    slot_count = shards * capacity
    shard_of = target_shard.reshape(-1)
    masked_flag = (keep.reshape(-1) == 0).astype(jnp.float32)
    order_ids = jnp.arange(blocks_here)
    earlier = (shard_of[:, None] == shard_of[None, :]) & (order_ids[:, None] < order_ids[None, :])
    slot_rank = jnp.sum(earlier.astype(jnp.int32), axis=0)
    slot_index = shard_of * capacity + slot_rank
    onehot = slot_index[None, :] == jnp.arange(slot_count)[:, None]
    divisor = float(block_len * full_width)
    halves = lax.all_to_all(latent[None], "grp", split_axis=1, concat_axis=0, tiled=True)
    half_count = blocks_here // 2
    first_block = group_index * half_count
    own_flags = lax.dynamic_slice_in_dim(masked_flag, first_block, half_count)
    losses = predict(halves[0], halves[1], own_flags, pred_weight, divisor)
    spread = lax.dynamic_update_slice_in_dim(
        jnp.zeros((blocks_here,), jnp.float32), losses, first_block, 0
    )
    slotted = jnp.sum(jnp.where(onehot, spread[None, :], 0.0), axis=1).reshape(shards, capacity)
    arrived = lax.all_to_all(slotted, "seq", split_axis=0, concat_axis=0, tiled=True)
    result = lax.psum_scatter(arrived, "grp", scatter_dimension=0, tiled=True)
    return result.reshape(1, -1)


def move(x, target):
    pairs = []
    for c in range(2):
        for s in range(8):
            for m in range(2):
                c2, z2, y2, m2 = target(c, s // 2, s % 2, m)
                pairs.append(((c * 8 + s) * 2 + m, (c2 * 8 + 2 * z2 + y2) * 2 + m2))
    return lax.ppermute(x, AXES, pairs)


def places():
    s = lax.axis_index("seq")
    return lax.axis_index("grp"), s // 2, lax.rem(s, 2), lax.axis_index("mdl")


def mask_kernel(signal_ref, token_ref, keep_ref, mine_ref, given_ref):
    core, _, y, _ = places()
    length = signal_ref.shape[1]
    blocks = keep_ref.shape[1]
    block_len = length // blocks
    row = lax.broadcasted_iota(jnp.int32, (length, blocks), 0)
    first = lax.broadcasted_iota(jnp.int32, (length, blocks), 1) * block_len
    covers = (row >= first) & (row < first + block_len)
    token = token_ref[...].astype(jnp.float32).reshape(1, -1)
    for target, chosen in ((mine_ref, y), (given_ref, 1 - y)):
        kept = jnp.where(covers, keep_ref[pl.ds(chosen, 1), :], 0)
        kept = jnp.sum(kept, axis=1, keepdims=True) + core
        rows = signal_ref[chosen].astype(jnp.float32)
        target[...] = jnp.where(kept > 0, rows, token).astype(target.dtype)


def slice_kernel(after_ref, weight_ref, pred_ref, near_ref, far_ref, early_ref, late_ref, sems):
    core, z, _, _ = places()
    wide = near_ref.shape[2]
    cut = early_ref.shape[0]
    t = lax.rem(z, 2)
    copies = []
    for target, chosen in ((near_ref, t), (far_ref, 1 - t)):
        lanes = pl.ds(pl.multiple_of(chosen * wide, 128), wide)
        copies.append((weight_ref.at[0, :, :, lanes], target))
    for index, target in enumerate((early_ref, late_ref)):
        first = pl.multiple_of((2 * core + index) * cut, 128)
        copies.append((pred_ref.at[pl.ds(first, cut), :], target))
    copies = [
        pltpu.make_async_copy(source, target, sems.at[index])
        for index, (source, target) in enumerate(copies)
    ]
    for copy in copies:
        copy.start()
    for copy in copies:
        copy.wait()


def encode_kernel(x_own, x_across, x_near, x_near_across, halo_ref, *refs):
    pieces = refs[:PIECES]
    out_ref, x_buf, w_buf, q_buf, k_buf, v_buf, sems = refs[PIECES:]
    core, z, y, m = places()
    half = x_own.shape[-1]
    rows = x_own.shape[1]
    depth = pieces[0].shape[1]
    wide = pieces[0].shape[2]
    own_rows = 4 * rows
    copies = []
    side = lax.rem(z, 2)
    for piece, near, across in (
        (x_own, 0, 0), (x_across, 0, 1), (x_near, 1, 0), (x_near_across, 1, 1)
    ):
        first = WIN + 2 * rows * (side if near == 0 else 1 - side)
        lane = half * (m if across == 0 else 1 - m)
        for part in range(2):
            copies.append((
                piece.at[part],
                x_buf.at[
                    pl.ds(pl.multiple_of(first + (y if part == 0 else 1 - y) * rows, 64), rows),
                    pl.ds(pl.multiple_of(lane, 128), half),
                ],
            ))
    halo_first = pl.multiple_of((1 - core) * (WIN + own_rows), 64)
    empty_first = pl.multiple_of(core * (WIN + own_rows), 64)
    for across in range(2):
        lane = half * (m if across == 0 else 1 - m)
        copies.append((
            halo_ref.at[across],
            x_buf.at[pl.ds(halo_first, WIN), pl.ds(pl.multiple_of(lane, 128), half)],
        ))
    t = lax.rem(z, 2)
    for index, piece in enumerate(pieces):
        crossed, other = (index // 2) % 2, index % 2
        pos_z = 2 * (core if other == 0 else 1 - core) + (t if index < 4 else 1 - t)
        pos = 2 * pos_z + (y if crossed == 0 else 1 - y)
        copies.append((
            piece, w_buf.at[:, pl.ds(pl.multiple_of(pos * depth, 64), depth), :]
        ))
    started = []
    for index, (source, target) in enumerate(copies):
        copy = pltpu.make_async_copy(source, target, sems.at[index])
        copy.start()
        started.append(copy)
    x_buf[pl.ds(empty_first, WIN), :] = jnp.zeros((WIN, 2 * half), x_buf.dtype)
    for copy in started:
        copy.wait()
    x = x_buf[...]
    q_buf[...] = jnp.dot(
        x[WIN:WIN + own_rows], w_buf[0], preferred_element_type=jnp.float32
    ).astype(q_buf.dtype)
    k_buf[...] = jnp.dot(x, w_buf[1], preferred_element_type=jnp.float32).astype(k_buf.dtype)
    v_buf[...] = jnp.dot(x, w_buf[2], preferred_element_type=jnp.float32).astype(v_buf.dtype)
    keys = rows + 2 * WIN
    a = lax.broadcasted_iota(jnp.int32, (rows, keys), 0)
    b = lax.broadcasted_iota(jnp.int32, (rows, keys), 1)
    band = (b >= a) & (b <= a + 2 * WIN)
    for j in range(4):
        admitted = band
        if j == 0:
            admitted = admitted & (b >= WIN * (1 - core))
        if j == 3:
            admitted = admitted & (b < keys - WIN * core)
        for h in range(wide // HD):
            lanes = slice(h * HD, (h + 1) * HD)
            scores = lax.dot_general(
                q_buf[j * rows:(j + 1) * rows, lanes],
                k_buf[j * rows:j * rows + keys, lanes],
                (((1,), (1,)), ((), ())),
                preferred_element_type=jnp.float32,
            ) * (1.0 / math.sqrt(HD))
            scores = jnp.where(admitted, scores, -jnp.inf)
            peak = jnp.max(scores, axis=-1, keepdims=True)
            exps = jnp.exp(scores - peak)
            attention = (exps / jnp.sum(exps, axis=-1, keepdims=True)).astype(jnp.bfloat16)
            out_ref[j, :, lanes] = jnp.dot(
                attention,
                v_buf[j * rows:j * rows + keys, lanes],
                preferred_element_type=jnp.float32,
            ).astype(out_ref.dtype)


def predict_kernel(slot_ref, lat_ref, own_ref, e0, e1, l0, l1, out_ref):
    core, _, _, m = places()
    wide = lat_ref.shape[2]
    lent = ((e0, e1), (l0, l1))
    total = None
    for side in range(2):
        predicted = None
        for t in range(2):
            for x in range(2):
                if side == 0:
                    source = lat_ref[2 * t + x]
                    weight = own_ref[(2 * x + t) * wide:(2 * x + t + 1) * wide, :]
                else:
                    source = lat_ref[2 * t + (core if x == 0 else 1 - core)]
                    weight = lent[t][x][...]
                term = jnp.dot(source, weight, preferred_element_type=jnp.float32)
                predicted = term if predicted is None else predicted + term
        for t in range(2):
            target = lat_ref[4 + 2 * t + (m if side == 0 else 1 - m)].astype(jnp.float32)
            residue = predicted[:, t * wide:(t + 1) * wide] - target
            for i in range(wide // 128):
                piece = residue[:, i * 128:(i + 1) * 128]
                total = piece * piece if total is None else total + piece * piece
    row_errors = jnp.sum(total, axis=1, keepdims=True)
    rows, slots = total.shape[0], out_ref.shape[2]
    chosen = slot_ref[...] == lax.broadcasted_iota(jnp.int32, (rows, slots), 1)
    routed = jnp.sum(jnp.where(chosen, row_errors, 0.0), axis=0, keepdims=True)
    for i in range(out_ref.shape[0]):
        out_ref[i] = routed


def local_lines(signal, mask_token, keep, target_shard, enc_weight, pred_weight):
    core = lax.axis_index("grp")
    s = lax.axis_index("seq")
    m = lax.axis_index("mdl")
    z, y = s // 2, s % 2
    sequences, length, half = signal.shape
    per_range = keep.shape[1]
    block_len = length // per_range
    depth = enc_weight.shape[2]
    wide = half // 2

    vmem = pl.BlockSpec(memory_space=pltpu.VMEM)
    anywhere = pl.BlockSpec(memory_space=pl.ANY)

    def to_line(c, z, y, m):
        return (z // 2, z % 2 + 2 * c, y, m)

    def to_far(c, z, y, m):
        return (z // 2, 1 - z % 2 + 2 * c, y, m)

    def to_line_y(c, z, y, m):
        return (z // 2, z % 2 + 2 * c, 1 - y, m)

    def flip_y(c, z, y, m):
        return (c, z, 1 - y, m)

    def flip_core(c, z, y, m):
        return (1 - c, z, y, m)

    def flip_x(c, z, y, m):
        return (c, z, y, 1 - m)

    def flip_z(c, z, y, m):
        return (c, z + 1 - 2 * (z % 2), y, m)

    cut = half // 2
    mine, given = pl.pallas_call(
        mask_kernel,
        out_shape=[jax.ShapeDtypeStruct((length, half), jnp.bfloat16)] * 2,
        in_specs=[vmem] * 3,
        out_specs=[vmem] * 2,
    )(signal, mask_token, keep)
    near, far, early, late = pl.pallas_call(
        slice_kernel,
        out_shape=[jax.ShapeDtypeStruct(shape, jnp.bfloat16) for shape in (
            (3, depth, wide), (3, depth, wide), (cut, half), (cut, half),
        )],
        in_specs=[anywhere] * 3,
        out_specs=[vmem] * 4,
        scratch_shapes=[pltpu.SemaphoreType.DMA((4,))],
    )(mine, enc_weight, pred_weight)
    x_own = jnp.stack([move(mine, to_line), move(given, to_line_y)])
    near_w = move(near, to_line)
    weight_early = move(early, flip_x)
    far, x_own = lax.optimization_barrier((far, x_own))
    far_w = move(far, to_far)
    x_near = move(x_own, flip_z)
    x_across = move(x_own, flip_x)
    near_y_source, weight_early = lax.optimization_barrier((near_w, weight_early))
    weight_early_c = move(weight_early, flip_core)
    near_y = move(near_y_source, flip_y)
    routing = move(
        jnp.stack([keep, target_shard]), lambda c, z, y, m: ((2 * z + y) // 4, (2 * z + y) % 4, c, m)
    )
    far_y_source, _, routing = lax.optimization_barrier((far_w, x_across, routing))
    far_y = move(far_y_source, flip_y)
    x_near_across = move(x_near, flip_x)
    late, _ = lax.optimization_barrier((late, x_near_across))
    weight_late = move(late, flip_x)
    weight_late_c = move(weight_late, flip_core)
    hidden = lax.dynamic_index_in_dim(routing[0], y, 0, keepdims=False) == 0
    shard_of = routing[1].reshape(-1)
    blocks = shard_of.shape[0]
    capacity = max(2, 2 * blocks // 8)
    order_ids = jnp.arange(blocks)
    earlier = (shard_of[:, None] == shard_of[None, :]) & (order_ids[:, None] < order_ids[None, :])
    slot = shard_of * capacity + jnp.sum(earlier.astype(jnp.int32), axis=0)
    slot = lax.dynamic_index_in_dim(slot.reshape(sequences, -1), y, 0, keepdims=False)
    slot = jnp.where(hidden, slot, -1)
    slot = lax.dynamic_slice_in_dim(slot, m * (per_range // 2), per_range // 2)
    slot = jnp.repeat(slot, block_len)[:, None]

    def edge(own, near):
        found = jnp.where(z % 2 == 1 - core, own, near)
        part = jnp.where(core == 0, 1 - y, y)
        first = jnp.where(core == 0, length - WIN, 0)
        return lax.dynamic_slice(found, (part, first, 0), (1, WIN, half))[0]

    halo = move(jnp.stack([edge(x_own, x_near), edge(x_across, x_near_across)]), flip_core)
    pieces = []
    for piece in (near_w, near_y, far_w, far_y):
        pieces += [piece, move(piece, flip_core)]
    span = 4 * length + 2 * WIN

    latent = pl.pallas_call(
        encode_kernel,
        out_shape=jax.ShapeDtypeStruct((4, length, wide), jnp.bfloat16),
        in_specs=[anywhere] * (5 + PIECES),
        out_specs=vmem,
        scratch_shapes=[
            pltpu.VMEM((span, 2 * half), jnp.bfloat16),
            pltpu.VMEM((3, 2 * half, wide), jnp.bfloat16),
            pltpu.VMEM((4 * length, wide), jnp.bfloat16),
            pltpu.VMEM((span, wide), jnp.bfloat16),
            pltpu.VMEM((span, wide), jnp.bfloat16),
            pltpu.SemaphoreType.DMA((10 + PIECES,)),
        ],
        compiler_params=pltpu.CompilerParams(vmem_limit_bytes=24 * 2**20),
    )(x_own, x_across, x_near, x_near_across, halo, *pieces)
    lines = [[4 * i + 2 * j + k for i in range(4) for k in range(2)] for j in range(2)]
    latents = lax.all_to_all(
        latent.reshape(8, length // 2, wide), ("seq", "mdl"),
        split_axis=0, concat_axis=0, tiled=True, axis_index_groups=lines,
    )
    routed = pl.pallas_call(
        predict_kernel,
        out_shape=jax.ShapeDtypeStruct((16, 1, 8 * capacity), jnp.float32),
        in_specs=[vmem] * 7,
        out_specs=vmem,
        compiler_params=pltpu.CompilerParams(vmem_limit_bytes=24 * 2**20),
    )(
        slot, latents, pred_weight,
        weight_early, weight_early_c, weight_late, weight_late_c,
    )
    arrived = lax.all_to_all(routed, ("seq", "mdl"), split_axis=0, concat_axis=0, tiled=True)
    mine = lax.dynamic_slice_in_dim(arrived[:, 0], capacity * s, capacity, 1)
    summed = jnp.sum(mine.reshape(4, 4, capacity), axis=1)
    return summed.reshape(1, -1) / float(block_len * 2 * half)


def solution(mesh):
    placed = (
        P(None, "seq", "mdl"),
        P("mdl"),
        P(None, "seq"),
        P(None, "seq"),
        P("grp", None, "seq", "mdl"),
        P(None, "mdl"),
    )
    plan = local_lines if mesh.shape["seq"] == 8 else local
    return jax.shard_map(
        plan, mesh=mesh, in_specs=placed, out_specs=P("seq", "grp"), check_vma=False
    )
```

```python
import functools
import math

import jax
import jax.numpy as jnp
from jax import lax
from jax.experimental import pallas as pl
from jax.experimental.pallas import tpu as pltpu
from jax.sharding import PartitionSpec as P

HD = 128
WIN = 64
AXES = ("grp", "seq", "mdl")
PIECES = 8


def padded(x, sides, width):
    for axis, dim in sides:
        count, length = (lax.axis_size(axis), x.shape[dim])
        up = [(i, (i + 1) % count) for i in range(count - 1)]
        down = [(j, i) for i, j in up]
        last = lax.slice_in_dim(x, length - width, length, axis=dim)
        leading = lax.slice_in_dim(x, 0, width, axis=dim)
        before = lax.ppermute(last, axis, up)
        after = lax.ppermute(leading, axis, down)
        x = jnp.concatenate([before, x, after], axis=dim)
    return x


def predict(context, target, live_flags, pred_weight, divisor):
    flat_rows = context.reshape(-1, context.shape[-1])
    wide_rows = lax.all_gather(flat_rows, "mdl", axis=1, tiled=True)
    predicted = jnp.dot(wide_rows, pred_weight, preferred_element_type=jnp.float32)
    residue = predicted - target.reshape(flat_rows.shape).astype(jnp.float32)
    partial_sums = jnp.sum((residue * residue).reshape(live_flags.shape[0], -1), axis=1)
    summed = lax.psum(partial_sums, "mdl")
    return summed / divisor * live_flags


def local(signal, mask_token, keep, target_shard, enc_weight, pred_weight):
    group_index = lax.axis_index("grp")
    seq_index = lax.axis_index("seq")
    shards = lax.axis_size("seq")
    sequences, length, half_width = signal.shape
    per_range = keep.shape[1]
    block_len = length // per_range
    kept_rows = jnp.repeat(keep, block_len, axis=1)[:, :, None]
    masked_in = jnp.where(kept_rows == 1, signal, mask_token[None, None, :])
    source = jnp.where(group_index == 0, masked_in, signal)
    wide_in = lax.all_gather(source, "mdl", axis=2, tiled=True)
    full_width = wide_in.shape[2]
    flat_in = wide_in.reshape(-1, full_width)
    span = length + 2 * WIN
    weight_all = lax.all_gather(enc_weight, "seq", axis=2, tiled=True)[0]
    queries = jnp.dot(flat_in, weight_all[0], preferred_element_type=jnp.float32).astype(
        jnp.bfloat16
    )
    pair_made = jnp.einsum(
        "nd,cde->cne", flat_in, weight_all[1:], preferred_element_type=jnp.float32
    ).astype(jnp.bfloat16)
    own_pairs = pair_made.reshape(2, sequences, length, half_width)
    pair_rows = padded(own_pairs, (("seq", 2),), WIN)
    head_count = half_width // HD
    query_heads = queries.reshape(sequences, length, head_count, HD)
    key_heads = pair_rows[0].reshape(sequences, span, head_count, HD)
    value_heads = pair_rows[1].reshape(sequences, span, head_count, HD)
    query_pos = seq_index * length + jnp.arange(length)
    key_pos = seq_index * length - WIN + jnp.arange(span)
    total_len = length * shards
    in_window = (
        (jnp.abs(query_pos[:, None] - key_pos[None, :]) <= WIN)
        & (key_pos[None, :] >= 0)
        & (key_pos[None, :] < total_len)
    )
    scores = jnp.einsum(
        "sahd,sbhd->shab", query_heads, key_heads, preferred_element_type=jnp.float32
    ) * (1.0 / math.sqrt(HD))
    scores = jnp.where(in_window[None, None], scores, -jnp.inf)
    row_peak = jnp.max(scores, axis=-1, keepdims=True)
    exp_scores = jnp.exp(scores - row_peak)
    attention = (exp_scores / jnp.sum(exp_scores, axis=-1, keepdims=True)).astype(jnp.bfloat16)
    attended = jnp.einsum(
        "shab,sbhd->sahd", attention, value_heads, preferred_element_type=jnp.float32
    ).astype(jnp.bfloat16)
    latent = attended.reshape(sequences * per_range, block_len, half_width)
    blocks_here = latent.shape[0]
    capacity = max(2, 2 * blocks_here // shards)
    slot_count = shards * capacity
    shard_of = target_shard.reshape(-1)
    masked_flag = (keep.reshape(-1) == 0).astype(jnp.float32)
    order_ids = jnp.arange(blocks_here)
    earlier = (shard_of[:, None] == shard_of[None, :]) & (order_ids[:, None] < order_ids[None, :])
    slot_rank = jnp.sum(earlier.astype(jnp.int32), axis=0)
    slot_index = shard_of * capacity + slot_rank
    onehot = slot_index[None, :] == jnp.arange(slot_count)[:, None]
    divisor = float(block_len * full_width)
    halves = lax.all_to_all(latent[None], "grp", split_axis=1, concat_axis=0, tiled=True)
    half_count = blocks_here // 2
    first_block = group_index * half_count
    own_flags = lax.dynamic_slice_in_dim(masked_flag, first_block, half_count)
    losses = predict(halves[0], halves[1], own_flags, pred_weight, divisor)
    spread = lax.dynamic_update_slice_in_dim(
        jnp.zeros((blocks_here,), jnp.float32), losses, first_block, 0
    )
    slotted = jnp.sum(jnp.where(onehot, spread[None, :], 0.0), axis=1).reshape(shards, capacity)
    arrived = lax.all_to_all(slotted, "seq", split_axis=0, concat_axis=0, tiled=True)
    result = lax.psum_scatter(arrived, "grp", scatter_dimension=0, tiled=True)
    return result.reshape(1, -1)


def move(x, target):
    pairs = []
    for c in range(2):
        for s in range(8):
            for m in range(2):
                c2, z2, y2, m2 = target(c, s // 2, s % 2, m)
                pairs.append(((c * 8 + s) * 2 + m, (c2 * 8 + 2 * z2 + y2) * 2 + m2))
    return lax.ppermute(x, AXES, pairs)


def places():
    s = lax.axis_index("seq")
    return lax.axis_index("grp"), s // 2, lax.rem(s, 2), lax.axis_index("mdl")


def mask_kernel(signal_ref, token_ref, keep_ref, mine_ref, given_ref):
    core, _, y, _ = places()
    length = signal_ref.shape[1]
    blocks = keep_ref.shape[1]
    block_len = length // blocks
    row = lax.broadcasted_iota(jnp.int32, (length, blocks), 0)
    first = lax.broadcasted_iota(jnp.int32, (length, blocks), 1) * block_len
    covers = (row >= first) & (row < first + block_len)
    token = token_ref[...].astype(jnp.float32).reshape(1, -1)
    for target, chosen in ((mine_ref, y), (given_ref, 1 - y)):
        kept = jnp.where(covers, keep_ref[pl.ds(chosen, 1), :], 0)
        kept = jnp.sum(kept, axis=1, keepdims=True) + 1 - core
        rows = signal_ref[chosen].astype(jnp.float32)
        target[...] = jnp.where(kept > 0, rows, token).astype(target.dtype)


def slice_kernel(after_ref, weight_ref, pred_ref, near_ref, far_ref, early_ref, late_ref, sems):
    core, z, _, _ = places()
    wide = near_ref.shape[2]
    cut = early_ref.shape[0]
    t = lax.rem(z, 2)
    copies = []
    for target, chosen in ((near_ref, t), (far_ref, 1 - t)):
        lanes = pl.ds(pl.multiple_of(chosen * wide, 128), wide)
        copies.append((weight_ref.at[0, :, :, lanes], target))
    for index, target in enumerate((early_ref, late_ref)):
        first = pl.multiple_of((2 * core + index) * cut, 128)
        copies.append((pred_ref.at[pl.ds(first, cut), :], target))
    copies = [
        pltpu.make_async_copy(source, target, sems.at[index])
        for index, (source, target) in enumerate(copies)
    ]
    for copy in copies:
        copy.start()
    for copy in copies:
        copy.wait()


def edge_kernel(x_own, x_across, x_near, x_near_across, out_ref, sems):
    core, z, y, _ = places()
    part = jnp.where(core == 0, 1 - y, y)
    first = pl.multiple_of((1 - core) * (x_own.shape[1] - WIN), 64)
    inside = lax.rem(z, 2) == 1 - core

    def fetch(pair):
        copies = [
            pltpu.make_async_copy(
                piece.at[part, pl.ds(first, WIN), :], out_ref.at[index], sems.at[index]
            )
            for index, piece in enumerate(pair)
        ]
        for copy in copies:
            copy.start()
        for copy in copies:
            copy.wait()

    @pl.when(inside)
    def _():
        fetch((x_own, x_across))

    @pl.when(jnp.logical_not(inside))
    def _():
        fetch((x_near, x_near_across))


def encode_kernel(x_own, x_across, x_near, x_near_across, halo_ref, *refs):
    pieces = refs[:PIECES]
    out_ref, x_buf, w_buf, q_buf, k_buf, v_buf, sems = refs[PIECES:]
    core, z, y, m = places()
    half = x_own.shape[-1]
    rows = x_own.shape[1]
    depth = pieces[0].shape[1]
    wide = pieces[0].shape[2]
    own_rows = 4 * rows
    copies = []
    side = lax.rem(z, 2)
    for piece, near, across in (
        (x_own, 0, 0), (x_across, 0, 1), (x_near, 1, 0), (x_near_across, 1, 1)
    ):
        first = WIN + 2 * rows * (side if near == 0 else 1 - side)
        lane = half * (m if across == 0 else 1 - m)
        for part in range(2):
            copies.append((
                piece.at[part],
                x_buf.at[
                    pl.ds(pl.multiple_of(first + (y if part == 0 else 1 - y) * rows, 64), rows),
                    pl.ds(pl.multiple_of(lane, 128), half),
                ],
            ))
    halo_first = pl.multiple_of((1 - core) * (WIN + own_rows), 64)
    empty_first = pl.multiple_of(core * (WIN + own_rows), 64)
    for across in range(2):
        lane = half * (m if across == 0 else 1 - m)
        copies.append((
            halo_ref.at[across],
            x_buf.at[pl.ds(halo_first, WIN), pl.ds(pl.multiple_of(lane, 128), half)],
        ))
    t = lax.rem(z, 2)
    for index, piece in enumerate(pieces):
        crossed, other = (index // 2) % 2, index % 2
        low = core if (other == 0) == (index >= 4) else 1 - core
        pos_z = 2 * low + (t if index < 4 else 1 - t)
        pos = 2 * pos_z + (y if crossed == 0 else 1 - y)
        copies.append((
            piece, w_buf.at[:, pl.ds(pl.multiple_of(pos * depth, 64), depth), :]
        ))
    started = []
    for index, (source, target) in enumerate(copies):
        copy = pltpu.make_async_copy(source, target, sems.at[index])
        copy.start()
        started.append(copy)
    x_buf[pl.ds(empty_first, WIN), :] = jnp.zeros((WIN, 2 * half), x_buf.dtype)
    for copy in started:
        copy.wait()
    x = x_buf[...]
    q_buf[...] = jnp.dot(
        x[WIN:WIN + own_rows], w_buf[0], preferred_element_type=jnp.float32
    ).astype(q_buf.dtype)
    k_buf[...] = jnp.dot(x, w_buf[1], preferred_element_type=jnp.float32).astype(k_buf.dtype)
    v_buf[...] = jnp.dot(x, w_buf[2], preferred_element_type=jnp.float32).astype(v_buf.dtype)
    keys = rows + 2 * WIN
    a = lax.broadcasted_iota(jnp.int32, (rows, keys), 0)
    b = lax.broadcasted_iota(jnp.int32, (rows, keys), 1)
    band = (b >= a) & (b <= a + 2 * WIN)
    for j in range(4):
        admitted = band
        if j == 0:
            admitted = admitted & (b >= WIN * (1 - core))
        if j == 3:
            admitted = admitted & (b < keys - WIN * core)
        for h in range(wide // HD):
            lanes = slice(h * HD, (h + 1) * HD)
            scores = lax.dot_general(
                q_buf[j * rows:(j + 1) * rows, lanes],
                k_buf[j * rows:j * rows + keys, lanes],
                (((1,), (1,)), ((), ())),
                preferred_element_type=jnp.float32,
            ) * (1.0 / math.sqrt(HD))
            scores = jnp.where(admitted, scores, -jnp.inf)
            peak = jnp.max(scores, axis=-1, keepdims=True)
            exps = jnp.exp(scores - peak)
            attention = (exps / jnp.sum(exps, axis=-1, keepdims=True)).astype(jnp.bfloat16)
            out_ref[j, :, lanes] = jnp.dot(
                attention,
                v_buf[j * rows:j * rows + keys, lanes],
                preferred_element_type=jnp.float32,
            ).astype(out_ref.dtype)


def predict_kernel(slot_ref, lat_ref, own_ref, e0, e1, l0, l1, out_ref):
    core, _, _, m = places()
    wide = lat_ref.shape[2]
    lent = ((e0, e1), (l0, l1))
    total = None
    for side in range(2):
        predicted = None
        for t in range(2):
            for x in range(2):
                if side == 0:
                    source = lat_ref[2 * t + x]
                    weight = own_ref[(2 * x + t) * wide:(2 * x + t + 1) * wide, :]
                else:
                    source = lat_ref[2 * t + (core if x == 0 else 1 - core)]
                    weight = lent[t][x][...]
                term = jnp.dot(source, weight, preferred_element_type=jnp.float32)
                predicted = term if predicted is None else predicted + term
        for t in range(2):
            target = lat_ref[4 + 2 * t + (m if side == 0 else 1 - m)].astype(jnp.float32)
            residue = predicted[:, t * wide:(t + 1) * wide] - target
            for i in range(wide // 128):
                piece = residue[:, i * 128:(i + 1) * 128]
                total = piece * piece if total is None else total + piece * piece
    row_errors = jnp.sum(total, axis=1, keepdims=True)
    rows, slots = total.shape[0], out_ref.shape[2]
    chosen = slot_ref[...] == lax.broadcasted_iota(jnp.int32, (rows, slots), 1)
    routed = jnp.sum(jnp.where(chosen, row_errors, 0.0), axis=0, keepdims=True)
    for i in range(out_ref.shape[0]):
        out_ref[i] = routed


def local_lines(signal, mask_token, keep, target_shard, enc_weight, pred_weight):
    core = lax.axis_index("grp")
    s = lax.axis_index("seq")
    m = lax.axis_index("mdl")
    z, y = s // 2, s % 2
    sequences, length, half = signal.shape
    per_range = keep.shape[1]
    block_len = length // per_range
    depth = enc_weight.shape[2]
    wide = half // 2

    vmem = pl.BlockSpec(memory_space=pltpu.VMEM)
    anywhere = pl.BlockSpec(memory_space=pl.ANY)

    def to_near(c, z, y, m):
        return (1 - z // 2, z % 2 + 2 * c, y, m)

    def to_far(c, z, y, m):
        return (z // 2, 1 - z % 2 + 2 * c, y, m)

    def across_z(c, z, y, m):
        if z // 2 == c:
            return (c, (z + 2) % 4, y, m)
        return (1 - c, z, y, m)

    def across_zy(c, z, y, m):
        c, z, y, m = across_z(c, z, y, m)
        return (c, z, 1 - y, m)

    def flip_y(c, z, y, m):
        return (c, z, 1 - y, m)

    def flip_core(c, z, y, m):
        return (1 - c, z, y, m)

    def flip_x(c, z, y, m):
        return (c, z, y, 1 - m)

    def flip_z(c, z, y, m):
        return (c, z + 1 - 2 * (z % 2), y, m)

    cut = half // 2
    mine, given = pl.pallas_call(
        mask_kernel,
        out_shape=[jax.ShapeDtypeStruct((length, half), jnp.bfloat16)] * 2,
        in_specs=[vmem] * 3,
        out_specs=[vmem] * 2,
    )(signal, mask_token, keep)
    near, far, early, late = pl.pallas_call(
        slice_kernel,
        out_shape=[jax.ShapeDtypeStruct(shape, jnp.bfloat16) for shape in (
            (3, depth, wide), (3, depth, wide), (cut, half), (cut, half),
        )],
        in_specs=[anywhere] * 3,
        out_specs=[vmem] * 4,
        scratch_shapes=[pltpu.SemaphoreType.DMA((4,))],
    )(mine, enc_weight, pred_weight)
    x_own = jnp.stack([move(mine, across_z), move(given, across_zy)])
    near_w = move(near, to_near)
    weight_early = move(early, flip_x)
    far, x_own = lax.optimization_barrier((far, x_own))
    far_w = move(far, to_far)
    x_near = move(x_own, flip_z)
    x_across = move(x_own, flip_x)
    near_y_source, weight_early = lax.optimization_barrier((near_w, weight_early))
    weight_early_c = move(weight_early, flip_core)
    near_y = move(near_y_source, flip_y)
    routing = move(
        jnp.stack([keep, target_shard]), lambda c, z, y, m: ((2 * z + y) // 4, (2 * z + y) % 4, c, m)
    )
    far_y_source, _, routing = lax.optimization_barrier((far_w, x_across, routing))
    far_y = move(far_y_source, flip_y)
    x_near_across = move(x_near, flip_x)
    late, _ = lax.optimization_barrier((late, x_near_across))
    weight_late = move(late, flip_x)
    weight_late_c = move(weight_late, flip_core)
    hidden = lax.dynamic_index_in_dim(routing[0], y, 0, keepdims=False) == 0
    shard_of = routing[1].reshape(-1)
    blocks = shard_of.shape[0]
    capacity = max(2, 2 * blocks // 8)
    order_ids = jnp.arange(blocks)
    earlier = (shard_of[:, None] == shard_of[None, :]) & (order_ids[:, None] < order_ids[None, :])
    slot = shard_of * capacity + jnp.sum(earlier.astype(jnp.int32), axis=0)
    slot = lax.dynamic_index_in_dim(slot.reshape(sequences, -1), y, 0, keepdims=False)
    slot = jnp.where(hidden, slot, -1)
    slot = lax.dynamic_slice_in_dim(slot, m * (per_range // 2), per_range // 2)
    slot = jnp.repeat(slot, block_len)[:, None]

    edges = pl.pallas_call(
        edge_kernel,
        out_shape=jax.ShapeDtypeStruct((2, WIN, half), jnp.bfloat16),
        in_specs=[anywhere] * 4,
        out_specs=vmem,
        scratch_shapes=[pltpu.SemaphoreType.DMA((2,))],
    )(x_own, x_across, x_near, x_near_across)
    halo = move(edges, flip_core)
    pieces = []
    for piece in (near_w, near_y, far_w, far_y):
        pieces += [piece, move(piece, flip_core)]
    span = 4 * length + 2 * WIN

    latent = pl.pallas_call(
        encode_kernel,
        out_shape=jax.ShapeDtypeStruct((4, length, wide), jnp.bfloat16),
        in_specs=[anywhere] * (5 + PIECES),
        out_specs=vmem,
        scratch_shapes=[
            pltpu.VMEM((span, 2 * half), jnp.bfloat16),
            pltpu.VMEM((3, 2 * half, wide), jnp.bfloat16),
            pltpu.VMEM((4 * length, wide), jnp.bfloat16),
            pltpu.VMEM((span, wide), jnp.bfloat16),
            pltpu.VMEM((span, wide), jnp.bfloat16),
            pltpu.SemaphoreType.DMA((10 + PIECES,)),
        ],
        compiler_params=pltpu.CompilerParams(vmem_limit_bytes=24 * 2**20),
    )(x_own, x_across, x_near, x_near_across, halo, *pieces)
    lines = [[4 * i + 2 * j + k for i in range(4) for k in range(2)] for j in range(2)]
    latents = lax.all_to_all(
        latent.reshape(8, length // 2, wide), ("seq", "mdl"),
        split_axis=0, concat_axis=0, tiled=True, axis_index_groups=lines,
    )
    routed = pl.pallas_call(
        predict_kernel,
        out_shape=jax.ShapeDtypeStruct((16, 1, 8 * capacity), jnp.float32),
        in_specs=[vmem] * 7,
        out_specs=vmem,
        compiler_params=pltpu.CompilerParams(vmem_limit_bytes=24 * 2**20),
    )(
        slot, latents, pred_weight,
        weight_early, weight_early_c, weight_late, weight_late_c,
    )
    arrived = lax.all_to_all(routed, ("seq", "mdl"), split_axis=0, concat_axis=0, tiled=True)
    mine = lax.dynamic_slice_in_dim(arrived[:, 0], capacity * s, capacity, 1)
    summed = jnp.sum(mine.reshape(4, 4, capacity), axis=1)
    return summed.reshape(1, -1) / float(block_len * 2 * half)


def solution(mesh):
    placed = (
        P(None, "seq", "mdl"),
        P("mdl"),
        P(None, "seq"),
        P(None, "seq"),
        P("grp", None, "seq", "mdl"),
        P(None, "mdl"),
    )
    plan = local_lines if mesh.shape["seq"] == 8 else local
    return jax.shard_map(
        plan, mesh=mesh, in_specs=placed, out_specs=P("seq", "grp"), check_vma=False
    )
```

```python
import functools
import math

import jax
import jax.numpy as jnp
from jax import lax
from jax.experimental import pallas as pl
from jax.experimental.pallas import tpu as pltpu
from jax.sharding import PartitionSpec as P

HD = 128
WIN = 64
AXES = ("grp", "seq", "mdl")
PIECES = 8


def padded(x, sides, width):
    for axis, dim in sides:
        count, length = (lax.axis_size(axis), x.shape[dim])
        up = [(i, (i + 1) % count) for i in range(count - 1)]
        down = [(j, i) for i, j in up]
        last = lax.slice_in_dim(x, length - width, length, axis=dim)
        leading = lax.slice_in_dim(x, 0, width, axis=dim)
        before = lax.ppermute(last, axis, up)
        after = lax.ppermute(leading, axis, down)
        x = jnp.concatenate([before, x, after], axis=dim)
    return x


def predict(context, target, live_flags, pred_weight, divisor):
    flat_rows = context.reshape(-1, context.shape[-1])
    wide_rows = lax.all_gather(flat_rows, "mdl", axis=1, tiled=True)
    predicted = jnp.dot(wide_rows, pred_weight, preferred_element_type=jnp.float32)
    residue = predicted - target.reshape(flat_rows.shape).astype(jnp.float32)
    partial_sums = jnp.sum((residue * residue).reshape(live_flags.shape[0], -1), axis=1)
    summed = lax.psum(partial_sums, "mdl")
    return summed / divisor * live_flags


def local(signal, mask_token, keep, target_shard, enc_weight, pred_weight):
    group_index = lax.axis_index("grp")
    seq_index = lax.axis_index("seq")
    shards = lax.axis_size("seq")
    sequences, length, half_width = signal.shape
    per_range = keep.shape[1]
    block_len = length // per_range
    kept_rows = jnp.repeat(keep, block_len, axis=1)[:, :, None]
    masked_in = jnp.where(kept_rows == 1, signal, mask_token[None, None, :])
    source = jnp.where(group_index == 0, masked_in, signal)
    wide_in = lax.all_gather(source, "mdl", axis=2, tiled=True)
    full_width = wide_in.shape[2]
    flat_in = wide_in.reshape(-1, full_width)
    span = length + 2 * WIN
    weight_all = lax.all_gather(enc_weight, "seq", axis=2, tiled=True)[0]
    queries = jnp.dot(flat_in, weight_all[0], preferred_element_type=jnp.float32).astype(
        jnp.bfloat16
    )
    pair_made = jnp.einsum(
        "nd,cde->cne", flat_in, weight_all[1:], preferred_element_type=jnp.float32
    ).astype(jnp.bfloat16)
    own_pairs = pair_made.reshape(2, sequences, length, half_width)
    pair_rows = padded(own_pairs, (("seq", 2),), WIN)
    head_count = half_width // HD
    query_heads = queries.reshape(sequences, length, head_count, HD)
    key_heads = pair_rows[0].reshape(sequences, span, head_count, HD)
    value_heads = pair_rows[1].reshape(sequences, span, head_count, HD)
    query_pos = seq_index * length + jnp.arange(length)
    key_pos = seq_index * length - WIN + jnp.arange(span)
    total_len = length * shards
    in_window = (
        (jnp.abs(query_pos[:, None] - key_pos[None, :]) <= WIN)
        & (key_pos[None, :] >= 0)
        & (key_pos[None, :] < total_len)
    )
    scores = jnp.einsum(
        "sahd,sbhd->shab", query_heads, key_heads, preferred_element_type=jnp.float32
    ) * (1.0 / math.sqrt(HD))
    scores = jnp.where(in_window[None, None], scores, -jnp.inf)
    row_peak = jnp.max(scores, axis=-1, keepdims=True)
    exp_scores = jnp.exp(scores - row_peak)
    attention = (exp_scores / jnp.sum(exp_scores, axis=-1, keepdims=True)).astype(jnp.bfloat16)
    attended = jnp.einsum(
        "shab,sbhd->sahd", attention, value_heads, preferred_element_type=jnp.float32
    ).astype(jnp.bfloat16)
    latent = attended.reshape(sequences * per_range, block_len, half_width)
    blocks_here = latent.shape[0]
    capacity = max(2, 2 * blocks_here // shards)
    slot_count = shards * capacity
    shard_of = target_shard.reshape(-1)
    masked_flag = (keep.reshape(-1) == 0).astype(jnp.float32)
    order_ids = jnp.arange(blocks_here)
    earlier = (shard_of[:, None] == shard_of[None, :]) & (order_ids[:, None] < order_ids[None, :])
    slot_rank = jnp.sum(earlier.astype(jnp.int32), axis=0)
    slot_index = shard_of * capacity + slot_rank
    onehot = slot_index[None, :] == jnp.arange(slot_count)[:, None]
    divisor = float(block_len * full_width)
    halves = lax.all_to_all(latent[None], "grp", split_axis=1, concat_axis=0, tiled=True)
    half_count = blocks_here // 2
    first_block = group_index * half_count
    own_flags = lax.dynamic_slice_in_dim(masked_flag, first_block, half_count)
    losses = predict(halves[0], halves[1], own_flags, pred_weight, divisor)
    spread = lax.dynamic_update_slice_in_dim(
        jnp.zeros((blocks_here,), jnp.float32), losses, first_block, 0
    )
    slotted = jnp.sum(jnp.where(onehot, spread[None, :], 0.0), axis=1).reshape(shards, capacity)
    arrived = lax.all_to_all(slotted, "seq", split_axis=0, concat_axis=0, tiled=True)
    result = lax.psum_scatter(arrived, "grp", scatter_dimension=0, tiled=True)
    return result.reshape(1, -1)


def move(x, target):
    pairs = []
    for c in range(2):
        for s in range(8):
            for m in range(2):
                c2, z2, y2, m2 = target(c, s // 2, s % 2, m)
                pairs.append(((c * 8 + s) * 2 + m, (c2 * 8 + 2 * z2 + y2) * 2 + m2))
    return lax.ppermute(x, AXES, pairs)


def places():
    s = lax.axis_index("seq")
    return lax.axis_index("grp"), s // 2, lax.rem(s, 2), lax.axis_index("mdl")


def mask_kernel(signal_ref, token_ref, keep_ref, mine_ref, given_ref):
    core, _, y, _ = places()
    length = signal_ref.shape[1]
    blocks = keep_ref.shape[1]
    block_len = length // blocks
    row = lax.broadcasted_iota(jnp.int32, (length, blocks), 0)
    first = lax.broadcasted_iota(jnp.int32, (length, blocks), 1) * block_len
    covers = (row >= first) & (row < first + block_len)
    token = token_ref[...].astype(jnp.float32).reshape(1, -1)
    for target, chosen in ((mine_ref, y), (given_ref, 1 - y)):
        kept = jnp.where(covers, keep_ref[pl.ds(chosen, 1), :], 0)
        kept = jnp.sum(kept, axis=1, keepdims=True) + 1 - core
        rows = signal_ref[chosen].astype(jnp.float32)
        target[...] = jnp.where(kept > 0, rows, token).astype(target.dtype)


def slice_kernel(after_ref, weight_ref, pred_ref, near_ref, far_ref, early_ref, late_ref, sems):
    core, z, _, _ = places()
    wide = near_ref.shape[2]
    cut = early_ref.shape[0]
    t = lax.rem(z, 2)
    copies = []
    for target, chosen in ((near_ref, t), (far_ref, 1 - t)):
        lanes = pl.ds(pl.multiple_of(chosen * wide, 128), wide)
        copies.append((weight_ref.at[0, :, :, lanes], target))
    for index, target in enumerate((early_ref, late_ref)):
        first = pl.multiple_of((2 * core + index) * cut, 128)
        copies.append((pred_ref.at[pl.ds(first, cut), :], target))
    copies = [
        pltpu.make_async_copy(source, target, sems.at[index])
        for index, (source, target) in enumerate(copies)
    ]
    for copy in copies:
        copy.start()
    for copy in copies:
        copy.wait()


def encode_kernel(x_own, x_across, x_near, x_near_across, halo_ref, *refs):
    pieces = refs[:PIECES]
    out_ref, x_buf, w_buf, q_buf, k_buf, v_buf, sems = refs[PIECES:]
    core, z, y, m = places()
    half = x_own.shape[-1]
    rows = x_own.shape[1]
    depth = pieces[0].shape[1]
    wide = pieces[0].shape[2]
    own_rows = 4 * rows
    copies = []
    side = lax.rem(z, 2)
    for piece, near, across in (
        (x_own, 0, 0), (x_across, 0, 1), (x_near, 1, 0), (x_near_across, 1, 1)
    ):
        first = WIN + 2 * rows * (side if near == 0 else 1 - side)
        lane = half * (m if across == 0 else 1 - m)
        for part in range(2):
            copies.append((
                piece.at[part],
                x_buf.at[
                    pl.ds(pl.multiple_of(first + (y if part == 0 else 1 - y) * rows, 64), rows),
                    pl.ds(pl.multiple_of(lane, 128), half),
                ],
            ))
    halo_first = pl.multiple_of((1 - core) * (WIN + own_rows), 64)
    empty_first = pl.multiple_of(core * (WIN + own_rows), 64)
    for across in range(2):
        lane = half * (m if across == 0 else 1 - m)
        copies.append((
            halo_ref.at[across],
            x_buf.at[pl.ds(halo_first, WIN), pl.ds(pl.multiple_of(lane, 128), half)],
        ))
    t = lax.rem(z, 2)
    for index, piece in enumerate(pieces):
        crossed, other = (index // 2) % 2, index % 2
        low = core if (other == 0) == (index >= 4) else 1 - core
        pos_z = 2 * low + (t if index < 4 else 1 - t)
        pos = 2 * pos_z + (y if crossed == 0 else 1 - y)
        copies.append((
            piece, w_buf.at[:, pl.ds(pl.multiple_of(pos * depth, 64), depth), :]
        ))
    started = []
    for index, (source, target) in enumerate(copies):
        copy = pltpu.make_async_copy(source, target, sems.at[index])
        copy.start()
        started.append(copy)
    x_buf[pl.ds(empty_first, WIN), :] = jnp.zeros((WIN, 2 * half), x_buf.dtype)
    for copy in started:
        copy.wait()
    x = x_buf[...]
    q_buf[...] = jnp.dot(
        x[WIN:WIN + own_rows], w_buf[0], preferred_element_type=jnp.float32
    ).astype(q_buf.dtype)
    k_buf[...] = jnp.dot(x, w_buf[1], preferred_element_type=jnp.float32).astype(k_buf.dtype)
    v_buf[...] = jnp.dot(x, w_buf[2], preferred_element_type=jnp.float32).astype(v_buf.dtype)
    keys = rows + 2 * WIN
    a = lax.broadcasted_iota(jnp.int32, (rows, keys), 0)
    b = lax.broadcasted_iota(jnp.int32, (rows, keys), 1)
    band = (b >= a) & (b <= a + 2 * WIN)
    for j in range(4):
        admitted = band
        if j == 0:
            admitted = admitted & (b >= WIN * (1 - core))
        if j == 3:
            admitted = admitted & (b < keys - WIN * core)
        for h in range(wide // HD):
            lanes = slice(h * HD, (h + 1) * HD)
            scores = lax.dot_general(
                q_buf[j * rows:(j + 1) * rows, lanes],
                k_buf[j * rows:j * rows + keys, lanes],
                (((1,), (1,)), ((), ())),
                preferred_element_type=jnp.float32,
            ) * (1.0 / math.sqrt(HD))
            scores = jnp.where(admitted, scores, -jnp.inf)
            peak = jnp.max(scores, axis=-1, keepdims=True)
            exps = jnp.exp(scores - peak)
            attention = (exps / jnp.sum(exps, axis=-1, keepdims=True)).astype(jnp.bfloat16)
            out_ref[j, :, lanes] = jnp.dot(
                attention,
                v_buf[j * rows:j * rows + keys, lanes],
                preferred_element_type=jnp.float32,
            ).astype(out_ref.dtype)


def predict_kernel(slot_ref, lat_ref, own_ref, e0, e1, l0, l1, out_ref):
    core, _, _, m = places()
    wide = lat_ref.shape[2]
    lent = ((e0, e1), (l0, l1))
    total = None
    for side in range(2):
        predicted = None
        for t in range(2):
            for x in range(2):
                if side == 0:
                    source = lat_ref[2 * t + x]
                    weight = own_ref[(2 * x + t) * wide:(2 * x + t + 1) * wide, :]
                else:
                    source = lat_ref[2 * t + (core if x == 0 else 1 - core)]
                    weight = lent[t][x][...]
                term = jnp.dot(source, weight, preferred_element_type=jnp.float32)
                predicted = term if predicted is None else predicted + term
        for t in range(2):
            target = lat_ref[4 + 2 * t + (m if side == 0 else 1 - m)].astype(jnp.float32)
            residue = predicted[:, t * wide:(t + 1) * wide] - target
            for i in range(wide // 128):
                piece = residue[:, i * 128:(i + 1) * 128]
                total = piece * piece if total is None else total + piece * piece
    row_errors = jnp.sum(total, axis=1, keepdims=True)
    rows, slots = total.shape[0], out_ref.shape[2]
    chosen = slot_ref[...] == lax.broadcasted_iota(jnp.int32, (rows, slots), 1)
    routed = jnp.sum(jnp.where(chosen, row_errors, 0.0), axis=0, keepdims=True)
    for i in range(out_ref.shape[0]):
        out_ref[i] = routed


def local_lines(signal, mask_token, keep, target_shard, enc_weight, pred_weight):
    core = lax.axis_index("grp")
    s = lax.axis_index("seq")
    m = lax.axis_index("mdl")
    z, y = s // 2, s % 2
    sequences, length, half = signal.shape
    per_range = keep.shape[1]
    block_len = length // per_range
    depth = enc_weight.shape[2]
    wide = half // 2

    vmem = pl.BlockSpec(memory_space=pltpu.VMEM)
    anywhere = pl.BlockSpec(memory_space=pl.ANY)

    def to_near(c, z, y, m):
        return (1 - z // 2, z % 2 + 2 * c, y, m)

    def to_far(c, z, y, m):
        return (z // 2, 1 - z % 2 + 2 * c, y, m)

    def across_z(c, z, y, m):
        if z // 2 == c:
            return (c, (z + 2) % 4, y, m)
        return (1 - c, z, y, m)

    def across_zy(c, z, y, m):
        c, z, y, m = across_z(c, z, y, m)
        return (c, z, 1 - y, m)

    def flip_y(c, z, y, m):
        return (c, z, 1 - y, m)

    def flip_core(c, z, y, m):
        return (1 - c, z, y, m)

    def flip_x(c, z, y, m):
        return (c, z, y, 1 - m)

    def flip_z(c, z, y, m):
        return (c, z + 1 - 2 * (z % 2), y, m)

    cut = half // 2
    mine, given = pl.pallas_call(
        mask_kernel,
        out_shape=[jax.ShapeDtypeStruct((length, half), jnp.bfloat16)] * 2,
        in_specs=[vmem] * 3,
        out_specs=[vmem] * 2,
    )(signal, mask_token, keep)
    near, far, early, late = pl.pallas_call(
        slice_kernel,
        out_shape=[jax.ShapeDtypeStruct(shape, jnp.bfloat16) for shape in (
            (3, depth, wide), (3, depth, wide), (cut, half), (cut, half),
        )],
        in_specs=[anywhere] * 3,
        out_specs=[vmem] * 4,
        scratch_shapes=[pltpu.SemaphoreType.DMA((4,))],
    )(mine, enc_weight, pred_weight)
    x_own = jnp.stack([move(mine, across_z), move(given, across_zy)])
    routing = move(
        jnp.stack([keep, target_shard]), lambda c, z, y, m: ((2 * z + y) // 4, (2 * z + y) % 4, c, m)
    )
    near, routing = lax.optimization_barrier((near, routing))
    near_w = move(near, to_near)
    weight_early = move(early, flip_x)
    x_near = move(x_own, flip_z)
    x_across = move(x_own, flip_x)
    far, _ = lax.optimization_barrier((far, near_w))
    far_w = move(far, to_far)
    near_y = move(near_w, flip_y)
    far_y_source, _, weight_early = lax.optimization_barrier((far_w, x_across, weight_early))
    far_y = move(far_y_source, flip_y)
    weight_early_c = move(weight_early, flip_core)
    x_near_across = move(x_near, flip_x)
    late, _ = lax.optimization_barrier((late, x_near_across))
    weight_late = move(late, flip_x)
    weight_late_c = move(weight_late, flip_core)
    hidden = lax.dynamic_index_in_dim(routing[0], y, 0, keepdims=False) == 0
    shard_of = routing[1].reshape(-1)
    blocks = shard_of.shape[0]
    capacity = max(2, 2 * blocks // 8)
    order_ids = jnp.arange(blocks)
    earlier = (shard_of[:, None] == shard_of[None, :]) & (order_ids[:, None] < order_ids[None, :])
    slot = shard_of * capacity + jnp.sum(earlier.astype(jnp.int32), axis=0)
    slot = lax.dynamic_index_in_dim(slot.reshape(sequences, -1), y, 0, keepdims=False)
    slot = jnp.where(hidden, slot, -1)
    slot = lax.dynamic_slice_in_dim(slot, m * (per_range // 2), per_range // 2)
    slot = jnp.repeat(slot, block_len)[:, None]

    def edge(own, near):
        found = jnp.where(z % 2 == 1 - core, own, near)
        part = jnp.where(core == 0, 1 - y, y)
        first = jnp.where(core == 0, length - WIN, 0)
        return lax.dynamic_slice(found, (part, first, 0), (1, WIN, half))[0]

    halo = move(jnp.stack([edge(x_own, x_near), edge(x_across, x_near_across)]), flip_core)
    pieces = []
    for piece in (near_w, near_y, far_w, far_y):
        pieces += [piece, move(piece, flip_core)]
    span = 4 * length + 2 * WIN

    latent = pl.pallas_call(
        encode_kernel,
        out_shape=jax.ShapeDtypeStruct((4, length, wide), jnp.bfloat16),
        in_specs=[anywhere] * (5 + PIECES),
        out_specs=vmem,
        scratch_shapes=[
            pltpu.VMEM((span, 2 * half), jnp.bfloat16),
            pltpu.VMEM((3, 2 * half, wide), jnp.bfloat16),
            pltpu.VMEM((4 * length, wide), jnp.bfloat16),
            pltpu.VMEM((span, wide), jnp.bfloat16),
            pltpu.VMEM((span, wide), jnp.bfloat16),
            pltpu.SemaphoreType.DMA((10 + PIECES,)),
        ],
        compiler_params=pltpu.CompilerParams(vmem_limit_bytes=24 * 2**20),
    )(x_own, x_across, x_near, x_near_across, halo, *pieces)
    lines = [[4 * i + 2 * j + k for i in range(4) for k in range(2)] for j in range(2)]
    latents = lax.all_to_all(
        latent.reshape(8, length // 2, wide), ("seq", "mdl"),
        split_axis=0, concat_axis=0, tiled=True, axis_index_groups=lines,
    )
    routed = pl.pallas_call(
        predict_kernel,
        out_shape=jax.ShapeDtypeStruct((16, 1, 8 * capacity), jnp.float32),
        in_specs=[vmem] * 7,
        out_specs=vmem,
        compiler_params=pltpu.CompilerParams(vmem_limit_bytes=24 * 2**20),
    )(
        slot, latents, pred_weight,
        weight_early, weight_early_c, weight_late, weight_late_c,
    )
    arrived = lax.all_to_all(routed, ("seq", "mdl"), split_axis=0, concat_axis=0, tiled=True)
    mine = lax.dynamic_slice_in_dim(arrived[:, 0], capacity * s, capacity, 1)
    summed = jnp.sum(mine.reshape(4, 4, capacity), axis=1)
    return summed.reshape(1, -1) / float(block_len * 2 * half)


def solution(mesh):
    placed = (
        P(None, "seq", "mdl"),
        P("mdl"),
        P(None, "seq"),
        P(None, "seq"),
        P("grp", None, "seq", "mdl"),
        P(None, "mdl"),
    )
    plan = local_lines if mesh.shape["seq"] == 8 else local
    return jax.shard_map(
        plan, mesh=mesh, in_specs=placed, out_specs=P("seq", "grp"), check_vma=False
    )
```

```python
import functools
import math

import jax
import jax.numpy as jnp
from jax import lax
from jax.experimental import pallas as pl
from jax.experimental.pallas import tpu as pltpu
from jax.sharding import PartitionSpec as P

HD = 128
WIN = 64
AXES = ("grp", "seq", "mdl")
PIECES = 8


def padded(x, sides, width):
    for axis, dim in sides:
        count, length = (lax.axis_size(axis), x.shape[dim])
        up = [(i, (i + 1) % count) for i in range(count - 1)]
        down = [(j, i) for i, j in up]
        last = lax.slice_in_dim(x, length - width, length, axis=dim)
        leading = lax.slice_in_dim(x, 0, width, axis=dim)
        before = lax.ppermute(last, axis, up)
        after = lax.ppermute(leading, axis, down)
        x = jnp.concatenate([before, x, after], axis=dim)
    return x


def predict(context, target, live_flags, pred_weight, divisor):
    flat_rows = context.reshape(-1, context.shape[-1])
    wide_rows = lax.all_gather(flat_rows, "mdl", axis=1, tiled=True)
    predicted = jnp.dot(wide_rows, pred_weight, preferred_element_type=jnp.float32)
    residue = predicted - target.reshape(flat_rows.shape).astype(jnp.float32)
    partial_sums = jnp.sum((residue * residue).reshape(live_flags.shape[0], -1), axis=1)
    summed = lax.psum(partial_sums, "mdl")
    return summed / divisor * live_flags


def local(signal, mask_token, keep, target_shard, enc_weight, pred_weight):
    group_index = lax.axis_index("grp")
    seq_index = lax.axis_index("seq")
    shards = lax.axis_size("seq")
    sequences, length, half_width = signal.shape
    per_range = keep.shape[1]
    block_len = length // per_range
    kept_rows = jnp.repeat(keep, block_len, axis=1)[:, :, None]
    masked_in = jnp.where(kept_rows == 1, signal, mask_token[None, None, :])
    source = jnp.where(group_index == 0, masked_in, signal)
    wide_in = lax.all_gather(source, "mdl", axis=2, tiled=True)
    full_width = wide_in.shape[2]
    flat_in = wide_in.reshape(-1, full_width)
    span = length + 2 * WIN
    weight_all = lax.all_gather(enc_weight, "seq", axis=2, tiled=True)[0]
    queries = jnp.dot(flat_in, weight_all[0], preferred_element_type=jnp.float32).astype(
        jnp.bfloat16
    )
    pair_made = jnp.einsum(
        "nd,cde->cne", flat_in, weight_all[1:], preferred_element_type=jnp.float32
    ).astype(jnp.bfloat16)
    own_pairs = pair_made.reshape(2, sequences, length, half_width)
    pair_rows = padded(own_pairs, (("seq", 2),), WIN)
    head_count = half_width // HD
    query_heads = queries.reshape(sequences, length, head_count, HD)
    key_heads = pair_rows[0].reshape(sequences, span, head_count, HD)
    value_heads = pair_rows[1].reshape(sequences, span, head_count, HD)
    query_pos = seq_index * length + jnp.arange(length)
    key_pos = seq_index * length - WIN + jnp.arange(span)
    total_len = length * shards
    in_window = (
        (jnp.abs(query_pos[:, None] - key_pos[None, :]) <= WIN)
        & (key_pos[None, :] >= 0)
        & (key_pos[None, :] < total_len)
    )
    scores = jnp.einsum(
        "sahd,sbhd->shab", query_heads, key_heads, preferred_element_type=jnp.float32
    ) * (1.0 / math.sqrt(HD))
    scores = jnp.where(in_window[None, None], scores, -jnp.inf)
    row_peak = jnp.max(scores, axis=-1, keepdims=True)
    exp_scores = jnp.exp(scores - row_peak)
    attention = (exp_scores / jnp.sum(exp_scores, axis=-1, keepdims=True)).astype(jnp.bfloat16)
    attended = jnp.einsum(
        "shab,sbhd->sahd", attention, value_heads, preferred_element_type=jnp.float32
    ).astype(jnp.bfloat16)
    latent = attended.reshape(sequences * per_range, block_len, half_width)
    blocks_here = latent.shape[0]
    capacity = max(2, 2 * blocks_here // shards)
    slot_count = shards * capacity
    shard_of = target_shard.reshape(-1)
    masked_flag = (keep.reshape(-1) == 0).astype(jnp.float32)
    order_ids = jnp.arange(blocks_here)
    earlier = (shard_of[:, None] == shard_of[None, :]) & (order_ids[:, None] < order_ids[None, :])
    slot_rank = jnp.sum(earlier.astype(jnp.int32), axis=0)
    slot_index = shard_of * capacity + slot_rank
    onehot = slot_index[None, :] == jnp.arange(slot_count)[:, None]
    divisor = float(block_len * full_width)
    halves = lax.all_to_all(latent[None], "grp", split_axis=1, concat_axis=0, tiled=True)
    half_count = blocks_here // 2
    first_block = group_index * half_count
    own_flags = lax.dynamic_slice_in_dim(masked_flag, first_block, half_count)
    losses = predict(halves[0], halves[1], own_flags, pred_weight, divisor)
    spread = lax.dynamic_update_slice_in_dim(
        jnp.zeros((blocks_here,), jnp.float32), losses, first_block, 0
    )
    slotted = jnp.sum(jnp.where(onehot, spread[None, :], 0.0), axis=1).reshape(shards, capacity)
    arrived = lax.all_to_all(slotted, "seq", split_axis=0, concat_axis=0, tiled=True)
    result = lax.psum_scatter(arrived, "grp", scatter_dimension=0, tiled=True)
    return result.reshape(1, -1)


def move(x, target):
    pairs = []
    for c in range(2):
        for s in range(8):
            for m in range(2):
                c2, z2, y2, m2 = target(c, s // 2, s % 2, m)
                pairs.append(((c * 8 + s) * 2 + m, (c2 * 8 + 2 * z2 + y2) * 2 + m2))
    return lax.ppermute(x, AXES, pairs)


def places():
    s = lax.axis_index("seq")
    return lax.axis_index("grp"), s // 2, lax.rem(s, 2), lax.axis_index("mdl")


def mask_kernel(signal_ref, token_ref, keep_ref, mine_ref, given_ref):
    core, _, y, _ = places()
    length = signal_ref.shape[1]
    blocks = keep_ref.shape[1]
    block_len = length // blocks
    row = lax.broadcasted_iota(jnp.int32, (length, blocks), 0)
    first = lax.broadcasted_iota(jnp.int32, (length, blocks), 1) * block_len
    covers = (row >= first) & (row < first + block_len)
    token = token_ref[...].astype(jnp.float32).reshape(1, -1)
    for target, chosen in ((mine_ref, y), (given_ref, 1 - y)):
        kept = jnp.where(covers, keep_ref[pl.ds(chosen, 1), :], 0)
        kept = jnp.sum(kept, axis=1, keepdims=True) + 1 - core
        rows = signal_ref[chosen].astype(jnp.float32)
        target[...] = jnp.where(kept > 0, rows, token).astype(target.dtype)


def slice_kernel(after_ref, weight_ref, pred_ref, near_ref, far_ref, early_ref, late_ref, sems):
    core, z, _, _ = places()
    wide = near_ref.shape[2]
    cut = early_ref.shape[0]
    t = lax.rem(z, 2)
    copies = []
    for target, chosen in ((near_ref, t), (far_ref, 1 - t)):
        lanes = pl.ds(pl.multiple_of(chosen * wide, 128), wide)
        copies.append((weight_ref.at[0, :, :, lanes], target))
    for index, target in enumerate((early_ref, late_ref)):
        first = pl.multiple_of((2 * core + index) * cut, 128)
        copies.append((pred_ref.at[pl.ds(first, cut), :], target))
    copies = [
        pltpu.make_async_copy(source, target, sems.at[index])
        for index, (source, target) in enumerate(copies)
    ]
    for copy in copies:
        copy.start()
    for copy in copies:
        copy.wait()


def encode_kernel(x_own, x_across, x_near, x_near_across, halo_ref, *refs):
    pieces = refs[:PIECES]
    out_ref, x_buf, w_buf, q_buf, k_buf, v_buf, sems = refs[PIECES:]
    core, z, y, m = places()
    half = x_own.shape[-1]
    rows = x_own.shape[1]
    depth = pieces[0].shape[1]
    wide = pieces[0].shape[2]
    own_rows = 4 * rows
    copies = []
    side = lax.rem(z, 2)
    for piece, near, across in (
        (x_own, 0, 0), (x_across, 0, 1), (x_near, 1, 0), (x_near_across, 1, 1)
    ):
        first = WIN + 2 * rows * (side if near == 0 else 1 - side)
        lane = half * (m if across == 0 else 1 - m)
        for part in range(2):
            copies.append((
                piece.at[part],
                x_buf.at[
                    pl.ds(pl.multiple_of(first + (y if part == 0 else 1 - y) * rows, 64), rows),
                    pl.ds(pl.multiple_of(lane, 128), half),
                ],
            ))
    halo_first = pl.multiple_of((1 - core) * (WIN + own_rows), 64)
    empty_first = pl.multiple_of(core * (WIN + own_rows), 64)
    for across in range(2):
        lane = half * (m if across == 0 else 1 - m)
        copies.append((
            halo_ref.at[across],
            x_buf.at[pl.ds(halo_first, WIN), pl.ds(pl.multiple_of(lane, 128), half)],
        ))
    t = lax.rem(z, 2)
    for index, piece in enumerate(pieces):
        crossed, other = (index // 2) % 2, index % 2
        low = core if (other == 0) == (index >= 4) else 1 - core
        pos_z = 2 * low + (t if index < 4 else 1 - t)
        pos = 2 * pos_z + (y if crossed == 0 else 1 - y)
        copies.append((
            piece, w_buf.at[:, pl.ds(pl.multiple_of(pos * depth, 64), depth), :]
        ))
    started = []
    for index, (source, target) in enumerate(copies):
        copy = pltpu.make_async_copy(source, target, sems.at[index])
        copy.start()
        started.append(copy)
    x_buf[pl.ds(empty_first, WIN), :] = jnp.zeros((WIN, 2 * half), x_buf.dtype)
    for copy in started:
        copy.wait()
    x = x_buf[...]
    q_buf[...] = jnp.dot(
        x[WIN:WIN + own_rows], w_buf[0], preferred_element_type=jnp.float32
    ).astype(q_buf.dtype)
    k_buf[...] = jnp.dot(x, w_buf[1], preferred_element_type=jnp.float32).astype(k_buf.dtype)
    v_buf[...] = jnp.dot(x, w_buf[2], preferred_element_type=jnp.float32).astype(v_buf.dtype)
    keys = rows + 2 * WIN
    a = lax.broadcasted_iota(jnp.int32, (rows, keys), 0)
    b = lax.broadcasted_iota(jnp.int32, (rows, keys), 1)
    band = (b >= a) & (b <= a + 2 * WIN)
    for j in range(4):
        admitted = band
        if j == 0:
            admitted = admitted & (b >= WIN * (1 - core))
        if j == 3:
            admitted = admitted & (b < keys - WIN * core)
        for h in range(wide // HD):
            lanes = slice(h * HD, (h + 1) * HD)
            scores = lax.dot_general(
                q_buf[j * rows:(j + 1) * rows, lanes],
                k_buf[j * rows:j * rows + keys, lanes],
                (((1,), (1,)), ((), ())),
                preferred_element_type=jnp.float32,
            ) * (1.0 / math.sqrt(HD))
            scores = jnp.where(admitted, scores, -jnp.inf)
            peak = jnp.max(scores, axis=-1, keepdims=True)
            exps = jnp.exp(scores - peak)
            attention = (exps / jnp.sum(exps, axis=-1, keepdims=True)).astype(jnp.bfloat16)
            out_ref[j, :, lanes] = jnp.dot(
                attention,
                v_buf[j * rows:j * rows + keys, lanes],
                preferred_element_type=jnp.float32,
            ).astype(out_ref.dtype)


def predict_kernel(slot_ref, lat_ref, own_ref, e0, e1, l0, l1, out_ref):
    core, _, _, m = places()
    wide = lat_ref.shape[2]
    lent = ((e0, e1), (l0, l1))
    total = None
    for side in range(2):
        predicted = None
        for t in range(2):
            for x in range(2):
                if side == 0:
                    source = lat_ref[2 * t + x]
                    weight = own_ref[(2 * x + t) * wide:(2 * x + t + 1) * wide, :]
                else:
                    source = lat_ref[2 * t + (core if x == 0 else 1 - core)]
                    weight = lent[t][x][...]
                term = jnp.dot(source, weight, preferred_element_type=jnp.float32)
                predicted = term if predicted is None else predicted + term
        for t in range(2):
            target = lat_ref[4 + 2 * t + (m if side == 0 else 1 - m)].astype(jnp.float32)
            residue = predicted[:, t * wide:(t + 1) * wide] - target
            for i in range(wide // 128):
                piece = residue[:, i * 128:(i + 1) * 128]
                total = piece * piece if total is None else total + piece * piece
    row_errors = jnp.sum(total, axis=1, keepdims=True)
    rows, slots = total.shape[0], out_ref.shape[2]
    chosen = slot_ref[...] == lax.broadcasted_iota(jnp.int32, (rows, slots), 1)
    routed = jnp.sum(jnp.where(chosen, row_errors, 0.0), axis=0, keepdims=True)
    for i in range(out_ref.shape[0]):
        out_ref[i] = routed


def local_lines(signal, mask_token, keep, target_shard, enc_weight, pred_weight):
    core = lax.axis_index("grp")
    s = lax.axis_index("seq")
    m = lax.axis_index("mdl")
    z, y = s // 2, s % 2
    sequences, length, half = signal.shape
    per_range = keep.shape[1]
    block_len = length // per_range
    depth = enc_weight.shape[2]
    wide = half // 2

    vmem = pl.BlockSpec(memory_space=pltpu.VMEM)
    anywhere = pl.BlockSpec(memory_space=pl.ANY)

    def to_near(c, z, y, m):
        return (1 - z // 2, z % 2 + 2 * c, y, m)

    def to_far(c, z, y, m):
        return (z // 2, 1 - z % 2 + 2 * c, y, m)

    def across_z(c, z, y, m):
        if z // 2 == c:
            return (c, (z + 2) % 4, y, m)
        return (1 - c, z, y, m)

    def across_zy(c, z, y, m):
        c, z, y, m = across_z(c, z, y, m)
        return (c, z, 1 - y, m)

    def flip_y(c, z, y, m):
        return (c, z, 1 - y, m)

    def flip_core(c, z, y, m):
        return (1 - c, z, y, m)

    def flip_x(c, z, y, m):
        return (c, z, y, 1 - m)

    def flip_z(c, z, y, m):
        return (c, z + 1 - 2 * (z % 2), y, m)

    cut = half // 2
    mine, given = pl.pallas_call(
        mask_kernel,
        out_shape=[jax.ShapeDtypeStruct((length, half), jnp.bfloat16)] * 2,
        in_specs=[vmem] * 3,
        out_specs=[vmem] * 2,
    )(signal, mask_token, keep)
    near, far, early, late = pl.pallas_call(
        slice_kernel,
        out_shape=[jax.ShapeDtypeStruct(shape, jnp.bfloat16) for shape in (
            (3, depth, wide), (3, depth, wide), (cut, half), (cut, half),
        )],
        in_specs=[anywhere] * 3,
        out_specs=[vmem] * 4,
        scratch_shapes=[pltpu.SemaphoreType.DMA((4,))],
    )(mine, enc_weight, pred_weight)
    first, second = move(mine, across_z), move(given, across_zy)
    small = jnp.stack([keep, target_shard])
    small, _ = lax.optimization_barrier((small, mine))
    routing = move(small, lambda c, z, y, m: ((2 * z + y) // 4, (2 * z + y) % 4, c, m))
    near, routing, first, second = lax.optimization_barrier((near, routing, first, second))
    near_w = move(near, to_near)
    x_own = jnp.stack([first, second])
    x_near = move(x_own, flip_z)
    x_across = move(x_own, flip_x)
    weight_early = move(early, flip_x)
    far, near_w, x_across = lax.optimization_barrier((far, near_w, x_across))
    far_w = move(far, to_far)
    near_y = move(near_w, flip_y)
    x_near_across = move(x_near, flip_x)
    far_y_source, weight_early, near_y = lax.optimization_barrier((far_w, weight_early, near_y))
    far_y = move(far_y_source, flip_y)
    weight_early_c = move(weight_early, flip_core)
    late, _ = lax.optimization_barrier((late, x_near_across))
    weight_late = move(late, flip_x)
    weight_late_c = move(weight_late, flip_core)
    hidden = lax.dynamic_index_in_dim(routing[0], y, 0, keepdims=False) == 0
    shard_of = routing[1].reshape(-1)
    blocks = shard_of.shape[0]
    capacity = max(2, 2 * blocks // 8)
    order_ids = jnp.arange(blocks)
    earlier = (shard_of[:, None] == shard_of[None, :]) & (order_ids[:, None] < order_ids[None, :])
    slot = shard_of * capacity + jnp.sum(earlier.astype(jnp.int32), axis=0)
    slot = lax.dynamic_index_in_dim(slot.reshape(sequences, -1), y, 0, keepdims=False)
    slot = jnp.where(hidden, slot, -1)
    slot = lax.dynamic_slice_in_dim(slot, m * (per_range // 2), per_range // 2)
    slot = jnp.repeat(slot, block_len)[:, None]

    def edge(own, near):
        found = jnp.where(z % 2 == 1 - core, own, near)
        part = jnp.where(core == 0, 1 - y, y)
        first = jnp.where(core == 0, length - WIN, 0)
        return lax.dynamic_slice(found, (part, first, 0), (1, WIN, half))[0]

    halo = move(jnp.stack([edge(x_own, x_near), edge(x_across, x_near_across)]), flip_core)
    pieces = []
    for piece in (near_w, near_y, far_w, far_y):
        pieces += [piece, move(piece, flip_core)]
    span = 4 * length + 2 * WIN

    latent = pl.pallas_call(
        encode_kernel,
        out_shape=jax.ShapeDtypeStruct((4, length, wide), jnp.bfloat16),
        in_specs=[anywhere] * (5 + PIECES),
        out_specs=vmem,
        scratch_shapes=[
            pltpu.VMEM((span, 2 * half), jnp.bfloat16),
            pltpu.VMEM((3, 2 * half, wide), jnp.bfloat16),
            pltpu.VMEM((4 * length, wide), jnp.bfloat16),
            pltpu.VMEM((span, wide), jnp.bfloat16),
            pltpu.VMEM((span, wide), jnp.bfloat16),
            pltpu.SemaphoreType.DMA((10 + PIECES,)),
        ],
        compiler_params=pltpu.CompilerParams(vmem_limit_bytes=24 * 2**20),
    )(x_own, x_across, x_near, x_near_across, halo, *pieces)
    lines = [[4 * i + 2 * j + k for i in range(4) for k in range(2)] for j in range(2)]
    latents = lax.all_to_all(
        latent.reshape(8, length // 2, wide), ("seq", "mdl"),
        split_axis=0, concat_axis=0, tiled=True, axis_index_groups=lines,
    )
    routed = pl.pallas_call(
        predict_kernel,
        out_shape=jax.ShapeDtypeStruct((16, 1, 8 * capacity), jnp.float32),
        in_specs=[vmem] * 7,
        out_specs=vmem,
        compiler_params=pltpu.CompilerParams(vmem_limit_bytes=24 * 2**20),
    )(
        slot, latents, pred_weight,
        weight_early, weight_early_c, weight_late, weight_late_c,
    )
    arrived = lax.all_to_all(routed, ("seq", "mdl"), split_axis=0, concat_axis=0, tiled=True)
    mine = lax.dynamic_slice_in_dim(arrived[:, 0], capacity * s, capacity, 1)
    summed = jnp.sum(mine.reshape(4, 4, capacity), axis=1)
    return summed.reshape(1, -1) / float(block_len * 2 * half)


def solution(mesh):
    placed = (
        P(None, "seq", "mdl"),
        P("mdl"),
        P(None, "seq"),
        P(None, "seq"),
        P("grp", None, "seq", "mdl"),
        P(None, "mdl"),
    )
    plan = local_lines if mesh.shape["seq"] == 8 else local
    return jax.shard_map(
        plan, mesh=mesh, in_specs=placed, out_specs=P("seq", "grp"), check_vma=False
    )
```

```python
import functools
import math

import jax
import jax.numpy as jnp
from jax import lax
from jax.experimental import pallas as pl
from jax.experimental.pallas import tpu as pltpu
from jax.sharding import PartitionSpec as P

HD = 128
WIN = 64
AXES = ("grp", "seq", "mdl")
PIECES = 8
INFO = 16


def padded(x, sides, width):
    for axis, dim in sides:
        count, length = (lax.axis_size(axis), x.shape[dim])
        up = [(i, (i + 1) % count) for i in range(count - 1)]
        down = [(j, i) for i, j in up]
        last = lax.slice_in_dim(x, length - width, length, axis=dim)
        leading = lax.slice_in_dim(x, 0, width, axis=dim)
        before = lax.ppermute(last, axis, up)
        after = lax.ppermute(leading, axis, down)
        x = jnp.concatenate([before, x, after], axis=dim)
    return x


def predict(context, target, live_flags, pred_weight, divisor):
    flat_rows = context.reshape(-1, context.shape[-1])
    wide_rows = lax.all_gather(flat_rows, "mdl", axis=1, tiled=True)
    predicted = jnp.dot(wide_rows, pred_weight, preferred_element_type=jnp.float32)
    residue = predicted - target.reshape(flat_rows.shape).astype(jnp.float32)
    partial_sums = jnp.sum((residue * residue).reshape(live_flags.shape[0], -1), axis=1)
    summed = lax.psum(partial_sums, "mdl")
    return summed / divisor * live_flags


def local(signal, mask_token, keep, target_shard, enc_weight, pred_weight):
    group_index = lax.axis_index("grp")
    seq_index = lax.axis_index("seq")
    shards = lax.axis_size("seq")
    sequences, length, half_width = signal.shape
    per_range = keep.shape[1]
    block_len = length // per_range
    kept_rows = jnp.repeat(keep, block_len, axis=1)[:, :, None]
    masked_in = jnp.where(kept_rows == 1, signal, mask_token[None, None, :])
    source = jnp.where(group_index == 0, masked_in, signal)
    wide_in = lax.all_gather(source, "mdl", axis=2, tiled=True)
    full_width = wide_in.shape[2]
    flat_in = wide_in.reshape(-1, full_width)
    span = length + 2 * WIN
    weight_all = lax.all_gather(enc_weight, "seq", axis=2, tiled=True)[0]
    queries = jnp.dot(flat_in, weight_all[0], preferred_element_type=jnp.float32).astype(
        jnp.bfloat16
    )
    pair_made = jnp.einsum(
        "nd,cde->cne", flat_in, weight_all[1:], preferred_element_type=jnp.float32
    ).astype(jnp.bfloat16)
    own_pairs = pair_made.reshape(2, sequences, length, half_width)
    pair_rows = padded(own_pairs, (("seq", 2),), WIN)
    head_count = half_width // HD
    query_heads = queries.reshape(sequences, length, head_count, HD)
    key_heads = pair_rows[0].reshape(sequences, span, head_count, HD)
    value_heads = pair_rows[1].reshape(sequences, span, head_count, HD)
    query_pos = seq_index * length + jnp.arange(length)
    key_pos = seq_index * length - WIN + jnp.arange(span)
    total_len = length * shards
    in_window = (
        (jnp.abs(query_pos[:, None] - key_pos[None, :]) <= WIN)
        & (key_pos[None, :] >= 0)
        & (key_pos[None, :] < total_len)
    )
    scores = jnp.einsum(
        "sahd,sbhd->shab", query_heads, key_heads, preferred_element_type=jnp.float32
    ) * (1.0 / math.sqrt(HD))
    scores = jnp.where(in_window[None, None], scores, -jnp.inf)
    row_peak = jnp.max(scores, axis=-1, keepdims=True)
    exp_scores = jnp.exp(scores - row_peak)
    attention = (exp_scores / jnp.sum(exp_scores, axis=-1, keepdims=True)).astype(jnp.bfloat16)
    attended = jnp.einsum(
        "shab,sbhd->sahd", attention, value_heads, preferred_element_type=jnp.float32
    ).astype(jnp.bfloat16)
    latent = attended.reshape(sequences * per_range, block_len, half_width)
    blocks_here = latent.shape[0]
    capacity = max(2, 2 * blocks_here // shards)
    slot_count = shards * capacity
    shard_of = target_shard.reshape(-1)
    masked_flag = (keep.reshape(-1) == 0).astype(jnp.float32)
    order_ids = jnp.arange(blocks_here)
    earlier = (shard_of[:, None] == shard_of[None, :]) & (order_ids[:, None] < order_ids[None, :])
    slot_rank = jnp.sum(earlier.astype(jnp.int32), axis=0)
    slot_index = shard_of * capacity + slot_rank
    onehot = slot_index[None, :] == jnp.arange(slot_count)[:, None]
    divisor = float(block_len * full_width)
    halves = lax.all_to_all(latent[None], "grp", split_axis=1, concat_axis=0, tiled=True)
    half_count = blocks_here // 2
    first_block = group_index * half_count
    own_flags = lax.dynamic_slice_in_dim(masked_flag, first_block, half_count)
    losses = predict(halves[0], halves[1], own_flags, pred_weight, divisor)
    spread = lax.dynamic_update_slice_in_dim(
        jnp.zeros((blocks_here,), jnp.float32), losses, first_block, 0
    )
    slotted = jnp.sum(jnp.where(onehot, spread[None, :], 0.0), axis=1).reshape(shards, capacity)
    arrived = lax.all_to_all(slotted, "seq", split_axis=0, concat_axis=0, tiled=True)
    result = lax.psum_scatter(arrived, "grp", scatter_dimension=0, tiled=True)
    return result.reshape(1, -1)


def move(x, target):
    pairs = []
    for c in range(2):
        for s in range(8):
            for m in range(2):
                c2, z2, y2, m2 = target(c, s // 2, s % 2, m)
                pairs.append(((c * 8 + s) * 2 + m, (c2 * 8 + 2 * z2 + y2) * 2 + m2))
    return lax.ppermute(x, AXES, pairs)


def places():
    s = lax.axis_index("seq")
    return lax.axis_index("grp"), s // 2, lax.rem(s, 2), lax.axis_index("mdl")


def mask_kernel(signal_ref, token_ref, keep_ref, shard_ref, mine_ref, given_ref):
    core, _, y, _ = places()
    length = signal_ref.shape[1]
    blocks = keep_ref.shape[1]
    block_len = length // blocks
    row = lax.broadcasted_iota(jnp.int32, (length, blocks), 0)
    first = lax.broadcasted_iota(jnp.int32, (length, blocks), 1) * block_len
    covers = (row >= first) & (row < first + block_len)
    token = token_ref[...].astype(jnp.float32).reshape(1, -1)
    words = jnp.concatenate([shard_ref[0:1, :], shard_ref[1:2, :], keep_ref[0:1, :], keep_ref[1:2, :]], axis=1)
    words = jnp.broadcast_to(words.astype(jnp.float32), (INFO, 4 * blocks)).astype(mine_ref.dtype)
    for target, chosen in ((mine_ref, y), (given_ref, 1 - y)):
        kept = jnp.where(covers, keep_ref[pl.ds(chosen, 1), :], 0)
        kept = jnp.sum(kept, axis=1, keepdims=True) + 1 - core
        rows = signal_ref[chosen].astype(jnp.float32)
        target[0:length, :] = jnp.where(kept > 0, rows, token).astype(target.dtype)
        target[length:, 0:4 * blocks] = words
        target[length:, 4 * blocks:] = jnp.zeros((INFO, target.shape[1] - 4 * blocks), target.dtype)


def slice_kernel(after_ref, weight_ref, pred_ref, near_ref, far_ref, lent_ref, sems):
    core, z, _, _ = places()
    wide = near_ref.shape[2]
    count = lent_ref.shape[0]
    t = lax.rem(z, 2)
    first = pl.multiple_of(core * count, 128)
    copies = [(pred_ref.at[pl.ds(first, count), :], lent_ref)]
    for target, chosen in ((near_ref, t), (far_ref, 1 - t)):
        lanes = pl.ds(pl.multiple_of(chosen * wide, 128), wide)
        copies.append((weight_ref.at[0, :, :, lanes], target))
    copies = [
        pltpu.make_async_copy(source, target, sems.at[index])
        for index, (source, target) in enumerate(copies)
    ]
    for copy in copies:
        copy.start()
    for copy in copies:
        copy.wait()


def encode_kernel(*refs):
    shown, lent, pieces = refs[:4], refs[4:8], refs[8:8 + PIECES]
    out_ref, info_ref, x_buf, w_buf, q_buf, k_buf, v_buf, sems = refs[8 + PIECES:]
    core, z, y, m = places()
    half = shown[0].shape[-1]
    rows = shown[0].shape[1] - INFO
    depth = pieces[0].shape[1]
    wide = pieces[0].shape[2]
    own_rows = 4 * rows
    copies = []
    side = lax.rem(z, 2)
    lanes = [
        pl.ds(pl.multiple_of(half * (m if across == 0 else 1 - m), 128), half)
        for across in range(2)
    ]
    for index, piece in enumerate(shown):
        first = WIN + 2 * rows * (side if index < 2 else 1 - side)
        for part in range(2):
            start = pl.multiple_of(first + (y if part == 0 else 1 - y) * rows, 64)
            copies.append((
                piece.at[part, pl.ds(0, rows), :],
                x_buf.at[pl.ds(start, rows), lanes[index % 2]],
            ))
    part = jnp.where(core == 0, y, 1 - y)
    edge = pl.multiple_of(core * (rows - WIN), 64)
    halo_first = pl.multiple_of((1 - core) * (WIN + own_rows), 64)
    empty_first = pl.multiple_of(core * (WIN + own_rows), 64)
    inside = side == core
    info_part = jnp.where(side == y, 0, 1)
    for index in range(2):
        copies.append((
            shown[2 * index].at[info_part, pl.ds(rows, INFO), pl.ds(0, 128)], info_ref.at[index]
        ))
    t = lax.rem(z, 2)
    for index, piece in enumerate(pieces):
        crossed, other = (index // 2) % 2, index % 2
        low = core if (other == 0) == (index >= 4) else 1 - core
        pos_z = 2 * low + (t if index < 4 else 1 - t)
        pos = 2 * pos_z + (y if crossed == 0 else 1 - y)
        copies.append((
            piece, w_buf.at[:, pl.ds(pl.multiple_of(pos * depth, 64), depth), :]
        ))
    copies = [
        pltpu.make_async_copy(source, target, sems.at[index])
        for index, (source, target) in enumerate(copies)
    ]
    for copy in copies:
        copy.start()

    def fetch_halo(pair):
        halo = [
            pltpu.make_async_copy(
                piece.at[part, pl.ds(edge, WIN), :],
                x_buf.at[pl.ds(halo_first, WIN), lanes[across]],
                sems.at[len(copies) + across],
            )
            for across, piece in enumerate(pair)
        ]
        for copy in halo:
            copy.start()
        for copy in halo:
            copy.wait()

    @pl.when(inside)
    def _():
        fetch_halo(lent[:2])

    @pl.when(jnp.logical_not(inside))
    def _():
        fetch_halo(lent[2:])

    x_buf[pl.ds(empty_first, WIN), :] = jnp.zeros((WIN, 2 * half), x_buf.dtype)
    for copy in copies:
        copy.wait()
    x = x_buf[...]
    q_buf[...] = jnp.dot(
        x[WIN:WIN + own_rows], w_buf[0], preferred_element_type=jnp.float32
    ).astype(q_buf.dtype)
    k_buf[...] = jnp.dot(x, w_buf[1], preferred_element_type=jnp.float32).astype(k_buf.dtype)
    v_buf[...] = jnp.dot(x, w_buf[2], preferred_element_type=jnp.float32).astype(v_buf.dtype)
    keys = rows + 2 * WIN
    a = lax.broadcasted_iota(jnp.int32, (rows, keys), 0)
    b = lax.broadcasted_iota(jnp.int32, (rows, keys), 1)
    band = (b >= a) & (b <= a + 2 * WIN)
    for j in range(4):
        admitted = band
        if j == 0:
            admitted = admitted & (b >= WIN * (1 - core))
        if j == 3:
            admitted = admitted & (b < keys - WIN * core)
        for h in range(wide // HD):
            lanes = slice(h * HD, (h + 1) * HD)
            scores = lax.dot_general(
                q_buf[j * rows:(j + 1) * rows, lanes],
                k_buf[j * rows:j * rows + keys, lanes],
                (((1,), (1,)), ((), ())),
                preferred_element_type=jnp.float32,
            ) * (1.0 / math.sqrt(HD))
            scores = jnp.where(admitted, scores, -jnp.inf)
            peak = jnp.max(scores, axis=-1, keepdims=True)
            exps = jnp.exp(scores - peak)
            attention = (exps / jnp.sum(exps, axis=-1, keepdims=True)).astype(jnp.bfloat16)
            out_ref[j, :, lanes] = jnp.dot(
                attention,
                v_buf[j * rows:j * rows + keys, lanes],
                preferred_element_type=jnp.float32,
            ).astype(out_ref.dtype)


def predict_kernel(slot_ref, lat_ref, own_ref, lent_ref, lent_c_ref, out_ref):
    core, _, _, m = places()
    wide = lat_ref.shape[2]
    total = None
    for side in range(2):
        predicted = None
        for t in range(2):
            for x in range(2):
                if side == 0:
                    source = lat_ref[2 * t + x]
                    weight = own_ref[(2 * x + t) * wide:(2 * x + t + 1) * wide, :]
                else:
                    source = lat_ref[2 * t + (core if x == 0 else 1 - core)]
                    weight = (lent_ref, lent_c_ref)[x][t * wide:(t + 1) * wide, :]
                term = jnp.dot(source, weight, preferred_element_type=jnp.float32)
                predicted = term if predicted is None else predicted + term
        for t in range(2):
            target = lat_ref[4 + 2 * t + (m if side == 0 else 1 - m)].astype(jnp.float32)
            residue = predicted[:, t * wide:(t + 1) * wide] - target
            for i in range(wide // 128):
                piece = residue[:, i * 128:(i + 1) * 128]
                total = piece * piece if total is None else total + piece * piece
    row_errors = jnp.sum(total, axis=1, keepdims=True)
    rows, slots = total.shape[0], out_ref.shape[2]
    chosen = slot_ref[...] == lax.broadcasted_iota(jnp.int32, (rows, slots), 1)
    routed = jnp.sum(jnp.where(chosen, row_errors, 0.0), axis=0, keepdims=True)
    for i in range(out_ref.shape[0]):
        out_ref[i] = routed


def local_lines(signal, mask_token, keep, target_shard, enc_weight, pred_weight):
    core = lax.axis_index("grp")
    s = lax.axis_index("seq")
    m = lax.axis_index("mdl")
    z, y = s // 2, s % 2
    sequences, length, half = signal.shape
    per_range = keep.shape[1]
    block_len = length // per_range
    depth = enc_weight.shape[2]
    wide = half // 2

    vmem = pl.BlockSpec(memory_space=pltpu.VMEM)
    anywhere = pl.BlockSpec(memory_space=pl.ANY)

    def to_near(c, z, y, m):
        return (1 - z // 2, z % 2 + 2 * c, y, m)

    def to_far(c, z, y, m):
        return (z // 2, 1 - z % 2 + 2 * c, y, m)

    def across_z(c, z, y, m):
        if z // 2 == c:
            return (c, (z + 2) % 4, y, m)
        return (1 - c, z, y, m)

    def across_zy(c, z, y, m):
        c, z, y, m = across_z(c, z, y, m)
        return (c, z, 1 - y, m)

    def flip_y(c, z, y, m):
        return (c, z, 1 - y, m)

    def flip_core(c, z, y, m):
        return (1 - c, z, y, m)

    def flip_x(c, z, y, m):
        return (c, z, y, 1 - m)

    def flip_z(c, z, y, m):
        return (c, z + 1 - 2 * (z % 2), y, m)

    mine, given = pl.pallas_call(
        mask_kernel,
        out_shape=[jax.ShapeDtypeStruct((length + INFO, half), jnp.bfloat16)] * 2,
        in_specs=[vmem] * 4,
        out_specs=[vmem] * 2,
    )(signal, mask_token, keep, target_shard)
    near, far, columns = pl.pallas_call(
        slice_kernel,
        out_shape=[jax.ShapeDtypeStruct(shape, jnp.bfloat16) for shape in (
            (3, depth, wide), (3, depth, wide), (half, half),
        )],
        in_specs=[anywhere] * 3,
        out_specs=[vmem] * 3,
        scratch_shapes=[pltpu.SemaphoreType.DMA((3,))],
    )(mine, enc_weight, pred_weight)
    first, second = move(mine, across_z), move(given, across_zy)
    near, first, second = lax.optimization_barrier((near, first, second))
    near_w = move(near, to_near)
    x_own = jnp.stack([first, second])
    x_near = move(x_own, flip_z)
    x_across = move(x_own, flip_x)
    far, near_w = lax.optimization_barrier((far, near_w))
    far_w = move(far, to_far)
    near_y = move(near_w, flip_y)
    x_near_across = move(x_near, flip_x)
    far_y_source, x_near_across, near_y = lax.optimization_barrier((far_w, x_near_across, near_y))
    far_y = move(far_y_source, flip_y)
    columns, _ = lax.optimization_barrier((columns, x_near_across))
    columns = move(columns, flip_x)
    columns_c = move(columns, flip_core)
    shown = [x_own, x_across, x_near, x_near_across]
    lent = [move(piece, flip_core) for piece in shown]
    pieces = []
    for piece in (near_w, near_y, far_w, far_y):
        pieces += [piece, move(piece, flip_core)]
    span = 4 * length + 2 * WIN

    latent, info = pl.pallas_call(
        encode_kernel,
        out_shape=[
            jax.ShapeDtypeStruct((4, length, wide), jnp.bfloat16),
            jax.ShapeDtypeStruct((2, INFO, 128), jnp.bfloat16),
        ],
        in_specs=[anywhere] * (8 + PIECES),
        out_specs=[vmem] * 2,
        scratch_shapes=[
            pltpu.VMEM((span, 2 * half), jnp.bfloat16),
            pltpu.VMEM((3, 2 * half, wide), jnp.bfloat16),
            pltpu.VMEM((4 * length, wide), jnp.bfloat16),
            pltpu.VMEM((span, wide), jnp.bfloat16),
            pltpu.VMEM((span, wide), jnp.bfloat16),
            pltpu.SemaphoreType.DMA((12 + PIECES,)),
        ],
        compiler_params=pltpu.CompilerParams(vmem_limit_bytes=24 * 2**20),
    )(*shown, *lent, *pieces)
    words = jnp.where(z // 2 == z % 2, info[0, 0], info[1, 0]).astype(jnp.int32)
    words = words.reshape(2, sequences, per_range)
    shard_of = words[0].reshape(-1)
    hidden = lax.dynamic_index_in_dim(words[1], y, 0, keepdims=False) == 0
    blocks = shard_of.shape[0]
    capacity = max(2, 2 * blocks // 8)
    order_ids = jnp.arange(blocks)
    earlier = (shard_of[:, None] == shard_of[None, :]) & (order_ids[:, None] < order_ids[None, :])
    slot = shard_of * capacity + jnp.sum(earlier.astype(jnp.int32), axis=0)
    slot = lax.dynamic_index_in_dim(slot.reshape(sequences, -1), y, 0, keepdims=False)
    slot = jnp.where(hidden, slot, -1)
    slot = lax.dynamic_slice_in_dim(slot, m * (per_range // 2), per_range // 2)
    slot = jnp.repeat(slot, block_len)[:, None]
    lines = [[4 * i + 2 * j + k for i in range(4) for k in range(2)] for j in range(2)]
    latents = lax.all_to_all(
        latent.reshape(8, length // 2, wide), ("seq", "mdl"),
        split_axis=0, concat_axis=0, tiled=True, axis_index_groups=lines,
    )
    routed = pl.pallas_call(
        predict_kernel,
        out_shape=jax.ShapeDtypeStruct((16, 1, 8 * capacity), jnp.float32),
        in_specs=[vmem] * 5,
        out_specs=vmem,
        compiler_params=pltpu.CompilerParams(vmem_limit_bytes=24 * 2**20),
    )(
        slot, latents, pred_weight, columns, columns_c
    )
    arrived = lax.all_to_all(routed, ("seq", "mdl"), split_axis=0, concat_axis=0, tiled=True)
    mine = lax.dynamic_slice_in_dim(arrived[:, 0], capacity * s, capacity, 1)
    summed = jnp.sum(mine.reshape(4, 4, capacity), axis=1)
    return summed.reshape(1, -1) / float(block_len * 2 * half)


def solution(mesh):
    placed = (
        P(None, "seq", "mdl"),
        P("mdl"),
        P(None, "seq"),
        P(None, "seq"),
        P("grp", None, "seq", "mdl"),
        P(None, "mdl"),
    )
    plan = local_lines if mesh.shape["seq"] == 8 else local
    return jax.shard_map(
        plan, mesh=mesh, in_specs=placed, out_specs=P("seq", "grp"), check_vma=False
    )
```

```python
import functools
import math

import jax
import jax.numpy as jnp
from jax import lax
from jax.experimental import pallas as pl
from jax.experimental.pallas import tpu as pltpu
from jax.sharding import PartitionSpec as P

HD = 128
WIN = 64
AXES = ("grp", "seq", "mdl")
PIECES = 8
INFO = 16


def padded(x, sides, width):
    for axis, dim in sides:
        count, length = (lax.axis_size(axis), x.shape[dim])
        up = [(i, (i + 1) % count) for i in range(count - 1)]
        down = [(j, i) for i, j in up]
        last = lax.slice_in_dim(x, length - width, length, axis=dim)
        leading = lax.slice_in_dim(x, 0, width, axis=dim)
        before = lax.ppermute(last, axis, up)
        after = lax.ppermute(leading, axis, down)
        x = jnp.concatenate([before, x, after], axis=dim)
    return x


def predict(context, target, live_flags, pred_weight, divisor):
    flat_rows = context.reshape(-1, context.shape[-1])
    wide_rows = lax.all_gather(flat_rows, "mdl", axis=1, tiled=True)
    predicted = jnp.dot(wide_rows, pred_weight, preferred_element_type=jnp.float32)
    residue = predicted - target.reshape(flat_rows.shape).astype(jnp.float32)
    partial_sums = jnp.sum((residue * residue).reshape(live_flags.shape[0], -1), axis=1)
    summed = lax.psum(partial_sums, "mdl")
    return summed / divisor * live_flags


def local(signal, mask_token, keep, target_shard, enc_weight, pred_weight):
    group_index = lax.axis_index("grp")
    seq_index = lax.axis_index("seq")
    shards = lax.axis_size("seq")
    sequences, length, half_width = signal.shape
    per_range = keep.shape[1]
    block_len = length // per_range
    kept_rows = jnp.repeat(keep, block_len, axis=1)[:, :, None]
    masked_in = jnp.where(kept_rows == 1, signal, mask_token[None, None, :])
    source = jnp.where(group_index == 0, masked_in, signal)
    wide_in = lax.all_gather(source, "mdl", axis=2, tiled=True)
    full_width = wide_in.shape[2]
    flat_in = wide_in.reshape(-1, full_width)
    span = length + 2 * WIN
    weight_all = lax.all_gather(enc_weight, "seq", axis=2, tiled=True)[0]
    queries = jnp.dot(flat_in, weight_all[0], preferred_element_type=jnp.float32).astype(
        jnp.bfloat16
    )
    pair_made = jnp.einsum(
        "nd,cde->cne", flat_in, weight_all[1:], preferred_element_type=jnp.float32
    ).astype(jnp.bfloat16)
    own_pairs = pair_made.reshape(2, sequences, length, half_width)
    pair_rows = padded(own_pairs, (("seq", 2),), WIN)
    head_count = half_width // HD
    query_heads = queries.reshape(sequences, length, head_count, HD)
    key_heads = pair_rows[0].reshape(sequences, span, head_count, HD)
    value_heads = pair_rows[1].reshape(sequences, span, head_count, HD)
    query_pos = seq_index * length + jnp.arange(length)
    key_pos = seq_index * length - WIN + jnp.arange(span)
    total_len = length * shards
    in_window = (
        (jnp.abs(query_pos[:, None] - key_pos[None, :]) <= WIN)
        & (key_pos[None, :] >= 0)
        & (key_pos[None, :] < total_len)
    )
    scores = jnp.einsum(
        "sahd,sbhd->shab", query_heads, key_heads, preferred_element_type=jnp.float32
    ) * (1.0 / math.sqrt(HD))
    scores = jnp.where(in_window[None, None], scores, -jnp.inf)
    row_peak = jnp.max(scores, axis=-1, keepdims=True)
    exp_scores = jnp.exp(scores - row_peak)
    attention = (exp_scores / jnp.sum(exp_scores, axis=-1, keepdims=True)).astype(jnp.bfloat16)
    attended = jnp.einsum(
        "shab,sbhd->sahd", attention, value_heads, preferred_element_type=jnp.float32
    ).astype(jnp.bfloat16)
    latent = attended.reshape(sequences * per_range, block_len, half_width)
    blocks_here = latent.shape[0]
    capacity = max(2, 2 * blocks_here // shards)
    slot_count = shards * capacity
    shard_of = target_shard.reshape(-1)
    masked_flag = (keep.reshape(-1) == 0).astype(jnp.float32)
    order_ids = jnp.arange(blocks_here)
    earlier = (shard_of[:, None] == shard_of[None, :]) & (order_ids[:, None] < order_ids[None, :])
    slot_rank = jnp.sum(earlier.astype(jnp.int32), axis=0)
    slot_index = shard_of * capacity + slot_rank
    onehot = slot_index[None, :] == jnp.arange(slot_count)[:, None]
    divisor = float(block_len * full_width)
    halves = lax.all_to_all(latent[None], "grp", split_axis=1, concat_axis=0, tiled=True)
    half_count = blocks_here // 2
    first_block = group_index * half_count
    own_flags = lax.dynamic_slice_in_dim(masked_flag, first_block, half_count)
    losses = predict(halves[0], halves[1], own_flags, pred_weight, divisor)
    spread = lax.dynamic_update_slice_in_dim(
        jnp.zeros((blocks_here,), jnp.float32), losses, first_block, 0
    )
    slotted = jnp.sum(jnp.where(onehot, spread[None, :], 0.0), axis=1).reshape(shards, capacity)
    arrived = lax.all_to_all(slotted, "seq", split_axis=0, concat_axis=0, tiled=True)
    result = lax.psum_scatter(arrived, "grp", scatter_dimension=0, tiled=True)
    return result.reshape(1, -1)


def move(x, target):
    pairs = []
    for c in range(2):
        for s in range(8):
            for m in range(2):
                c2, z2, y2, m2 = target(c, s // 2, s % 2, m)
                pairs.append(((c * 8 + s) * 2 + m, (c2 * 8 + 2 * z2 + y2) * 2 + m2))
    return lax.ppermute(x, AXES, pairs)


def places():
    s = lax.axis_index("seq")
    return lax.axis_index("grp"), s // 2, lax.rem(s, 2), lax.axis_index("mdl")


def mask_kernel(signal_ref, token_ref, keep_ref, shard_ref, mine_ref, given_ref):
    core, _, y, _ = places()
    length = signal_ref.shape[1]
    blocks = keep_ref.shape[1]
    block_len = length // blocks
    row = lax.broadcasted_iota(jnp.int32, (length, blocks), 0)
    first = lax.broadcasted_iota(jnp.int32, (length, blocks), 1) * block_len
    covers = (row >= first) & (row < first + block_len)
    token = token_ref[...].astype(jnp.float32).reshape(1, -1)
    words = jnp.concatenate([shard_ref[0:1, :], shard_ref[1:2, :], keep_ref[0:1, :], keep_ref[1:2, :]], axis=1)
    words = jnp.broadcast_to(words.astype(jnp.float32), (INFO, 4 * blocks)).astype(mine_ref.dtype)
    for target, chosen in ((mine_ref, y), (given_ref, 1 - y)):
        kept = jnp.where(covers, keep_ref[pl.ds(chosen, 1), :], 0)
        kept = jnp.sum(kept, axis=1, keepdims=True) + 1 - core
        rows = signal_ref[chosen].astype(jnp.float32)
        target[0:length, :] = jnp.where(kept > 0, rows, token).astype(target.dtype)
        target[length:, 0:4 * blocks] = words
        target[length:, 4 * blocks:] = jnp.zeros((INFO, target.shape[1] - 4 * blocks), target.dtype)


def slice_kernel(after_ref, weight_ref, pred_ref, near_ref, far_ref, lent_ref, sems):
    core, z, _, _ = places()
    wide = near_ref.shape[2]
    count = lent_ref.shape[0]
    t = lax.rem(z, 2)
    first = pl.multiple_of(core * count, 128)
    copies = [(pred_ref.at[pl.ds(first, count), :], lent_ref)]
    for target, chosen in ((near_ref, t), (far_ref, 1 - t)):
        lanes = pl.ds(pl.multiple_of(chosen * wide, 128), wide)
        copies.append((weight_ref.at[0, :, :, lanes], target))
    copies = [
        pltpu.make_async_copy(source, target, sems.at[index])
        for index, (source, target) in enumerate(copies)
    ]
    for copy in copies:
        copy.start()
    for copy in copies:
        copy.wait()


def encode_kernel(*refs):
    shown, halo_ref, pieces = refs[:4], refs[4], refs[5:5 + PIECES]
    out_ref, info_ref, x_buf, w_buf, q_buf, k_buf, v_buf, sems = refs[5 + PIECES:]
    core, z, y, m = places()
    half = shown[0].shape[-1]
    rows = shown[0].shape[1] - INFO
    depth = pieces[0].shape[1]
    wide = pieces[0].shape[2]
    own_rows = 4 * rows
    copies = []
    side = lax.rem(z, 2)
    lanes = [
        pl.ds(pl.multiple_of(half * (m if across == 0 else 1 - m), 128), half)
        for across in range(2)
    ]
    for index, piece in enumerate(shown):
        first = WIN + 2 * rows * (side if index < 2 else 1 - side)
        for part in range(2):
            start = pl.multiple_of(first + (y if part == 0 else 1 - y) * rows, 64)
            copies.append((
                piece.at[part, pl.ds(0, rows), :],
                x_buf.at[pl.ds(start, rows), lanes[index % 2]],
            ))
    halo_first = pl.multiple_of((1 - core) * (WIN + own_rows), 64)
    empty_first = pl.multiple_of(core * (WIN + own_rows), 64)
    info_part = jnp.where(side == y, 0, 1)
    for index in range(2):
        copies.append((
            halo_ref.at[index], x_buf.at[pl.ds(halo_first, WIN), lanes[index]]
        ))
        copies.append((
            shown[2 * index].at[info_part, pl.ds(rows, INFO), pl.ds(0, 128)], info_ref.at[index]
        ))
    t = lax.rem(z, 2)
    for index, piece in enumerate(pieces):
        crossed, other = (index // 2) % 2, index % 2
        low = core if (other == 0) == (index >= 4) else 1 - core
        pos_z = 2 * low + (t if index < 4 else 1 - t)
        pos = 2 * pos_z + (y if crossed == 0 else 1 - y)
        copies.append((
            piece, w_buf.at[:, pl.ds(pl.multiple_of(pos * depth, 64), depth), :]
        ))
    copies = [
        pltpu.make_async_copy(source, target, sems.at[index])
        for index, (source, target) in enumerate(copies)
    ]
    for copy in copies:
        copy.start()
    x_buf[pl.ds(empty_first, WIN), :] = jnp.zeros((WIN, 2 * half), x_buf.dtype)
    for copy in copies:
        copy.wait()
    x = x_buf[...]
    q_buf[...] = jnp.dot(
        x[WIN:WIN + own_rows], w_buf[0], preferred_element_type=jnp.float32
    ).astype(q_buf.dtype)
    k_buf[...] = jnp.dot(x, w_buf[1], preferred_element_type=jnp.float32).astype(k_buf.dtype)
    v_buf[...] = jnp.dot(x, w_buf[2], preferred_element_type=jnp.float32).astype(v_buf.dtype)
    keys = rows + 2 * WIN
    a = lax.broadcasted_iota(jnp.int32, (rows, keys), 0)
    b = lax.broadcasted_iota(jnp.int32, (rows, keys), 1)
    band = (b >= a) & (b <= a + 2 * WIN)
    for j in range(4):
        admitted = band
        if j == 0:
            admitted = admitted & (b >= WIN * (1 - core))
        if j == 3:
            admitted = admitted & (b < keys - WIN * core)
        for h in range(wide // HD):
            lanes = slice(h * HD, (h + 1) * HD)
            scores = lax.dot_general(
                q_buf[j * rows:(j + 1) * rows, lanes],
                k_buf[j * rows:j * rows + keys, lanes],
                (((1,), (1,)), ((), ())),
                preferred_element_type=jnp.float32,
            ) * (1.0 / math.sqrt(HD))
            scores = jnp.where(admitted, scores, -jnp.inf)
            peak = jnp.max(scores, axis=-1, keepdims=True)
            exps = jnp.exp(scores - peak)
            attention = (exps / jnp.sum(exps, axis=-1, keepdims=True)).astype(jnp.bfloat16)
            out_ref[j, :, lanes] = jnp.dot(
                attention,
                v_buf[j * rows:j * rows + keys, lanes],
                preferred_element_type=jnp.float32,
            ).astype(out_ref.dtype)


def predict_kernel(slot_ref, lat_ref, own_ref, lent_ref, lent_c_ref, out_ref):
    core, _, _, m = places()
    wide = lat_ref.shape[2]
    total = None
    for side in range(2):
        predicted = None
        for t in range(2):
            for x in range(2):
                if side == 0:
                    source = lat_ref[2 * t + x]
                    weight = own_ref[(2 * x + t) * wide:(2 * x + t + 1) * wide, :]
                else:
                    source = lat_ref[2 * t + (core if x == 0 else 1 - core)]
                    weight = (lent_ref, lent_c_ref)[x][t * wide:(t + 1) * wide, :]
                term = jnp.dot(source, weight, preferred_element_type=jnp.float32)
                predicted = term if predicted is None else predicted + term
        for t in range(2):
            target = lat_ref[4 + 2 * t + (m if side == 0 else 1 - m)].astype(jnp.float32)
            residue = predicted[:, t * wide:(t + 1) * wide] - target
            for i in range(wide // 128):
                piece = residue[:, i * 128:(i + 1) * 128]
                total = piece * piece if total is None else total + piece * piece
    row_errors = jnp.sum(total, axis=1, keepdims=True)
    rows, slots = total.shape[0], out_ref.shape[2]
    chosen = slot_ref[...] == lax.broadcasted_iota(jnp.int32, (rows, slots), 1)
    routed = jnp.sum(jnp.where(chosen, row_errors, 0.0), axis=0, keepdims=True)
    for i in range(out_ref.shape[0]):
        out_ref[i] = routed


def local_lines(signal, mask_token, keep, target_shard, enc_weight, pred_weight):
    core = lax.axis_index("grp")
    s = lax.axis_index("seq")
    m = lax.axis_index("mdl")
    z, y = s // 2, s % 2
    sequences, length, half = signal.shape
    per_range = keep.shape[1]
    block_len = length // per_range
    depth = enc_weight.shape[2]
    wide = half // 2

    vmem = pl.BlockSpec(memory_space=pltpu.VMEM)
    anywhere = pl.BlockSpec(memory_space=pl.ANY)

    def to_near(c, z, y, m):
        return (1 - z // 2, z % 2 + 2 * c, y, m)

    def to_far(c, z, y, m):
        return (z // 2, 1 - z % 2 + 2 * c, y, m)

    def across_z(c, z, y, m):
        if z // 2 == c:
            return (c, (z + 2) % 4, y, m)
        return (1 - c, z, y, m)

    def across_zy(c, z, y, m):
        c, z, y, m = across_z(c, z, y, m)
        return (c, z, 1 - y, m)

    def flip_y(c, z, y, m):
        return (c, z, 1 - y, m)

    def flip_core(c, z, y, m):
        return (1 - c, z, y, m)

    def flip_x(c, z, y, m):
        return (c, z, y, 1 - m)

    def flip_z(c, z, y, m):
        return (c, z + 1 - 2 * (z % 2), y, m)

    mine, given = pl.pallas_call(
        mask_kernel,
        out_shape=[jax.ShapeDtypeStruct((length + INFO, half), jnp.bfloat16)] * 2,
        in_specs=[vmem] * 4,
        out_specs=[vmem] * 2,
        compiler_params=pltpu.CompilerParams(vmem_limit_bytes=16 * 2**20),
    )(signal, mask_token, keep, target_shard)
    near, far, columns = pl.pallas_call(
        slice_kernel,
        out_shape=[jax.ShapeDtypeStruct(shape, jnp.bfloat16) for shape in (
            (3, depth, wide), (3, depth, wide), (half, half),
        )],
        in_specs=[anywhere] * 3,
        out_specs=[vmem] * 3,
        scratch_shapes=[pltpu.SemaphoreType.DMA((3,))],
        compiler_params=pltpu.CompilerParams(vmem_limit_bytes=16 * 2**20),
    )(mine, enc_weight, pred_weight)
    first, second = move(mine, across_z), move(given, across_zy)
    near_w = move(near, to_near)
    first, second, near = lax.optimization_barrier((first, second, near))
    x_own = jnp.stack([first, second])
    x_near = move(x_own, flip_z)
    x_across = move(x_own, flip_x)
    far, x_across = lax.optimization_barrier((far, x_across))
    far_w = move(far, to_far)
    near_y = move(near_w, flip_y)
    x_near, x_across = lax.optimization_barrier((x_near, x_across))
    x_near_across = move(x_near, flip_x)
    far_y_source, near_y = lax.optimization_barrier((far_w, near_y))
    far_y = move(far_y_source, flip_y)
    columns, _ = lax.optimization_barrier((columns, x_near_across))
    columns = move(columns, flip_x)
    shown = [x_own, x_across, x_near, x_near_across]

    def edge(own, near):
        found = jnp.where(z % 2 == 1 - core, own, near)
        part = jnp.where(core == 0, 1 - y, y)
        first = jnp.where(core == 0, length - WIN, 0)
        return lax.dynamic_slice(found, (part, first, 0), (1, WIN, half))[0]

    halo = move(jnp.stack([edge(x_own, x_near), edge(x_across, x_near_across)]), flip_core)
    pieces = []
    for piece in (near_w, near_y, far_w, far_y):
        pieces += [piece, move(piece, flip_core)]
    span = 4 * length + 2 * WIN

    latent, info = pl.pallas_call(
        encode_kernel,
        out_shape=[
            jax.ShapeDtypeStruct((4, length, wide), jnp.bfloat16),
            jax.ShapeDtypeStruct((2, INFO, 128), jnp.bfloat16),
        ],
        in_specs=[pl.BlockSpec(memory_space=pltpu.HBM)] * (5 + PIECES),
        out_specs=[vmem] * 2,
        scratch_shapes=[
            pltpu.VMEM((span, 2 * half), jnp.bfloat16),
            pltpu.VMEM((3, 2 * half, wide), jnp.bfloat16),
            pltpu.VMEM((4 * length, wide), jnp.bfloat16),
            pltpu.VMEM((span, wide), jnp.bfloat16),
            pltpu.VMEM((span, wide), jnp.bfloat16),
            pltpu.SemaphoreType.DMA((12 + PIECES,)),
        ],
        compiler_params=pltpu.CompilerParams(vmem_limit_bytes=56 * 2**20),
    )(*shown, halo, *pieces)
    columns, latent = lax.optimization_barrier((columns, latent))
    columns_c = move(columns, flip_core)
    words = jnp.where(z // 2 == z % 2, info[0, 0], info[1, 0]).astype(jnp.int32)
    words = words.reshape(2, sequences, per_range)
    shard_of = words[0].reshape(-1)
    hidden = lax.dynamic_index_in_dim(words[1], y, 0, keepdims=False) == 0
    blocks = shard_of.shape[0]
    capacity = max(2, 2 * blocks // 8)
    order_ids = jnp.arange(blocks)
    earlier = (shard_of[:, None] == shard_of[None, :]) & (order_ids[:, None] < order_ids[None, :])
    slot = shard_of * capacity + jnp.sum(earlier.astype(jnp.int32), axis=0)
    slot = lax.dynamic_index_in_dim(slot.reshape(sequences, -1), y, 0, keepdims=False)
    slot = jnp.where(hidden, slot, -1)
    slot = lax.dynamic_slice_in_dim(slot, m * (per_range // 2), per_range // 2)
    slot = jnp.repeat(slot, block_len)[:, None]
    lines = [[4 * i + 2 * j + k for i in range(4) for k in range(2)] for j in range(2)]
    latents = lax.all_to_all(
        latent.reshape(8, length // 2, wide), ("seq", "mdl"),
        split_axis=0, concat_axis=0, tiled=True, axis_index_groups=lines,
    )
    routed = pl.pallas_call(
        predict_kernel,
        out_shape=jax.ShapeDtypeStruct((16, 1, 8 * capacity), jnp.float32),
        in_specs=[vmem] * 5,
        out_specs=vmem,
        compiler_params=pltpu.CompilerParams(vmem_limit_bytes=16 * 2**20),
    )(
        slot, latents, pred_weight, columns, columns_c
    )
    arrived = lax.all_to_all(routed, ("seq", "mdl"), split_axis=0, concat_axis=0, tiled=True)
    mine = lax.dynamic_slice_in_dim(arrived[:, 0], capacity * s, capacity, 1)
    summed = jnp.sum(mine.reshape(4, 4, capacity), axis=1)
    return summed.reshape(1, -1) / float(block_len * 2 * half)


def solution(mesh):
    placed = (
        P(None, "seq", "mdl"),
        P("mdl"),
        P(None, "seq"),
        P(None, "seq"),
        P("grp", None, "seq", "mdl"),
        P(None, "mdl"),
    )
    plan = local_lines if mesh.shape["seq"] == 8 else local
    return jax.shard_map(
        plan, mesh=mesh, in_specs=placed, out_specs=P("seq", "grp"), check_vma=False
    )
```

```python
import functools
import math

import jax
import jax.numpy as jnp
from jax import lax
from jax.experimental import pallas as pl
from jax.experimental.pallas import tpu as pltpu
from jax.sharding import PartitionSpec as P

HD = 128
WIN = 64
AXES = ("grp", "seq", "mdl")
PIECES = 8
INFO = 16


def padded(x, sides, width):
    for axis, dim in sides:
        count, length = (lax.axis_size(axis), x.shape[dim])
        up = [(i, (i + 1) % count) for i in range(count - 1)]
        down = [(j, i) for i, j in up]
        last = lax.slice_in_dim(x, length - width, length, axis=dim)
        leading = lax.slice_in_dim(x, 0, width, axis=dim)
        before = lax.ppermute(last, axis, up)
        after = lax.ppermute(leading, axis, down)
        x = jnp.concatenate([before, x, after], axis=dim)
    return x


def predict(context, target, live_flags, pred_weight, divisor):
    flat_rows = context.reshape(-1, context.shape[-1])
    wide_rows = lax.all_gather(flat_rows, "mdl", axis=1, tiled=True)
    predicted = jnp.dot(wide_rows, pred_weight, preferred_element_type=jnp.float32)
    residue = predicted - target.reshape(flat_rows.shape).astype(jnp.float32)
    partial_sums = jnp.sum((residue * residue).reshape(live_flags.shape[0], -1), axis=1)
    summed = lax.psum(partial_sums, "mdl")
    return summed / divisor * live_flags


def local(signal, mask_token, keep, target_shard, enc_weight, pred_weight):
    group_index = lax.axis_index("grp")
    seq_index = lax.axis_index("seq")
    shards = lax.axis_size("seq")
    sequences, length, half_width = signal.shape
    per_range = keep.shape[1]
    block_len = length // per_range
    kept_rows = jnp.repeat(keep, block_len, axis=1)[:, :, None]
    masked_in = jnp.where(kept_rows == 1, signal, mask_token[None, None, :])
    source = jnp.where(group_index == 0, masked_in, signal)
    wide_in = lax.all_gather(source, "mdl", axis=2, tiled=True)
    full_width = wide_in.shape[2]
    flat_in = wide_in.reshape(-1, full_width)
    span = length + 2 * WIN
    weight_all = lax.all_gather(enc_weight, "seq", axis=2, tiled=True)[0]
    queries = jnp.dot(flat_in, weight_all[0], preferred_element_type=jnp.float32).astype(
        jnp.bfloat16
    )
    pair_made = jnp.einsum(
        "nd,cde->cne", flat_in, weight_all[1:], preferred_element_type=jnp.float32
    ).astype(jnp.bfloat16)
    own_pairs = pair_made.reshape(2, sequences, length, half_width)
    pair_rows = padded(own_pairs, (("seq", 2),), WIN)
    head_count = half_width // HD
    query_heads = queries.reshape(sequences, length, head_count, HD)
    key_heads = pair_rows[0].reshape(sequences, span, head_count, HD)
    value_heads = pair_rows[1].reshape(sequences, span, head_count, HD)
    query_pos = seq_index * length + jnp.arange(length)
    key_pos = seq_index * length - WIN + jnp.arange(span)
    total_len = length * shards
    in_window = (
        (jnp.abs(query_pos[:, None] - key_pos[None, :]) <= WIN)
        & (key_pos[None, :] >= 0)
        & (key_pos[None, :] < total_len)
    )
    scores = jnp.einsum(
        "sahd,sbhd->shab", query_heads, key_heads, preferred_element_type=jnp.float32
    ) * (1.0 / math.sqrt(HD))
    scores = jnp.where(in_window[None, None], scores, -jnp.inf)
    row_peak = jnp.max(scores, axis=-1, keepdims=True)
    exp_scores = jnp.exp(scores - row_peak)
    attention = (exp_scores / jnp.sum(exp_scores, axis=-1, keepdims=True)).astype(jnp.bfloat16)
    attended = jnp.einsum(
        "shab,sbhd->sahd", attention, value_heads, preferred_element_type=jnp.float32
    ).astype(jnp.bfloat16)
    latent = attended.reshape(sequences * per_range, block_len, half_width)
    blocks_here = latent.shape[0]
    capacity = max(2, 2 * blocks_here // shards)
    slot_count = shards * capacity
    shard_of = target_shard.reshape(-1)
    masked_flag = (keep.reshape(-1) == 0).astype(jnp.float32)
    order_ids = jnp.arange(blocks_here)
    earlier = (shard_of[:, None] == shard_of[None, :]) & (order_ids[:, None] < order_ids[None, :])
    slot_rank = jnp.sum(earlier.astype(jnp.int32), axis=0)
    slot_index = shard_of * capacity + slot_rank
    onehot = slot_index[None, :] == jnp.arange(slot_count)[:, None]
    divisor = float(block_len * full_width)
    halves = lax.all_to_all(latent[None], "grp", split_axis=1, concat_axis=0, tiled=True)
    half_count = blocks_here // 2
    first_block = group_index * half_count
    own_flags = lax.dynamic_slice_in_dim(masked_flag, first_block, half_count)
    losses = predict(halves[0], halves[1], own_flags, pred_weight, divisor)
    spread = lax.dynamic_update_slice_in_dim(
        jnp.zeros((blocks_here,), jnp.float32), losses, first_block, 0
    )
    slotted = jnp.sum(jnp.where(onehot, spread[None, :], 0.0), axis=1).reshape(shards, capacity)
    arrived = lax.all_to_all(slotted, "seq", split_axis=0, concat_axis=0, tiled=True)
    result = lax.psum_scatter(arrived, "grp", scatter_dimension=0, tiled=True)
    return result.reshape(1, -1)


def move(x, target):
    pairs = []
    for c in range(2):
        for s in range(8):
            for m in range(2):
                c2, z2, y2, m2 = target(c, s // 2, s % 2, m)
                pairs.append(((c * 8 + s) * 2 + m, (c2 * 8 + 2 * z2 + y2) * 2 + m2))
    return lax.ppermute(x, AXES, pairs)


def places():
    s = lax.axis_index("seq")
    return lax.axis_index("grp"), s // 2, lax.rem(s, 2), lax.axis_index("mdl")


def mask_kernel(signal_ref, token_ref, keep_ref, shard_ref, mine_ref, given_ref):
    core, _, y, _ = places()
    length = signal_ref.shape[1]
    blocks = keep_ref.shape[1]
    block_len = length // blocks
    row = lax.broadcasted_iota(jnp.int32, (length, blocks), 0)
    first = lax.broadcasted_iota(jnp.int32, (length, blocks), 1) * block_len
    covers = (row >= first) & (row < first + block_len)
    token = token_ref[...].astype(jnp.float32).reshape(1, -1)
    words = jnp.concatenate([shard_ref[0:1, :], shard_ref[1:2, :], keep_ref[0:1, :], keep_ref[1:2, :]], axis=1)
    words = jnp.broadcast_to(words.astype(jnp.float32), (INFO, 4 * blocks)).astype(mine_ref.dtype)
    for target, chosen in ((mine_ref, y), (given_ref, 1 - y)):
        kept = jnp.where(covers, keep_ref[pl.ds(chosen, 1), :], 0)
        kept = jnp.sum(kept, axis=1, keepdims=True) + 1 - core
        rows = signal_ref[chosen].astype(jnp.float32)
        target[0:length, :] = jnp.where(kept > 0, rows, token).astype(target.dtype)
        target[length:, 0:4 * blocks] = words
        target[length:, 4 * blocks:] = jnp.zeros((INFO, target.shape[1] - 4 * blocks), target.dtype)


def slice_kernel(after_ref, weight_ref, pred_ref, near_ref, far_ref, lent_ref, sems):
    core, z, _, _ = places()
    wide = near_ref.shape[2]
    count = lent_ref.shape[0]
    t = lax.rem(z, 2)
    first = pl.multiple_of(core * count, 128)
    copies = [(pred_ref.at[pl.ds(first, count), :], lent_ref)]
    for target, chosen in ((near_ref, t), (far_ref, 1 - t)):
        lanes = pl.ds(pl.multiple_of(chosen * wide, 128), wide)
        copies.append((weight_ref.at[0, :, :, lanes], target))
    copies = [
        pltpu.make_async_copy(source, target, sems.at[index])
        for index, (source, target) in enumerate(copies)
    ]
    for copy in copies:
        copy.start()
    for copy in copies:
        copy.wait()


def encode_kernel(*refs):
    shown, halo_ref, pieces = refs[:4], refs[4], refs[5:5 + PIECES]
    out_ref, info_ref, x_buf, w_buf, q_buf, k_buf, v_buf, sems = refs[5 + PIECES:]
    core, z, y, m = places()
    half = shown[0].shape[-1]
    rows = shown[0].shape[1] - INFO
    depth = pieces[0].shape[1]
    wide = pieces[0].shape[2]
    own_rows = 4 * rows
    copies = []
    side = lax.rem(z, 2)
    lanes = [
        pl.ds(pl.multiple_of(half * (m if across == 0 else 1 - m), 128), half)
        for across in range(2)
    ]
    for index, piece in enumerate(shown):
        first = WIN + 2 * rows * (side if index < 2 else 1 - side)
        for part in range(2):
            start = pl.multiple_of(first + (y if part == 0 else 1 - y) * rows, 64)
            copies.append((
                piece.at[part, pl.ds(0, rows), :],
                x_buf.at[pl.ds(start, rows), lanes[index % 2]],
            ))
    halo_first = pl.multiple_of((1 - core) * (WIN + own_rows), 64)
    empty_first = pl.multiple_of(core * (WIN + own_rows), 64)
    info_part = jnp.where(side == y, 0, 1)
    for index in range(2):
        copies.append((
            halo_ref.at[index], x_buf.at[pl.ds(halo_first, WIN), lanes[index]]
        ))
        copies.append((
            shown[2 * index].at[info_part, pl.ds(rows, INFO), pl.ds(0, 128)], info_ref.at[index]
        ))
    t = lax.rem(z, 2)
    for index, piece in enumerate(pieces):
        crossed, other = (index // 2) % 2, index % 2
        low = core if (other == 0) == (index >= 4) else 1 - core
        pos_z = 2 * low + (t if index < 4 else 1 - t)
        pos = 2 * pos_z + (y if crossed == 0 else 1 - y)
        copies.append((
            piece, w_buf.at[:, pl.ds(pl.multiple_of(pos * depth, 64), depth), :]
        ))
    copies = [
        pltpu.make_async_copy(source, target, sems.at[index])
        for index, (source, target) in enumerate(copies)
    ]
    for copy in copies:
        copy.start()
    x_buf[pl.ds(empty_first, WIN), :] = jnp.zeros((WIN, 2 * half), x_buf.dtype)
    for copy in copies:
        copy.wait()
    x = x_buf[...]
    q_buf[...] = jnp.dot(
        x[WIN:WIN + own_rows], w_buf[0], preferred_element_type=jnp.float32
    ).astype(q_buf.dtype)
    k_buf[...] = jnp.dot(x, w_buf[1], preferred_element_type=jnp.float32).astype(k_buf.dtype)
    v_buf[...] = jnp.dot(x, w_buf[2], preferred_element_type=jnp.float32).astype(v_buf.dtype)
    keys = rows + 2 * WIN
    a = lax.broadcasted_iota(jnp.int32, (rows, keys), 0)
    b = lax.broadcasted_iota(jnp.int32, (rows, keys), 1)
    band = (b >= a) & (b <= a + 2 * WIN)
    for j in range(4):
        admitted = band
        if j == 0:
            admitted = admitted & (b >= WIN * (1 - core))
        if j == 3:
            admitted = admitted & (b < keys - WIN * core)
        for h in range(wide // HD):
            lanes = slice(h * HD, (h + 1) * HD)
            scores = lax.dot_general(
                q_buf[j * rows:(j + 1) * rows, lanes],
                k_buf[j * rows:j * rows + keys, lanes],
                (((1,), (1,)), ((), ())),
                preferred_element_type=jnp.float32,
            ) * (1.0 / math.sqrt(HD))
            scores = jnp.where(admitted, scores, -jnp.inf)
            peak = jnp.max(scores, axis=-1, keepdims=True)
            exps = jnp.exp(scores - peak)
            attention = (exps / jnp.sum(exps, axis=-1, keepdims=True)).astype(jnp.bfloat16)
            out_ref[j, :, lanes] = jnp.dot(
                attention,
                v_buf[j * rows:j * rows + keys, lanes],
                preferred_element_type=jnp.float32,
            ).astype(out_ref.dtype)


def predict_kernel(slot_ref, lat_ref, own_ref, lent_ref, lent_c_ref, out_ref):
    core, _, _, m = places()
    wide = lat_ref.shape[2]
    total = None
    for side in range(2):
        predicted = None
        for t in range(2):
            for x in range(2):
                if side == 0:
                    source = lat_ref[2 * t + x]
                    weight = own_ref[(2 * x + t) * wide:(2 * x + t + 1) * wide, :]
                else:
                    source = lat_ref[2 * t + (core if x == 0 else 1 - core)]
                    weight = (lent_ref, lent_c_ref)[x][t * wide:(t + 1) * wide, :]
                term = jnp.dot(source, weight, preferred_element_type=jnp.float32)
                predicted = term if predicted is None else predicted + term
        for t in range(2):
            target = lat_ref[4 + 2 * t + (m if side == 0 else 1 - m)].astype(jnp.float32)
            residue = predicted[:, t * wide:(t + 1) * wide] - target
            for i in range(wide // 128):
                piece = residue[:, i * 128:(i + 1) * 128]
                total = piece * piece if total is None else total + piece * piece
    row_errors = jnp.sum(total, axis=1, keepdims=True)
    rows, slots = total.shape[0], out_ref.shape[2]
    chosen = slot_ref[...] == lax.broadcasted_iota(jnp.int32, (rows, slots), 1)
    routed = jnp.sum(jnp.where(chosen, row_errors, 0.0), axis=0, keepdims=True)
    for i in range(out_ref.shape[0]):
        out_ref[i] = routed


def local_lines(signal, mask_token, keep, target_shard, enc_weight, pred_weight):
    core = lax.axis_index("grp")
    s = lax.axis_index("seq")
    m = lax.axis_index("mdl")
    z, y = s // 2, s % 2
    sequences, length, half = signal.shape
    per_range = keep.shape[1]
    block_len = length // per_range
    depth = enc_weight.shape[2]
    wide = half // 2

    vmem = pl.BlockSpec(memory_space=pltpu.VMEM)
    anywhere = pl.BlockSpec(memory_space=pl.ANY)

    def to_near(c, z, y, m):
        return (1 - z // 2, z % 2 + 2 * c, y, m)

    def to_far(c, z, y, m):
        return (z // 2, 1 - z % 2 + 2 * c, y, m)

    def across_z(c, z, y, m):
        if z // 2 == c:
            return (c, (z + 2) % 4, y, m)
        return (1 - c, z, y, m)

    def across_zy(c, z, y, m):
        c, z, y, m = across_z(c, z, y, m)
        return (c, z, 1 - y, m)

    def flip_y(c, z, y, m):
        return (c, z, 1 - y, m)

    def flip_core(c, z, y, m):
        return (1 - c, z, y, m)

    def flip_x(c, z, y, m):
        return (c, z, y, 1 - m)

    def flip_z(c, z, y, m):
        return (c, z + 1 - 2 * (z % 2), y, m)

    mine, given = pl.pallas_call(
        mask_kernel,
        out_shape=[jax.ShapeDtypeStruct((length + INFO, half), jnp.bfloat16)] * 2,
        in_specs=[vmem] * 4,
        out_specs=[vmem] * 2,
        compiler_params=pltpu.CompilerParams(vmem_limit_bytes=56 * 2**20),
    )(signal, mask_token, keep, target_shard)
    near, far, columns = pl.pallas_call(
        slice_kernel,
        out_shape=[jax.ShapeDtypeStruct(shape, jnp.bfloat16) for shape in (
            (3, depth, wide), (3, depth, wide), (half, half),
        )],
        in_specs=[anywhere] * 3,
        out_specs=[vmem] * 3,
        scratch_shapes=[pltpu.SemaphoreType.DMA((3,))],
        compiler_params=pltpu.CompilerParams(vmem_limit_bytes=56 * 2**20),
    )(mine, enc_weight, pred_weight)
    first, second = move(mine, across_z), move(given, across_zy)
    first, second, near = lax.optimization_barrier((first, second, near))
    x_own = jnp.stack([first, second])
    near_w = move(near, to_near)
    x_near = move(x_own, flip_z)
    x_across = move(x_own, flip_x)
    far, x_across = lax.optimization_barrier((far, x_across))
    far_w = move(far, to_far)
    near_y = move(near_w, flip_y)
    x_near, x_across = lax.optimization_barrier((x_near, x_across))
    x_near_across = move(x_near, flip_x)
    far_y = move(far_w, flip_y)
    columns, _ = lax.optimization_barrier((columns, x_near_across))
    columns = move(columns, flip_x)
    shown = [x_own, x_across, x_near, x_near_across]

    def edge(own, near):
        found = jnp.where(z % 2 == 1 - core, own, near)
        part = jnp.where(core == 0, 1 - y, y)
        first = jnp.where(core == 0, length - WIN, 0)
        return lax.dynamic_slice(found, (part, first, 0), (1, WIN, half))[0]

    halo = move(jnp.stack([edge(x_own, x_near), edge(x_across, x_near_across)]), flip_core)
    near_yc = move(near_y, flip_core)
    far_yc_source, near_yc, halo = lax.optimization_barrier((far_y, near_yc, halo))
    pieces = [
        near_w, move(near_w, flip_core), near_y, near_yc,
        far_w, move(far_w, flip_core), far_y, move(far_yc_source, flip_core),
    ]
    span = 4 * length + 2 * WIN

    latent, info = pl.pallas_call(
        encode_kernel,
        out_shape=[
            jax.ShapeDtypeStruct((4, length, wide), jnp.bfloat16),
            jax.ShapeDtypeStruct((2, INFO, 128), jnp.bfloat16),
        ],
        in_specs=[pl.BlockSpec(memory_space=pltpu.HBM)] * (5 + PIECES),
        out_specs=[vmem] * 2,
        scratch_shapes=[
            pltpu.VMEM((span, 2 * half), jnp.bfloat16),
            pltpu.VMEM((3, 2 * half, wide), jnp.bfloat16),
            pltpu.VMEM((4 * length, wide), jnp.bfloat16),
            pltpu.VMEM((span, wide), jnp.bfloat16),
            pltpu.VMEM((span, wide), jnp.bfloat16),
            pltpu.SemaphoreType.DMA((12 + PIECES,)),
        ],
        compiler_params=pltpu.CompilerParams(vmem_limit_bytes=56 * 2**20),
    )(*shown, halo, *pieces)
    columns, latent = lax.optimization_barrier((columns, latent))
    columns_c = move(columns, flip_core)
    words = jnp.where(z // 2 == z % 2, info[0, 0], info[1, 0]).astype(jnp.int32)
    words = words.reshape(2, sequences, per_range)
    shard_of = words[0].reshape(-1)
    hidden = lax.dynamic_index_in_dim(words[1], y, 0, keepdims=False) == 0
    blocks = shard_of.shape[0]
    capacity = max(2, 2 * blocks // 8)
    order_ids = jnp.arange(blocks)
    earlier = (shard_of[:, None] == shard_of[None, :]) & (order_ids[:, None] < order_ids[None, :])
    slot = shard_of * capacity + jnp.sum(earlier.astype(jnp.int32), axis=0)
    slot = lax.dynamic_index_in_dim(slot.reshape(sequences, -1), y, 0, keepdims=False)
    slot = jnp.where(hidden, slot, -1)
    slot = lax.dynamic_slice_in_dim(slot, m * (per_range // 2), per_range // 2)
    slot = jnp.repeat(slot, block_len)[:, None]
    lines = [[4 * i + 2 * j + k for i in range(4) for k in range(2)] for j in range(2)]
    latents = lax.all_to_all(
        latent.reshape(8, length // 2, wide), ("seq", "mdl"),
        split_axis=0, concat_axis=0, tiled=True, axis_index_groups=lines,
    )
    routed = pl.pallas_call(
        predict_kernel,
        out_shape=jax.ShapeDtypeStruct((16, 1, 8 * capacity), jnp.float32),
        in_specs=[vmem] * 5,
        out_specs=vmem,
        compiler_params=pltpu.CompilerParams(vmem_limit_bytes=56 * 2**20),
    )(
        slot, latents, pred_weight, columns, columns_c
    )
    arrived = lax.all_to_all(routed, ("seq", "mdl"), split_axis=0, concat_axis=0, tiled=True)
    mine = lax.dynamic_slice_in_dim(arrived[:, 0], capacity * s, capacity, 1)
    summed = jnp.sum(mine.reshape(4, 4, capacity), axis=1)
    return summed.reshape(1, -1) / float(block_len * 2 * half)


def solution(mesh):
    placed = (
        P(None, "seq", "mdl"),
        P("mdl"),
        P(None, "seq"),
        P(None, "seq"),
        P("grp", None, "seq", "mdl"),
        P(None, "mdl"),
    )
    plan = local_lines if mesh.shape["seq"] == 8 else local
    return jax.shard_map(
        plan, mesh=mesh, in_specs=placed, out_specs=P("seq", "grp"), check_vma=False
    )
```

```python
import functools
import math

import jax
import jax.numpy as jnp
from jax import lax
from jax.experimental import pallas as pl
from jax.experimental.pallas import tpu as pltpu
from jax.sharding import PartitionSpec as P

HD = 128
WIN = 64
AXES = ("grp", "seq", "mdl")
PIECES = 8


def padded(x, sides, width):
    for axis, dim in sides:
        count, length = (lax.axis_size(axis), x.shape[dim])
        up = [(i, (i + 1) % count) for i in range(count - 1)]
        down = [(j, i) for i, j in up]
        last = lax.slice_in_dim(x, length - width, length, axis=dim)
        leading = lax.slice_in_dim(x, 0, width, axis=dim)
        before = lax.ppermute(last, axis, up)
        after = lax.ppermute(leading, axis, down)
        x = jnp.concatenate([before, x, after], axis=dim)
    return x


def predict(context, target, live_flags, pred_weight, divisor):
    flat_rows = context.reshape(-1, context.shape[-1])
    wide_rows = lax.all_gather(flat_rows, "mdl", axis=1, tiled=True)
    predicted = jnp.dot(wide_rows, pred_weight, preferred_element_type=jnp.float32)
    residue = predicted - target.reshape(flat_rows.shape).astype(jnp.float32)
    partial_sums = jnp.sum((residue * residue).reshape(live_flags.shape[0], -1), axis=1)
    summed = lax.psum(partial_sums, "mdl")
    return summed / divisor * live_flags


def local(signal, mask_token, keep, target_shard, enc_weight, pred_weight):
    group_index = lax.axis_index("grp")
    seq_index = lax.axis_index("seq")
    shards = lax.axis_size("seq")
    sequences, length, half_width = signal.shape
    per_range = keep.shape[1]
    block_len = length // per_range
    kept_rows = jnp.repeat(keep, block_len, axis=1)[:, :, None]
    masked_in = jnp.where(kept_rows == 1, signal, mask_token[None, None, :])
    source = jnp.where(group_index == 0, masked_in, signal)
    wide_in = lax.all_gather(source, "mdl", axis=2, tiled=True)
    full_width = wide_in.shape[2]
    flat_in = wide_in.reshape(-1, full_width)
    span = length + 2 * WIN
    weight_all = lax.all_gather(enc_weight, "seq", axis=2, tiled=True)[0]
    queries = jnp.dot(flat_in, weight_all[0], preferred_element_type=jnp.float32).astype(
        jnp.bfloat16
    )
    pair_made = jnp.einsum(
        "nd,cde->cne", flat_in, weight_all[1:], preferred_element_type=jnp.float32
    ).astype(jnp.bfloat16)
    own_pairs = pair_made.reshape(2, sequences, length, half_width)
    pair_rows = padded(own_pairs, (("seq", 2),), WIN)
    head_count = half_width // HD
    query_heads = queries.reshape(sequences, length, head_count, HD)
    key_heads = pair_rows[0].reshape(sequences, span, head_count, HD)
    value_heads = pair_rows[1].reshape(sequences, span, head_count, HD)
    query_pos = seq_index * length + jnp.arange(length)
    key_pos = seq_index * length - WIN + jnp.arange(span)
    total_len = length * shards
    in_window = (
        (jnp.abs(query_pos[:, None] - key_pos[None, :]) <= WIN)
        & (key_pos[None, :] >= 0)
        & (key_pos[None, :] < total_len)
    )
    scores = jnp.einsum(
        "sahd,sbhd->shab", query_heads, key_heads, preferred_element_type=jnp.float32
    ) * (1.0 / math.sqrt(HD))
    scores = jnp.where(in_window[None, None], scores, -jnp.inf)
    row_peak = jnp.max(scores, axis=-1, keepdims=True)
    exp_scores = jnp.exp(scores - row_peak)
    attention = (exp_scores / jnp.sum(exp_scores, axis=-1, keepdims=True)).astype(jnp.bfloat16)
    attended = jnp.einsum(
        "shab,sbhd->sahd", attention, value_heads, preferred_element_type=jnp.float32
    ).astype(jnp.bfloat16)
    latent = attended.reshape(sequences * per_range, block_len, half_width)
    blocks_here = latent.shape[0]
    capacity = max(2, 2 * blocks_here // shards)
    slot_count = shards * capacity
    shard_of = target_shard.reshape(-1)
    masked_flag = (keep.reshape(-1) == 0).astype(jnp.float32)
    order_ids = jnp.arange(blocks_here)
    earlier = (shard_of[:, None] == shard_of[None, :]) & (order_ids[:, None] < order_ids[None, :])
    slot_rank = jnp.sum(earlier.astype(jnp.int32), axis=0)
    slot_index = shard_of * capacity + slot_rank
    onehot = slot_index[None, :] == jnp.arange(slot_count)[:, None]
    divisor = float(block_len * full_width)
    halves = lax.all_to_all(latent[None], "grp", split_axis=1, concat_axis=0, tiled=True)
    half_count = blocks_here // 2
    first_block = group_index * half_count
    own_flags = lax.dynamic_slice_in_dim(masked_flag, first_block, half_count)
    losses = predict(halves[0], halves[1], own_flags, pred_weight, divisor)
    spread = lax.dynamic_update_slice_in_dim(
        jnp.zeros((blocks_here,), jnp.float32), losses, first_block, 0
    )
    slotted = jnp.sum(jnp.where(onehot, spread[None, :], 0.0), axis=1).reshape(shards, capacity)
    arrived = lax.all_to_all(slotted, "seq", split_axis=0, concat_axis=0, tiled=True)
    result = lax.psum_scatter(arrived, "grp", scatter_dimension=0, tiled=True)
    return result.reshape(1, -1)


def move(x, target):
    pairs = []
    for c in range(2):
        for s in range(8):
            for m in range(2):
                c2, z2, y2, m2 = target(c, s // 2, s % 2, m)
                pairs.append(((c * 8 + s) * 2 + m, (c2 * 8 + 2 * z2 + y2) * 2 + m2))
    return lax.ppermute(x, AXES, pairs)


def places():
    s = lax.axis_index("seq")
    return lax.axis_index("grp"), s // 2, lax.rem(s, 2), lax.axis_index("mdl")


def mask_kernel(signal_ref, token_ref, keep_ref, mine_ref, given_ref):
    core, _, y, _ = places()
    length = signal_ref.shape[1]
    blocks = keep_ref.shape[1]
    block_len = length // blocks
    row = lax.broadcasted_iota(jnp.int32, (length, blocks), 0)
    first = lax.broadcasted_iota(jnp.int32, (length, blocks), 1) * block_len
    covers = (row >= first) & (row < first + block_len)
    token = token_ref[...].astype(jnp.float32).reshape(1, -1)
    for target, chosen in ((mine_ref, y), (given_ref, 1 - y)):
        kept = jnp.where(covers, keep_ref[pl.ds(chosen, 1), :], 0)
        kept = jnp.sum(kept, axis=1, keepdims=True) + 1 - core
        rows = signal_ref[chosen].astype(jnp.float32)
        target[...] = jnp.where(kept > 0, rows, token).astype(target.dtype)


def slice_kernel(after_ref, weight_ref, pred_ref, near_ref, far_ref, early_ref, late_ref, sems):
    core, z, _, _ = places()
    wide = near_ref.shape[2]
    cut = early_ref.shape[0]
    t = lax.rem(z, 2)
    copies = []
    for target, chosen in ((near_ref, t), (far_ref, 1 - t)):
        lanes = pl.ds(pl.multiple_of(chosen * wide, 128), wide)
        copies.append((weight_ref.at[0, :, :, lanes], target))
    for index, target in enumerate((early_ref, late_ref)):
        first = pl.multiple_of((2 * core + index) * cut, 128)
        copies.append((pred_ref.at[pl.ds(first, cut), :], target))
    copies = [
        pltpu.make_async_copy(source, target, sems.at[index])
        for index, (source, target) in enumerate(copies)
    ]
    for copy in copies:
        copy.start()
    for copy in copies:
        copy.wait()


def encode_kernel(x_own, x_across, x_near, x_near_across, halo_ref, *refs):
    pieces = refs[:PIECES]
    out_ref, x_buf, w_buf, q_buf, k_buf, v_buf, sems = refs[PIECES:]
    core, z, y, m = places()
    half = x_own.shape[-1]
    rows = x_own.shape[1]
    depth = pieces[0].shape[1]
    wide = pieces[0].shape[2]
    own_rows = 4 * rows
    copies = []
    side = lax.rem(z, 2)
    for piece, near, across in (
        (x_own, 0, 0), (x_across, 0, 1), (x_near, 1, 0), (x_near_across, 1, 1)
    ):
        first = WIN + 2 * rows * (side if near == 0 else 1 - side)
        lane = half * (m if across == 0 else 1 - m)
        for part in range(2):
            copies.append((
                piece.at[part],
                x_buf.at[
                    pl.ds(pl.multiple_of(first + (y if part == 0 else 1 - y) * rows, 64), rows),
                    pl.ds(pl.multiple_of(lane, 128), half),
                ],
            ))
    halo_first = pl.multiple_of((1 - core) * (WIN + own_rows), 64)
    empty_first = pl.multiple_of(core * (WIN + own_rows), 64)
    for across in range(2):
        lane = half * (m if across == 0 else 1 - m)
        copies.append((
            halo_ref.at[across],
            x_buf.at[pl.ds(halo_first, WIN), pl.ds(pl.multiple_of(lane, 128), half)],
        ))
    t = lax.rem(z, 2)
    for index, piece in enumerate(pieces):
        crossed, other = (index // 2) % 2, index % 2
        low = core if (other == 0) == (index >= 4) else 1 - core
        pos_z = 2 * low + (t if index < 4 else 1 - t)
        pos = 2 * pos_z + (y if crossed == 0 else 1 - y)
        copies.append((
            piece, w_buf.at[:, pl.ds(pl.multiple_of(pos * depth, 64), depth), :]
        ))
    started = []
    for index, (source, target) in enumerate(copies):
        copy = pltpu.make_async_copy(source, target, sems.at[index])
        copy.start()
        started.append(copy)
    x_buf[pl.ds(empty_first, WIN), :] = jnp.zeros((WIN, 2 * half), x_buf.dtype)
    for copy in started:
        copy.wait()
    x = x_buf[...]
    q_buf[...] = jnp.dot(
        x[WIN:WIN + own_rows], w_buf[0], preferred_element_type=jnp.float32
    ).astype(q_buf.dtype)
    k_buf[...] = jnp.dot(x, w_buf[1], preferred_element_type=jnp.float32).astype(k_buf.dtype)
    v_buf[...] = jnp.dot(x, w_buf[2], preferred_element_type=jnp.float32).astype(v_buf.dtype)
    keys = rows + 2 * WIN
    a = lax.broadcasted_iota(jnp.int32, (rows, keys), 0)
    b = lax.broadcasted_iota(jnp.int32, (rows, keys), 1)
    band = (b >= a) & (b <= a + 2 * WIN)
    for j in range(4):
        admitted = band
        if j == 0:
            admitted = admitted & (b >= WIN * (1 - core))
        if j == 3:
            admitted = admitted & (b < keys - WIN * core)
        for h in range(wide // HD):
            lanes = slice(h * HD, (h + 1) * HD)
            scores = lax.dot_general(
                q_buf[j * rows:(j + 1) * rows, lanes],
                k_buf[j * rows:j * rows + keys, lanes],
                (((1,), (1,)), ((), ())),
                preferred_element_type=jnp.float32,
            ) * (1.0 / math.sqrt(HD))
            scores = jnp.where(admitted, scores, -jnp.inf)
            peak = jnp.max(scores, axis=-1, keepdims=True)
            exps = jnp.exp(scores - peak)
            attention = (exps / jnp.sum(exps, axis=-1, keepdims=True)).astype(jnp.bfloat16)
            out_ref[j, :, lanes] = jnp.dot(
                attention,
                v_buf[j * rows:j * rows + keys, lanes],
                preferred_element_type=jnp.float32,
            ).astype(out_ref.dtype)


def predict_kernel(slot_ref, lat_ref, own_ref, e0, e1, l0, l1, out_ref):
    core, _, _, m = places()
    wide = lat_ref.shape[2]
    lent = ((e0, e1), (l0, l1))
    total = None
    for side in range(2):
        predicted = None
        for t in range(2):
            for x in range(2):
                if side == 0:
                    source = lat_ref[2 * t + x]
                    weight = own_ref[(2 * x + t) * wide:(2 * x + t + 1) * wide, :]
                else:
                    source = lat_ref[2 * t + (core if x == 0 else 1 - core)]
                    weight = lent[t][x][...]
                term = jnp.dot(source, weight, preferred_element_type=jnp.float32)
                predicted = term if predicted is None else predicted + term
        for t in range(2):
            target = lat_ref[4 + 2 * t + (m if side == 0 else 1 - m)].astype(jnp.float32)
            residue = predicted[:, t * wide:(t + 1) * wide] - target
            for i in range(wide // 128):
                piece = residue[:, i * 128:(i + 1) * 128]
                total = piece * piece if total is None else total + piece * piece
    row_errors = jnp.sum(total, axis=1, keepdims=True)
    rows, slots = total.shape[0], out_ref.shape[2]
    chosen = slot_ref[...] == lax.broadcasted_iota(jnp.int32, (rows, slots), 1)
    routed = jnp.sum(jnp.where(chosen, row_errors, 0.0), axis=0, keepdims=True)
    for i in range(out_ref.shape[0]):
        out_ref[i] = routed


def local_lines(signal, mask_token, keep, target_shard, enc_weight, pred_weight):
    core = lax.axis_index("grp")
    s = lax.axis_index("seq")
    m = lax.axis_index("mdl")
    z, y = s // 2, s % 2
    sequences, length, half = signal.shape
    per_range = keep.shape[1]
    block_len = length // per_range
    depth = enc_weight.shape[2]
    wide = half // 2

    vmem = pl.BlockSpec(memory_space=pltpu.VMEM)
    anywhere = pl.BlockSpec(memory_space=pl.ANY)

    def to_near(c, z, y, m):
        return (1 - z // 2, z % 2 + 2 * c, y, m)

    def to_far(c, z, y, m):
        return (z // 2, 1 - z % 2 + 2 * c, y, m)

    def across_z(c, z, y, m):
        if z // 2 == c:
            return (c, (z + 2) % 4, y, m)
        return (1 - c, z, y, m)

    def across_zy(c, z, y, m):
        c, z, y, m = across_z(c, z, y, m)
        return (c, z, 1 - y, m)

    def flip_y(c, z, y, m):
        return (c, z, 1 - y, m)

    def flip_core(c, z, y, m):
        return (1 - c, z, y, m)

    def flip_x(c, z, y, m):
        return (c, z, y, 1 - m)

    def flip_z(c, z, y, m):
        return (c, z + 1 - 2 * (z % 2), y, m)

    cut = half // 2
    mine, given = pl.pallas_call(
        mask_kernel,
        out_shape=[jax.ShapeDtypeStruct((length, half), jnp.bfloat16)] * 2,
        in_specs=[vmem] * 3,
        out_specs=[vmem] * 2,
    )(signal, mask_token, keep)
    near, far, early, late = pl.pallas_call(
        slice_kernel,
        out_shape=[jax.ShapeDtypeStruct(shape, jnp.bfloat16) for shape in (
            (3, depth, wide), (3, depth, wide), (cut, half), (cut, half),
        )],
        in_specs=[anywhere] * 3,
        out_specs=[vmem] * 4,
        scratch_shapes=[pltpu.SemaphoreType.DMA((4,))],
    )(mine, enc_weight, pred_weight)
    first, second = move(mine, across_z), move(given, across_zy)
    small = jnp.stack([keep, target_shard])
    small, _ = lax.optimization_barrier((small, mine))
    routing = move(small, lambda c, z, y, m: ((2 * z + y) // 4, (2 * z + y) % 4, c, m))
    near, routing, first, second = lax.optimization_barrier((near, routing, first, second))
    x_own = jnp.stack([first, second])
    near_w = move(near, to_near)
    weight_early = move(early, flip_x)
    far, x_own = lax.optimization_barrier((far, x_own))
    far_w = move(far, to_far)
    x_near = move(x_own, flip_z)
    x_across = move(x_own, flip_x)
    near_y_source, weight_early = lax.optimization_barrier((near_w, weight_early))
    near_y = move(near_y_source, flip_y)
    far_y_source, near_y = lax.optimization_barrier((far_w, near_y))
    far_y = move(far_y_source, flip_y)
    weight_early_c = move(weight_early, flip_core)
    x_near, x_across = lax.optimization_barrier((x_near, x_across))
    x_near_across = move(x_near, flip_x)
    late, _ = lax.optimization_barrier((late, x_near_across))
    weight_late = move(late, flip_x)
    weight_late_c = move(weight_late, flip_core)
    hidden = lax.dynamic_index_in_dim(routing[0], y, 0, keepdims=False) == 0
    shard_of = routing[1].reshape(-1)
    blocks = shard_of.shape[0]
    capacity = max(2, 2 * blocks // 8)
    order_ids = jnp.arange(blocks)
    earlier = (shard_of[:, None] == shard_of[None, :]) & (order_ids[:, None] < order_ids[None, :])
    slot = shard_of * capacity + jnp.sum(earlier.astype(jnp.int32), axis=0)
    slot = lax.dynamic_index_in_dim(slot.reshape(sequences, -1), y, 0, keepdims=False)
    slot = jnp.where(hidden, slot, -1)
    slot = lax.dynamic_slice_in_dim(slot, m * (per_range // 2), per_range // 2)
    slot = jnp.repeat(slot, block_len)[:, None]

    def edge(own, near):
        found = jnp.where(z % 2 == 1 - core, own, near)
        part = jnp.where(core == 0, 1 - y, y)
        first = jnp.where(core == 0, length - WIN, 0)
        return lax.dynamic_slice(found, (part, first, 0), (1, WIN, half))[0]

    halo = move(jnp.stack([edge(x_own, x_near), edge(x_across, x_near_across)]), flip_core)
    far_yc_source, halo = lax.optimization_barrier((far_y, halo))
    pieces = [
        near_w, move(near_w, flip_core), near_y, move(near_y, flip_core),
        far_w, move(far_w, flip_core), far_y, move(far_yc_source, flip_core),
    ]
    span = 4 * length + 2 * WIN

    latent = pl.pallas_call(
        encode_kernel,
        out_shape=jax.ShapeDtypeStruct((4, length, wide), jnp.bfloat16),
        in_specs=[anywhere] * (5 + PIECES),
        out_specs=vmem,
        scratch_shapes=[
            pltpu.VMEM((span, 2 * half), jnp.bfloat16),
            pltpu.VMEM((3, 2 * half, wide), jnp.bfloat16),
            pltpu.VMEM((4 * length, wide), jnp.bfloat16),
            pltpu.VMEM((span, wide), jnp.bfloat16),
            pltpu.VMEM((span, wide), jnp.bfloat16),
            pltpu.SemaphoreType.DMA((10 + PIECES,)),
        ],
        compiler_params=pltpu.CompilerParams(vmem_limit_bytes=56 * 2**20),
    )(x_own, x_across, x_near, x_near_across, halo, *pieces)
    lines = [[4 * i + 2 * j + k for i in range(4) for k in range(2)] for j in range(2)]
    latents = lax.all_to_all(
        latent.reshape(8, length // 2, wide), ("seq", "mdl"),
        split_axis=0, concat_axis=0, tiled=True, axis_index_groups=lines,
    )
    routed = pl.pallas_call(
        predict_kernel,
        out_shape=jax.ShapeDtypeStruct((16, 1, 8 * capacity), jnp.float32),
        in_specs=[vmem] * 7,
        out_specs=vmem,
        compiler_params=pltpu.CompilerParams(vmem_limit_bytes=24 * 2**20),
    )(
        slot, latents, pred_weight,
        weight_early, weight_early_c, weight_late, weight_late_c,
    )
    arrived = lax.all_to_all(routed, ("seq", "mdl"), split_axis=0, concat_axis=0, tiled=True)
    mine = lax.dynamic_slice_in_dim(arrived[:, 0], capacity * s, capacity, 1)
    summed = jnp.sum(mine.reshape(4, 4, capacity), axis=1)
    return summed.reshape(1, -1) / float(block_len * 2 * half)


def solution(mesh):
    placed = (
        P(None, "seq", "mdl"),
        P("mdl"),
        P(None, "seq"),
        P(None, "seq"),
        P("grp", None, "seq", "mdl"),
        P(None, "mdl"),
    )
    plan = local_lines if mesh.shape["seq"] == 8 else local
    return jax.shard_map(
        plan, mesh=mesh, in_specs=placed, out_specs=P("seq", "grp"), check_vma=False
    )
```

```python
import functools
import math

import jax
import jax.numpy as jnp
from jax import lax
from jax.experimental import pallas as pl
from jax.experimental.pallas import tpu as pltpu
from jax.sharding import PartitionSpec as P

HD = 128
WIN = 64
AXES = ("grp", "seq", "mdl")
PIECES = 8


def padded(x, sides, width):
    for axis, dim in sides:
        count, length = (lax.axis_size(axis), x.shape[dim])
        up = [(i, (i + 1) % count) for i in range(count - 1)]
        down = [(j, i) for i, j in up]
        last = lax.slice_in_dim(x, length - width, length, axis=dim)
        leading = lax.slice_in_dim(x, 0, width, axis=dim)
        before = lax.ppermute(last, axis, up)
        after = lax.ppermute(leading, axis, down)
        x = jnp.concatenate([before, x, after], axis=dim)
    return x


def predict(context, target, live_flags, pred_weight, divisor):
    flat_rows = context.reshape(-1, context.shape[-1])
    wide_rows = lax.all_gather(flat_rows, "mdl", axis=1, tiled=True)
    predicted = jnp.dot(wide_rows, pred_weight, preferred_element_type=jnp.float32)
    residue = predicted - target.reshape(flat_rows.shape).astype(jnp.float32)
    partial_sums = jnp.sum((residue * residue).reshape(live_flags.shape[0], -1), axis=1)
    summed = lax.psum(partial_sums, "mdl")
    return summed / divisor * live_flags


def local(signal, mask_token, keep, target_shard, enc_weight, pred_weight):
    group_index = lax.axis_index("grp")
    seq_index = lax.axis_index("seq")
    shards = lax.axis_size("seq")
    sequences, length, half_width = signal.shape
    per_range = keep.shape[1]
    block_len = length // per_range
    kept_rows = jnp.repeat(keep, block_len, axis=1)[:, :, None]
    masked_in = jnp.where(kept_rows == 1, signal, mask_token[None, None, :])
    source = jnp.where(group_index == 0, masked_in, signal)
    wide_in = lax.all_gather(source, "mdl", axis=2, tiled=True)
    full_width = wide_in.shape[2]
    flat_in = wide_in.reshape(-1, full_width)
    span = length + 2 * WIN
    weight_all = lax.all_gather(enc_weight, "seq", axis=2, tiled=True)[0]
    queries = jnp.dot(flat_in, weight_all[0], preferred_element_type=jnp.float32).astype(
        jnp.bfloat16
    )
    pair_made = jnp.einsum(
        "nd,cde->cne", flat_in, weight_all[1:], preferred_element_type=jnp.float32
    ).astype(jnp.bfloat16)
    own_pairs = pair_made.reshape(2, sequences, length, half_width)
    pair_rows = padded(own_pairs, (("seq", 2),), WIN)
    head_count = half_width // HD
    query_heads = queries.reshape(sequences, length, head_count, HD)
    key_heads = pair_rows[0].reshape(sequences, span, head_count, HD)
    value_heads = pair_rows[1].reshape(sequences, span, head_count, HD)
    query_pos = seq_index * length + jnp.arange(length)
    key_pos = seq_index * length - WIN + jnp.arange(span)
    total_len = length * shards
    in_window = (
        (jnp.abs(query_pos[:, None] - key_pos[None, :]) <= WIN)
        & (key_pos[None, :] >= 0)
        & (key_pos[None, :] < total_len)
    )
    scores = jnp.einsum(
        "sahd,sbhd->shab", query_heads, key_heads, preferred_element_type=jnp.float32
    ) * (1.0 / math.sqrt(HD))
    scores = jnp.where(in_window[None, None], scores, -jnp.inf)
    row_peak = jnp.max(scores, axis=-1, keepdims=True)
    exp_scores = jnp.exp(scores - row_peak)
    attention = (exp_scores / jnp.sum(exp_scores, axis=-1, keepdims=True)).astype(jnp.bfloat16)
    attended = jnp.einsum(
        "shab,sbhd->sahd", attention, value_heads, preferred_element_type=jnp.float32
    ).astype(jnp.bfloat16)
    latent = attended.reshape(sequences * per_range, block_len, half_width)
    blocks_here = latent.shape[0]
    capacity = max(2, 2 * blocks_here // shards)
    slot_count = shards * capacity
    shard_of = target_shard.reshape(-1)
    masked_flag = (keep.reshape(-1) == 0).astype(jnp.float32)
    order_ids = jnp.arange(blocks_here)
    earlier = (shard_of[:, None] == shard_of[None, :]) & (order_ids[:, None] < order_ids[None, :])
    slot_rank = jnp.sum(earlier.astype(jnp.int32), axis=0)
    slot_index = shard_of * capacity + slot_rank
    onehot = slot_index[None, :] == jnp.arange(slot_count)[:, None]
    divisor = float(block_len * full_width)
    halves = lax.all_to_all(latent[None], "grp", split_axis=1, concat_axis=0, tiled=True)
    half_count = blocks_here // 2
    first_block = group_index * half_count
    own_flags = lax.dynamic_slice_in_dim(masked_flag, first_block, half_count)
    losses = predict(halves[0], halves[1], own_flags, pred_weight, divisor)
    spread = lax.dynamic_update_slice_in_dim(
        jnp.zeros((blocks_here,), jnp.float32), losses, first_block, 0
    )
    slotted = jnp.sum(jnp.where(onehot, spread[None, :], 0.0), axis=1).reshape(shards, capacity)
    arrived = lax.all_to_all(slotted, "seq", split_axis=0, concat_axis=0, tiled=True)
    result = lax.psum_scatter(arrived, "grp", scatter_dimension=0, tiled=True)
    return result.reshape(1, -1)


def move(x, target):
    pairs = []
    for c in range(2):
        for s in range(8):
            for m in range(2):
                c2, z2, y2, m2 = target(c, s // 2, s % 2, m)
                pairs.append(((c * 8 + s) * 2 + m, (c2 * 8 + 2 * z2 + y2) * 2 + m2))
    return lax.ppermute(x, AXES, pairs)


def places():
    s = lax.axis_index("seq")
    return lax.axis_index("grp"), s // 2, lax.rem(s, 2), lax.axis_index("mdl")


def mask_kernel(signal_ref, token_ref, keep_ref, mine_ref, given_ref):
    core, _, y, _ = places()
    length = signal_ref.shape[1]
    blocks = keep_ref.shape[1]
    block_len = length // blocks
    row = lax.broadcasted_iota(jnp.int32, (length, blocks), 0)
    first = lax.broadcasted_iota(jnp.int32, (length, blocks), 1) * block_len
    covers = (row >= first) & (row < first + block_len)
    token = token_ref[...].astype(jnp.float32).reshape(1, -1)
    for target, chosen in ((mine_ref, y), (given_ref, 1 - y)):
        kept = jnp.where(covers, keep_ref[pl.ds(chosen, 1), :], 0)
        kept = jnp.sum(kept, axis=1, keepdims=True) + 1 - core
        rows = signal_ref[chosen].astype(jnp.float32)
        target[...] = jnp.where(kept > 0, rows, token).astype(target.dtype)


def copy_all(pairs, sems):
    copies = [
        pltpu.make_async_copy(source, target, sems.at[index])
        for index, (source, target) in enumerate(pairs)
    ]
    for copy in copies:
        copy.start()
    return copies


def slice_kernel(
    after_ref, weight_ref, pred_ref, near_ref, far_ref, far_v_ref, early_ref, late_ref, sems
):
    core, z, _, _ = places()
    wide = near_ref.shape[2]
    cut = early_ref.shape[0]
    t = lax.rem(z, 2)
    lanes = [
        pl.ds(pl.multiple_of(chosen * wide, 128), wide) for chosen in (t, 1 - t)
    ]
    pairs = [
        (weight_ref.at[0, :, :, lanes[0]], near_ref),
        (weight_ref.at[0, pl.ds(0, 2), :, lanes[1]], far_ref),
        (weight_ref.at[0, pl.ds(2, 1), :, lanes[1]], far_v_ref),
    ]
    for index, target in enumerate((early_ref, late_ref)):
        first = pl.multiple_of((2 * core + index) * cut, 128)
        pairs.append((pred_ref.at[pl.ds(first, cut), :], target))
    for copy in copy_all(pairs, sems):
        copy.wait()


def row_places(index, depth):
    core, z, y, _ = places()
    t = lax.rem(z, 2)
    crossed, other = (index // 2) % 2, index % 2
    low = core if (other == 0) == (index >= 4) else 1 - core
    pos = 2 * (2 * low + (t if index < 4 else 1 - t)) + (y if crossed == 0 else 1 - y)
    return pl.ds(pl.multiple_of(pos * depth, 64), depth)


def score_kernel(x_own, x_across, x_near, x_near_across, halo_ref, *refs):
    pieces = refs[:PIECES]
    out_ref, x_buf, w_buf, q_buf, k_buf, sems = refs[PIECES:]
    core, z, y, m = places()
    half = x_own.shape[-1]
    rows = x_own.shape[1]
    depth = pieces[0].shape[1]
    wide = pieces[0].shape[2]
    own_rows = 4 * rows
    pairs = []
    side = lax.rem(z, 2)
    for piece, near, across in (
        (x_own, 0, 0), (x_across, 0, 1), (x_near, 1, 0), (x_near_across, 1, 1)
    ):
        first = WIN + 2 * rows * (side if near == 0 else 1 - side)
        lane = half * (m if across == 0 else 1 - m)
        for part in range(2):
            pairs.append((
                piece.at[part],
                x_buf.at[
                    pl.ds(pl.multiple_of(first + (y if part == 0 else 1 - y) * rows, 64), rows),
                    pl.ds(pl.multiple_of(lane, 128), half),
                ],
            ))
    halo_first = pl.multiple_of((1 - core) * (WIN + own_rows), 64)
    empty_first = pl.multiple_of(core * (WIN + own_rows), 64)
    for across in range(2):
        lane = half * (m if across == 0 else 1 - m)
        pairs.append((
            halo_ref.at[across],
            x_buf.at[pl.ds(halo_first, WIN), pl.ds(pl.multiple_of(lane, 128), half)],
        ))
    for index, piece in enumerate(pieces):
        pairs.append((piece.at[pl.ds(0, 2)], w_buf.at[:, row_places(index, depth), :]))
    copies = copy_all(pairs, sems)
    x_buf[pl.ds(empty_first, WIN), :] = jnp.zeros((WIN, 2 * half), x_buf.dtype)
    for copy in copies:
        copy.wait()
    x = x_buf[...]
    q_buf[...] = jnp.dot(
        x[WIN:WIN + own_rows], w_buf[0], preferred_element_type=jnp.float32
    ).astype(q_buf.dtype)
    k_buf[...] = jnp.dot(x, w_buf[1], preferred_element_type=jnp.float32).astype(k_buf.dtype)
    keys = rows + 2 * WIN
    a = lax.broadcasted_iota(jnp.int32, (rows, keys), 0)
    b = lax.broadcasted_iota(jnp.int32, (rows, keys), 1)
    band = (b >= a) & (b <= a + 2 * WIN)
    for j in range(4):
        admitted = band
        if j == 0:
            admitted = admitted & (b >= WIN * (1 - core))
        if j == 3:
            admitted = admitted & (b < keys - WIN * core)
        for h in range(wide // HD):
            lanes = slice(h * HD, (h + 1) * HD)
            scores = lax.dot_general(
                q_buf[j * rows:(j + 1) * rows, lanes],
                k_buf[j * rows:j * rows + keys, lanes],
                (((1,), (1,)), ((), ())),
                preferred_element_type=jnp.float32,
            ) * (1.0 / math.sqrt(HD))
            scores = jnp.where(admitted, scores, -jnp.inf)
            peak = jnp.max(scores, axis=-1, keepdims=True)
            exps = jnp.exp(scores - peak)
            out_ref[j, h] = (exps / jnp.sum(exps, axis=-1, keepdims=True)).astype(out_ref.dtype)


def value_kernel(attention_ref, x_ref, *refs):
    pieces = refs[:PIECES]
    out_ref, w_buf, v_buf, sems = refs[PIECES:]
    depth = pieces[0].shape[1]
    pairs = [
        (piece.at[piece.shape[0] - 1], w_buf.at[row_places(index, depth), :])
        for index, piece in enumerate(pieces)
    ]
    for copy in copy_all(pairs, sems):
        copy.wait()
    v_buf[...] = jnp.dot(
        x_ref[...], w_buf[...], preferred_element_type=jnp.float32
    ).astype(v_buf.dtype)
    _, heads, rows, keys = attention_ref.shape
    for j in range(4):
        for h in range(heads):
            lanes = slice(h * HD, (h + 1) * HD)
            out_ref[j, :, lanes] = jnp.dot(
                attention_ref[j, h],
                v_buf[j * rows:j * rows + keys, lanes],
                preferred_element_type=jnp.float32,
            ).astype(out_ref.dtype)


def predict_kernel(slot_ref, lat_ref, own_ref, e0, e1, l0, l1, out_ref):
    core, _, _, m = places()
    wide = lat_ref.shape[2]
    lent = ((e0, e1), (l0, l1))
    total = None
    for side in range(2):
        predicted = None
        for t in range(2):
            for x in range(2):
                if side == 0:
                    source = lat_ref[2 * t + x]
                    weight = own_ref[(2 * x + t) * wide:(2 * x + t + 1) * wide, :]
                else:
                    source = lat_ref[2 * t + (core if x == 0 else 1 - core)]
                    weight = lent[t][x][...]
                term = jnp.dot(source, weight, preferred_element_type=jnp.float32)
                predicted = term if predicted is None else predicted + term
        for t in range(2):
            target = lat_ref[4 + 2 * t + (m if side == 0 else 1 - m)].astype(jnp.float32)
            residue = predicted[:, t * wide:(t + 1) * wide] - target
            for i in range(wide // 128):
                piece = residue[:, i * 128:(i + 1) * 128]
                total = piece * piece if total is None else total + piece * piece
    row_errors = jnp.sum(total, axis=1, keepdims=True)
    rows, slots = total.shape[0], out_ref.shape[2]
    chosen = slot_ref[...] == lax.broadcasted_iota(jnp.int32, (rows, slots), 1)
    routed = jnp.sum(jnp.where(chosen, row_errors, 0.0), axis=0, keepdims=True)
    for i in range(out_ref.shape[0]):
        out_ref[i] = routed


def local_lines(signal, mask_token, keep, target_shard, enc_weight, pred_weight):
    core = lax.axis_index("grp")
    s = lax.axis_index("seq")
    m = lax.axis_index("mdl")
    z, y = s // 2, s % 2
    sequences, length, half = signal.shape
    per_range = keep.shape[1]
    block_len = length // per_range
    depth = enc_weight.shape[2]
    wide = half // 2

    vmem = pl.BlockSpec(memory_space=pltpu.VMEM)
    anywhere = pl.BlockSpec(memory_space=pl.ANY)

    def to_near(c, z, y, m):
        return (1 - z // 2, z % 2 + 2 * c, y, m)

    def to_far(c, z, y, m):
        return (z // 2, 1 - z % 2 + 2 * c, y, m)

    def across_z(c, z, y, m):
        if z // 2 == c:
            return (c, (z + 2) % 4, y, m)
        return (1 - c, z, y, m)

    def across_zy(c, z, y, m):
        c, z, y, m = across_z(c, z, y, m)
        return (c, z, 1 - y, m)

    def flip_y(c, z, y, m):
        return (c, z, 1 - y, m)

    def flip_core(c, z, y, m):
        return (1 - c, z, y, m)

    def flip_x(c, z, y, m):
        return (c, z, y, 1 - m)

    def flip_z(c, z, y, m):
        return (c, z + 1 - 2 * (z % 2), y, m)

    cut = half // 2
    mine, given = pl.pallas_call(
        mask_kernel,
        out_shape=[jax.ShapeDtypeStruct((length, half), jnp.bfloat16)] * 2,
        in_specs=[vmem] * 3,
        out_specs=[vmem] * 2,
    )(signal, mask_token, keep)
    near, far, far_v, early, late = pl.pallas_call(
        slice_kernel,
        out_shape=[jax.ShapeDtypeStruct(shape, jnp.bfloat16) for shape in (
            (3, depth, wide), (2, depth, wide), (1, depth, wide), (cut, half), (cut, half),
        )],
        in_specs=[anywhere] * 3,
        out_specs=[vmem] * 5,
        scratch_shapes=[pltpu.SemaphoreType.DMA((5,))],
        compiler_params=pltpu.CompilerParams(vmem_limit_bytes=62 * 2**20),
    )(mine, enc_weight, pred_weight)
    first, second = move(mine, across_z), move(given, across_zy)
    small = jnp.stack([keep, target_shard])
    small, _ = lax.optimization_barrier((small, mine))
    routing = move(small, lambda c, z, y, m: ((2 * z + y) // 4, (2 * z + y) % 4, c, m))
    near, routing, first, second = lax.optimization_barrier((near, routing, first, second))
    x_own = jnp.stack([first, second])
    near_w = move(near, to_near)
    weight_early = move(early, flip_x)
    x_near = move(x_own, flip_z)
    x_across = move(x_own, flip_x)
    far, x_across = lax.optimization_barrier((far, x_across))
    far_w = move(far, to_far)
    near_y = move(near_w, flip_y)
    far_v, near_w = lax.optimization_barrier((far_v, near_w))
    far_v = move(far_v, to_far)
    x_near, x_across, far_w = lax.optimization_barrier((x_near, x_across, far_w))
    x_near_across = move(x_near, flip_x)
    far_y_source, near_y, weight_early = lax.optimization_barrier((far_w, near_y, weight_early))
    far_y = move(far_y_source, flip_y)
    far_vy = move(far_v, flip_y)
    weight_early_c = move(weight_early, flip_core)
    late, _ = lax.optimization_barrier((late, x_near_across))
    weight_late = move(late, flip_x)
    weight_late_c = move(weight_late, flip_core)
    hidden = lax.dynamic_index_in_dim(routing[0], y, 0, keepdims=False) == 0
    shard_of = routing[1].reshape(-1)
    blocks = shard_of.shape[0]
    capacity = max(2, 2 * blocks // 8)
    order_ids = jnp.arange(blocks)
    earlier = (shard_of[:, None] == shard_of[None, :]) & (order_ids[:, None] < order_ids[None, :])
    slot = shard_of * capacity + jnp.sum(earlier.astype(jnp.int32), axis=0)
    slot = lax.dynamic_index_in_dim(slot.reshape(sequences, -1), y, 0, keepdims=False)
    slot = jnp.where(hidden, slot, -1)
    slot = lax.dynamic_slice_in_dim(slot, m * (per_range // 2), per_range // 2)
    slot = jnp.repeat(slot, block_len)[:, None]

    def edge(own, near):
        found = jnp.where(z % 2 == 1 - core, own, near)
        part = jnp.where(core == 0, 1 - y, y)
        first = jnp.where(core == 0, length - WIN, 0)
        return lax.dynamic_slice(found, (part, first, 0), (1, WIN, half))[0]

    edges = jnp.stack([edge(x_own, x_near), edge(x_across, x_near_across)])
    edges, far_v, near_y = lax.optimization_barrier((edges, far_v, near_y))
    halo = move(edges, flip_core)
    far_yc_source, halo = lax.optimization_barrier((far_y, halo))
    far_yc, far_vy = lax.optimization_barrier((move(far_yc_source, flip_core), far_vy))
    near_all = [near_w, move(near_w, flip_core), near_y, move(near_y, flip_core)]
    far_all = [far_w, move(far_w, flip_core), far_y, far_yc]
    far_v_all = [far_v, move(far_v, flip_core), far_vy, move(far_vy, flip_core)]
    span = 4 * length + 2 * WIN

    heads = wide // HD
    attention, shown = pl.pallas_call(
        score_kernel,
        out_shape=[
            jax.ShapeDtypeStruct((4, heads, length, length + 2 * WIN), jnp.bfloat16),
            jax.ShapeDtypeStruct((span, 2 * half), jnp.bfloat16),
        ],
        in_specs=[anywhere] * (5 + PIECES),
        out_specs=[vmem] * 2,
        scratch_shapes=[
            pltpu.VMEM((2, 2 * half, wide), jnp.bfloat16),
            pltpu.VMEM((4 * length, wide), jnp.bfloat16),
            pltpu.VMEM((span, wide), jnp.bfloat16),
            pltpu.SemaphoreType.DMA((10 + PIECES,)),
        ],
        compiler_params=pltpu.CompilerParams(vmem_limit_bytes=56 * 2**20),
    )(x_own, x_across, x_near, x_near_across, halo, *near_all, *far_all)
    latent = pl.pallas_call(
        value_kernel,
        out_shape=jax.ShapeDtypeStruct((4, length, wide), jnp.bfloat16),
        in_specs=[vmem] * 2 + [anywhere] * PIECES,
        out_specs=vmem,
        scratch_shapes=[
            pltpu.VMEM((2 * half, wide), jnp.bfloat16),
            pltpu.VMEM((span, wide), jnp.bfloat16),
            pltpu.SemaphoreType.DMA((PIECES,)),
        ],
        compiler_params=pltpu.CompilerParams(vmem_limit_bytes=56 * 2**20),
    )(attention, shown, *near_all, *far_v_all)
    lines = [[4 * i + 2 * j + k for i in range(4) for k in range(2)] for j in range(2)]
    latents = lax.all_to_all(
        latent.reshape(8, length // 2, wide), ("seq", "mdl"),
        split_axis=0, concat_axis=0, tiled=True, axis_index_groups=lines,
    )
    routed = pl.pallas_call(
        predict_kernel,
        out_shape=jax.ShapeDtypeStruct((16, 1, 8 * capacity), jnp.float32),
        in_specs=[vmem] * 7,
        out_specs=vmem,
        compiler_params=pltpu.CompilerParams(vmem_limit_bytes=24 * 2**20),
    )(
        slot, latents, pred_weight,
        weight_early, weight_early_c, weight_late, weight_late_c,
    )
    arrived = lax.all_to_all(routed, ("seq", "mdl"), split_axis=0, concat_axis=0, tiled=True)
    mine = lax.dynamic_slice_in_dim(arrived[:, 0], capacity * s, capacity, 1)
    summed = jnp.sum(mine.reshape(4, 4, capacity), axis=1)
    return summed.reshape(1, -1) / float(block_len * 2 * half)


def solution(mesh):
    placed = (
        P(None, "seq", "mdl"),
        P("mdl"),
        P(None, "seq"),
        P(None, "seq"),
        P("grp", None, "seq", "mdl"),
        P(None, "mdl"),
    )
    plan = local_lines if mesh.shape["seq"] == 8 else local
    return jax.shard_map(
        plan, mesh=mesh, in_specs=placed, out_specs=P("seq", "grp"), check_vma=False
    )
```

```python
import functools
import math

import jax
import jax.numpy as jnp
from jax import lax
from jax.experimental import pallas as pl
from jax.experimental.pallas import tpu as pltpu
from jax.sharding import PartitionSpec as P

HD = 128
WIN = 64
AXES = ("grp", "seq", "mdl")
PIECES = 8


def padded(x, sides, width):
    for axis, dim in sides:
        count, length = (lax.axis_size(axis), x.shape[dim])
        up = [(i, (i + 1) % count) for i in range(count - 1)]
        down = [(j, i) for i, j in up]
        last = lax.slice_in_dim(x, length - width, length, axis=dim)
        leading = lax.slice_in_dim(x, 0, width, axis=dim)
        before = lax.ppermute(last, axis, up)
        after = lax.ppermute(leading, axis, down)
        x = jnp.concatenate([before, x, after], axis=dim)
    return x


def predict(context, target, live_flags, pred_weight, divisor):
    flat_rows = context.reshape(-1, context.shape[-1])
    wide_rows = lax.all_gather(flat_rows, "mdl", axis=1, tiled=True)
    predicted = jnp.dot(wide_rows, pred_weight, preferred_element_type=jnp.float32)
    residue = predicted - target.reshape(flat_rows.shape).astype(jnp.float32)
    partial_sums = jnp.sum((residue * residue).reshape(live_flags.shape[0], -1), axis=1)
    summed = lax.psum(partial_sums, "mdl")
    return summed / divisor * live_flags


def local(signal, mask_token, keep, target_shard, enc_weight, pred_weight):
    group_index = lax.axis_index("grp")
    seq_index = lax.axis_index("seq")
    shards = lax.axis_size("seq")
    sequences, length, half_width = signal.shape
    per_range = keep.shape[1]
    block_len = length // per_range
    kept_rows = jnp.repeat(keep, block_len, axis=1)[:, :, None]
    masked_in = jnp.where(kept_rows == 1, signal, mask_token[None, None, :])
    source = jnp.where(group_index == 0, masked_in, signal)
    wide_in = lax.all_gather(source, "mdl", axis=2, tiled=True)
    full_width = wide_in.shape[2]
    flat_in = wide_in.reshape(-1, full_width)
    span = length + 2 * WIN
    weight_all = lax.all_gather(enc_weight, "seq", axis=2, tiled=True)[0]
    queries = jnp.dot(flat_in, weight_all[0], preferred_element_type=jnp.float32).astype(
        jnp.bfloat16
    )
    pair_made = jnp.einsum(
        "nd,cde->cne", flat_in, weight_all[1:], preferred_element_type=jnp.float32
    ).astype(jnp.bfloat16)
    own_pairs = pair_made.reshape(2, sequences, length, half_width)
    pair_rows = padded(own_pairs, (("seq", 2),), WIN)
    head_count = half_width // HD
    query_heads = queries.reshape(sequences, length, head_count, HD)
    key_heads = pair_rows[0].reshape(sequences, span, head_count, HD)
    value_heads = pair_rows[1].reshape(sequences, span, head_count, HD)
    query_pos = seq_index * length + jnp.arange(length)
    key_pos = seq_index * length - WIN + jnp.arange(span)
    total_len = length * shards
    in_window = (
        (jnp.abs(query_pos[:, None] - key_pos[None, :]) <= WIN)
        & (key_pos[None, :] >= 0)
        & (key_pos[None, :] < total_len)
    )
    scores = jnp.einsum(
        "sahd,sbhd->shab", query_heads, key_heads, preferred_element_type=jnp.float32
    ) * (1.0 / math.sqrt(HD))
    scores = jnp.where(in_window[None, None], scores, -jnp.inf)
    row_peak = jnp.max(scores, axis=-1, keepdims=True)
    exp_scores = jnp.exp(scores - row_peak)
    attention = (exp_scores / jnp.sum(exp_scores, axis=-1, keepdims=True)).astype(jnp.bfloat16)
    attended = jnp.einsum(
        "shab,sbhd->sahd", attention, value_heads, preferred_element_type=jnp.float32
    ).astype(jnp.bfloat16)
    latent = attended.reshape(sequences * per_range, block_len, half_width)
    blocks_here = latent.shape[0]
    capacity = max(2, 2 * blocks_here // shards)
    slot_count = shards * capacity
    shard_of = target_shard.reshape(-1)
    masked_flag = (keep.reshape(-1) == 0).astype(jnp.float32)
    order_ids = jnp.arange(blocks_here)
    earlier = (shard_of[:, None] == shard_of[None, :]) & (order_ids[:, None] < order_ids[None, :])
    slot_rank = jnp.sum(earlier.astype(jnp.int32), axis=0)
    slot_index = shard_of * capacity + slot_rank
    onehot = slot_index[None, :] == jnp.arange(slot_count)[:, None]
    divisor = float(block_len * full_width)
    halves = lax.all_to_all(latent[None], "grp", split_axis=1, concat_axis=0, tiled=True)
    half_count = blocks_here // 2
    first_block = group_index * half_count
    own_flags = lax.dynamic_slice_in_dim(masked_flag, first_block, half_count)
    losses = predict(halves[0], halves[1], own_flags, pred_weight, divisor)
    spread = lax.dynamic_update_slice_in_dim(
        jnp.zeros((blocks_here,), jnp.float32), losses, first_block, 0
    )
    slotted = jnp.sum(jnp.where(onehot, spread[None, :], 0.0), axis=1).reshape(shards, capacity)
    arrived = lax.all_to_all(slotted, "seq", split_axis=0, concat_axis=0, tiled=True)
    result = lax.psum_scatter(arrived, "grp", scatter_dimension=0, tiled=True)
    return result.reshape(1, -1)


def move(x, target):
    pairs = []
    for c in range(2):
        for s in range(8):
            for m in range(2):
                c2, z2, y2, m2 = target(c, s // 2, s % 2, m)
                pairs.append(((c * 8 + s) * 2 + m, (c2 * 8 + 2 * z2 + y2) * 2 + m2))
    return lax.ppermute(x, AXES, pairs)


def places():
    s = lax.axis_index("seq")
    return lax.axis_index("grp"), s // 2, lax.rem(s, 2), lax.axis_index("mdl")


def mask_kernel(signal_ref, token_ref, keep_ref, mine_ref, given_ref):
    core, _, y, _ = places()
    length = signal_ref.shape[1]
    blocks = keep_ref.shape[1]
    block_len = length // blocks
    row = lax.broadcasted_iota(jnp.int32, (length, blocks), 0)
    first = lax.broadcasted_iota(jnp.int32, (length, blocks), 1) * block_len
    covers = (row >= first) & (row < first + block_len)
    token = token_ref[...].astype(jnp.float32).reshape(1, -1)
    for target, chosen in ((mine_ref, y), (given_ref, 1 - y)):
        kept = jnp.where(covers, keep_ref[pl.ds(chosen, 1), :], 0)
        kept = jnp.sum(kept, axis=1, keepdims=True) + 1 - core
        rows = signal_ref[chosen].astype(jnp.float32)
        target[...] = jnp.where(kept > 0, rows, token).astype(target.dtype)


def slice_kernel(after_ref, weight_ref, pred_ref, near_ref, far_ref, early_ref, late_ref, sems):
    core, z, _, _ = places()
    wide = near_ref.shape[2]
    t = lax.rem(z, 2)
    copies = []
    for target, chosen in ((near_ref, t), (far_ref, 1 - t)):
        lanes = pl.ds(pl.multiple_of(chosen * wide, 128), wide)
        copies.append((weight_ref.at[0, :, :, lanes], target))
    count = early_ref.shape[0] + late_ref.shape[0]
    for target, skipped in ((early_ref, 0), (late_ref, early_ref.shape[0])):
        first = pl.multiple_of(core * count + skipped, 128)
        copies.append((pred_ref.at[pl.ds(first, target.shape[0]), :], target))
    copies = [
        pltpu.make_async_copy(source, target, sems.at[index])
        for index, (source, target) in enumerate(copies)
    ]
    for copy in copies:
        copy.start()
    for copy in copies:
        copy.wait()


def encode_kernel(x_own, x_across, x_near, x_near_across, halo_ref, *refs):
    pieces = refs[:PIECES]
    outs = refs[PIECES:PIECES + 8]
    x_buf, w_buf, q_buf, k_buf, v_buf, o_buf, sems = refs[PIECES + 8:]
    core, z, y, m = places()
    half = x_own.shape[-1]
    rows = x_own.shape[1]
    depth = pieces[0].shape[1]
    wide = pieces[0].shape[2]
    own_rows = 4 * rows
    copies = []
    side = lax.rem(z, 2)
    for piece, near, across in (
        (x_own, 0, 0), (x_across, 0, 1), (x_near, 1, 0), (x_near_across, 1, 1)
    ):
        first = WIN + 2 * rows * (side if near == 0 else 1 - side)
        lane = half * (m if across == 0 else 1 - m)
        for part in range(2):
            copies.append((
                piece.at[part],
                x_buf.at[
                    pl.ds(pl.multiple_of(first + (y if part == 0 else 1 - y) * rows, 64), rows),
                    pl.ds(pl.multiple_of(lane, 128), half),
                ],
            ))
    halo_first = pl.multiple_of((1 - core) * (WIN + own_rows), 64)
    empty_first = pl.multiple_of(core * (WIN + own_rows), 64)
    for across in range(2):
        lane = half * (m if across == 0 else 1 - m)
        copies.append((
            halo_ref.at[across],
            x_buf.at[pl.ds(halo_first, WIN), pl.ds(pl.multiple_of(lane, 128), half)],
        ))
    t = lax.rem(z, 2)
    for index, piece in enumerate(pieces):
        crossed, other = (index // 2) % 2, index % 2
        low = core if (other == 0) == (index >= 4) else 1 - core
        pos_z = 2 * low + (t if index < 4 else 1 - t)
        pos = 2 * pos_z + (y if crossed == 0 else 1 - y)
        copies.append((
            piece, w_buf.at[:, pl.ds(pl.multiple_of(pos * depth, 64), depth), :]
        ))
    started = []
    for index, (source, target) in enumerate(copies):
        copy = pltpu.make_async_copy(source, target, sems.at[index])
        copy.start()
        started.append(copy)
    x_buf[pl.ds(empty_first, WIN), :] = jnp.zeros((WIN, 2 * half), x_buf.dtype)
    for copy in started:
        copy.wait()
    x = x_buf[...]
    q_buf[...] = jnp.dot(
        x[WIN:WIN + own_rows], w_buf[0], preferred_element_type=jnp.float32
    ).astype(q_buf.dtype)
    k_buf[...] = jnp.dot(x, w_buf[1], preferred_element_type=jnp.float32).astype(k_buf.dtype)
    v_buf[...] = jnp.dot(x, w_buf[2], preferred_element_type=jnp.float32).astype(v_buf.dtype)
    keys = rows + 2 * WIN
    a = lax.broadcasted_iota(jnp.int32, (rows, keys), 0)
    b = lax.broadcasted_iota(jnp.int32, (rows, keys), 1)
    band = (b >= a) & (b <= a + 2 * WIN)
    for j in range(4):
        admitted = band
        if j == 0:
            admitted = admitted & (b >= WIN * (1 - core))
        if j == 3:
            admitted = admitted & (b < keys - WIN * core)
        for h in range(wide // HD):
            lanes = slice(h * HD, (h + 1) * HD)
            scores = lax.dot_general(
                q_buf[j * rows:(j + 1) * rows, lanes],
                k_buf[j * rows:j * rows + keys, lanes],
                (((1,), (1,)), ((), ())),
                preferred_element_type=jnp.float32,
            ) * (1.0 / math.sqrt(HD))
            scores = jnp.where(admitted, scores, -jnp.inf)
            peak = jnp.max(scores, axis=-1, keepdims=True)
            exps = jnp.exp(scores - peak)
            attention = (exps / jnp.sum(exps, axis=-1, keepdims=True)).astype(jnp.bfloat16)
            o_buf[j, :, lanes] = jnp.dot(
                attention,
                v_buf[j * rows:j * rows + keys, lanes],
                preferred_element_type=jnp.float32,
            ).astype(o_buf.dtype)
    for step in range(4):
        for side in range(2):
            first = pl.multiple_of((m if side == 0 else 1 - m) * (rows // 2), 64)
            outs[2 * step + side][...] = o_buf[lax.rem(z + step, 4), pl.ds(first, rows // 2), :]


def predict_kernel(slot_ref, *refs):
    latents, (own_ref, e0, e1, l0, l1, out_ref, lat_ref) = refs[:8], refs[8:]
    core, z, _, m = places()
    wide = lat_ref.shape[2]
    for index, piece in enumerate(latents):
        step, side = index // 2, index % 2
        lat_ref[2 * lax.rem(z + 4 - step, 4) + (m if side == 0 else 1 - m)] = piece[...]
    cut = e0.shape[0]
    total = None
    for side in range(2):
        terms = []
        for t in range(2):
            for x in range(2):
                if side == 0:
                    source = lat_ref[2 * t + x]
                    terms.append((source, own_ref[(2 * x + t) * wide:(2 * x + t + 1) * wide, :]))
                    continue
                early, late = ((e0, l0), (e1, l1))[x]
                source = lat_ref[2 * t + (core if x == 0 else 1 - core)]
                if t == 0:
                    terms.append((source, early[:wide, :]))
                else:
                    terms.append((source[:, :cut - wide], early[wide:, :]))
                    terms.append((source[:, cut - wide:], late[...]))
        predicted = None
        for source, weight in terms:
            term = jnp.dot(source, weight, preferred_element_type=jnp.float32)
            predicted = term if predicted is None else predicted + term
        for t in range(2):
            target = lat_ref[4 + 2 * t + (m if side == 0 else 1 - m)].astype(jnp.float32)
            residue = predicted[:, t * wide:(t + 1) * wide] - target
            for i in range(wide // 128):
                piece = residue[:, i * 128:(i + 1) * 128]
                total = piece * piece if total is None else total + piece * piece
    row_errors = jnp.sum(total, axis=1, keepdims=True)
    rows, slots = total.shape[0], out_ref.shape[2]
    chosen = slot_ref[...] == lax.broadcasted_iota(jnp.int32, (rows, slots), 1)
    routed = jnp.sum(jnp.where(chosen, row_errors, 0.0), axis=0, keepdims=True)
    for i in range(out_ref.shape[0]):
        out_ref[i] = routed


def local_lines(signal, mask_token, keep, target_shard, enc_weight, pred_weight):
    core = lax.axis_index("grp")
    s = lax.axis_index("seq")
    m = lax.axis_index("mdl")
    z, y = s // 2, s % 2
    sequences, length, half = signal.shape
    per_range = keep.shape[1]
    block_len = length // per_range
    depth = enc_weight.shape[2]
    wide = half // 2

    vmem = pl.BlockSpec(memory_space=pltpu.VMEM)
    anywhere = pl.BlockSpec(memory_space=pl.ANY)

    def to_near(c, z, y, m):
        return (1 - z // 2, z % 2 + 2 * c, y, m)

    def to_far(c, z, y, m):
        return (z // 2, 1 - z % 2 + 2 * c, y, m)

    def across_z(c, z, y, m):
        if z // 2 == c:
            return (c, (z + 2) % 4, y, m)
        return (1 - c, z, y, m)

    def across_zy(c, z, y, m):
        c, z, y, m = across_z(c, z, y, m)
        return (c, z, 1 - y, m)

    def flip_y(c, z, y, m):
        return (c, z, 1 - y, m)

    def flip_core(c, z, y, m):
        return (1 - c, z, y, m)

    def flip_x(c, z, y, m):
        return (c, z, y, 1 - m)

    def flip_z(c, z, y, m):
        return (c, z + 1 - 2 * (z % 2), y, m)

    cut = 2 * half // 3
    mine, given = pl.pallas_call(
        mask_kernel,
        out_shape=[jax.ShapeDtypeStruct((length, half), jnp.bfloat16)] * 2,
        in_specs=[vmem] * 3,
        out_specs=[vmem] * 2,
    )(signal, mask_token, keep)
    near, far, early, late = pl.pallas_call(
        slice_kernel,
        out_shape=[jax.ShapeDtypeStruct(shape, jnp.bfloat16) for shape in (
            (3, depth, wide), (3, depth, wide), (cut, half), (half - cut, half),
        )],
        in_specs=[anywhere] * 3,
        out_specs=[vmem] * 4,
        scratch_shapes=[pltpu.SemaphoreType.DMA((4,))],
    )(mine, enc_weight, pred_weight)
    first, second = move(mine, across_z), move(given, across_zy)
    small = jnp.stack([keep, target_shard])
    small, _ = lax.optimization_barrier((small, mine))
    routing = move(small, lambda c, z, y, m: ((2 * z + y) // 4, (2 * z + y) % 4, c, m))
    near, routing, first, second = lax.optimization_barrier((near, routing, first, second))
    x_own = jnp.stack([first, second])
    near_w = move(near, to_near)
    weight_early = move(early, flip_x)
    far, x_own = lax.optimization_barrier((far, x_own))
    far_w = move(far, to_far)
    x_near = move(x_own, flip_z)
    x_across = move(x_own, flip_x)
    near_y_source, weight_early = lax.optimization_barrier((near_w, weight_early))
    near_y = move(near_y_source, flip_y)
    far_y_source, near_y = lax.optimization_barrier((far_w, near_y))
    far_y = move(far_y_source, flip_y)
    weight_early_c = move(weight_early, flip_core)
    x_near, x_across = lax.optimization_barrier((x_near, x_across))
    x_near_across = move(x_near, flip_x)
    late, _ = lax.optimization_barrier((late, x_near_across))
    weight_late = move(late, flip_x)
    weight_late_c = move(weight_late, flip_core)
    hidden = lax.dynamic_index_in_dim(routing[0], y, 0, keepdims=False) == 0
    shard_of = routing[1].reshape(-1)
    blocks = shard_of.shape[0]
    capacity = max(2, 2 * blocks // 8)
    order_ids = jnp.arange(blocks)
    earlier = (shard_of[:, None] == shard_of[None, :]) & (order_ids[:, None] < order_ids[None, :])
    slot = shard_of * capacity + jnp.sum(earlier.astype(jnp.int32), axis=0)
    slot = lax.dynamic_index_in_dim(slot.reshape(sequences, -1), y, 0, keepdims=False)
    slot = jnp.where(hidden, slot, -1)
    slot = lax.dynamic_slice_in_dim(slot, m * (per_range // 2), per_range // 2)
    slot = jnp.repeat(slot, block_len)[:, None]

    def edge(own, near):
        found = jnp.where(z % 2 == 1 - core, own, near)
        part = jnp.where(core == 0, 1 - y, y)
        first = jnp.where(core == 0, length - WIN, 0)
        return lax.dynamic_slice(found, (part, first, 0), (1, WIN, half))[0]

    halo = move(jnp.stack([edge(x_own, x_near), edge(x_across, x_near_across)]), flip_core)
    far_yc_source, halo = lax.optimization_barrier((far_y, halo))
    pieces = [
        near_w, move(near_w, flip_core), near_y, move(near_y, flip_core),
        far_w, move(far_w, flip_core), far_y, move(far_yc_source, flip_core),
    ]
    span = 4 * length + 2 * WIN

    parts = pl.pallas_call(
        encode_kernel,
        out_shape=[jax.ShapeDtypeStruct((length // 2, wide), jnp.bfloat16)] * 8,
        in_specs=[anywhere] * (5 + PIECES),
        out_specs=[vmem] * 8,
        scratch_shapes=[
            pltpu.VMEM((span, 2 * half), jnp.bfloat16),
            pltpu.VMEM((3, 2 * half, wide), jnp.bfloat16),
            pltpu.VMEM((4 * length, wide), jnp.bfloat16),
            pltpu.VMEM((span, wide), jnp.bfloat16),
            pltpu.VMEM((span, wide), jnp.bfloat16),
            pltpu.VMEM((4, length, wide), jnp.bfloat16),
            pltpu.SemaphoreType.DMA((10 + PIECES,)),
        ],
        compiler_params=pltpu.CompilerParams(vmem_limit_bytes=56 * 2**20),
    )(x_own, x_across, x_near, x_near_across, halo, *pieces)

    def step_to(step, side):
        return lambda c, z, y, m: (c, (z + step) % 4, y, (m + side) % 2)

    latents = list(parts)
    for index in (4, 5, 2, 3, 6, 7, 1):
        latents[index] = move(parts[index], step_to(index // 2, index % 2))
    routed = pl.pallas_call(
        predict_kernel,
        out_shape=jax.ShapeDtypeStruct((16, 1, 8 * capacity), jnp.float32),
        in_specs=[vmem] * 14,
        out_specs=vmem,
        scratch_shapes=[pltpu.VMEM((8, length // 2, wide), jnp.bfloat16)],
        compiler_params=pltpu.CompilerParams(vmem_limit_bytes=24 * 2**20),
    )(
        slot, *latents, pred_weight,
        weight_early, weight_early_c, weight_late, weight_late_c,
    )
    arrived = lax.all_to_all(routed, ("seq", "mdl"), split_axis=0, concat_axis=0, tiled=True)
    mine = lax.dynamic_slice_in_dim(arrived[:, 0], capacity * s, capacity, 1)
    summed = jnp.sum(mine.reshape(4, 4, capacity), axis=1)
    return summed.reshape(1, -1) / float(block_len * 2 * half)


def solution(mesh):
    placed = (
        P(None, "seq", "mdl"),
        P("mdl"),
        P(None, "seq"),
        P(None, "seq"),
        P("grp", None, "seq", "mdl"),
        P(None, "mdl"),
    )
    plan = local_lines if mesh.shape["seq"] == 8 else local
    return jax.shard_map(
        plan, mesh=mesh, in_specs=placed, out_specs=P("seq", "grp"), check_vma=False
    )
```

```python
import functools
import math

import jax
import jax.numpy as jnp
from jax import lax
from jax.experimental import pallas as pl
from jax.experimental.pallas import tpu as pltpu
from jax.sharding import PartitionSpec as P

HD = 128
WIN = 64
AXES = ("grp", "seq", "mdl")
PIECES = 15


def padded(x, sides, width):
    for axis, dim in sides:
        count, length = (lax.axis_size(axis), x.shape[dim])
        up = [(i, (i + 1) % count) for i in range(count - 1)]
        down = [(j, i) for i, j in up]
        last = lax.slice_in_dim(x, length - width, length, axis=dim)
        leading = lax.slice_in_dim(x, 0, width, axis=dim)
        before = lax.ppermute(last, axis, up)
        after = lax.ppermute(leading, axis, down)
        x = jnp.concatenate([before, x, after], axis=dim)
    return x


def predict(context, target, live_flags, pred_weight, divisor):
    flat_rows = context.reshape(-1, context.shape[-1])
    wide_rows = lax.all_gather(flat_rows, "mdl", axis=1, tiled=True)
    predicted = jnp.dot(wide_rows, pred_weight, preferred_element_type=jnp.float32)
    residue = predicted - target.reshape(flat_rows.shape).astype(jnp.float32)
    partial_sums = jnp.sum((residue * residue).reshape(live_flags.shape[0], -1), axis=1)
    summed = lax.psum(partial_sums, "mdl")
    return summed / divisor * live_flags


def local(signal, mask_token, keep, target_shard, enc_weight, pred_weight):
    group_index = lax.axis_index("grp")
    seq_index = lax.axis_index("seq")
    shards = lax.axis_size("seq")
    sequences, length, half_width = signal.shape
    per_range = keep.shape[1]
    block_len = length // per_range
    kept_rows = jnp.repeat(keep, block_len, axis=1)[:, :, None]
    masked_in = jnp.where(kept_rows == 1, signal, mask_token[None, None, :])
    source = jnp.where(group_index == 0, masked_in, signal)
    wide_in = lax.all_gather(source, "mdl", axis=2, tiled=True)
    full_width = wide_in.shape[2]
    flat_in = wide_in.reshape(-1, full_width)
    span = length + 2 * WIN
    weight_all = lax.all_gather(enc_weight, "seq", axis=2, tiled=True)[0]
    queries = jnp.dot(flat_in, weight_all[0], preferred_element_type=jnp.float32).astype(
        jnp.bfloat16
    )
    pair_made = jnp.einsum(
        "nd,cde->cne", flat_in, weight_all[1:], preferred_element_type=jnp.float32
    ).astype(jnp.bfloat16)
    own_pairs = pair_made.reshape(2, sequences, length, half_width)
    pair_rows = padded(own_pairs, (("seq", 2),), WIN)
    head_count = half_width // HD
    query_heads = queries.reshape(sequences, length, head_count, HD)
    key_heads = pair_rows[0].reshape(sequences, span, head_count, HD)
    value_heads = pair_rows[1].reshape(sequences, span, head_count, HD)
    query_pos = seq_index * length + jnp.arange(length)
    key_pos = seq_index * length - WIN + jnp.arange(span)
    total_len = length * shards
    in_window = (
        (jnp.abs(query_pos[:, None] - key_pos[None, :]) <= WIN)
        & (key_pos[None, :] >= 0)
        & (key_pos[None, :] < total_len)
    )
    scores = jnp.einsum(
        "sahd,sbhd->shab", query_heads, key_heads, preferred_element_type=jnp.float32
    ) * (1.0 / math.sqrt(HD))
    scores = jnp.where(in_window[None, None], scores, -jnp.inf)
    row_peak = jnp.max(scores, axis=-1, keepdims=True)
    exp_scores = jnp.exp(scores - row_peak)
    attention = (exp_scores / jnp.sum(exp_scores, axis=-1, keepdims=True)).astype(jnp.bfloat16)
    attended = jnp.einsum(
        "shab,sbhd->sahd", attention, value_heads, preferred_element_type=jnp.float32
    ).astype(jnp.bfloat16)
    latent = attended.reshape(sequences * per_range, block_len, half_width)
    blocks_here = latent.shape[0]
    capacity = max(2, 2 * blocks_here // shards)
    slot_count = shards * capacity
    shard_of = target_shard.reshape(-1)
    masked_flag = (keep.reshape(-1) == 0).astype(jnp.float32)
    order_ids = jnp.arange(blocks_here)
    earlier = (shard_of[:, None] == shard_of[None, :]) & (order_ids[:, None] < order_ids[None, :])
    slot_rank = jnp.sum(earlier.astype(jnp.int32), axis=0)
    slot_index = shard_of * capacity + slot_rank
    onehot = slot_index[None, :] == jnp.arange(slot_count)[:, None]
    divisor = float(block_len * full_width)
    halves = lax.all_to_all(latent[None], "grp", split_axis=1, concat_axis=0, tiled=True)
    half_count = blocks_here // 2
    first_block = group_index * half_count
    own_flags = lax.dynamic_slice_in_dim(masked_flag, first_block, half_count)
    losses = predict(halves[0], halves[1], own_flags, pred_weight, divisor)
    spread = lax.dynamic_update_slice_in_dim(
        jnp.zeros((blocks_here,), jnp.float32), losses, first_block, 0
    )
    slotted = jnp.sum(jnp.where(onehot, spread[None, :], 0.0), axis=1).reshape(shards, capacity)
    arrived = lax.all_to_all(slotted, "seq", split_axis=0, concat_axis=0, tiled=True)
    result = lax.psum_scatter(arrived, "grp", scatter_dimension=0, tiled=True)
    return result.reshape(1, -1)


def move(x, target):
    pairs = []
    for c in range(2):
        for s in range(8):
            for m in range(2):
                goal = target(c, s // 2, s % 2, m)
                if goal is None:
                    continue
                c2, z2, y2, m2 = goal
                pairs.append(((c * 8 + s) * 2 + m, (c2 * 8 + 2 * z2 + y2) * 2 + m2))
    return lax.ppermute(x, AXES, pairs)


def places():
    s = lax.axis_index("seq")
    return lax.axis_index("grp"), s // 2, lax.rem(s, 2), lax.axis_index("mdl")


def prepare_kernel(
    signal_ref, token_ref, keep_ref, weight_ref, pred_ref,
    mine_ref, given_ref, near_ref, far_ref, early_ref, sems,
):
    core, z, y, _ = places()
    wide = near_ref.shape[2]
    t = lax.rem(z, 2)
    copies = []
    for target, chosen in ((near_ref, t), (far_ref, 1 - t)):
        lanes = pl.ds(pl.multiple_of(chosen * wide, 128), wide)
        copies.append((weight_ref.at[0, :, :, lanes], target))
    first = pl.multiple_of(core * (pred_ref.shape[0] // 2), 128)
    copies.append((pred_ref.at[pl.ds(first, early_ref.shape[0]), :], early_ref))
    copies = [
        pltpu.make_async_copy(source, target, sems.at[index])
        for index, (source, target) in enumerate(copies)
    ]
    for copy in copies:
        copy.start()
    length = signal_ref.shape[1]
    blocks = keep_ref.shape[1]
    block_len = length // blocks
    row = lax.broadcasted_iota(jnp.int32, (length, blocks), 0)
    first = lax.broadcasted_iota(jnp.int32, (length, blocks), 1) * block_len
    covers = (row >= first) & (row < first + block_len)
    token = token_ref[...].astype(jnp.float32).reshape(1, -1)
    for target, chosen in ((mine_ref, y), (given_ref, 1 - y)):
        kept = jnp.where(covers, keep_ref[pl.ds(chosen, 1), :], 0)
        kept = jnp.sum(kept, axis=1, keepdims=True) + 1 - core
        rows = signal_ref[chosen].astype(jnp.float32)
        target[...] = jnp.where(kept > 0, rows, token).astype(target.dtype)
    for copy in copies:
        copy.wait()


def encode_kernel(x_own, x_across, x_near, x_near_across, halo_ref, *refs):
    pieces = refs[:PIECES]
    out_ref, x_buf, w_buf, q_buf, k_buf, v_buf, sems = refs[PIECES:]
    core, z, y, m = places()
    half = x_own.shape[-1]
    rows = x_own.shape[1]
    depth = pieces[0].shape[1]
    wide = pieces[0].shape[2]
    own_rows = 4 * rows
    copies = []
    side = lax.rem(z, 2)
    for piece, near, across in (
        (x_own, 0, 0), (x_across, 0, 1), (x_near, 1, 0), (x_near_across, 1, 1)
    ):
        first = WIN + 2 * rows * (side if near == 0 else 1 - side)
        lane = half * (m if across == 0 else 1 - m)
        for part in range(2):
            copies.append((
                piece.at[part],
                x_buf.at[
                    pl.ds(pl.multiple_of(first + (y if part == 0 else 1 - y) * rows, 64), rows),
                    pl.ds(pl.multiple_of(lane, 128), half),
                ],
            ))
    halo_first = pl.multiple_of((1 - core) * (WIN + own_rows), 64)
    empty_first = pl.multiple_of(core * (WIN + own_rows), 64)
    for across in range(2):
        lane = half * (m if across == 0 else 1 - m)
        copies.append((
            halo_ref.at[across],
            x_buf.at[pl.ds(halo_first, WIN), pl.ds(pl.multiple_of(lane, 128), half)],
        ))
    (
        own_w, cross_w, own_wy, next_w, next_wy, cross_wy, last_w, last_wy,
        own_wyc, next_wc, next_wyc, cross_wc, cross_wyc, last_wc, last_wyc,
    ) = pieces
    inner = (own_w, own_wy, next_w, next_wy, cross_w, cross_wy, last_wc, last_wyc)
    outer = (cross_w, own_wyc, next_wc, next_wyc, cross_wc, cross_wyc, last_w, last_wy)
    other_half = 2 * (1 - z // 2)
    sources = (z, z + 1 - 2 * side, other_half + side, other_half + 1 - side)
    slots = [
        w_buf.at[:, pl.ds(pl.multiple_of((2 * source + row) * depth, 64), depth), :]
        for source in sources for row in (y, 1 - y)
    ]

    def weight_copies(chosen):
        return [
            pltpu.make_async_copy(piece, slot, sems.at[len(copies) + index])
            for index, (piece, slot) in enumerate(zip(chosen, slots))
        ]

    is_inner = core == z // 2
    started = []
    for index, (source, target) in enumerate(copies):
        copy = pltpu.make_async_copy(source, target, sems.at[index])
        copy.start()
        started.append(copy)
    for wanted, chosen in ((is_inner, inner), (jnp.logical_not(is_inner), outer)):
        @pl.when(wanted)
        def _(chosen=chosen):
            held = weight_copies(chosen)
            for copy in held:
                copy.start()
            for copy in held:
                copy.wait()

    x_buf[pl.ds(empty_first, WIN), :] = jnp.zeros((WIN, 2 * half), x_buf.dtype)
    for copy in started:
        copy.wait()
    x = x_buf[...]
    q_buf[...] = jnp.dot(
        x[WIN:WIN + own_rows], w_buf[0], preferred_element_type=jnp.float32
    ).astype(q_buf.dtype)
    k_buf[...] = jnp.dot(x, w_buf[1], preferred_element_type=jnp.float32).astype(k_buf.dtype)
    v_buf[...] = jnp.dot(x, w_buf[2], preferred_element_type=jnp.float32).astype(v_buf.dtype)
    keys = rows + 2 * WIN
    a = lax.broadcasted_iota(jnp.int32, (rows, keys), 0)
    b = lax.broadcasted_iota(jnp.int32, (rows, keys), 1)
    band = (b >= a) & (b <= a + 2 * WIN)
    for j in range(4):
        admitted = band
        if j == 0:
            admitted = admitted & (b >= WIN * (1 - core))
        if j == 3:
            admitted = admitted & (b < keys - WIN * core)
        for h in range(wide // HD):
            lanes = slice(h * HD, (h + 1) * HD)
            scores = lax.dot_general(
                q_buf[j * rows:(j + 1) * rows, lanes],
                k_buf[j * rows:j * rows + keys, lanes],
                (((1,), (1,)), ((), ())),
                preferred_element_type=jnp.float32,
            ) * (1.0 / math.sqrt(HD))
            scores = jnp.where(admitted, scores, -jnp.inf)
            peak = jnp.max(scores, axis=-1, keepdims=True)
            exps = jnp.exp(scores - peak)
            attention = (exps / jnp.sum(exps, axis=-1, keepdims=True)).astype(jnp.bfloat16)
            out_ref[j, :, lanes] = jnp.dot(
                attention,
                v_buf[j * rows:j * rows + keys, lanes],
                preferred_element_type=jnp.float32,
            ).astype(out_ref.dtype)


def predict_kernel(slot_ref, lat_ref, own_ref, *refs):
    lent, out_ref = (refs[:3], refs[3:6]), refs[6]
    core, _, _, m = places()
    wide = lat_ref.shape[2]
    cut = lent[0][0].shape[0]
    total = None
    for side in range(2):
        terms = []
        for t in range(2):
            for x in range(2):
                if side == 0:
                    source = lat_ref[2 * t + x]
                    terms.append((source, own_ref[(2 * x + t) * wide:(2 * x + t + 1) * wide, :]))
                    continue
                source = lat_ref[2 * t + (core if x == 0 else 1 - core)]
                first, second, third = lent[x]
                if t == 0:
                    terms.append((source[:, :cut], first[...]))
                    terms.append((source[:, cut:], second[:wide - cut, :]))
                else:
                    terms.append((source[:, :wide - cut], second[wide - cut:, :]))
                    terms.append((source[:, wide - cut:], third[...]))
        predicted = None
        for source, weight in terms:
            term = jnp.dot(source, weight, preferred_element_type=jnp.float32)
            predicted = term if predicted is None else predicted + term
        for t in range(2):
            target = lat_ref[4 + 2 * t + (m if side == 0 else 1 - m)].astype(jnp.float32)
            residue = predicted[:, t * wide:(t + 1) * wide] - target
            for i in range(wide // 128):
                piece = residue[:, i * 128:(i + 1) * 128]
                total = piece * piece if total is None else total + piece * piece
    row_errors = jnp.sum(total, axis=1, keepdims=True)
    rows, slots = total.shape[0], out_ref.shape[2]
    chosen = slot_ref[...] == lax.broadcasted_iota(jnp.int32, (rows, slots), 1)
    routed = jnp.sum(jnp.where(chosen, row_errors, 0.0), axis=0, keepdims=True)
    for i in range(out_ref.shape[0]):
        out_ref[i] = routed


def local_lines(signal, mask_token, keep, target_shard, enc_weight, pred_weight):
    core = lax.axis_index("grp")
    s = lax.axis_index("seq")
    m = lax.axis_index("mdl")
    z, y = s // 2, s % 2
    sequences, length, half = signal.shape
    per_range = keep.shape[1]
    block_len = length // per_range
    depth = enc_weight.shape[2]
    wide = half // 2

    vmem = pl.BlockSpec(memory_space=pltpu.VMEM)
    anywhere = pl.BlockSpec(memory_space=pl.ANY)

    def to_near(c, z, y, m):
        return (1 - z // 2, z % 2 + 2 * c, y, m)

    def inner_only(target):
        return lambda c, z, y, m: target(c, z, y, m) if c == z // 2 else None

    def outer_only(target):
        return lambda c, z, y, m: target(c, z, y, m) if c != z // 2 else None

    def to_far(c, z, y, m):
        return (z // 2, 1 - z % 2 + 2 * c, y, m)

    def across_z(c, z, y, m):
        if z // 2 == c:
            return (c, (z + 2) % 4, y, m)
        return (1 - c, z, y, m)

    def across_zy(c, z, y, m):
        c, z, y, m = across_z(c, z, y, m)
        return (c, z, 1 - y, m)

    def flip_y(c, z, y, m):
        return (c, z, 1 - y, m)

    def flip_core(c, z, y, m):
        return (1 - c, z, y, m)

    def flip_x(c, z, y, m):
        return (c, z, y, 1 - m)

    def flip_z(c, z, y, m):
        return (c, z + 1 - 2 * (z % 2), y, m)

    cut = half // 3
    mine, given, near, far, early = pl.pallas_call(
        prepare_kernel,
        out_shape=[jax.ShapeDtypeStruct(shape, jnp.bfloat16) for shape in (
            (length, half), (length, half), (3, depth, wide), (3, depth, wide), (cut, half),
        )],
        in_specs=[vmem] * 3 + [anywhere] * 2,
        out_specs=[vmem] * 5,
        scratch_shapes=[pltpu.SemaphoreType.DMA((3,))],
    )(signal, mask_token, keep, enc_weight, pred_weight)
    first, second = move(mine, across_z), move(given, across_zy)
    small = jnp.stack([keep, target_shard])
    small, _ = lax.optimization_barrier((small, mine))
    routing = move(small, lambda c, z, y, m: ((2 * z + y) // 4, (2 * z + y) % 4, c, m))
    near_own = near
    own_wy = move(near_own, inner_only(flip_y))
    next_w = move(far, inner_only(flip_z))
    weight_early = move(early, flip_x)
    near, routing, first, second, own_wy, next_w, weight_early = lax.optimization_barrier(
        (near, routing, first, second, own_wy, next_w, weight_early)
    )
    x_own = jnp.stack([first, second])
    next_wy = move(next_w, inner_only(flip_y))
    cross_w = move(near, to_near)
    x_near = move(x_own, flip_z)
    x_across = move(x_own, flip_x)
    last, next_w = lax.optimization_barrier((far, next_w))
    last_w = move(last, outer_only(to_far))
    cross_wy = move(cross_w, inner_only(flip_y))
    last_wy = move(last_w, outer_only(flip_y))
    middle, late = (
        lax.dynamic_slice_in_dim(pred_weight, core * half + i * cut, cut, 0) for i in (1, 2)
    )
    middle, x_across = lax.optimization_barrier((middle, x_across))
    weight_middle = move(middle, flip_x)
    x_near, x_across, last_w, next_wy, weight_middle = lax.optimization_barrier(
        (x_near, x_across, last_w, next_wy, weight_middle)
    )
    x_near_across = move(x_near, flip_x)
    late, _ = lax.optimization_barrier((late, x_near_across))
    columns = [weight_early, weight_middle, move(late, flip_x)]
    columns += [move(piece, flip_core) for piece in columns]
    hidden = lax.dynamic_index_in_dim(routing[0], y, 0, keepdims=False) == 0
    shard_of = routing[1].reshape(-1)
    blocks = shard_of.shape[0]
    capacity = max(2, 2 * blocks // 8)
    order_ids = jnp.arange(blocks)
    earlier = (shard_of[:, None] == shard_of[None, :]) & (order_ids[:, None] < order_ids[None, :])
    slot = shard_of * capacity + jnp.sum(earlier.astype(jnp.int32), axis=0)
    slot = lax.dynamic_index_in_dim(slot.reshape(sequences, -1), y, 0, keepdims=False)
    slot = jnp.where(hidden, slot, -1)
    slot = lax.dynamic_slice_in_dim(slot, m * (per_range // 2), per_range // 2)
    slot = jnp.repeat(slot, block_len)[:, None]

    def edge(own, near):
        found = jnp.where(z % 2 == 1 - core, own, near)
        part = jnp.where(core == 0, 1 - y, y)
        first = jnp.where(core == 0, length - WIN, 0)
        return lax.dynamic_slice(found, (part, first, 0), (1, WIN, half))[0]

    halo = move(jnp.stack([edge(x_own, x_near), edge(x_across, x_near_across)]), flip_core)
    last_wyc_source, halo = lax.optimization_barrier((last_wy, halo))
    to_outer, to_inner = inner_only(flip_core), outer_only(flip_core)
    pieces = [
        near_own, cross_w, own_wy, next_w, next_wy, cross_wy, last_w, last_wy,
        move(own_wy, to_outer), move(next_w, to_outer), move(next_wy, to_outer),
        move(cross_w, to_outer), move(cross_wy, to_outer),
        move(last_w, to_inner), move(last_wyc_source, to_inner),
    ]
    span = 4 * length + 2 * WIN

    latent = pl.pallas_call(
        encode_kernel,
        out_shape=jax.ShapeDtypeStruct((4, length, wide), jnp.bfloat16),
        in_specs=[anywhere] * (5 + PIECES),
        out_specs=vmem,
        scratch_shapes=[
            pltpu.VMEM((span, 2 * half), jnp.bfloat16),
            pltpu.VMEM((3, 2 * half, wide), jnp.bfloat16),
            pltpu.VMEM((4 * length, wide), jnp.bfloat16),
            pltpu.VMEM((span, wide), jnp.bfloat16),
            pltpu.VMEM((span, wide), jnp.bfloat16),
            pltpu.SemaphoreType.DMA((18,)),
        ],
        compiler_params=pltpu.CompilerParams(vmem_limit_bytes=56 * 2**20),
    )(x_own, x_across, x_near, x_near_across, halo, *pieces)
    lines = [[4 * i + 2 * j + k for i in range(4) for k in range(2)] for j in range(2)]
    latents = lax.all_to_all(
        latent.reshape(8, length // 2, wide), ("seq", "mdl"),
        split_axis=0, concat_axis=0, tiled=True, axis_index_groups=lines,
    )
    routed = pl.pallas_call(
        predict_kernel,
        out_shape=jax.ShapeDtypeStruct((16, 1, 8 * capacity), jnp.float32),
        in_specs=[vmem] * 9,
        out_specs=vmem,
        compiler_params=pltpu.CompilerParams(vmem_limit_bytes=24 * 2**20),
    )(
        slot, latents, pred_weight,
        *columns,
    )
    arrived = lax.all_to_all(routed, ("seq", "mdl"), split_axis=0, concat_axis=0, tiled=True)
    mine = lax.dynamic_slice_in_dim(arrived[:, 0], capacity * s, capacity, 1)
    summed = jnp.sum(mine.reshape(4, 4, capacity), axis=1)
    return summed.reshape(1, -1) / float(block_len * 2 * half)


def solution(mesh):
    placed = (
        P(None, "seq", "mdl"),
        P("mdl"),
        P(None, "seq"),
        P(None, "seq"),
        P("grp", None, "seq", "mdl"),
        P(None, "mdl"),
    )
    plan = local_lines if mesh.shape["seq"] == 8 else local
    return jax.shard_map(
        plan, mesh=mesh, in_specs=placed, out_specs=P("seq", "grp"), check_vma=False
    )
```

```python
import functools
import math

import jax
import jax.numpy as jnp
from jax import lax
from jax.experimental import pallas as pl
from jax.experimental.pallas import tpu as pltpu
from jax.sharding import PartitionSpec as P

HD = 128
WIN = 64
AXES = ("grp", "seq", "mdl")
PIECES = 8


def padded(x, sides, width):
    for axis, dim in sides:
        count, length = (lax.axis_size(axis), x.shape[dim])
        up = [(i, (i + 1) % count) for i in range(count - 1)]
        down = [(j, i) for i, j in up]
        last = lax.slice_in_dim(x, length - width, length, axis=dim)
        leading = lax.slice_in_dim(x, 0, width, axis=dim)
        before = lax.ppermute(last, axis, up)
        after = lax.ppermute(leading, axis, down)
        x = jnp.concatenate([before, x, after], axis=dim)
    return x


def predict(context, target, live_flags, pred_weight, divisor):
    flat_rows = context.reshape(-1, context.shape[-1])
    wide_rows = lax.all_gather(flat_rows, "mdl", axis=1, tiled=True)
    predicted = jnp.dot(wide_rows, pred_weight, preferred_element_type=jnp.float32)
    residue = predicted - target.reshape(flat_rows.shape).astype(jnp.float32)
    partial_sums = jnp.sum((residue * residue).reshape(live_flags.shape[0], -1), axis=1)
    summed = lax.psum(partial_sums, "mdl")
    return summed / divisor * live_flags


def local(signal, mask_token, keep, target_shard, enc_weight, pred_weight):
    group_index = lax.axis_index("grp")
    seq_index = lax.axis_index("seq")
    shards = lax.axis_size("seq")
    sequences, length, half_width = signal.shape
    per_range = keep.shape[1]
    block_len = length // per_range
    kept_rows = jnp.repeat(keep, block_len, axis=1)[:, :, None]
    masked_in = jnp.where(kept_rows == 1, signal, mask_token[None, None, :])
    source = jnp.where(group_index == 0, masked_in, signal)
    wide_in = lax.all_gather(source, "mdl", axis=2, tiled=True)
    full_width = wide_in.shape[2]
    flat_in = wide_in.reshape(-1, full_width)
    span = length + 2 * WIN
    weight_all = lax.all_gather(enc_weight, "seq", axis=2, tiled=True)[0]
    queries = jnp.dot(flat_in, weight_all[0], preferred_element_type=jnp.float32).astype(
        jnp.bfloat16
    )
    pair_made = jnp.einsum(
        "nd,cde->cne", flat_in, weight_all[1:], preferred_element_type=jnp.float32
    ).astype(jnp.bfloat16)
    own_pairs = pair_made.reshape(2, sequences, length, half_width)
    pair_rows = padded(own_pairs, (("seq", 2),), WIN)
    head_count = half_width // HD
    query_heads = queries.reshape(sequences, length, head_count, HD)
    key_heads = pair_rows[0].reshape(sequences, span, head_count, HD)
    value_heads = pair_rows[1].reshape(sequences, span, head_count, HD)
    query_pos = seq_index * length + jnp.arange(length)
    key_pos = seq_index * length - WIN + jnp.arange(span)
    total_len = length * shards
    in_window = (
        (jnp.abs(query_pos[:, None] - key_pos[None, :]) <= WIN)
        & (key_pos[None, :] >= 0)
        & (key_pos[None, :] < total_len)
    )
    scores = jnp.einsum(
        "sahd,sbhd->shab", query_heads, key_heads, preferred_element_type=jnp.float32
    ) * (1.0 / math.sqrt(HD))
    scores = jnp.where(in_window[None, None], scores, -jnp.inf)
    row_peak = jnp.max(scores, axis=-1, keepdims=True)
    exp_scores = jnp.exp(scores - row_peak)
    attention = (exp_scores / jnp.sum(exp_scores, axis=-1, keepdims=True)).astype(jnp.bfloat16)
    attended = jnp.einsum(
        "shab,sbhd->sahd", attention, value_heads, preferred_element_type=jnp.float32
    ).astype(jnp.bfloat16)
    latent = attended.reshape(sequences * per_range, block_len, half_width)
    blocks_here = latent.shape[0]
    capacity = max(2, 2 * blocks_here // shards)
    slot_count = shards * capacity
    shard_of = target_shard.reshape(-1)
    masked_flag = (keep.reshape(-1) == 0).astype(jnp.float32)
    order_ids = jnp.arange(blocks_here)
    earlier = (shard_of[:, None] == shard_of[None, :]) & (order_ids[:, None] < order_ids[None, :])
    slot_rank = jnp.sum(earlier.astype(jnp.int32), axis=0)
    slot_index = shard_of * capacity + slot_rank
    onehot = slot_index[None, :] == jnp.arange(slot_count)[:, None]
    divisor = float(block_len * full_width)
    halves = lax.all_to_all(latent[None], "grp", split_axis=1, concat_axis=0, tiled=True)
    half_count = blocks_here // 2
    first_block = group_index * half_count
    own_flags = lax.dynamic_slice_in_dim(masked_flag, first_block, half_count)
    losses = predict(halves[0], halves[1], own_flags, pred_weight, divisor)
    spread = lax.dynamic_update_slice_in_dim(
        jnp.zeros((blocks_here,), jnp.float32), losses, first_block, 0
    )
    slotted = jnp.sum(jnp.where(onehot, spread[None, :], 0.0), axis=1).reshape(shards, capacity)
    arrived = lax.all_to_all(slotted, "seq", split_axis=0, concat_axis=0, tiled=True)
    result = lax.psum_scatter(arrived, "grp", scatter_dimension=0, tiled=True)
    return result.reshape(1, -1)


def move(x, target):
    pairs = []
    for c in range(2):
        for s in range(8):
            for m in range(2):
                c2, z2, y2, m2 = target(c, s // 2, s % 2, m)
                pairs.append(((c * 8 + s) * 2 + m, (c2 * 8 + 2 * z2 + y2) * 2 + m2))
    return lax.ppermute(x, AXES, pairs)


def places():
    s = lax.axis_index("seq")
    return lax.axis_index("grp"), s // 2, lax.rem(s, 2), lax.axis_index("mdl")


def mask_kernel(
    signal_ref, token_ref, keep_ref, mine_ref, given_ref, mine_own_ref, given_own_ref
):
    core, _, y, _ = places()
    length = signal_ref.shape[1]
    blocks = keep_ref.shape[1]
    block_len = length // blocks
    row = lax.broadcasted_iota(jnp.int32, (length, blocks), 0)
    first = lax.broadcasted_iota(jnp.int32, (length, blocks), 1) * block_len
    covers = (row >= first) & (row < first + block_len)
    token = token_ref[...].astype(jnp.float32).reshape(1, -1)
    for other, own, chosen in ((mine_ref, mine_own_ref, y), (given_ref, given_own_ref, 1 - y)):
        kept = jnp.where(covers, keep_ref[pl.ds(chosen, 1), :], 0)
        kept = jnp.sum(kept, axis=1, keepdims=True)
        rows = signal_ref[chosen].astype(jnp.float32)
        other[...] = jnp.where(kept + 1 - core > 0, rows, token).astype(other.dtype)
        own[...] = jnp.where(kept + core > 0, rows, token).astype(own.dtype)


def slice_kernel(after_ref, weight_ref, pred_ref, near_ref, far_ref, early_ref, late_ref, sems):
    core, z, _, _ = places()
    wide = near_ref.shape[2]
    cut = early_ref.shape[0]
    t = lax.rem(z, 2)
    copies = []
    for target, chosen in ((near_ref, t), (far_ref, 1 - t)):
        lanes = pl.ds(pl.multiple_of(chosen * wide, 128), wide)
        copies.append((weight_ref.at[0, :, :, lanes], target))
    for index, target in enumerate((early_ref, late_ref)):
        first = pl.multiple_of((2 * core + index) * cut, 128)
        copies.append((pred_ref.at[pl.ds(first, cut), :], target))
    copies = [
        pltpu.make_async_copy(source, target, sems.at[index])
        for index, (source, target) in enumerate(copies)
    ]
    for copy in copies:
        copy.start()
    for copy in copies:
        copy.wait()


def encode_kernel(x_own, x_across, x_near, x_near_across, halo_ref, *refs):
    pieces = refs[:PIECES]
    out_ref, x_buf, w_buf, q_buf, k_buf, v_buf, sems = refs[PIECES:]
    core, z, y, m = places()
    half = x_own.shape[-1]
    rows = x_own.shape[1]
    depth = pieces[0].shape[1]
    wide = pieces[0].shape[2]
    own_rows = 4 * rows
    copies = []
    side = jnp.where(core == z // 2, 1 - lax.rem(z, 2), lax.rem(z, 2))
    for piece, near, across in (
        (x_own, 0, 0), (x_across, 0, 1), (x_near, 1, 0), (x_near_across, 1, 1)
    ):
        first = WIN + 2 * rows * (side if near == 0 else 1 - side)
        lane = half * (m if across == 0 else 1 - m)
        for part in range(2):
            copies.append((
                piece.at[part],
                x_buf.at[
                    pl.ds(pl.multiple_of(first + (y if part == 0 else 1 - y) * rows, 64), rows),
                    pl.ds(pl.multiple_of(lane, 128), half),
                ],
            ))
    halo_first = pl.multiple_of((1 - core) * (WIN + own_rows), 64)
    empty_first = pl.multiple_of(core * (WIN + own_rows), 64)
    for across in range(2):
        lane = half * (m if across == 0 else 1 - m)
        copies.append((
            halo_ref.at[across],
            x_buf.at[pl.ds(halo_first, WIN), pl.ds(pl.multiple_of(lane, 128), half)],
        ))
    t = lax.rem(z, 2)
    for index, piece in enumerate(pieces):
        crossed, other = (index // 2) % 2, index % 2
        low = core if (other == 0) == (index >= 4) else 1 - core
        pos_z = 2 * low + (t if index < 4 else 1 - t)
        pos = 2 * pos_z + (y if crossed == 0 else 1 - y)
        copies.append((
            piece, w_buf.at[:, pl.ds(pl.multiple_of(pos * depth, 64), depth), :]
        ))
    started = []
    for index, (source, target) in enumerate(copies):
        copy = pltpu.make_async_copy(source, target, sems.at[index])
        copy.start()
        started.append(copy)
    x_buf[pl.ds(empty_first, WIN), :] = jnp.zeros((WIN, 2 * half), x_buf.dtype)
    for copy in started:
        copy.wait()
    x = x_buf[...]
    q_buf[...] = jnp.dot(
        x[WIN:WIN + own_rows], w_buf[0], preferred_element_type=jnp.float32
    ).astype(q_buf.dtype)
    k_buf[...] = jnp.dot(x, w_buf[1], preferred_element_type=jnp.float32).astype(k_buf.dtype)
    v_buf[...] = jnp.dot(x, w_buf[2], preferred_element_type=jnp.float32).astype(v_buf.dtype)
    keys = rows + 2 * WIN
    a = lax.broadcasted_iota(jnp.int32, (rows, keys), 0)
    b = lax.broadcasted_iota(jnp.int32, (rows, keys), 1)
    band = (b >= a) & (b <= a + 2 * WIN)
    for j in range(4):
        admitted = band
        if j == 0:
            admitted = admitted & (b >= WIN * (1 - core))
        if j == 3:
            admitted = admitted & (b < keys - WIN * core)
        for h in range(wide // HD):
            lanes = slice(h * HD, (h + 1) * HD)
            scores = lax.dot_general(
                q_buf[j * rows:(j + 1) * rows, lanes],
                k_buf[j * rows:j * rows + keys, lanes],
                (((1,), (1,)), ((), ())),
                preferred_element_type=jnp.float32,
            ) * (1.0 / math.sqrt(HD))
            scores = jnp.where(admitted, scores, -jnp.inf)
            peak = jnp.max(scores, axis=-1, keepdims=True)
            exps = jnp.exp(scores - peak)
            attention = (exps / jnp.sum(exps, axis=-1, keepdims=True)).astype(jnp.bfloat16)
            out_ref[j, :, lanes] = jnp.dot(
                attention,
                v_buf[j * rows:j * rows + keys, lanes],
                preferred_element_type=jnp.float32,
            ).astype(out_ref.dtype)


def predict_kernel(slot_ref, lat_ref, own_ref, e0, e1, l0, l1, out_ref):
    core, _, _, m = places()
    wide = lat_ref.shape[2]
    lent = ((e0, e1), (l0, l1))
    total = None
    for side in range(2):
        predicted = None
        for t in range(2):
            for x in range(2):
                if side == 0:
                    source = lat_ref[2 * t + x]
                    weight = own_ref[(2 * x + t) * wide:(2 * x + t + 1) * wide, :]
                else:
                    source = lat_ref[2 * t + (core if x == 0 else 1 - core)]
                    weight = lent[t][x][...]
                term = jnp.dot(source, weight, preferred_element_type=jnp.float32)
                predicted = term if predicted is None else predicted + term
        for t in range(2):
            target = lat_ref[4 + 2 * t + (m if side == 0 else 1 - m)].astype(jnp.float32)
            residue = predicted[:, t * wide:(t + 1) * wide] - target
            for i in range(wide // 128):
                piece = residue[:, i * 128:(i + 1) * 128]
                total = piece * piece if total is None else total + piece * piece
    row_errors = jnp.sum(total, axis=1, keepdims=True)
    rows, slots = total.shape[0], out_ref.shape[2]
    chosen = slot_ref[...] == lax.broadcasted_iota(jnp.int32, (rows, slots), 1)
    routed = jnp.sum(jnp.where(chosen, row_errors, 0.0), axis=0, keepdims=True)
    for i in range(out_ref.shape[0]):
        out_ref[i] = routed


def local_lines(signal, mask_token, keep, target_shard, enc_weight, pred_weight):
    core = lax.axis_index("grp")
    s = lax.axis_index("seq")
    m = lax.axis_index("mdl")
    z, y = s // 2, s % 2
    sequences, length, half = signal.shape
    per_range = keep.shape[1]
    block_len = length // per_range
    depth = enc_weight.shape[2]
    wide = half // 2

    vmem = pl.BlockSpec(memory_space=pltpu.VMEM)
    anywhere = pl.BlockSpec(memory_space=pl.ANY)

    def to_near(c, z, y, m):
        return (1 - z // 2, z % 2 + 2 * c, y, m)

    def to_far(c, z, y, m):
        return (z // 2, 1 - z % 2 + 2 * c, y, m)

    def across_z(c, z, y, m):
        if z // 2 == c:
            return (c, (z + 2) % 4, y, m)
        return (1 - c, z + 1 - 2 * (z % 2), y, m)

    def across_zy(c, z, y, m):
        c, z, y, m = across_z(c, z, y, m)
        return (c, z, 1 - y, m)

    def flip_y(c, z, y, m):
        return (c, z, 1 - y, m)

    def flip_core(c, z, y, m):
        return (1 - c, z, y, m)

    def flip_x(c, z, y, m):
        return (c, z, y, 1 - m)

    def second_hop(c, z, y, m):
        if z // 2 == c:
            return (c, z, 1 - y, m)
        return (c, z + 1 - 2 * (z % 2), y, m)

    cut = half // 2
    mine, given, mine_own, given_own = pl.pallas_call(
        mask_kernel,
        out_shape=[jax.ShapeDtypeStruct((length, half), jnp.bfloat16)] * 4,
        in_specs=[vmem] * 3,
        out_specs=[vmem] * 4,
    )(signal, mask_token, keep)
    near, far, early, late = pl.pallas_call(
        slice_kernel,
        out_shape=[jax.ShapeDtypeStruct(shape, jnp.bfloat16) for shape in (
            (3, depth, wide), (3, depth, wide), (cut, half), (cut, half),
        )],
        in_specs=[anywhere] * 3,
        out_specs=[vmem] * 4,
        scratch_shapes=[pltpu.SemaphoreType.DMA((4,))],
    )(mine, enc_weight, pred_weight)
    first, second = move(mine, across_z), move(given, across_zy)
    small = jnp.stack([keep, target_shard])
    small, _ = lax.optimization_barrier((small, mine))
    routing = move(small, lambda c, z, y, m: ((2 * z + y) // 4, (2 * z + y) % 4, c, m))
    near, routing, first, second = lax.optimization_barrier((near, routing, first, second))
    x_own = jnp.stack([first, second])
    near_w = move(near, to_near)
    weight_early = move(early, flip_x)
    far, x_own = lax.optimization_barrier((far, x_own))
    far_w = move(far, to_far)
    home = core == z // 2
    sent = jnp.where(home, jnp.stack([mine_own, given_own]), x_own)
    come = move(sent, second_hop)
    kept_home = (jnp.arange(2) == 0)[:, None, None] & home
    x_near = jnp.where(kept_home, mine_own[None], come)
    x_across = move(x_own, flip_x)
    near_y_source, weight_early = lax.optimization_barrier((near_w, weight_early))
    near_y = move(near_y_source, flip_y)
    far_y_source, near_y = lax.optimization_barrier((far_w, near_y))
    far_y = move(far_y_source, flip_y)
    weight_early_c = move(weight_early, flip_core)
    x_near, x_across = lax.optimization_barrier((x_near, x_across))
    x_near_across = move(x_near, flip_x)
    late, _ = lax.optimization_barrier((late, x_near_across))
    weight_late = move(late, flip_x)
    weight_late_c = move(weight_late, flip_core)
    hidden = lax.dynamic_index_in_dim(routing[0], y, 0, keepdims=False) == 0
    shard_of = routing[1].reshape(-1)
    blocks = shard_of.shape[0]
    capacity = max(2, 2 * blocks // 8)
    order_ids = jnp.arange(blocks)
    earlier = (shard_of[:, None] == shard_of[None, :]) & (order_ids[:, None] < order_ids[None, :])
    slot = shard_of * capacity + jnp.sum(earlier.astype(jnp.int32), axis=0)
    slot = lax.dynamic_index_in_dim(slot.reshape(sequences, -1), y, 0, keepdims=False)
    slot = jnp.where(hidden, slot, -1)
    slot = lax.dynamic_slice_in_dim(slot, m * (per_range // 2), per_range // 2)
    slot = jnp.repeat(slot, block_len)[:, None]

    def edge(own, near):
        found = jnp.where(jnp.where(home, 1 - z % 2, z % 2) == 1 - core, own, near)
        part = jnp.where(core == 0, 1 - y, y)
        first = jnp.where(core == 0, length - WIN, 0)
        return lax.dynamic_slice(found, (part, first, 0), (1, WIN, half))[0]

    halo = move(jnp.stack([edge(x_own, x_near), edge(x_across, x_near_across)]), flip_core)
    far_yc_source, halo = lax.optimization_barrier((far_y, halo))
    pieces = [
        near_w, move(near_w, flip_core), near_y, move(near_y, flip_core),
        far_w, move(far_w, flip_core), far_y, move(far_yc_source, flip_core),
    ]
    span = 4 * length + 2 * WIN

    latent = pl.pallas_call(
        encode_kernel,
        out_shape=jax.ShapeDtypeStruct((4, length, wide), jnp.bfloat16),
        in_specs=[anywhere] * (5 + PIECES),
        out_specs=vmem,
        scratch_shapes=[
            pltpu.VMEM((span, 2 * half), jnp.bfloat16),
            pltpu.VMEM((3, 2 * half, wide), jnp.bfloat16),
            pltpu.VMEM((4 * length, wide), jnp.bfloat16),
            pltpu.VMEM((span, wide), jnp.bfloat16),
            pltpu.VMEM((span, wide), jnp.bfloat16),
            pltpu.SemaphoreType.DMA((10 + PIECES,)),
        ],
        compiler_params=pltpu.CompilerParams(vmem_limit_bytes=56 * 2**20),
    )(x_own, x_across, x_near, x_near_across, halo, *pieces)
    lines = [[4 * i + 2 * j + k for i in range(4) for k in range(2)] for j in range(2)]
    latents = lax.all_to_all(
        latent.reshape(8, length // 2, wide), ("seq", "mdl"),
        split_axis=0, concat_axis=0, tiled=True, axis_index_groups=lines,
    )
    routed = pl.pallas_call(
        predict_kernel,
        out_shape=jax.ShapeDtypeStruct((16, 1, 8 * capacity), jnp.float32),
        in_specs=[vmem] * 7,
        out_specs=vmem,
        compiler_params=pltpu.CompilerParams(vmem_limit_bytes=24 * 2**20),
    )(
        slot, latents, pred_weight,
        weight_early, weight_early_c, weight_late, weight_late_c,
    )
    arrived = lax.all_to_all(routed, ("seq", "mdl"), split_axis=0, concat_axis=0, tiled=True)
    mine = lax.dynamic_slice_in_dim(arrived[:, 0], capacity * s, capacity, 1)
    summed = jnp.sum(mine.reshape(4, 4, capacity), axis=1)
    return summed.reshape(1, -1) / float(block_len * 2 * half)


def solution(mesh):
    placed = (
        P(None, "seq", "mdl"),
        P("mdl"),
        P(None, "seq"),
        P(None, "seq"),
        P("grp", None, "seq", "mdl"),
        P(None, "mdl"),
    )
    plan = local_lines if mesh.shape["seq"] == 8 else local
    return jax.shard_map(
        plan, mesh=mesh, in_specs=placed, out_specs=P("seq", "grp"), check_vma=False
    )
```

```python
import functools
import math

import jax
import jax.numpy as jnp
from jax import lax
from jax.experimental import pallas as pl
from jax.experimental.pallas import tpu as pltpu
from jax.sharding import PartitionSpec as P

HD = 128
WIN = 64
AXES = ("grp", "seq", "mdl")
PIECES = 8


def padded(x, sides, width):
    for axis, dim in sides:
        count, length = (lax.axis_size(axis), x.shape[dim])
        up = [(i, (i + 1) % count) for i in range(count - 1)]
        down = [(j, i) for i, j in up]
        last = lax.slice_in_dim(x, length - width, length, axis=dim)
        leading = lax.slice_in_dim(x, 0, width, axis=dim)
        before = lax.ppermute(last, axis, up)
        after = lax.ppermute(leading, axis, down)
        x = jnp.concatenate([before, x, after], axis=dim)
    return x


def predict(context, target, live_flags, pred_weight, divisor):
    flat_rows = context.reshape(-1, context.shape[-1])
    wide_rows = lax.all_gather(flat_rows, "mdl", axis=1, tiled=True)
    predicted = jnp.dot(wide_rows, pred_weight, preferred_element_type=jnp.float32)
    residue = predicted - target.reshape(flat_rows.shape).astype(jnp.float32)
    partial_sums = jnp.sum((residue * residue).reshape(live_flags.shape[0], -1), axis=1)
    summed = lax.psum(partial_sums, "mdl")
    return summed / divisor * live_flags


def local(signal, mask_token, keep, target_shard, enc_weight, pred_weight):
    group_index = lax.axis_index("grp")
    seq_index = lax.axis_index("seq")
    shards = lax.axis_size("seq")
    sequences, length, half_width = signal.shape
    per_range = keep.shape[1]
    block_len = length // per_range
    kept_rows = jnp.repeat(keep, block_len, axis=1)[:, :, None]
    masked_in = jnp.where(kept_rows == 1, signal, mask_token[None, None, :])
    source = jnp.where(group_index == 0, masked_in, signal)
    wide_in = lax.all_gather(source, "mdl", axis=2, tiled=True)
    full_width = wide_in.shape[2]
    flat_in = wide_in.reshape(-1, full_width)
    span = length + 2 * WIN
    weight_all = lax.all_gather(enc_weight, "seq", axis=2, tiled=True)[0]
    queries = jnp.dot(flat_in, weight_all[0], preferred_element_type=jnp.float32).astype(
        jnp.bfloat16
    )
    pair_made = jnp.einsum(
        "nd,cde->cne", flat_in, weight_all[1:], preferred_element_type=jnp.float32
    ).astype(jnp.bfloat16)
    own_pairs = pair_made.reshape(2, sequences, length, half_width)
    pair_rows = padded(own_pairs, (("seq", 2),), WIN)
    head_count = half_width // HD
    query_heads = queries.reshape(sequences, length, head_count, HD)
    key_heads = pair_rows[0].reshape(sequences, span, head_count, HD)
    value_heads = pair_rows[1].reshape(sequences, span, head_count, HD)
    query_pos = seq_index * length + jnp.arange(length)
    key_pos = seq_index * length - WIN + jnp.arange(span)
    total_len = length * shards
    in_window = (
        (jnp.abs(query_pos[:, None] - key_pos[None, :]) <= WIN)
        & (key_pos[None, :] >= 0)
        & (key_pos[None, :] < total_len)
    )
    scores = jnp.einsum(
        "sahd,sbhd->shab", query_heads, key_heads, preferred_element_type=jnp.float32
    ) * (1.0 / math.sqrt(HD))
    scores = jnp.where(in_window[None, None], scores, -jnp.inf)
    row_peak = jnp.max(scores, axis=-1, keepdims=True)
    exp_scores = jnp.exp(scores - row_peak)
    attention = (exp_scores / jnp.sum(exp_scores, axis=-1, keepdims=True)).astype(jnp.bfloat16)
    attended = jnp.einsum(
        "shab,sbhd->sahd", attention, value_heads, preferred_element_type=jnp.float32
    ).astype(jnp.bfloat16)
    latent = attended.reshape(sequences * per_range, block_len, half_width)
    blocks_here = latent.shape[0]
    capacity = max(2, 2 * blocks_here // shards)
    slot_count = shards * capacity
    shard_of = target_shard.reshape(-1)
    masked_flag = (keep.reshape(-1) == 0).astype(jnp.float32)
    order_ids = jnp.arange(blocks_here)
    earlier = (shard_of[:, None] == shard_of[None, :]) & (order_ids[:, None] < order_ids[None, :])
    slot_rank = jnp.sum(earlier.astype(jnp.int32), axis=0)
    slot_index = shard_of * capacity + slot_rank
    onehot = slot_index[None, :] == jnp.arange(slot_count)[:, None]
    divisor = float(block_len * full_width)
    halves = lax.all_to_all(latent[None], "grp", split_axis=1, concat_axis=0, tiled=True)
    half_count = blocks_here // 2
    first_block = group_index * half_count
    own_flags = lax.dynamic_slice_in_dim(masked_flag, first_block, half_count)
    losses = predict(halves[0], halves[1], own_flags, pred_weight, divisor)
    spread = lax.dynamic_update_slice_in_dim(
        jnp.zeros((blocks_here,), jnp.float32), losses, first_block, 0
    )
    slotted = jnp.sum(jnp.where(onehot, spread[None, :], 0.0), axis=1).reshape(shards, capacity)
    arrived = lax.all_to_all(slotted, "seq", split_axis=0, concat_axis=0, tiled=True)
    result = lax.psum_scatter(arrived, "grp", scatter_dimension=0, tiled=True)
    return result.reshape(1, -1)


def move(x, target):
    pairs = []
    for c in range(2):
        for s in range(8):
            for m in range(2):
                c2, z2, y2, m2 = target(c, s // 2, s % 2, m)
                pairs.append(((c * 8 + s) * 2 + m, (c2 * 8 + 2 * z2 + y2) * 2 + m2))
    return lax.ppermute(x, AXES, pairs)


def places():
    s = lax.axis_index("seq")
    return lax.axis_index("grp"), s // 2, lax.rem(s, 2), lax.axis_index("mdl")


def mask_kernel(
    signal_ref, token_ref, keep_ref, mine_ref, given_ref, mine_own_ref, given_own_ref
):
    core, _, y, _ = places()
    length = signal_ref.shape[1]
    blocks = keep_ref.shape[1]
    block_len = length // blocks
    row = lax.broadcasted_iota(jnp.int32, (length, blocks), 0)
    first = lax.broadcasted_iota(jnp.int32, (length, blocks), 1) * block_len
    covers = (row >= first) & (row < first + block_len)
    token = token_ref[...].astype(jnp.float32).reshape(1, -1)
    for other, own, chosen in ((mine_ref, mine_own_ref, y), (given_ref, given_own_ref, 1 - y)):
        kept = jnp.where(covers, keep_ref[pl.ds(chosen, 1), :], 0)
        kept = jnp.sum(kept, axis=1, keepdims=True)
        rows = signal_ref[chosen].astype(jnp.float32)
        other[...] = jnp.where(kept + 1 - core > 0, rows, token).astype(other.dtype)
        own[...] = jnp.where(kept + core > 0, rows, token).astype(own.dtype)


def slice_kernel(after_ref, weight_ref, pred_ref, near_ref, far_ref, early_ref, late_ref, sems):
    core, z, _, _ = places()
    wide = near_ref.shape[2]
    cut = early_ref.shape[0]
    t = lax.rem(z, 2)
    copies = []
    for target, chosen in ((near_ref, t), (far_ref, 1 - t)):
        lanes = pl.ds(pl.multiple_of(chosen * wide, 128), wide)
        copies.append((weight_ref.at[0, :, :, lanes], target))
    for index, target in enumerate((early_ref, late_ref)):
        first = pl.multiple_of((2 * core + index) * cut, 128)
        copies.append((pred_ref.at[pl.ds(first, cut), :], target))
    copies = [
        pltpu.make_async_copy(source, target, sems.at[index])
        for index, (source, target) in enumerate(copies)
    ]
    for copy in copies:
        copy.start()
    for copy in copies:
        copy.wait()


def encode_kernel(x_own, x_across, x_near, x_near_across, halo_ref, *refs):
    pieces = refs[:PIECES]
    out_ref, x_buf, w_buf, q_buf, k_buf, v_buf, sems = refs[PIECES:]
    core, z, y, m = places()
    half = x_own.shape[-1]
    rows = x_own.shape[1]
    depth = pieces[0].shape[1]
    wide = pieces[0].shape[2]
    own_rows = 4 * rows
    copies = []
    side = jnp.where(core == z // 2, 1 - lax.rem(z, 2), lax.rem(z, 2))
    for piece, near, across in (
        (x_own, 0, 0), (x_across, 0, 1), (x_near, 1, 0), (x_near_across, 1, 1)
    ):
        first = WIN + 2 * rows * (side if near == 0 else 1 - side)
        lane = half * (m if across == 0 else 1 - m)
        for part in range(2):
            copies.append((
                piece.at[part],
                x_buf.at[
                    pl.ds(pl.multiple_of(first + (y if part == 0 else 1 - y) * rows, 64), rows),
                    pl.ds(pl.multiple_of(lane, 128), half),
                ],
            ))
    halo_first = pl.multiple_of((1 - core) * (WIN + own_rows), 64)
    empty_first = pl.multiple_of(core * (WIN + own_rows), 64)
    for across in range(2):
        lane = half * (m if across == 0 else 1 - m)
        copies.append((
            halo_ref.at[across],
            x_buf.at[pl.ds(halo_first, WIN), pl.ds(pl.multiple_of(lane, 128), half)],
        ))
    t = lax.rem(z, 2)
    ready = [[], [], []]
    for index, piece in enumerate(pieces):
        crossed, other = (index // 2) % 2, index % 2
        low = core if (other == 0) == (index >= 4) else 1 - core
        pos_z = 2 * low + (t if index < 4 else 1 - t)
        pos = 2 * pos_z + (y if crossed == 0 else 1 - y)
        span = pl.ds(pl.multiple_of(pos * depth, 64), depth)
        for kind in range(3):
            ready[kind].append((piece.at[kind], w_buf.at[kind, span, :]))
    started = []
    for group, pairs in enumerate([copies + ready[0], ready[1], ready[2]]):
        started.append([
            pltpu.make_async_copy(source, target, sems.at[group, index])
            for index, (source, target) in enumerate(pairs)
        ])
        for copy in started[-1]:
            copy.start()
    x_buf[pl.ds(empty_first, WIN), :] = jnp.zeros((WIN, 2 * half), x_buf.dtype)
    for copy in started[0]:
        copy.wait()
    x = x_buf[...]
    q_buf[...] = jnp.dot(
        x[WIN:WIN + own_rows], w_buf[0], preferred_element_type=jnp.float32
    ).astype(q_buf.dtype)
    for copy in started[1]:
        copy.wait()
    k_buf[...] = jnp.dot(x, w_buf[1], preferred_element_type=jnp.float32).astype(k_buf.dtype)
    for copy in started[2]:
        copy.wait()
    v_buf[...] = jnp.dot(x, w_buf[2], preferred_element_type=jnp.float32).astype(v_buf.dtype)
    keys = rows + 2 * WIN
    a = lax.broadcasted_iota(jnp.int32, (rows, keys), 0)
    b = lax.broadcasted_iota(jnp.int32, (rows, keys), 1)
    band = (b >= a) & (b <= a + 2 * WIN)
    for j in range(4):
        admitted = band
        if j == 0:
            admitted = admitted & (b >= WIN * (1 - core))
        if j == 3:
            admitted = admitted & (b < keys - WIN * core)
        for h in range(wide // HD):
            lanes = slice(h * HD, (h + 1) * HD)
            scores = lax.dot_general(
                q_buf[j * rows:(j + 1) * rows, lanes],
                k_buf[j * rows:j * rows + keys, lanes],
                (((1,), (1,)), ((), ())),
                preferred_element_type=jnp.float32,
            )
            scores = jnp.where(admitted, scores, -jnp.inf)
            peak = jnp.max(scores, axis=-1, keepdims=True)
            exps = jnp.exp((scores - peak) * (1.0 / math.sqrt(HD)))
            share = 1.0 / jnp.sum(exps, axis=-1, keepdims=True)
            attention = (exps * share).astype(jnp.bfloat16)
            out_ref[j, :, lanes] = jnp.dot(
                attention,
                v_buf[j * rows:j * rows + keys, lanes],
                preferred_element_type=jnp.float32,
            ).astype(out_ref.dtype)


def predict_kernel(
    slot_ref, lat_ref, own_hbm, e0, e1, l0, l1, out_ref, own_ref, lent_ref, sems
):
    core, _, _, m = places()
    wide = lat_ref.shape[2]
    cut = e0.shape[0]
    copies = [pltpu.make_async_copy(own_hbm, own_ref, sems.at[0])]
    for index, piece in enumerate((e0, l0, e1, l1)):
        copies.append(pltpu.make_async_copy(
            piece, lent_ref.at[pl.ds(index * cut, cut), :], sems.at[1 + index]
        ))
    for copy in copies:
        copy.start()
    total = None
    for side in range(2):
        predicted = None
        if side == 0:
            copies[0].wait()
        else:
            for copy in copies[1:]:
                copy.wait()
        for x in range(2):
            for t in range(2):
                rows = slice((2 * x + t) * wide, (2 * x + t + 1) * wide)
                if side == 0:
                    source, weight = lat_ref[2 * t + x], own_ref[rows, :]
                else:
                    source = lat_ref[2 * t + (core if x == 0 else 1 - core)]
                    weight = lent_ref[rows, :]
                term = jnp.dot(source, weight, preferred_element_type=jnp.float32)
                predicted = term if predicted is None else predicted + term
        for t in range(2):
            target = lat_ref[4 + 2 * t + (m if side == 0 else 1 - m)].astype(jnp.float32)
            residue = predicted[:, t * wide:(t + 1) * wide] - target
            for i in range(wide // 128):
                piece = residue[:, i * 128:(i + 1) * 128]
                total = piece * piece if total is None else total + piece * piece
    row_errors = jnp.sum(total, axis=1, keepdims=True)
    rows, slots = total.shape[0], out_ref.shape[2]
    chosen = slot_ref[...] == lax.broadcasted_iota(jnp.int32, (rows, slots), 1)
    routed = jnp.sum(jnp.where(chosen, row_errors, 0.0), axis=0, keepdims=True)
    for i in range(out_ref.shape[0]):
        out_ref[i] = routed


def local_lines(signal, mask_token, keep, target_shard, enc_weight, pred_weight):
    core = lax.axis_index("grp")
    s = lax.axis_index("seq")
    m = lax.axis_index("mdl")
    z, y = s // 2, s % 2
    sequences, length, half = signal.shape
    per_range = keep.shape[1]
    block_len = length // per_range
    depth = enc_weight.shape[2]
    wide = half // 2

    vmem = pl.BlockSpec(memory_space=pltpu.VMEM)
    anywhere = pl.BlockSpec(memory_space=pl.ANY)

    def to_near(c, z, y, m):
        return (1 - z // 2, z % 2 + 2 * c, y, m)

    def to_far(c, z, y, m):
        return (z // 2, 1 - z % 2 + 2 * c, y, m)

    def across_z(c, z, y, m):
        if z // 2 == c:
            return (c, (z + 2) % 4, y, m)
        return (1 - c, z + 1 - 2 * (z % 2), y, m)

    def across_zy(c, z, y, m):
        c, z, y, m = across_z(c, z, y, m)
        return (c, z, 1 - y, m)

    def flip_y(c, z, y, m):
        return (c, z, 1 - y, m)

    def flip_core(c, z, y, m):
        return (1 - c, z, y, m)

    def flip_x(c, z, y, m):
        return (c, z, y, 1 - m)

    def second_hop(c, z, y, m):
        if z // 2 == c:
            return (c, z, 1 - y, m)
        return (c, z + 1 - 2 * (z % 2), y, m)

    cut = half // 2
    mine, given, mine_own, given_own = pl.pallas_call(
        mask_kernel,
        out_shape=[jax.ShapeDtypeStruct((length, half), jnp.bfloat16)] * 4,
        in_specs=[vmem] * 3,
        out_specs=[vmem] * 4,
    )(signal, mask_token, keep)
    near, far, early, late = pl.pallas_call(
        slice_kernel,
        out_shape=[jax.ShapeDtypeStruct(shape, jnp.bfloat16) for shape in (
            (3, depth, wide), (3, depth, wide), (cut, half), (cut, half),
        )],
        in_specs=[anywhere] * 3,
        out_specs=[vmem] * 4,
        scratch_shapes=[pltpu.SemaphoreType.DMA((4,))],
    )(mine, enc_weight, pred_weight)
    first, second = move(mine, across_z), move(given, across_zy)
    small = jnp.stack([keep, target_shard])
    small, _ = lax.optimization_barrier((small, mine))
    routing = move(small, lambda c, z, y, m: ((2 * z + y) // 4, (2 * z + y) % 4, c, m))
    near, routing, first, second = lax.optimization_barrier((near, routing, first, second))
    x_own = jnp.stack([first, second])
    near_w = move(near, to_near)
    weight_early = move(early, flip_x)
    far, x_own = lax.optimization_barrier((far, x_own))
    far_w = move(far, to_far)
    home = core == z // 2
    sent = jnp.where(home, jnp.stack([mine_own, given_own]), x_own)
    come = move(sent, second_hop)
    kept_home = (jnp.arange(2) == 0)[:, None, None] & home
    x_near = jnp.where(kept_home, mine_own[None], come)
    x_across = move(x_own, flip_x)
    near_y_source, weight_early = lax.optimization_barrier((near_w, weight_early))
    near_y = move(near_y_source, flip_y)
    far_y_source, near_y = lax.optimization_barrier((far_w, near_y))
    far_y = move(far_y_source, flip_y)
    weight_early_c = move(weight_early, flip_core)
    x_near, x_across = lax.optimization_barrier((x_near, x_across))
    x_near_across = move(x_near, flip_x)
    late, _ = lax.optimization_barrier((late, x_near_across))
    weight_late = move(late, flip_x)
    weight_late_c = move(weight_late, flip_core)
    hidden = lax.dynamic_index_in_dim(routing[0], y, 0, keepdims=False) == 0
    shard_of = routing[1].reshape(-1)
    blocks = shard_of.shape[0]
    capacity = max(2, 2 * blocks // 8)
    order_ids = jnp.arange(blocks)
    earlier = (shard_of[:, None] == shard_of[None, :]) & (order_ids[:, None] < order_ids[None, :])
    slot = shard_of * capacity + jnp.sum(earlier.astype(jnp.int32), axis=0)
    slot = lax.dynamic_index_in_dim(slot.reshape(sequences, -1), y, 0, keepdims=False)
    slot = jnp.where(hidden, slot, -1)
    slot = lax.dynamic_slice_in_dim(slot, m * (per_range // 2), per_range // 2)
    slot = jnp.repeat(slot, block_len)[:, None]

    def edge(own, near):
        found = jnp.where(jnp.where(home, 1 - z % 2, z % 2) == 1 - core, own, near)
        part = jnp.where(core == 0, 1 - y, y)
        first = jnp.where(core == 0, length - WIN, 0)
        return lax.dynamic_slice(found, (part, first, 0), (1, WIN, half))[0]

    halo = move(jnp.stack([edge(x_own, x_near), edge(x_across, x_near_across)]), flip_core)
    far_yc_source, halo = lax.optimization_barrier((far_y, halo))
    pieces = [
        near_w, move(near_w, flip_core), near_y, move(near_y, flip_core),
        far_w, move(far_w, flip_core), far_y, move(far_yc_source, flip_core),
    ]
    span = 4 * length + 2 * WIN

    latent = pl.pallas_call(
        encode_kernel,
        out_shape=jax.ShapeDtypeStruct((4, length, wide), jnp.bfloat16),
        in_specs=[anywhere] * (5 + PIECES),
        out_specs=vmem,
        scratch_shapes=[
            pltpu.VMEM((span, 2 * half), jnp.bfloat16),
            pltpu.VMEM((3, 2 * half, wide), jnp.bfloat16),
            pltpu.VMEM((4 * length, wide), jnp.bfloat16),
            pltpu.VMEM((span, wide), jnp.bfloat16),
            pltpu.VMEM((span, wide), jnp.bfloat16),
            pltpu.SemaphoreType.DMA((3, 10 + PIECES)),
        ],
        compiler_params=pltpu.CompilerParams(vmem_limit_bytes=56 * 2**20),
    )(x_own, x_across, x_near, x_near_across, halo, *pieces)
    lines = [[4 * i + 2 * j + k for i in range(4) for k in range(2)] for j in range(2)]
    latents = lax.all_to_all(
        latent.reshape(8, length // 2, wide), ("seq", "mdl"),
        split_axis=0, concat_axis=0, tiled=True, axis_index_groups=lines,
    )
    routed = pl.pallas_call(
        predict_kernel,
        out_shape=jax.ShapeDtypeStruct((16, 1, 8 * capacity), jnp.float32),
        in_specs=[vmem] * 2 + [anywhere] * 5,
        out_specs=vmem,
        scratch_shapes=[
            pltpu.VMEM((2 * half, half), jnp.bfloat16),
            pltpu.VMEM((2 * half, half), jnp.bfloat16),
            pltpu.SemaphoreType.DMA((5,)),
        ],
        compiler_params=pltpu.CompilerParams(vmem_limit_bytes=24 * 2**20),
    )(
        slot, latents, pred_weight,
        weight_early, weight_early_c, weight_late, weight_late_c,
    )
    arrived = lax.all_to_all(routed, ("seq", "mdl"), split_axis=0, concat_axis=0, tiled=True)
    mine = lax.dynamic_slice_in_dim(arrived[:, 0], capacity * s, capacity, 1)
    summed = jnp.sum(mine.reshape(4, 4, capacity), axis=1)
    return summed.reshape(1, -1) / float(block_len * 2 * half)


def solution(mesh):
    placed = (
        P(None, "seq", "mdl"),
        P("mdl"),
        P(None, "seq"),
        P(None, "seq"),
        P("grp", None, "seq", "mdl"),
        P(None, "mdl"),
    )
    plan = local_lines if mesh.shape["seq"] == 8 else local
    return jax.shard_map(
        plan, mesh=mesh, in_specs=placed, out_specs=P("seq", "grp"), check_vma=False
    )
```

```python
import functools
import math

import jax
import jax.numpy as jnp
from jax import lax
from jax.experimental import pallas as pl
from jax.experimental.pallas import tpu as pltpu
from jax.sharding import PartitionSpec as P

HD = 128
WIN = 64
AXES = ("grp", "seq", "mdl")
PIECES = 10


def padded(x, sides, width):
    for axis, dim in sides:
        count, length = (lax.axis_size(axis), x.shape[dim])
        up = [(i, (i + 1) % count) for i in range(count - 1)]
        down = [(j, i) for i, j in up]
        last = lax.slice_in_dim(x, length - width, length, axis=dim)
        leading = lax.slice_in_dim(x, 0, width, axis=dim)
        before = lax.ppermute(last, axis, up)
        after = lax.ppermute(leading, axis, down)
        x = jnp.concatenate([before, x, after], axis=dim)
    return x


def predict(context, target, live_flags, pred_weight, divisor):
    flat_rows = context.reshape(-1, context.shape[-1])
    wide_rows = lax.all_gather(flat_rows, "mdl", axis=1, tiled=True)
    predicted = jnp.dot(wide_rows, pred_weight, preferred_element_type=jnp.float32)
    residue = predicted - target.reshape(flat_rows.shape).astype(jnp.float32)
    partial_sums = jnp.sum((residue * residue).reshape(live_flags.shape[0], -1), axis=1)
    summed = lax.psum(partial_sums, "mdl")
    return summed / divisor * live_flags


def local(signal, mask_token, keep, target_shard, enc_weight, pred_weight):
    group_index = lax.axis_index("grp")
    seq_index = lax.axis_index("seq")
    shards = lax.axis_size("seq")
    sequences, length, half_width = signal.shape
    per_range = keep.shape[1]
    block_len = length // per_range
    kept_rows = jnp.repeat(keep, block_len, axis=1)[:, :, None]
    masked_in = jnp.where(kept_rows == 1, signal, mask_token[None, None, :])
    source = jnp.where(group_index == 0, masked_in, signal)
    wide_in = lax.all_gather(source, "mdl", axis=2, tiled=True)
    full_width = wide_in.shape[2]
    flat_in = wide_in.reshape(-1, full_width)
    span = length + 2 * WIN
    weight_all = lax.all_gather(enc_weight, "seq", axis=2, tiled=True)[0]
    queries = jnp.dot(flat_in, weight_all[0], preferred_element_type=jnp.float32).astype(
        jnp.bfloat16
    )
    pair_made = jnp.einsum(
        "nd,cde->cne", flat_in, weight_all[1:], preferred_element_type=jnp.float32
    ).astype(jnp.bfloat16)
    own_pairs = pair_made.reshape(2, sequences, length, half_width)
    pair_rows = padded(own_pairs, (("seq", 2),), WIN)
    head_count = half_width // HD
    query_heads = queries.reshape(sequences, length, head_count, HD)
    key_heads = pair_rows[0].reshape(sequences, span, head_count, HD)
    value_heads = pair_rows[1].reshape(sequences, span, head_count, HD)
    query_pos = seq_index * length + jnp.arange(length)
    key_pos = seq_index * length - WIN + jnp.arange(span)
    total_len = length * shards
    in_window = (
        (jnp.abs(query_pos[:, None] - key_pos[None, :]) <= WIN)
        & (key_pos[None, :] >= 0)
        & (key_pos[None, :] < total_len)
    )
    scores = jnp.einsum(
        "sahd,sbhd->shab", query_heads, key_heads, preferred_element_type=jnp.float32
    ) * (1.0 / math.sqrt(HD))
    scores = jnp.where(in_window[None, None], scores, -jnp.inf)
    row_peak = jnp.max(scores, axis=-1, keepdims=True)
    exp_scores = jnp.exp(scores - row_peak)
    attention = (exp_scores / jnp.sum(exp_scores, axis=-1, keepdims=True)).astype(jnp.bfloat16)
    attended = jnp.einsum(
        "shab,sbhd->sahd", attention, value_heads, preferred_element_type=jnp.float32
    ).astype(jnp.bfloat16)
    latent = attended.reshape(sequences * per_range, block_len, half_width)
    blocks_here = latent.shape[0]
    capacity = max(2, 2 * blocks_here // shards)
    slot_count = shards * capacity
    shard_of = target_shard.reshape(-1)
    masked_flag = (keep.reshape(-1) == 0).astype(jnp.float32)
    order_ids = jnp.arange(blocks_here)
    earlier = (shard_of[:, None] == shard_of[None, :]) & (order_ids[:, None] < order_ids[None, :])
    slot_rank = jnp.sum(earlier.astype(jnp.int32), axis=0)
    slot_index = shard_of * capacity + slot_rank
    onehot = slot_index[None, :] == jnp.arange(slot_count)[:, None]
    divisor = float(block_len * full_width)
    halves = lax.all_to_all(latent[None], "grp", split_axis=1, concat_axis=0, tiled=True)
    half_count = blocks_here // 2
    first_block = group_index * half_count
    own_flags = lax.dynamic_slice_in_dim(masked_flag, first_block, half_count)
    losses = predict(halves[0], halves[1], own_flags, pred_weight, divisor)
    spread = lax.dynamic_update_slice_in_dim(
        jnp.zeros((blocks_here,), jnp.float32), losses, first_block, 0
    )
    slotted = jnp.sum(jnp.where(onehot, spread[None, :], 0.0), axis=1).reshape(shards, capacity)
    arrived = lax.all_to_all(slotted, "seq", split_axis=0, concat_axis=0, tiled=True)
    result = lax.psum_scatter(arrived, "grp", scatter_dimension=0, tiled=True)
    return result.reshape(1, -1)


def move(x, target):
    pairs = []
    for c in range(2):
        for s in range(8):
            for m in range(2):
                c2, z2, y2, m2 = target(c, s // 2, s % 2, m)
                pairs.append(((c * 8 + s) * 2 + m, (c2 * 8 + 2 * z2 + y2) * 2 + m2))
    return lax.ppermute(x, AXES, pairs)


def places():
    s = lax.axis_index("seq")
    return lax.axis_index("grp"), s // 2, lax.rem(s, 2), lax.axis_index("mdl")


def mask_kernel(
    signal_ref, token_ref, keep_ref, mine_ref, given_ref, mine_own_ref, given_own_ref
):
    core, _, y, _ = places()
    length = signal_ref.shape[1]
    blocks = keep_ref.shape[1]
    block_len = length // blocks
    row = lax.broadcasted_iota(jnp.int32, (length, blocks), 0)
    first = lax.broadcasted_iota(jnp.int32, (length, blocks), 1) * block_len
    covers = (row >= first) & (row < first + block_len)
    token = token_ref[...].astype(jnp.float32).reshape(1, -1)
    for other, own, chosen in ((mine_ref, mine_own_ref, y), (given_ref, given_own_ref, 1 - y)):
        kept = jnp.where(covers, keep_ref[pl.ds(chosen, 1), :], 0)
        kept = jnp.sum(kept, axis=1, keepdims=True)
        rows = signal_ref[chosen].astype(jnp.float32)
        other[...] = jnp.where(kept + 1 - core > 0, rows, token).astype(other.dtype)
        own[...] = jnp.where(kept + core > 0, rows, token).astype(own.dtype)


def slice_kernel(after_ref, weight_ref, pred_ref, near_ref, far_ref, early_ref, late_ref, sems):
    core, z, _, _ = places()
    wide = near_ref.shape[2]
    cut = early_ref.shape[0]
    t = jnp.where(core == z // 2, 1 - lax.rem(z, 2), lax.rem(z, 2))
    copies = []
    for target, chosen in ((near_ref, t), (far_ref, 1 - t)):
        lanes = pl.ds(pl.multiple_of(chosen * wide, 128), wide)
        copies.append((weight_ref.at[0, :, :, lanes], target))
    for index, target in enumerate((early_ref, late_ref)):
        first = pl.multiple_of((2 * core + index) * cut, 128)
        copies.append((pred_ref.at[pl.ds(first, cut), :], target))
    copies = [
        pltpu.make_async_copy(source, target, sems.at[index])
        for index, (source, target) in enumerate(copies)
    ]
    for copy in copies:
        copy.start()
    for copy in copies:
        copy.wait()


def encode_kernel(x_own, x_across, x_near, x_near_across, halo_ref, *refs):
    pieces = refs[:PIECES]
    out_ref, x_buf, w_buf, q_buf, k_buf, v_buf, sems = refs[PIECES:]
    core, z, y, m = places()
    half = x_own.shape[-1]
    rows = x_own.shape[1]
    depth = pieces[0].shape[1]
    wide = pieces[0].shape[2]
    own_rows = 4 * rows
    copies = []
    side = jnp.where(core == z // 2, 1 - lax.rem(z, 2), lax.rem(z, 2))
    for piece, near, across in (
        (x_own, 0, 0), (x_across, 0, 1), (x_near, 1, 0), (x_near_across, 1, 1)
    ):
        first = WIN + 2 * rows * (side if near == 0 else 1 - side)
        lane = half * (m if across == 0 else 1 - m)
        for part in range(2):
            copies.append((
                piece.at[part],
                x_buf.at[
                    pl.ds(pl.multiple_of(first + (y if part == 0 else 1 - y) * rows, 64), rows),
                    pl.ds(pl.multiple_of(lane, 128), half),
                ],
            ))
    halo_first = pl.multiple_of((1 - core) * (WIN + own_rows), 64)
    empty_first = pl.multiple_of(core * (WIN + own_rows), 64)
    for across in range(2):
        lane = half * (m if across == 0 else 1 - m)
        copies.append((
            halo_ref.at[across],
            x_buf.at[pl.ds(halo_first, WIN), pl.ds(pl.multiple_of(lane, 128), half)],
        ))
    home = core == z // 2
    one, one_y, one_c, one_yc, two, two_c, own, own_c, two_y, two_yc = pieces
    parity = lax.rem(z, 2)
    beside, cross = z + 1 - 2 * parity, 2 * (1 - z // 2) + parity
    last = cross + 1 - 2 * parity

    def slot(source, row):
        first = pl.multiple_of((2 * source + row) * depth, 64)
        return w_buf.at[:, pl.ds(first, depth), :]

    here, there = jnp.where(home, cross, beside), jnp.where(home, beside, cross)
    copies += [
        (one, slot(here, y)), (one_y, slot(here, 1 - y)),
        (one_c, slot(there, y)), (one_yc, slot(there, 1 - y)),
        (two, slot(jnp.where(home, z, last), jnp.where(home, 1 - y, y))),
        (two_c, slot(jnp.where(home, last, z), jnp.where(home, y, 1 - y))),
    ]
    started = []
    for index, (source, target) in enumerate(copies):
        copy = pltpu.make_async_copy(source, target, sems.at[index])
        copy.start()
        started.append(copy)
    for wanted, pair in ((home, (own, two_yc)), (jnp.logical_not(home), (own_c, two_y))):
        @pl.when(wanted)
        def _(pair=pair):
            held = [
                pltpu.make_async_copy(pair[0], slot(z, y), sems.at[len(copies)]),
                pltpu.make_async_copy(pair[1], slot(last, 1 - y), sems.at[len(copies) + 1]),
            ]
            for copy in held:
                copy.start()
            for copy in held:
                copy.wait()

    x_buf[pl.ds(empty_first, WIN), :] = jnp.zeros((WIN, 2 * half), x_buf.dtype)
    for copy in started:
        copy.wait()
    x = x_buf[...]
    q_buf[...] = jnp.dot(
        x[WIN:WIN + own_rows], w_buf[0], preferred_element_type=jnp.float32
    ).astype(q_buf.dtype)
    k_buf[...] = jnp.dot(x, w_buf[1], preferred_element_type=jnp.float32).astype(k_buf.dtype)
    v_buf[...] = jnp.dot(x, w_buf[2], preferred_element_type=jnp.float32).astype(v_buf.dtype)
    keys = rows + 2 * WIN
    a = lax.broadcasted_iota(jnp.int32, (rows, keys), 0)
    b = lax.broadcasted_iota(jnp.int32, (rows, keys), 1)
    band = (b >= a) & (b <= a + 2 * WIN)
    for j in range(4):
        admitted = band
        if j == 0:
            admitted = admitted & (b >= WIN * (1 - core))
        if j == 3:
            admitted = admitted & (b < keys - WIN * core)
        for h in range(wide // HD):
            lanes = slice(h * HD, (h + 1) * HD)
            scores = lax.dot_general(
                q_buf[j * rows:(j + 1) * rows, lanes],
                k_buf[j * rows:j * rows + keys, lanes],
                (((1,), (1,)), ((), ())),
                preferred_element_type=jnp.float32,
            ) * (1.0 / math.sqrt(HD))
            scores = jnp.where(admitted, scores, -jnp.inf)
            peak = jnp.max(scores, axis=-1, keepdims=True)
            exps = jnp.exp(scores - peak)
            attention = (exps / jnp.sum(exps, axis=-1, keepdims=True)).astype(jnp.bfloat16)
            out_ref[j, :, lanes] = jnp.dot(
                attention,
                v_buf[j * rows:j * rows + keys, lanes],
                preferred_element_type=jnp.float32,
            ).astype(out_ref.dtype)


def predict_kernel(slot_ref, lat_ref, own_ref, e0, e1, l0, l1, out_ref):
    core, _, _, m = places()
    wide = lat_ref.shape[2]
    lent = ((e0, e1), (l0, l1))
    total = None
    for side in range(2):
        predicted = None
        for t in range(2):
            for x in range(2):
                if side == 0:
                    source = lat_ref[2 * t + x]
                    weight = own_ref[(2 * x + t) * wide:(2 * x + t + 1) * wide, :]
                else:
                    source = lat_ref[2 * t + (core if x == 0 else 1 - core)]
                    weight = lent[t][x][...]
                term = jnp.dot(source, weight, preferred_element_type=jnp.float32)
                predicted = term if predicted is None else predicted + term
        for t in range(2):
            target = lat_ref[4 + 2 * t + (m if side == 0 else 1 - m)].astype(jnp.float32)
            residue = predicted[:, t * wide:(t + 1) * wide] - target
            for i in range(wide // 128):
                piece = residue[:, i * 128:(i + 1) * 128]
                total = piece * piece if total is None else total + piece * piece
    row_errors = jnp.sum(total, axis=1, keepdims=True)
    rows, slots = total.shape[0], out_ref.shape[2]
    chosen = slot_ref[...] == lax.broadcasted_iota(jnp.int32, (rows, slots), 1)
    routed = jnp.sum(jnp.where(chosen, row_errors, 0.0), axis=0, keepdims=True)
    for i in range(out_ref.shape[0]):
        out_ref[i] = routed


def local_lines(signal, mask_token, keep, target_shard, enc_weight, pred_weight):
    core = lax.axis_index("grp")
    s = lax.axis_index("seq")
    m = lax.axis_index("mdl")
    z, y = s // 2, s % 2
    sequences, length, half = signal.shape
    per_range = keep.shape[1]
    block_len = length // per_range
    depth = enc_weight.shape[2]
    wide = half // 2

    vmem = pl.BlockSpec(memory_space=pltpu.VMEM)
    anywhere = pl.BlockSpec(memory_space=pl.ANY)

    def first_pairs(c, z, y, m):
        if z // 2 == c:
            return (1 - c, z + 1 - 2 * (z % 2), y, m)
        return (c, z % 2 + 2 * c, y, m)

    def second_pairs(c, z, y, m):
        if z // 2 == c:
            return (c, z, 1 - y, m)
        return (1 - c, 1 - z % 2 + 2 * c, y, m)

    def last_pairs(c, z, y, m):
        if z // 2 == c:
            return (c, z + 1 - 2 * (z % 2), y, m)
        return (c, z, 1 - y, m)

    def across_z(c, z, y, m):
        if z // 2 == c:
            return (c, (z + 2) % 4, y, m)
        return (1 - c, z + 1 - 2 * (z % 2), y, m)

    def across_zy(c, z, y, m):
        c, z, y, m = across_z(c, z, y, m)
        return (c, z, 1 - y, m)

    def flip_y(c, z, y, m):
        return (c, z, 1 - y, m)

    def flip_core(c, z, y, m):
        return (1 - c, z, y, m)

    def flip_x(c, z, y, m):
        return (c, z, y, 1 - m)

    def second_hop(c, z, y, m):
        if z // 2 == c:
            return (c, z, 1 - y, m)
        return (c, z + 1 - 2 * (z % 2), y, m)

    cut = half // 2
    mine, given, mine_own, given_own = pl.pallas_call(
        mask_kernel,
        out_shape=[jax.ShapeDtypeStruct((length, half), jnp.bfloat16)] * 4,
        in_specs=[vmem] * 3,
        out_specs=[vmem] * 4,
    )(signal, mask_token, keep)
    near, far, early, late = pl.pallas_call(
        slice_kernel,
        out_shape=[jax.ShapeDtypeStruct(shape, jnp.bfloat16) for shape in (
            (3, depth, wide), (3, depth, wide), (cut, half), (cut, half),
        )],
        in_specs=[anywhere] * 3,
        out_specs=[vmem] * 4,
        scratch_shapes=[pltpu.SemaphoreType.DMA((4,))],
    )(mine, enc_weight, pred_weight)
    first, second = move(mine, across_z), move(given, across_zy)
    small = jnp.stack([keep, target_shard])
    small, _ = lax.optimization_barrier((small, mine))
    routing = move(small, lambda c, z, y, m: ((2 * z + y) // 4, (2 * z + y) % 4, c, m))
    near, routing, first, second = lax.optimization_barrier((near, routing, first, second))
    x_own = jnp.stack([first, second])
    near_w = move(near, first_pairs)
    weight_early = move(early, flip_x)
    far, x_own = lax.optimization_barrier((far, x_own))
    far_w = move(far, second_pairs)
    home = core == z // 2
    sent = jnp.where(home, jnp.stack([mine_own, given_own]), x_own)
    come = move(sent, second_hop)
    kept_home = (jnp.arange(2) == 0)[:, None, None] & home
    x_near = jnp.where(kept_home, mine_own[None], come)
    x_across = move(x_own, flip_x)
    near_y_source, weight_early = lax.optimization_barrier((near_w, weight_early))
    near_y = move(near_y_source, flip_y)
    far_y_source, near_y = lax.optimization_barrier((far_w, near_y))
    far_y = move(far_y_source, last_pairs)
    weight_early_c = move(weight_early, flip_core)
    x_near, x_across = lax.optimization_barrier((x_near, x_across))
    x_near_across = move(x_near, flip_x)
    late, _ = lax.optimization_barrier((late, x_near_across))
    weight_late = move(late, flip_x)
    weight_late_c = move(weight_late, flip_core)
    hidden = lax.dynamic_index_in_dim(routing[0], y, 0, keepdims=False) == 0
    shard_of = routing[1].reshape(-1)
    blocks = shard_of.shape[0]
    capacity = max(2, 2 * blocks // 8)
    order_ids = jnp.arange(blocks)
    earlier = (shard_of[:, None] == shard_of[None, :]) & (order_ids[:, None] < order_ids[None, :])
    slot = shard_of * capacity + jnp.sum(earlier.astype(jnp.int32), axis=0)
    slot = lax.dynamic_index_in_dim(slot.reshape(sequences, -1), y, 0, keepdims=False)
    slot = jnp.where(hidden, slot, -1)
    slot = lax.dynamic_slice_in_dim(slot, m * (per_range // 2), per_range // 2)
    slot = jnp.repeat(slot, block_len)[:, None]

    def edge(own, near):
        found = jnp.where(jnp.where(home, 1 - z % 2, z % 2) == 1 - core, own, near)
        part = jnp.where(core == 0, 1 - y, y)
        first = jnp.where(core == 0, length - WIN, 0)
        return lax.dynamic_slice(found, (part, first, 0), (1, WIN, half))[0]

    halo = move(jnp.stack([edge(x_own, x_near), edge(x_across, x_near_across)]), flip_core)
    far_yc_source, halo = lax.optimization_barrier((far_y, halo))
    pieces = [
        near_w, near_y, move(near_w, flip_core), move(near_y, flip_core),
        far_w, move(far_w, flip_core), far, move(far, flip_core),
        far_y, move(far_yc_source, flip_core),
    ]
    span = 4 * length + 2 * WIN

    latent = pl.pallas_call(
        encode_kernel,
        out_shape=jax.ShapeDtypeStruct((4, length, wide), jnp.bfloat16),
        in_specs=[anywhere] * (5 + PIECES),
        out_specs=vmem,
        scratch_shapes=[
            pltpu.VMEM((span, 2 * half), jnp.bfloat16),
            pltpu.VMEM((3, 2 * half, wide), jnp.bfloat16),
            pltpu.VMEM((4 * length, wide), jnp.bfloat16),
            pltpu.VMEM((span, wide), jnp.bfloat16),
            pltpu.VMEM((span, wide), jnp.bfloat16),
            pltpu.SemaphoreType.DMA((18,)),
        ],
        compiler_params=pltpu.CompilerParams(vmem_limit_bytes=56 * 2**20),
    )(x_own, x_across, x_near, x_near_across, halo, *pieces)
    lines = [[4 * i + 2 * j + k for i in range(4) for k in range(2)] for j in range(2)]
    latents = lax.all_to_all(
        latent.reshape(8, length // 2, wide), ("seq", "mdl"),
        split_axis=0, concat_axis=0, tiled=True, axis_index_groups=lines,
    )
    routed = pl.pallas_call(
        predict_kernel,
        out_shape=jax.ShapeDtypeStruct((16, 1, 8 * capacity), jnp.float32),
        in_specs=[vmem] * 7,
        out_specs=vmem,
        compiler_params=pltpu.CompilerParams(vmem_limit_bytes=24 * 2**20),
    )(
        slot, latents, pred_weight,
        weight_early, weight_early_c, weight_late, weight_late_c,
    )
    arrived = lax.all_to_all(routed, ("seq", "mdl"), split_axis=0, concat_axis=0, tiled=True)
    mine = lax.dynamic_slice_in_dim(arrived[:, 0], capacity * s, capacity, 1)
    summed = jnp.sum(mine.reshape(4, 4, capacity), axis=1)
    return summed.reshape(1, -1) / float(block_len * 2 * half)


def solution(mesh):
    placed = (
        P(None, "seq", "mdl"),
        P("mdl"),
        P(None, "seq"),
        P(None, "seq"),
        P("grp", None, "seq", "mdl"),
        P(None, "mdl"),
    )
    plan = local_lines if mesh.shape["seq"] == 8 else local
    return jax.shard_map(
        plan, mesh=mesh, in_specs=placed, out_specs=P("seq", "grp"), check_vma=False
    )
```

```python
import functools
import math

import jax
import jax.numpy as jnp
from jax import lax
from jax.experimental import pallas as pl
from jax.experimental.pallas import tpu as pltpu
from jax.sharding import PartitionSpec as P

HD = 128
WIN = 64
AXES = ("grp", "seq", "mdl")
PIECES = 8


def padded(x, sides, width):
    for axis, dim in sides:
        count, length = (lax.axis_size(axis), x.shape[dim])
        up = [(i, (i + 1) % count) for i in range(count - 1)]
        down = [(j, i) for i, j in up]
        last = lax.slice_in_dim(x, length - width, length, axis=dim)
        leading = lax.slice_in_dim(x, 0, width, axis=dim)
        before = lax.ppermute(last, axis, up)
        after = lax.ppermute(leading, axis, down)
        x = jnp.concatenate([before, x, after], axis=dim)
    return x


def predict(context, target, live_flags, pred_weight, divisor):
    flat_rows = context.reshape(-1, context.shape[-1])
    wide_rows = lax.all_gather(flat_rows, "mdl", axis=1, tiled=True)
    predicted = jnp.dot(wide_rows, pred_weight, preferred_element_type=jnp.float32)
    residue = predicted - target.reshape(flat_rows.shape).astype(jnp.float32)
    partial_sums = jnp.sum((residue * residue).reshape(live_flags.shape[0], -1), axis=1)
    summed = lax.psum(partial_sums, "mdl")
    return summed / divisor * live_flags


def local(signal, mask_token, keep, target_shard, enc_weight, pred_weight):
    group_index = lax.axis_index("grp")
    seq_index = lax.axis_index("seq")
    shards = lax.axis_size("seq")
    sequences, length, half_width = signal.shape
    per_range = keep.shape[1]
    block_len = length // per_range
    kept_rows = jnp.repeat(keep, block_len, axis=1)[:, :, None]
    masked_in = jnp.where(kept_rows == 1, signal, mask_token[None, None, :])
    source = jnp.where(group_index == 0, masked_in, signal)
    wide_in = lax.all_gather(source, "mdl", axis=2, tiled=True)
    full_width = wide_in.shape[2]
    flat_in = wide_in.reshape(-1, full_width)
    span = length + 2 * WIN
    weight_all = lax.all_gather(enc_weight, "seq", axis=2, tiled=True)[0]
    queries = jnp.dot(flat_in, weight_all[0], preferred_element_type=jnp.float32).astype(
        jnp.bfloat16
    )
    pair_made = jnp.einsum(
        "nd,cde->cne", flat_in, weight_all[1:], preferred_element_type=jnp.float32
    ).astype(jnp.bfloat16)
    own_pairs = pair_made.reshape(2, sequences, length, half_width)
    pair_rows = padded(own_pairs, (("seq", 2),), WIN)
    head_count = half_width // HD
    query_heads = queries.reshape(sequences, length, head_count, HD)
    key_heads = pair_rows[0].reshape(sequences, span, head_count, HD)
    value_heads = pair_rows[1].reshape(sequences, span, head_count, HD)
    query_pos = seq_index * length + jnp.arange(length)
    key_pos = seq_index * length - WIN + jnp.arange(span)
    total_len = length * shards
    in_window = (
        (jnp.abs(query_pos[:, None] - key_pos[None, :]) <= WIN)
        & (key_pos[None, :] >= 0)
        & (key_pos[None, :] < total_len)
    )
    scores = jnp.einsum(
        "sahd,sbhd->shab", query_heads, key_heads, preferred_element_type=jnp.float32
    ) * (1.0 / math.sqrt(HD))
    scores = jnp.where(in_window[None, None], scores, -jnp.inf)
    row_peak = jnp.max(scores, axis=-1, keepdims=True)
    exp_scores = jnp.exp(scores - row_peak)
    attention = (exp_scores / jnp.sum(exp_scores, axis=-1, keepdims=True)).astype(jnp.bfloat16)
    attended = jnp.einsum(
        "shab,sbhd->sahd", attention, value_heads, preferred_element_type=jnp.float32
    ).astype(jnp.bfloat16)
    latent = attended.reshape(sequences * per_range, block_len, half_width)
    blocks_here = latent.shape[0]
    capacity = max(2, 2 * blocks_here // shards)
    slot_count = shards * capacity
    shard_of = target_shard.reshape(-1)
    masked_flag = (keep.reshape(-1) == 0).astype(jnp.float32)
    order_ids = jnp.arange(blocks_here)
    earlier = (shard_of[:, None] == shard_of[None, :]) & (order_ids[:, None] < order_ids[None, :])
    slot_rank = jnp.sum(earlier.astype(jnp.int32), axis=0)
    slot_index = shard_of * capacity + slot_rank
    onehot = slot_index[None, :] == jnp.arange(slot_count)[:, None]
    divisor = float(block_len * full_width)
    halves = lax.all_to_all(latent[None], "grp", split_axis=1, concat_axis=0, tiled=True)
    half_count = blocks_here // 2
    first_block = group_index * half_count
    own_flags = lax.dynamic_slice_in_dim(masked_flag, first_block, half_count)
    losses = predict(halves[0], halves[1], own_flags, pred_weight, divisor)
    spread = lax.dynamic_update_slice_in_dim(
        jnp.zeros((blocks_here,), jnp.float32), losses, first_block, 0
    )
    slotted = jnp.sum(jnp.where(onehot, spread[None, :], 0.0), axis=1).reshape(shards, capacity)
    arrived = lax.all_to_all(slotted, "seq", split_axis=0, concat_axis=0, tiled=True)
    result = lax.psum_scatter(arrived, "grp", scatter_dimension=0, tiled=True)
    return result.reshape(1, -1)


def move(x, target):
    pairs = []
    for c in range(2):
        for s in range(8):
            for m in range(2):
                c2, z2, y2, m2 = target(c, s // 2, s % 2, m)
                pairs.append(((c * 8 + s) * 2 + m, (c2 * 8 + 2 * z2 + y2) * 2 + m2))
    return lax.ppermute(x, AXES, pairs)


def places():
    s = lax.axis_index("seq")
    return lax.axis_index("grp"), s // 2, lax.rem(s, 2), lax.axis_index("mdl")


def mask_kernel(
    signal_ref, token_ref, keep_ref, mine_ref, given_ref, mine_own_ref, given_own_ref
):
    core, _, y, _ = places()
    length = signal_ref.shape[1]
    blocks = keep_ref.shape[1]
    block_len = length // blocks
    row = lax.broadcasted_iota(jnp.int32, (length, blocks), 0)
    first = lax.broadcasted_iota(jnp.int32, (length, blocks), 1) * block_len
    covers = (row >= first) & (row < first + block_len)
    token = token_ref[...].astype(jnp.float32).reshape(1, -1)
    for other, own, chosen in ((mine_ref, mine_own_ref, y), (given_ref, given_own_ref, 1 - y)):
        kept = jnp.where(covers, keep_ref[pl.ds(chosen, 1), :], 0)
        kept = jnp.sum(kept, axis=1, keepdims=True)
        rows = signal_ref[chosen].astype(jnp.float32)
        other[...] = jnp.where(kept + 1 - core > 0, rows, token).astype(other.dtype)
        own[...] = jnp.where(kept + core > 0, rows, token).astype(own.dtype)


def slice_kernel(after_ref, weight_ref, pred_ref, near_ref, far_ref, early_ref, late_ref, sems):
    core, z, _, _ = places()
    wide = near_ref.shape[2]
    t = lax.rem(z, 2)
    copies = []
    for target, chosen in ((near_ref, t), (far_ref, 1 - t)):
        lanes = pl.ds(pl.multiple_of(chosen * wide, 128), wide)
        copies.append((weight_ref.at[0, :, :, lanes], target))
    count = early_ref.shape[0] + late_ref.shape[0]
    for target, skipped in ((early_ref, 0), (late_ref, early_ref.shape[0])):
        first = pl.multiple_of(core * count + skipped, 128)
        copies.append((pred_ref.at[pl.ds(first, target.shape[0]), :], target))
    copies = [
        pltpu.make_async_copy(source, target, sems.at[index])
        for index, (source, target) in enumerate(copies)
    ]
    for copy in copies:
        copy.start()
    for copy in copies:
        copy.wait()


def encode_kernel(x_own, x_across, x_near, x_near_across, halo_ref, *refs):
    pieces = refs[:PIECES]
    out_ref, x_buf, w_buf, q_buf, k_buf, v_buf, sems = refs[PIECES:]
    core, z, y, m = places()
    half = x_own.shape[-1]
    rows = x_own.shape[1]
    depth = pieces[0].shape[1]
    wide = pieces[0].shape[2]
    own_rows = 4 * rows
    copies = []
    side = jnp.where(core == z // 2, 1 - lax.rem(z, 2), lax.rem(z, 2))
    for piece, near, across in (
        (x_own, 0, 0), (x_across, 0, 1), (x_near, 1, 0), (x_near_across, 1, 1)
    ):
        first = WIN + 2 * rows * (side if near == 0 else 1 - side)
        lane = half * (m if across == 0 else 1 - m)
        for part in range(2):
            copies.append((
                piece.at[part],
                x_buf.at[
                    pl.ds(pl.multiple_of(first + (y if part == 0 else 1 - y) * rows, 64), rows),
                    pl.ds(pl.multiple_of(lane, 128), half),
                ],
            ))
    halo_first = pl.multiple_of((1 - core) * (WIN + own_rows), 64)
    empty_first = pl.multiple_of(core * (WIN + own_rows), 64)
    for across in range(2):
        lane = half * (m if across == 0 else 1 - m)
        copies.append((
            halo_ref.at[across],
            x_buf.at[pl.ds(halo_first, WIN), pl.ds(pl.multiple_of(lane, 128), half)],
        ))
    t = lax.rem(z, 2)
    for index, piece in enumerate(pieces):
        crossed, other = (index // 2) % 2, index % 2
        low = core if (other == 0) == (index >= 4) else 1 - core
        pos_z = 2 * low + (t if index < 4 else 1 - t)
        pos = 2 * pos_z + (y if crossed == 0 else 1 - y)
        copies.append((
            piece, w_buf.at[:, pl.ds(pl.multiple_of(pos * depth, 64), depth), :]
        ))
    started = []
    for index, (source, target) in enumerate(copies):
        copy = pltpu.make_async_copy(source, target, sems.at[index])
        copy.start()
        started.append(copy)
    x_buf[pl.ds(empty_first, WIN), :] = jnp.zeros((WIN, 2 * half), x_buf.dtype)
    for copy in started:
        copy.wait()
    x = x_buf[...]
    q_buf[...] = jnp.dot(
        x[WIN:WIN + own_rows], w_buf[0], preferred_element_type=jnp.float32
    ).astype(q_buf.dtype)
    k_buf[...] = jnp.dot(x, w_buf[1], preferred_element_type=jnp.float32).astype(k_buf.dtype)
    v_buf[...] = jnp.dot(x, w_buf[2], preferred_element_type=jnp.float32).astype(v_buf.dtype)
    keys = rows + 2 * WIN
    a = lax.broadcasted_iota(jnp.int32, (rows, keys), 0)
    b = lax.broadcasted_iota(jnp.int32, (rows, keys), 1)
    band = (b >= a) & (b <= a + 2 * WIN)
    for j in range(4):
        admitted = band
        if j == 0:
            admitted = admitted & (b >= WIN * (1 - core))
        if j == 3:
            admitted = admitted & (b < keys - WIN * core)
        for h in range(wide // HD):
            lanes = slice(h * HD, (h + 1) * HD)
            scores = lax.dot_general(
                q_buf[j * rows:(j + 1) * rows, lanes],
                k_buf[j * rows:j * rows + keys, lanes],
                (((1,), (1,)), ((), ())),
                preferred_element_type=jnp.float32,
            ) * (1.0 / math.sqrt(HD))
            scores = jnp.where(admitted, scores, -jnp.inf)
            peak = jnp.max(scores, axis=-1, keepdims=True)
            exps = jnp.exp(scores - peak)
            attention = (exps / jnp.sum(exps, axis=-1, keepdims=True)).astype(jnp.bfloat16)
            out_ref[j, :, lanes] = jnp.dot(
                attention,
                v_buf[j * rows:j * rows + keys, lanes],
                preferred_element_type=jnp.float32,
            ).astype(out_ref.dtype)


def predict_kernel(slot_ref, lat_ref, own_ref, e0, e1, l0, l1, out_ref):
    core, _, _, m = places()
    wide = lat_ref.shape[2]
    cut = e0.shape[0]
    total = None
    for side in range(2):
        terms = []
        for t in range(2):
            for x in range(2):
                if side == 0:
                    source = lat_ref[2 * t + x]
                    terms.append((source, own_ref[(2 * x + t) * wide:(2 * x + t + 1) * wide, :]))
                    continue
                early, late = ((e0, l0), (e1, l1))[x]
                source = lat_ref[2 * t + (core if x == 0 else 1 - core)]
                if t == 0:
                    terms.append((source[:, :cut], early[...]))
                    terms.append((source[:, cut:], late[:wide - cut, :]))
                else:
                    terms.append((source, late[wide - cut:, :]))
        predicted = None
        for source, weight in terms:
            term = jnp.dot(source, weight, preferred_element_type=jnp.float32)
            predicted = term if predicted is None else predicted + term
        for t in range(2):
            target = lat_ref[4 + 2 * t + (m if side == 0 else 1 - m)].astype(jnp.float32)
            residue = predicted[:, t * wide:(t + 1) * wide] - target
            for i in range(wide // 128):
                piece = residue[:, i * 128:(i + 1) * 128]
                total = piece * piece if total is None else total + piece * piece
    row_errors = jnp.sum(total, axis=1, keepdims=True)
    rows, slots = total.shape[0], out_ref.shape[2]
    chosen = slot_ref[...] == lax.broadcasted_iota(jnp.int32, (rows, slots), 1)
    routed = jnp.sum(jnp.where(chosen, row_errors, 0.0), axis=0, keepdims=True)
    for i in range(out_ref.shape[0]):
        out_ref[i] = routed


def local_lines(signal, mask_token, keep, target_shard, enc_weight, pred_weight):
    core = lax.axis_index("grp")
    s = lax.axis_index("seq")
    m = lax.axis_index("mdl")
    z, y = s // 2, s % 2
    sequences, length, half = signal.shape
    per_range = keep.shape[1]
    block_len = length // per_range
    depth = enc_weight.shape[2]
    wide = half // 2

    vmem = pl.BlockSpec(memory_space=pltpu.VMEM)
    anywhere = pl.BlockSpec(memory_space=pl.ANY)

    def to_near(c, z, y, m):
        return (1 - z // 2, z % 2 + 2 * c, y, m)

    def to_far(c, z, y, m):
        return (z // 2, 1 - z % 2 + 2 * c, y, m)

    def across_z(c, z, y, m):
        if z // 2 == c:
            return (c, (z + 2) % 4, y, m)
        return (1 - c, z + 1 - 2 * (z % 2), y, m)

    def across_zy(c, z, y, m):
        c, z, y, m = across_z(c, z, y, m)
        return (c, z, 1 - y, m)

    def flip_y(c, z, y, m):
        return (c, z, 1 - y, m)

    def flip_core(c, z, y, m):
        return (1 - c, z, y, m)

    def flip_x(c, z, y, m):
        return (c, z, y, 1 - m)

    def second_hop(c, z, y, m):
        if z // 2 == c:
            return (c, z, 1 - y, m)
        return (c, z + 1 - 2 * (z % 2), y, m)

    cut = half // 3
    mine, given, mine_own, given_own = pl.pallas_call(
        mask_kernel,
        out_shape=[jax.ShapeDtypeStruct((length, half), jnp.bfloat16)] * 4,
        in_specs=[vmem] * 3,
        out_specs=[vmem] * 4,
    )(signal, mask_token, keep)
    near, far, early, late = pl.pallas_call(
        slice_kernel,
        out_shape=[jax.ShapeDtypeStruct(shape, jnp.bfloat16) for shape in (
            (3, depth, wide), (3, depth, wide), (cut, half), (half - cut, half),
        )],
        in_specs=[anywhere] * 3,
        out_specs=[vmem] * 4,
        scratch_shapes=[pltpu.SemaphoreType.DMA((4,))],
    )(mine, enc_weight, pred_weight)
    first, second = move(mine, across_z), move(given, across_zy)
    small = jnp.stack([keep, target_shard])
    small, _ = lax.optimization_barrier((small, mine))
    routing = move(small, lambda c, z, y, m: ((2 * z + y) // 4, (2 * z + y) % 4, c, m))
    near, routing, first, second = lax.optimization_barrier((near, routing, first, second))
    x_own = jnp.stack([first, second])
    near_w = move(near, to_near)
    weight_early = move(early, flip_x)
    far, x_own = lax.optimization_barrier((far, x_own))
    far_w = move(far, to_far)
    home = core == z // 2
    sent = jnp.where(home, jnp.stack([mine_own, given_own]), x_own)
    come = move(sent, second_hop)
    kept_home = (jnp.arange(2) == 0)[:, None, None] & home
    x_near = jnp.where(kept_home, mine_own[None], come)
    x_across = move(x_own, flip_x)
    near_y_source, weight_early = lax.optimization_barrier((near_w, weight_early))
    near_y = move(near_y_source, flip_y)
    far_y_source, near_y = lax.optimization_barrier((far_w, near_y))
    far_y = move(far_y_source, flip_y)
    weight_early_c = move(weight_early, flip_core)
    x_near, x_across = lax.optimization_barrier((x_near, x_across))
    x_near_across = move(x_near, flip_x)
    late, _, far_w = lax.optimization_barrier((late, x_near_across, far_w))
    weight_late = move(late, flip_x)
    hidden = lax.dynamic_index_in_dim(routing[0], y, 0, keepdims=False) == 0
    shard_of = routing[1].reshape(-1)
    blocks = shard_of.shape[0]
    capacity = max(2, 2 * blocks // 8)
    order_ids = jnp.arange(blocks)
    earlier = (shard_of[:, None] == shard_of[None, :]) & (order_ids[:, None] < order_ids[None, :])
    slot = shard_of * capacity + jnp.sum(earlier.astype(jnp.int32), axis=0)
    slot = lax.dynamic_index_in_dim(slot.reshape(sequences, -1), y, 0, keepdims=False)
    slot = jnp.where(hidden, slot, -1)
    slot = lax.dynamic_slice_in_dim(slot, m * (per_range // 2), per_range // 2)
    slot = jnp.repeat(slot, block_len)[:, None]

    def edge(own, near):
        found = jnp.where(jnp.where(home, 1 - z % 2, z % 2) == 1 - core, own, near)
        part = jnp.where(core == 0, 1 - y, y)
        first = jnp.where(core == 0, length - WIN, 0)
        return lax.dynamic_slice(found, (part, first, 0), (1, WIN, half))[0]

    halo = move(jnp.stack([edge(x_own, x_near), edge(x_across, x_near_across)]), flip_core)
    far_yc_source, halo = lax.optimization_barrier((far_y, halo))
    pieces = [
        near_w, move(near_w, flip_core), near_y, move(near_y, flip_core),
        far_w, move(far_w, flip_core), far_y, move(far_yc_source, flip_core),
    ]
    span = 4 * length + 2 * WIN

    latent = pl.pallas_call(
        encode_kernel,
        out_shape=jax.ShapeDtypeStruct((4, length, wide), jnp.bfloat16),
        in_specs=[anywhere] * (5 + PIECES),
        out_specs=vmem,
        scratch_shapes=[
            pltpu.VMEM((span, 2 * half), jnp.bfloat16),
            pltpu.VMEM((3, 2 * half, wide), jnp.bfloat16),
            pltpu.VMEM((4 * length, wide), jnp.bfloat16),
            pltpu.VMEM((span, wide), jnp.bfloat16),
            pltpu.VMEM((span, wide), jnp.bfloat16),
            pltpu.SemaphoreType.DMA((10 + PIECES,)),
        ],
        compiler_params=pltpu.CompilerParams(vmem_limit_bytes=56 * 2**20),
    )(x_own, x_across, x_near, x_near_across, halo, *pieces)
    weight_late, latent = lax.optimization_barrier((weight_late, latent))
    weight_late_c = move(weight_late, flip_core)
    lines = [[4 * i + 2 * j + k for i in range(4) for k in range(2)] for j in range(2)]
    latents = lax.all_to_all(
        latent.reshape(8, length // 2, wide), ("seq", "mdl"),
        split_axis=0, concat_axis=0, tiled=True, axis_index_groups=lines,
    )
    routed = pl.pallas_call(
        predict_kernel,
        out_shape=jax.ShapeDtypeStruct((16, 1, 8 * capacity), jnp.float32),
        in_specs=[vmem] * 7,
        out_specs=vmem,
        compiler_params=pltpu.CompilerParams(vmem_limit_bytes=24 * 2**20),
    )(
        slot, latents, pred_weight,
        weight_early, weight_early_c, weight_late, weight_late_c,
    )
    arrived = lax.all_to_all(routed, ("seq", "mdl"), split_axis=0, concat_axis=0, tiled=True)
    mine = lax.dynamic_slice_in_dim(arrived[:, 0], capacity * s, capacity, 1)
    summed = jnp.sum(mine.reshape(4, 4, capacity), axis=1)
    return summed.reshape(1, -1) / float(block_len * 2 * half)


def solution(mesh):
    placed = (
        P(None, "seq", "mdl"),
        P("mdl"),
        P(None, "seq"),
        P(None, "seq"),
        P("grp", None, "seq", "mdl"),
        P(None, "mdl"),
    )
    plan = local_lines if mesh.shape["seq"] == 8 else local
    return jax.shard_map(
        plan, mesh=mesh, in_specs=placed, out_specs=P("seq", "grp"), check_vma=False
    )
```

```python
import functools
import math

import jax
import jax.numpy as jnp
from jax import lax
from jax.experimental import pallas as pl
from jax.experimental.pallas import tpu as pltpu
from jax.sharding import PartitionSpec as P

HD = 128
WIN = 64
AXES = ("grp", "seq", "mdl")
PIECES = 8


def padded(x, sides, width):
    for axis, dim in sides:
        count, length = (lax.axis_size(axis), x.shape[dim])
        up = [(i, (i + 1) % count) for i in range(count - 1)]
        down = [(j, i) for i, j in up]
        last = lax.slice_in_dim(x, length - width, length, axis=dim)
        leading = lax.slice_in_dim(x, 0, width, axis=dim)
        before = lax.ppermute(last, axis, up)
        after = lax.ppermute(leading, axis, down)
        x = jnp.concatenate([before, x, after], axis=dim)
    return x


def predict(context, target, live_flags, pred_weight, divisor):
    flat_rows = context.reshape(-1, context.shape[-1])
    wide_rows = lax.all_gather(flat_rows, "mdl", axis=1, tiled=True)
    predicted = jnp.dot(wide_rows, pred_weight, preferred_element_type=jnp.float32)
    residue = predicted - target.reshape(flat_rows.shape).astype(jnp.float32)
    partial_sums = jnp.sum((residue * residue).reshape(live_flags.shape[0], -1), axis=1)
    summed = lax.psum(partial_sums, "mdl")
    return summed / divisor * live_flags


def local(signal, mask_token, keep, target_shard, enc_weight, pred_weight):
    group_index = lax.axis_index("grp")
    seq_index = lax.axis_index("seq")
    shards = lax.axis_size("seq")
    sequences, length, half_width = signal.shape
    per_range = keep.shape[1]
    block_len = length // per_range
    kept_rows = jnp.repeat(keep, block_len, axis=1)[:, :, None]
    masked_in = jnp.where(kept_rows == 1, signal, mask_token[None, None, :])
    source = jnp.where(group_index == 0, masked_in, signal)
    wide_in = lax.all_gather(source, "mdl", axis=2, tiled=True)
    full_width = wide_in.shape[2]
    flat_in = wide_in.reshape(-1, full_width)
    span = length + 2 * WIN
    weight_all = lax.all_gather(enc_weight, "seq", axis=2, tiled=True)[0]
    queries = jnp.dot(flat_in, weight_all[0], preferred_element_type=jnp.float32).astype(
        jnp.bfloat16
    )
    pair_made = jnp.einsum(
        "nd,cde->cne", flat_in, weight_all[1:], preferred_element_type=jnp.float32
    ).astype(jnp.bfloat16)
    own_pairs = pair_made.reshape(2, sequences, length, half_width)
    pair_rows = padded(own_pairs, (("seq", 2),), WIN)
    head_count = half_width // HD
    query_heads = queries.reshape(sequences, length, head_count, HD)
    key_heads = pair_rows[0].reshape(sequences, span, head_count, HD)
    value_heads = pair_rows[1].reshape(sequences, span, head_count, HD)
    query_pos = seq_index * length + jnp.arange(length)
    key_pos = seq_index * length - WIN + jnp.arange(span)
    total_len = length * shards
    in_window = (
        (jnp.abs(query_pos[:, None] - key_pos[None, :]) <= WIN)
        & (key_pos[None, :] >= 0)
        & (key_pos[None, :] < total_len)
    )
    scores = jnp.einsum(
        "sahd,sbhd->shab", query_heads, key_heads, preferred_element_type=jnp.float32
    ) * (1.0 / math.sqrt(HD))
    scores = jnp.where(in_window[None, None], scores, -jnp.inf)
    row_peak = jnp.max(scores, axis=-1, keepdims=True)
    exp_scores = jnp.exp(scores - row_peak)
    attention = (exp_scores / jnp.sum(exp_scores, axis=-1, keepdims=True)).astype(jnp.bfloat16)
    attended = jnp.einsum(
        "shab,sbhd->sahd", attention, value_heads, preferred_element_type=jnp.float32
    ).astype(jnp.bfloat16)
    latent = attended.reshape(sequences * per_range, block_len, half_width)
    blocks_here = latent.shape[0]
    capacity = max(2, 2 * blocks_here // shards)
    slot_count = shards * capacity
    shard_of = target_shard.reshape(-1)
    masked_flag = (keep.reshape(-1) == 0).astype(jnp.float32)
    order_ids = jnp.arange(blocks_here)
    earlier = (shard_of[:, None] == shard_of[None, :]) & (order_ids[:, None] < order_ids[None, :])
    slot_rank = jnp.sum(earlier.astype(jnp.int32), axis=0)
    slot_index = shard_of * capacity + slot_rank
    onehot = slot_index[None, :] == jnp.arange(slot_count)[:, None]
    divisor = float(block_len * full_width)
    halves = lax.all_to_all(latent[None], "grp", split_axis=1, concat_axis=0, tiled=True)
    half_count = blocks_here // 2
    first_block = group_index * half_count
    own_flags = lax.dynamic_slice_in_dim(masked_flag, first_block, half_count)
    losses = predict(halves[0], halves[1], own_flags, pred_weight, divisor)
    spread = lax.dynamic_update_slice_in_dim(
        jnp.zeros((blocks_here,), jnp.float32), losses, first_block, 0
    )
    slotted = jnp.sum(jnp.where(onehot, spread[None, :], 0.0), axis=1).reshape(shards, capacity)
    arrived = lax.all_to_all(slotted, "seq", split_axis=0, concat_axis=0, tiled=True)
    result = lax.psum_scatter(arrived, "grp", scatter_dimension=0, tiled=True)
    return result.reshape(1, -1)


def move(x, target):
    pairs = []
    for c in range(2):
        for s in range(8):
            for m in range(2):
                c2, z2, y2, m2 = target(c, s // 2, s % 2, m)
                pairs.append(((c * 8 + s) * 2 + m, (c2 * 8 + 2 * z2 + y2) * 2 + m2))
    return lax.ppermute(x, AXES, pairs)


def places():
    s = lax.axis_index("seq")
    return lax.axis_index("grp"), s // 2, lax.rem(s, 2), lax.axis_index("mdl")


def mask_kernel(
    signal_ref, token_ref, keep_ref, mine_ref, given_ref, mine_own_ref, given_own_ref
):
    core, _, y, _ = places()
    length = signal_ref.shape[1]
    blocks = keep_ref.shape[1]
    block_len = length // blocks
    row = lax.broadcasted_iota(jnp.int32, (length, blocks), 0)
    first = lax.broadcasted_iota(jnp.int32, (length, blocks), 1) * block_len
    covers = (row >= first) & (row < first + block_len)
    token = token_ref[...].astype(jnp.float32).reshape(1, -1)
    for other, own, chosen in ((mine_ref, mine_own_ref, y), (given_ref, given_own_ref, 1 - y)):
        kept = jnp.where(covers, keep_ref[pl.ds(chosen, 1), :], 0)
        kept = jnp.sum(kept, axis=1, keepdims=True)
        rows = signal_ref[chosen].astype(jnp.float32)
        other[...] = jnp.where(kept + 1 - core > 0, rows, token).astype(other.dtype)
        own[...] = jnp.where(kept + core > 0, rows, token).astype(own.dtype)


def slice_kernel(after_ref, weight_ref, pred_ref, near_ref, far_ref, early_ref, late_ref, sems):
    core, z, _, _ = places()
    wide = near_ref.shape[2]
    cut = early_ref.shape[0]
    t = lax.rem(z, 2)
    copies = []
    for target, chosen in ((near_ref, t), (far_ref, 1 - t)):
        lanes = pl.ds(pl.multiple_of(chosen * wide, 128), wide)
        copies.append((weight_ref.at[0, :, :, lanes], target))
    for index, target in enumerate((early_ref, late_ref)):
        first = pl.multiple_of((2 * core + index) * cut, 128)
        copies.append((pred_ref.at[pl.ds(first, cut), :], target))
    copies = [
        pltpu.make_async_copy(source, target, sems.at[index])
        for index, (source, target) in enumerate(copies)
    ]
    for copy in copies:
        copy.start()
    for copy in copies:
        copy.wait()


def encode_kernel(x_own, x_across, x_near, x_near_across, halo_ref, *refs):
    pieces = refs[:PIECES]
    out_ref, x_buf, w_buf, q_buf, k_buf, v_buf, sems = refs[PIECES:]
    core, z, y, m = places()
    half = x_own.shape[-1]
    rows = x_own.shape[1]
    depth = pieces[0].shape[1]
    wide = pieces[0].shape[2]
    own_rows = 4 * rows
    copies = []
    side = jnp.where(core == z // 2, 1 - lax.rem(z, 2), lax.rem(z, 2))
    for piece, near, across in (
        (x_own, 0, 0), (x_across, 0, 1), (x_near, 1, 0), (x_near_across, 1, 1)
    ):
        first = WIN + 2 * rows * (side if near == 0 else 1 - side)
        lane = half * (m if across == 0 else 1 - m)
        for part in range(2):
            copies.append((
                piece.at[part],
                x_buf.at[
                    pl.ds(pl.multiple_of(first + (y if part == 0 else 1 - y) * rows, 64), rows),
                    pl.ds(pl.multiple_of(lane, 128), half),
                ],
            ))
    halo_first = pl.multiple_of((1 - core) * (WIN + own_rows), 64)
    empty_first = pl.multiple_of(core * (WIN + own_rows), 64)
    for across in range(2):
        lane = half * (m if across == 0 else 1 - m)
        copies.append((
            halo_ref.at[across],
            x_buf.at[pl.ds(halo_first, WIN), pl.ds(pl.multiple_of(lane, 128), half)],
        ))
    t = lax.rem(z, 2)
    for index, piece in enumerate(pieces):
        crossed, other = (index // 2) % 2, index % 2
        low = core if (other == 0) == (index >= 4) else 1 - core
        pos_z = 2 * low + (t if index < 4 else 1 - t)
        pos = 2 * pos_z + (y if crossed == 0 else 1 - y)
        copies.append((
            piece, w_buf.at[:, pl.ds(pl.multiple_of(pos * depth, 64), depth), :]
        ))
    started = []
    for index, (source, target) in enumerate(copies):
        copy = pltpu.make_async_copy(source, target, sems.at[index])
        copy.start()
        started.append(copy)
    x_buf[pl.ds(empty_first, WIN), :] = jnp.zeros((WIN, 2 * half), x_buf.dtype)
    for copy in started:
        copy.wait()
    x = x_buf[...]
    q_buf[...] = jnp.dot(
        x[WIN:WIN + own_rows], w_buf[0], preferred_element_type=jnp.float32
    ).astype(q_buf.dtype)
    k_buf[...] = jnp.dot(x, w_buf[1], preferred_element_type=jnp.float32).astype(k_buf.dtype)
    v_buf[...] = jnp.dot(x, w_buf[2], preferred_element_type=jnp.float32).astype(v_buf.dtype)
    keys = rows + 2 * WIN
    a = lax.broadcasted_iota(jnp.int32, (rows, keys), 0)
    b = lax.broadcasted_iota(jnp.int32, (rows, keys), 1)
    band = (b >= a) & (b <= a + 2 * WIN)
    for j in range(4):
        admitted = band
        if j == 0:
            admitted = admitted & (b >= WIN * (1 - core))
        if j == 3:
            admitted = admitted & (b < keys - WIN * core)
        for h in range(wide // HD):
            lanes = slice(h * HD, (h + 1) * HD)
            scores = lax.dot_general(
                q_buf[j * rows:(j + 1) * rows, lanes],
                k_buf[j * rows:j * rows + keys, lanes],
                (((1,), (1,)), ((), ())),
                preferred_element_type=jnp.float32,
            ) * (1.0 / math.sqrt(HD))
            scores = jnp.where(admitted, scores, -jnp.inf)
            peak = jnp.max(scores, axis=-1, keepdims=True)
            exps = jnp.exp(scores - peak)
            attention = (exps / jnp.sum(exps, axis=-1, keepdims=True)).astype(jnp.bfloat16)
            out_ref[j, :, lanes] = jnp.dot(
                attention,
                v_buf[j * rows:j * rows + keys, lanes],
                preferred_element_type=jnp.float32,
            ).astype(out_ref.dtype)


def predict_kernel(slot_ref, lat_ref, own_ref, e0, e1, l0, l1, out_ref):
    core, _, _, m = places()
    wide = lat_ref.shape[2]
    lent = ((e0, e1), (l0, l1))
    total = None
    for side in range(2):
        predicted = None
        for t in range(2):
            for x in range(2):
                if side == 0:
                    source = lat_ref[2 * t + x]
                    weight = own_ref[(2 * x + t) * wide:(2 * x + t + 1) * wide, :]
                else:
                    source = lat_ref[2 * t + (core if x == 0 else 1 - core)]
                    weight = lent[t][x][...]
                term = jnp.dot(source, weight, preferred_element_type=jnp.float32)
                predicted = term if predicted is None else predicted + term
        for t in range(2):
            target = lat_ref[4 + 2 * t + (m if side == 0 else 1 - m)].astype(jnp.float32)
            residue = predicted[:, t * wide:(t + 1) * wide] - target
            for i in range(wide // 128):
                piece = residue[:, i * 128:(i + 1) * 128]
                total = piece * piece if total is None else total + piece * piece
    row_errors = jnp.sum(total, axis=1, keepdims=True)
    rows, slots = total.shape[0], out_ref.shape[2]
    chosen = slot_ref[...] == lax.broadcasted_iota(jnp.int32, (rows, slots), 1)
    routed = jnp.sum(jnp.where(chosen, row_errors, 0.0), axis=0, keepdims=True)
    for i in range(out_ref.shape[0]):
        out_ref[i] = routed


def local_lines(signal, mask_token, keep, target_shard, enc_weight, pred_weight):
    core = lax.axis_index("grp")
    s = lax.axis_index("seq")
    m = lax.axis_index("mdl")
    z, y = s // 2, s % 2
    sequences, length, half = signal.shape
    per_range = keep.shape[1]
    block_len = length // per_range
    depth = enc_weight.shape[2]
    wide = half // 2

    vmem = pl.BlockSpec(memory_space=pltpu.VMEM)
    anywhere = pl.BlockSpec(memory_space=pl.ANY)

    def to_near(c, z, y, m):
        return (1 - z // 2, z % 2 + 2 * c, y, m)

    def to_far(c, z, y, m):
        return (z // 2, 1 - z % 2 + 2 * c, y, m)

    def across_z(c, z, y, m):
        if z // 2 == c:
            return (c, (z + 2) % 4, y, m)
        return (1 - c, z + 1 - 2 * (z % 2), y, m)

    def across_zy(c, z, y, m):
        c, z, y, m = across_z(c, z, y, m)
        return (c, z, 1 - y, m)

    def flip_y(c, z, y, m):
        return (c, z, 1 - y, m)

    def flip_core(c, z, y, m):
        return (1 - c, z, y, m)

    def flip_x(c, z, y, m):
        return (c, z, y, 1 - m)

    def second_hop(c, z, y, m):
        if z // 2 == c:
            return (c, z, 1 - y, m)
        return (c, z + 1 - 2 * (z % 2), y, m)

    cut = half // 2
    mine, given, mine_own, given_own = pl.pallas_call(
        mask_kernel,
        out_shape=[jax.ShapeDtypeStruct((length, half), jnp.bfloat16)] * 4,
        in_specs=[vmem] * 3,
        out_specs=[vmem] * 4,
    )(signal, mask_token, keep)
    near, far, early, late = pl.pallas_call(
        slice_kernel,
        out_shape=[jax.ShapeDtypeStruct(shape, jnp.bfloat16) for shape in (
            (3, depth, wide), (3, depth, wide), (cut, half), (cut, half),
        )],
        in_specs=[anywhere] * 3,
        out_specs=[vmem] * 4,
        scratch_shapes=[pltpu.SemaphoreType.DMA((4,))],
    )(mine, enc_weight, pred_weight)
    first, second = move(mine, across_z), move(given, across_zy)
    small = jnp.stack([keep, target_shard])
    small, _ = lax.optimization_barrier((small, mine))
    routing = move(small, lambda c, z, y, m: ((2 * z + y) // 4, (2 * z + y) % 4, c, m))
    near, routing = lax.optimization_barrier((near, routing))
    x_own = jnp.stack([first, second])
    near_w = move(near, to_near)
    weight_early = move(early, flip_x)
    far, x_own = lax.optimization_barrier((far, x_own))
    far_w = move(far, to_far)
    home = core == z // 2
    sent = jnp.where(home, jnp.stack([mine_own, given_own]), x_own)
    come = move(sent, second_hop)
    kept_home = (jnp.arange(2) == 0)[:, None, None] & home
    x_near = jnp.where(kept_home, mine_own[None], come)
    x_across = move(x_own, flip_x)
    near_y_source, weight_early = lax.optimization_barrier((near_w, weight_early))
    near_y = move(near_y_source, flip_y)
    far_y_source, near_y = lax.optimization_barrier((far_w, near_y))
    far_y = move(far_y_source, flip_y)
    weight_early_c = move(weight_early, flip_core)
    x_near, x_across = lax.optimization_barrier((x_near, x_across))
    x_near_across = move(x_near, flip_x)
    late, _ = lax.optimization_barrier((late, x_near_across))
    weight_late = move(late, flip_x)
    weight_late_c = move(weight_late, flip_core)
    hidden = lax.dynamic_index_in_dim(routing[0], y, 0, keepdims=False) == 0
    shard_of = routing[1].reshape(-1)
    blocks = shard_of.shape[0]
    capacity = max(2, 2 * blocks // 8)
    order_ids = jnp.arange(blocks)
    earlier = (shard_of[:, None] == shard_of[None, :]) & (order_ids[:, None] < order_ids[None, :])
    slot = shard_of * capacity + jnp.sum(earlier.astype(jnp.int32), axis=0)
    slot = lax.dynamic_index_in_dim(slot.reshape(sequences, -1), y, 0, keepdims=False)
    slot = jnp.where(hidden, slot, -1)
    slot = lax.dynamic_slice_in_dim(slot, m * (per_range // 2), per_range // 2)
    slot = jnp.repeat(slot, block_len)[:, None]

    def edge(own, near):
        found = jnp.where(jnp.where(home, 1 - z % 2, z % 2) == 1 - core, own, near)
        part = jnp.where(core == 0, 1 - y, y)
        first = jnp.where(core == 0, length - WIN, 0)
        return lax.dynamic_slice(found, (part, first, 0), (1, WIN, half))[0]

    halo = move(jnp.stack([edge(x_own, x_near), edge(x_across, x_near_across)]), flip_core)
    far_yc_source, halo = lax.optimization_barrier((far_y, halo))
    pieces = [
        near_w, move(near_w, flip_core), near_y, move(near_y, flip_core),
        far_w, move(far_w, flip_core), far_y, move(far_yc_source, flip_core),
    ]
    span = 4 * length + 2 * WIN

    latent = pl.pallas_call(
        encode_kernel,
        out_shape=jax.ShapeDtypeStruct((4, length, wide), jnp.bfloat16),
        in_specs=[anywhere] * (5 + PIECES),
        out_specs=vmem,
        scratch_shapes=[
            pltpu.VMEM((span, 2 * half), jnp.bfloat16),
            pltpu.VMEM((3, 2 * half, wide), jnp.bfloat16),
            pltpu.VMEM((4 * length, wide), jnp.bfloat16),
            pltpu.VMEM((span, wide), jnp.bfloat16),
            pltpu.VMEM((span, wide), jnp.bfloat16),
            pltpu.SemaphoreType.DMA((10 + PIECES,)),
        ],
        compiler_params=pltpu.CompilerParams(vmem_limit_bytes=56 * 2**20),
    )(x_own, x_across, x_near, x_near_across, halo, *pieces)
    lines = [[4 * i + 2 * j + k for i in range(4) for k in range(2)] for j in range(2)]
    latents = lax.all_to_all(
        latent.reshape(8, length // 2, wide), ("seq", "mdl"),
        split_axis=0, concat_axis=0, tiled=True, axis_index_groups=lines,
    )
    routed = pl.pallas_call(
        predict_kernel,
        out_shape=jax.ShapeDtypeStruct((16, 1, 8 * capacity), jnp.float32),
        in_specs=[vmem] * 7,
        out_specs=vmem,
        compiler_params=pltpu.CompilerParams(vmem_limit_bytes=24 * 2**20),
    )(
        slot, latents, pred_weight,
        weight_early, weight_early_c, weight_late, weight_late_c,
    )
    arrived = lax.all_to_all(routed, ("seq", "mdl"), split_axis=0, concat_axis=0, tiled=True)
    mine = lax.dynamic_slice_in_dim(arrived[:, 0], capacity * s, capacity, 1)
    summed = jnp.sum(mine.reshape(4, 4, capacity), axis=1)
    return summed.reshape(1, -1) / float(block_len * 2 * half)


def solution(mesh):
    placed = (
        P(None, "seq", "mdl"),
        P("mdl"),
        P(None, "seq"),
        P(None, "seq"),
        P("grp", None, "seq", "mdl"),
        P(None, "mdl"),
    )
    plan = local_lines if mesh.shape["seq"] == 8 else local
    return jax.shard_map(
        plan, mesh=mesh, in_specs=placed, out_specs=P("seq", "grp"), check_vma=False
    )
```

```python
import functools
import math

import jax
import jax.numpy as jnp
from jax import lax
from jax.experimental import pallas as pl
from jax.experimental.pallas import tpu as pltpu
from jax.sharding import PartitionSpec as P

HD = 128
WIN = 64
AXES = ("grp", "seq", "mdl")
PIECES = 8


def padded(x, sides, width):
    for axis, dim in sides:
        count, length = (lax.axis_size(axis), x.shape[dim])
        up = [(i, (i + 1) % count) for i in range(count - 1)]
        down = [(j, i) for i, j in up]
        last = lax.slice_in_dim(x, length - width, length, axis=dim)
        leading = lax.slice_in_dim(x, 0, width, axis=dim)
        before = lax.ppermute(last, axis, up)
        after = lax.ppermute(leading, axis, down)
        x = jnp.concatenate([before, x, after], axis=dim)
    return x


def predict(context, target, live_flags, pred_weight, divisor):
    flat_rows = context.reshape(-1, context.shape[-1])
    wide_rows = lax.all_gather(flat_rows, "mdl", axis=1, tiled=True)
    predicted = jnp.dot(wide_rows, pred_weight, preferred_element_type=jnp.float32)
    residue = predicted - target.reshape(flat_rows.shape).astype(jnp.float32)
    partial_sums = jnp.sum((residue * residue).reshape(live_flags.shape[0], -1), axis=1)
    summed = lax.psum(partial_sums, "mdl")
    return summed / divisor * live_flags


def local(signal, mask_token, keep, target_shard, enc_weight, pred_weight):
    group_index = lax.axis_index("grp")
    seq_index = lax.axis_index("seq")
    shards = lax.axis_size("seq")
    sequences, length, half_width = signal.shape
    per_range = keep.shape[1]
    block_len = length // per_range
    kept_rows = jnp.repeat(keep, block_len, axis=1)[:, :, None]
    masked_in = jnp.where(kept_rows == 1, signal, mask_token[None, None, :])
    source = jnp.where(group_index == 0, masked_in, signal)
    wide_in = lax.all_gather(source, "mdl", axis=2, tiled=True)
    full_width = wide_in.shape[2]
    flat_in = wide_in.reshape(-1, full_width)
    span = length + 2 * WIN
    weight_all = lax.all_gather(enc_weight, "seq", axis=2, tiled=True)[0]
    queries = jnp.dot(flat_in, weight_all[0], preferred_element_type=jnp.float32).astype(
        jnp.bfloat16
    )
    pair_made = jnp.einsum(
        "nd,cde->cne", flat_in, weight_all[1:], preferred_element_type=jnp.float32
    ).astype(jnp.bfloat16)
    own_pairs = pair_made.reshape(2, sequences, length, half_width)
    pair_rows = padded(own_pairs, (("seq", 2),), WIN)
    head_count = half_width // HD
    query_heads = queries.reshape(sequences, length, head_count, HD)
    key_heads = pair_rows[0].reshape(sequences, span, head_count, HD)
    value_heads = pair_rows[1].reshape(sequences, span, head_count, HD)
    query_pos = seq_index * length + jnp.arange(length)
    key_pos = seq_index * length - WIN + jnp.arange(span)
    total_len = length * shards
    in_window = (
        (jnp.abs(query_pos[:, None] - key_pos[None, :]) <= WIN)
        & (key_pos[None, :] >= 0)
        & (key_pos[None, :] < total_len)
    )
    scores = jnp.einsum(
        "sahd,sbhd->shab", query_heads, key_heads, preferred_element_type=jnp.float32
    ) * (1.0 / math.sqrt(HD))
    scores = jnp.where(in_window[None, None], scores, -jnp.inf)
    row_peak = jnp.max(scores, axis=-1, keepdims=True)
    exp_scores = jnp.exp(scores - row_peak)
    attention = (exp_scores / jnp.sum(exp_scores, axis=-1, keepdims=True)).astype(jnp.bfloat16)
    attended = jnp.einsum(
        "shab,sbhd->sahd", attention, value_heads, preferred_element_type=jnp.float32
    ).astype(jnp.bfloat16)
    latent = attended.reshape(sequences * per_range, block_len, half_width)
    blocks_here = latent.shape[0]
    capacity = max(2, 2 * blocks_here // shards)
    slot_count = shards * capacity
    shard_of = target_shard.reshape(-1)
    masked_flag = (keep.reshape(-1) == 0).astype(jnp.float32)
    order_ids = jnp.arange(blocks_here)
    earlier = (shard_of[:, None] == shard_of[None, :]) & (order_ids[:, None] < order_ids[None, :])
    slot_rank = jnp.sum(earlier.astype(jnp.int32), axis=0)
    slot_index = shard_of * capacity + slot_rank
    onehot = slot_index[None, :] == jnp.arange(slot_count)[:, None]
    divisor = float(block_len * full_width)
    halves = lax.all_to_all(latent[None], "grp", split_axis=1, concat_axis=0, tiled=True)
    half_count = blocks_here // 2
    first_block = group_index * half_count
    own_flags = lax.dynamic_slice_in_dim(masked_flag, first_block, half_count)
    losses = predict(halves[0], halves[1], own_flags, pred_weight, divisor)
    spread = lax.dynamic_update_slice_in_dim(
        jnp.zeros((blocks_here,), jnp.float32), losses, first_block, 0
    )
    slotted = jnp.sum(jnp.where(onehot, spread[None, :], 0.0), axis=1).reshape(shards, capacity)
    arrived = lax.all_to_all(slotted, "seq", split_axis=0, concat_axis=0, tiled=True)
    result = lax.psum_scatter(arrived, "grp", scatter_dimension=0, tiled=True)
    return result.reshape(1, -1)


def move(x, target):
    pairs = []
    for c in range(2):
        for s in range(8):
            for m in range(2):
                c2, z2, y2, m2 = target(c, s // 2, s % 2, m)
                pairs.append(((c * 8 + s) * 2 + m, (c2 * 8 + 2 * z2 + y2) * 2 + m2))
    return lax.ppermute(x, AXES, pairs)


def places():
    s = lax.axis_index("seq")
    return lax.axis_index("grp"), s // 2, lax.rem(s, 2), lax.axis_index("mdl")


def mask_kernel(
    signal_ref, token_ref, keep_ref, mine_ref, given_ref, mine_own_ref, given_own_ref
):
    core, _, y, _ = places()
    length = signal_ref.shape[1]
    blocks = keep_ref.shape[1]
    block_len = length // blocks
    row = lax.broadcasted_iota(jnp.int32, (length, blocks), 0)
    first = lax.broadcasted_iota(jnp.int32, (length, blocks), 1) * block_len
    covers = (row >= first) & (row < first + block_len)
    token = token_ref[...].astype(jnp.float32).reshape(1, -1)
    for other, own, chosen in ((mine_ref, mine_own_ref, y), (given_ref, given_own_ref, 1 - y)):
        kept = jnp.where(covers, keep_ref[pl.ds(chosen, 1), :], 0)
        kept = jnp.sum(kept, axis=1, keepdims=True)
        rows = signal_ref[chosen].astype(jnp.float32)
        other[...] = jnp.where(kept + 1 - core > 0, rows, token).astype(other.dtype)
        own[...] = jnp.where(kept + core > 0, rows, token).astype(own.dtype)


def slice_kernel(after_ref, weight_ref, pred_ref, near_ref, far_ref, early_ref, late_ref, sems):
    core, z, _, _ = places()
    wide = near_ref.shape[2]
    cut = early_ref.shape[0]
    t = lax.rem(z, 2)
    copies = []
    for target, chosen in ((near_ref, t), (far_ref, 1 - t)):
        lanes = pl.ds(pl.multiple_of(chosen * wide, 128), wide)
        copies.append((weight_ref.at[0, :, :, lanes], target))
    for index, target in enumerate((early_ref, late_ref)):
        first = pl.multiple_of((2 * core + index) * cut, 128)
        copies.append((pred_ref.at[pl.ds(first, cut), :], target))
    copies = [
        pltpu.make_async_copy(source, target, sems.at[index])
        for index, (source, target) in enumerate(copies)
    ]
    for copy in copies:
        copy.start()
    for copy in copies:
        copy.wait()


def encode_kernel(x_own, x_across, x_near, x_near_across, halo_ref, *refs):
    pieces = refs[:PIECES]
    out_ref, x_buf, w_buf, made_buf, sems = refs[PIECES:]
    core, z, y, m = places()
    half = x_own.shape[-1]
    rows = x_own.shape[1]
    depth = pieces[0].shape[1]
    wide = pieces[0].shape[2]
    own_rows = 4 * rows
    copies = []
    side = jnp.where(core == z // 2, 1 - lax.rem(z, 2), lax.rem(z, 2))
    for piece, near, across in (
        (x_own, 0, 0), (x_across, 0, 1), (x_near, 1, 0), (x_near_across, 1, 1)
    ):
        first = WIN + 2 * rows * (side if near == 0 else 1 - side)
        lane = half * (m if across == 0 else 1 - m)
        for part in range(2):
            copies.append((
                piece.at[part],
                x_buf.at[
                    pl.ds(pl.multiple_of(first + (y if part == 0 else 1 - y) * rows, 64), rows),
                    pl.ds(pl.multiple_of(lane, 128), half),
                ],
            ))
    halo_first = pl.multiple_of((1 - core) * (WIN + own_rows), 64)
    empty_first = pl.multiple_of(core * (WIN + own_rows), 64)
    for across in range(2):
        lane = half * (m if across == 0 else 1 - m)
        copies.append((
            halo_ref.at[across],
            x_buf.at[pl.ds(halo_first, WIN), pl.ds(pl.multiple_of(lane, 128), half)],
        ))
    t = lax.rem(z, 2)
    for index, piece in enumerate(pieces):
        crossed, other = (index // 2) % 2, index % 2
        low = core if (other == 0) == (index >= 4) else 1 - core
        pos_z = 2 * low + (t if index < 4 else 1 - t)
        pos = 2 * pos_z + (y if crossed == 0 else 1 - y)
        for kind in range(3):
            copies.append((
                piece.at[kind],
                w_buf.at[
                    pl.ds(pl.multiple_of(pos * depth, 64), depth),
                    kind * wide:(kind + 1) * wide,
                ],
            ))
    started = []
    for index, (source, target) in enumerate(copies):
        copy = pltpu.make_async_copy(source, target, sems.at[index])
        copy.start()
        started.append(copy)
    x_buf[pl.ds(empty_first, WIN), :] = jnp.zeros((WIN, 2 * half), x_buf.dtype)
    for copy in started:
        copy.wait()
    columns = w_buf.shape[1]
    for first in range(0, columns, 256):
        lanes = slice(first, min(first + 256, columns))
        made_buf[:, lanes] = jnp.dot(
            x_buf[...], w_buf[:, lanes], preferred_element_type=jnp.float32
        ).astype(made_buf.dtype)
    keys = rows + 2 * WIN
    a = lax.broadcasted_iota(jnp.int32, (rows, keys), 0)
    b = lax.broadcasted_iota(jnp.int32, (rows, keys), 1)
    band = (b >= a) & (b <= a + 2 * WIN)
    for j in range(4):
        admitted = band
        if j == 0:
            admitted = admitted & (b >= WIN * (1 - core))
        if j == 3:
            admitted = admitted & (b < keys - WIN * core)
        for h in range(wide // HD):
            query, key, value = (
                slice(kind * wide + h * HD, kind * wide + (h + 1) * HD) for kind in range(3)
            )
            scores = lax.dot_general(
                made_buf[WIN + j * rows:WIN + (j + 1) * rows, query],
                made_buf[j * rows:j * rows + keys, key],
                (((1,), (1,)), ((), ())),
                preferred_element_type=jnp.float32,
            ) * (1.0 / math.sqrt(HD))
            scores = jnp.where(admitted, scores, -jnp.inf)
            peak = jnp.max(scores, axis=-1, keepdims=True)
            exps = jnp.exp(scores - peak)
            share = 1.0 / jnp.sum(exps, axis=-1, keepdims=True)
            attention = (exps * share).astype(jnp.bfloat16)
            out_ref[j, :, h * HD:(h + 1) * HD] = jnp.dot(
                attention,
                made_buf[j * rows:j * rows + keys, value],
                preferred_element_type=jnp.float32,
            ).astype(out_ref.dtype)


def predict_kernel(slot_ref, lat_ref, own_ref, e0, e1, l0, l1, out_ref):
    core, _, _, m = places()
    wide = lat_ref.shape[2]
    lent = ((e0, e1), (l0, l1))
    total = None
    for side in range(2):
        predicted = None
        for t in range(2):
            for x in range(2):
                if side == 0:
                    source = lat_ref[2 * t + x]
                    weight = own_ref[(2 * x + t) * wide:(2 * x + t + 1) * wide, :]
                else:
                    source = lat_ref[2 * t + (core if x == 0 else 1 - core)]
                    weight = lent[t][x][...]
                term = jnp.dot(source, weight, preferred_element_type=jnp.float32)
                predicted = term if predicted is None else predicted + term
        for t in range(2):
            target = lat_ref[4 + 2 * t + (m if side == 0 else 1 - m)].astype(jnp.float32)
            residue = predicted[:, t * wide:(t + 1) * wide] - target
            for i in range(wide // 128):
                piece = residue[:, i * 128:(i + 1) * 128]
                total = piece * piece if total is None else total + piece * piece
    row_errors = jnp.sum(total, axis=1, keepdims=True)
    rows, slots = total.shape[0], out_ref.shape[2]
    chosen = slot_ref[...] == lax.broadcasted_iota(jnp.int32, (rows, slots), 1)
    routed = jnp.sum(jnp.where(chosen, row_errors, 0.0), axis=0, keepdims=True)
    for i in range(out_ref.shape[0]):
        out_ref[i] = routed


def local_lines(signal, mask_token, keep, target_shard, enc_weight, pred_weight):
    core = lax.axis_index("grp")
    s = lax.axis_index("seq")
    m = lax.axis_index("mdl")
    z, y = s // 2, s % 2
    sequences, length, half = signal.shape
    per_range = keep.shape[1]
    block_len = length // per_range
    depth = enc_weight.shape[2]
    wide = half // 2

    vmem = pl.BlockSpec(memory_space=pltpu.VMEM)
    anywhere = pl.BlockSpec(memory_space=pl.ANY)

    def to_near(c, z, y, m):
        return (1 - z // 2, z % 2 + 2 * c, y, m)

    def to_far(c, z, y, m):
        return (z // 2, 1 - z % 2 + 2 * c, y, m)

    def across_z(c, z, y, m):
        if z // 2 == c:
            return (c, (z + 2) % 4, y, m)
        return (1 - c, z + 1 - 2 * (z % 2), y, m)

    def across_zy(c, z, y, m):
        c, z, y, m = across_z(c, z, y, m)
        return (c, z, 1 - y, m)

    def flip_y(c, z, y, m):
        return (c, z, 1 - y, m)

    def flip_core(c, z, y, m):
        return (1 - c, z, y, m)

    def flip_x(c, z, y, m):
        return (c, z, y, 1 - m)

    def second_hop(c, z, y, m):
        if z // 2 == c:
            return (c, z, 1 - y, m)
        return (c, z + 1 - 2 * (z % 2), y, m)

    cut = half // 2
    mine, given, mine_own, given_own = pl.pallas_call(
        mask_kernel,
        out_shape=[jax.ShapeDtypeStruct((length, half), jnp.bfloat16)] * 4,
        in_specs=[vmem] * 3,
        out_specs=[vmem] * 4,
    )(signal, mask_token, keep)
    near, far, early, late = pl.pallas_call(
        slice_kernel,
        out_shape=[jax.ShapeDtypeStruct(shape, jnp.bfloat16) for shape in (
            (3, depth, wide), (3, depth, wide), (cut, half), (cut, half),
        )],
        in_specs=[anywhere] * 3,
        out_specs=[vmem] * 4,
        scratch_shapes=[pltpu.SemaphoreType.DMA((4,))],
    )(mine, enc_weight, pred_weight)
    first, second = move(mine, across_z), move(given, across_zy)
    small = jnp.stack([keep, target_shard])
    small, _ = lax.optimization_barrier((small, mine))
    routing = move(small, lambda c, z, y, m: ((2 * z + y) // 4, (2 * z + y) % 4, c, m))
    near, routing, first, second = lax.optimization_barrier((near, routing, first, second))
    x_own = jnp.stack([first, second])
    near_w = move(near, to_near)
    weight_early = move(early, flip_x)
    far, x_own = lax.optimization_barrier((far, x_own))
    far_w = move(far, to_far)
    home = core == z // 2
    sent = jnp.where(home, jnp.stack([mine_own, given_own]), x_own)
    come = move(sent, second_hop)
    kept_home = (jnp.arange(2) == 0)[:, None, None] & home
    x_near = jnp.where(kept_home, mine_own[None], come)
    x_across = move(x_own, flip_x)
    near_y_source, weight_early = lax.optimization_barrier((near_w, weight_early))
    near_y = move(near_y_source, flip_y)
    far_y_source, near_y = lax.optimization_barrier((far_w, near_y))
    far_y = move(far_y_source, flip_y)
    weight_early_c = move(weight_early, flip_core)
    x_near, x_across = lax.optimization_barrier((x_near, x_across))
    x_near_across = move(x_near, flip_x)
    late, _ = lax.optimization_barrier((late, x_near_across))
    weight_late = move(late, flip_x)
    weight_late_c = move(weight_late, flip_core)
    hidden = lax.dynamic_index_in_dim(routing[0], y, 0, keepdims=False) == 0
    shard_of = routing[1].reshape(-1)
    blocks = shard_of.shape[0]
    capacity = max(2, 2 * blocks // 8)
    order_ids = jnp.arange(blocks)
    earlier = (shard_of[:, None] == shard_of[None, :]) & (order_ids[:, None] < order_ids[None, :])
    slot = shard_of * capacity + jnp.sum(earlier.astype(jnp.int32), axis=0)
    slot = lax.dynamic_index_in_dim(slot.reshape(sequences, -1), y, 0, keepdims=False)
    slot = jnp.where(hidden, slot, -1)
    slot = lax.dynamic_slice_in_dim(slot, m * (per_range // 2), per_range // 2)
    slot = jnp.repeat(slot, block_len)[:, None]

    def edge(own, near):
        found = jnp.where(jnp.where(home, 1 - z % 2, z % 2) == 1 - core, own, near)
        part = jnp.where(core == 0, 1 - y, y)
        first = jnp.where(core == 0, length - WIN, 0)
        return lax.dynamic_slice(found, (part, first, 0), (1, WIN, half))[0]

    halo = move(jnp.stack([edge(x_own, x_near), edge(x_across, x_near_across)]), flip_core)
    far_yc_source, halo = lax.optimization_barrier((far_y, halo))
    pieces = [
        near_w, move(near_w, flip_core), near_y, move(near_y, flip_core),
        far_w, move(far_w, flip_core), far_y, move(far_yc_source, flip_core),
    ]
    span = 4 * length + 2 * WIN

    latent = pl.pallas_call(
        encode_kernel,
        out_shape=jax.ShapeDtypeStruct((4, length, wide), jnp.bfloat16),
        in_specs=[anywhere] * (5 + PIECES),
        out_specs=vmem,
        scratch_shapes=[
            pltpu.VMEM((span, 2 * half), jnp.bfloat16),
            pltpu.VMEM((2 * half, 3 * wide), jnp.bfloat16),
            pltpu.VMEM((span, 3 * wide), jnp.bfloat16),
            pltpu.SemaphoreType.DMA((10 + 3 * PIECES,)),
        ],
        compiler_params=pltpu.CompilerParams(vmem_limit_bytes=56 * 2**20),
    )(x_own, x_across, x_near, x_near_across, halo, *pieces)
    lines = [[4 * i + 2 * j + k for i in range(4) for k in range(2)] for j in range(2)]
    latents = lax.all_to_all(
        latent.reshape(8, length // 2, wide), ("seq", "mdl"),
        split_axis=0, concat_axis=0, tiled=True, axis_index_groups=lines,
    )
    routed = pl.pallas_call(
        predict_kernel,
        out_shape=jax.ShapeDtypeStruct((16, 1, 8 * capacity), jnp.float32),
        in_specs=[vmem] * 7,
        out_specs=vmem,
        compiler_params=pltpu.CompilerParams(vmem_limit_bytes=24 * 2**20),
    )(
        slot, latents, pred_weight,
        weight_early, weight_early_c, weight_late, weight_late_c,
    )
    arrived = lax.all_to_all(routed, ("seq", "mdl"), split_axis=0, concat_axis=0, tiled=True)
    mine = lax.dynamic_slice_in_dim(arrived[:, 0], capacity * s, capacity, 1)
    summed = jnp.sum(mine.reshape(4, 4, capacity), axis=1)
    return summed.reshape(1, -1) / float(block_len * 2 * half)


def solution(mesh):
    placed = (
        P(None, "seq", "mdl"),
        P("mdl"),
        P(None, "seq"),
        P(None, "seq"),
        P("grp", None, "seq", "mdl"),
        P(None, "mdl"),
    )
    plan = local_lines if mesh.shape["seq"] == 8 else local
    return jax.shard_map(
        plan, mesh=mesh, in_specs=placed, out_specs=P("seq", "grp"), check_vma=False
    )
```

```python
import functools
import math

import jax
import jax.numpy as jnp
from jax import lax
from jax.experimental import pallas as pl
from jax.experimental.pallas import tpu as pltpu
from jax.sharding import PartitionSpec as P

HD = 128
WIN = 64
AXES = ("grp", "seq", "mdl")
PIECES = 12


def padded(x, sides, width):
    for axis, dim in sides:
        count, length = (lax.axis_size(axis), x.shape[dim])
        up = [(i, (i + 1) % count) for i in range(count - 1)]
        down = [(j, i) for i, j in up]
        last = lax.slice_in_dim(x, length - width, length, axis=dim)
        leading = lax.slice_in_dim(x, 0, width, axis=dim)
        before = lax.ppermute(last, axis, up)
        after = lax.ppermute(leading, axis, down)
        x = jnp.concatenate([before, x, after], axis=dim)
    return x


def predict(context, target, live_flags, pred_weight, divisor):
    flat_rows = context.reshape(-1, context.shape[-1])
    wide_rows = lax.all_gather(flat_rows, "mdl", axis=1, tiled=True)
    predicted = jnp.dot(wide_rows, pred_weight, preferred_element_type=jnp.float32)
    residue = predicted - target.reshape(flat_rows.shape).astype(jnp.float32)
    partial_sums = jnp.sum((residue * residue).reshape(live_flags.shape[0], -1), axis=1)
    summed = lax.psum(partial_sums, "mdl")
    return summed / divisor * live_flags


def local(signal, mask_token, keep, target_shard, enc_weight, pred_weight):
    group_index = lax.axis_index("grp")
    seq_index = lax.axis_index("seq")
    shards = lax.axis_size("seq")
    sequences, length, half_width = signal.shape
    per_range = keep.shape[1]
    block_len = length // per_range
    kept_rows = jnp.repeat(keep, block_len, axis=1)[:, :, None]
    masked_in = jnp.where(kept_rows == 1, signal, mask_token[None, None, :])
    source = jnp.where(group_index == 0, masked_in, signal)
    wide_in = lax.all_gather(source, "mdl", axis=2, tiled=True)
    full_width = wide_in.shape[2]
    flat_in = wide_in.reshape(-1, full_width)
    span = length + 2 * WIN
    weight_all = lax.all_gather(enc_weight, "seq", axis=2, tiled=True)[0]
    queries = jnp.dot(flat_in, weight_all[0], preferred_element_type=jnp.float32).astype(
        jnp.bfloat16
    )
    pair_made = jnp.einsum(
        "nd,cde->cne", flat_in, weight_all[1:], preferred_element_type=jnp.float32
    ).astype(jnp.bfloat16)
    own_pairs = pair_made.reshape(2, sequences, length, half_width)
    pair_rows = padded(own_pairs, (("seq", 2),), WIN)
    head_count = half_width // HD
    query_heads = queries.reshape(sequences, length, head_count, HD)
    key_heads = pair_rows[0].reshape(sequences, span, head_count, HD)
    value_heads = pair_rows[1].reshape(sequences, span, head_count, HD)
    query_pos = seq_index * length + jnp.arange(length)
    key_pos = seq_index * length - WIN + jnp.arange(span)
    total_len = length * shards
    in_window = (
        (jnp.abs(query_pos[:, None] - key_pos[None, :]) <= WIN)
        & (key_pos[None, :] >= 0)
        & (key_pos[None, :] < total_len)
    )
    scores = jnp.einsum(
        "sahd,sbhd->shab", query_heads, key_heads, preferred_element_type=jnp.float32
    ) * (1.0 / math.sqrt(HD))
    scores = jnp.where(in_window[None, None], scores, -jnp.inf)
    row_peak = jnp.max(scores, axis=-1, keepdims=True)
    exp_scores = jnp.exp(scores - row_peak)
    attention = (exp_scores / jnp.sum(exp_scores, axis=-1, keepdims=True)).astype(jnp.bfloat16)
    attended = jnp.einsum(
        "shab,sbhd->sahd", attention, value_heads, preferred_element_type=jnp.float32
    ).astype(jnp.bfloat16)
    latent = attended.reshape(sequences * per_range, block_len, half_width)
    blocks_here = latent.shape[0]
    capacity = max(2, 2 * blocks_here // shards)
    slot_count = shards * capacity
    shard_of = target_shard.reshape(-1)
    masked_flag = (keep.reshape(-1) == 0).astype(jnp.float32)
    order_ids = jnp.arange(blocks_here)
    earlier = (shard_of[:, None] == shard_of[None, :]) & (order_ids[:, None] < order_ids[None, :])
    slot_rank = jnp.sum(earlier.astype(jnp.int32), axis=0)
    slot_index = shard_of * capacity + slot_rank
    onehot = slot_index[None, :] == jnp.arange(slot_count)[:, None]
    divisor = float(block_len * full_width)
    halves = lax.all_to_all(latent[None], "grp", split_axis=1, concat_axis=0, tiled=True)
    half_count = blocks_here // 2
    first_block = group_index * half_count
    own_flags = lax.dynamic_slice_in_dim(masked_flag, first_block, half_count)
    losses = predict(halves[0], halves[1], own_flags, pred_weight, divisor)
    spread = lax.dynamic_update_slice_in_dim(
        jnp.zeros((blocks_here,), jnp.float32), losses, first_block, 0
    )
    slotted = jnp.sum(jnp.where(onehot, spread[None, :], 0.0), axis=1).reshape(shards, capacity)
    arrived = lax.all_to_all(slotted, "seq", split_axis=0, concat_axis=0, tiled=True)
    result = lax.psum_scatter(arrived, "grp", scatter_dimension=0, tiled=True)
    return result.reshape(1, -1)


def move(x, target):
    pairs = []
    for c in range(2):
        for s in range(8):
            for m in range(2):
                c2, z2, y2, m2 = target(c, s // 2, s % 2, m)
                pairs.append(((c * 8 + s) * 2 + m, (c2 * 8 + 2 * z2 + y2) * 2 + m2))
    return lax.ppermute(x, AXES, pairs)


def places():
    s = lax.axis_index("seq")
    return lax.axis_index("grp"), s // 2, lax.rem(s, 2), lax.axis_index("mdl")


def mask_kernel(
    signal_ref, token_ref, keep_ref, mine_ref, given_ref, mine_own_ref, given_own_ref
):
    core, _, y, _ = places()
    length = signal_ref.shape[1]
    blocks = keep_ref.shape[1]
    block_len = length // blocks
    row = lax.broadcasted_iota(jnp.int32, (length, blocks), 0)
    first = lax.broadcasted_iota(jnp.int32, (length, blocks), 1) * block_len
    covers = (row >= first) & (row < first + block_len)
    token = token_ref[...].astype(jnp.float32).reshape(1, -1)
    for other, own, chosen in ((mine_ref, mine_own_ref, y), (given_ref, given_own_ref, 1 - y)):
        kept = jnp.where(covers, keep_ref[pl.ds(chosen, 1), :], 0)
        kept = jnp.sum(kept, axis=1, keepdims=True)
        rows = signal_ref[chosen].astype(jnp.float32)
        other[...] = jnp.where(kept + 1 - core > 0, rows, token).astype(other.dtype)
        own[...] = jnp.where(kept + core > 0, rows, token).astype(own.dtype)


def slice_kernel(
    after_ref, weight_ref, pred_ref, near_ref, far_ref, rest_ref, early_ref, late_ref, sems
):
    core, z, _, _ = places()
    wide = near_ref.shape[2]
    cut = early_ref.shape[0]
    t = lax.rem(z, 2)
    copies = []
    cut_rows = far_ref.shape[1]
    for target, chosen, skipped in ((near_ref, t, 0), (far_ref, 1 - t, 0), (rest_ref, 1 - t, cut_rows)):
        lanes = pl.ds(pl.multiple_of(chosen * wide, 128), wide)
        rows = pl.ds(skipped, target.shape[1])
        copies.append((weight_ref.at[0, :, rows, lanes], target))
    for index, target in enumerate((early_ref, late_ref)):
        first = pl.multiple_of((2 * core + index) * cut, 128)
        copies.append((pred_ref.at[pl.ds(first, cut), :], target))
    copies = [
        pltpu.make_async_copy(source, target, sems.at[index])
        for index, (source, target) in enumerate(copies)
    ]
    for copy in copies:
        copy.start()
    for copy in copies:
        copy.wait()


def encode_kernel(x_own, x_across, x_near, x_near_across, halo_ref, *refs):
    pieces = refs[:PIECES]
    out_ref, x_buf, w_buf, q_buf, k_buf, v_buf, sems = refs[PIECES:]
    core, z, y, m = places()
    half = x_own.shape[-1]
    rows = x_own.shape[1]
    depth = pieces[0].shape[1]
    wide = pieces[0].shape[2]
    own_rows = 4 * rows
    copies = []
    side = jnp.where(core == z // 2, 1 - lax.rem(z, 2), lax.rem(z, 2))
    for piece, near, across in (
        (x_own, 0, 0), (x_across, 0, 1), (x_near, 1, 0), (x_near_across, 1, 1)
    ):
        first = WIN + 2 * rows * (side if near == 0 else 1 - side)
        lane = half * (m if across == 0 else 1 - m)
        for part in range(2):
            copies.append((
                piece.at[part],
                x_buf.at[
                    pl.ds(pl.multiple_of(first + (y if part == 0 else 1 - y) * rows, 64), rows),
                    pl.ds(pl.multiple_of(lane, 128), half),
                ],
            ))
    halo_first = pl.multiple_of((1 - core) * (WIN + own_rows), 64)
    empty_first = pl.multiple_of(core * (WIN + own_rows), 64)
    for across in range(2):
        lane = half * (m if across == 0 else 1 - m)
        copies.append((
            halo_ref.at[across],
            x_buf.at[pl.ds(halo_first, WIN), pl.ds(pl.multiple_of(lane, 128), half)],
        ))
    t = lax.rem(z, 2)
    for index, piece in enumerate(pieces):
        crossed, other = (index // 2) % 2, index % 2
        low = core if (other == 0) == (index >= 4) else 1 - core
        pos_z = 2 * low + (t if index < 4 else 1 - t)
        pos = 2 * pos_z + (y if crossed == 0 else 1 - y)
        count = piece.shape[1]
        first = pos * depth + (count if index >= 8 else 0)
        copies.append((piece, w_buf.at[:, pl.ds(pl.multiple_of(first, 32), count), :]))
    started = []
    for index, (source, target) in enumerate(copies):
        copy = pltpu.make_async_copy(source, target, sems.at[index])
        copy.start()
        started.append(copy)
    x_buf[pl.ds(empty_first, WIN), :] = jnp.zeros((WIN, 2 * half), x_buf.dtype)
    for copy in started:
        copy.wait()
    x = x_buf[...]
    q_buf[...] = jnp.dot(
        x[WIN:WIN + own_rows], w_buf[0], preferred_element_type=jnp.float32
    ).astype(q_buf.dtype)
    k_buf[...] = jnp.dot(x, w_buf[1], preferred_element_type=jnp.float32).astype(k_buf.dtype)
    v_buf[...] = jnp.dot(x, w_buf[2], preferred_element_type=jnp.float32).astype(v_buf.dtype)
    keys = rows + 2 * WIN
    a = lax.broadcasted_iota(jnp.int32, (rows, keys), 0)
    b = lax.broadcasted_iota(jnp.int32, (rows, keys), 1)
    band = (b >= a) & (b <= a + 2 * WIN)
    for j in range(4):
        admitted = band
        if j == 0:
            admitted = admitted & (b >= WIN * (1 - core))
        if j == 3:
            admitted = admitted & (b < keys - WIN * core)
        for h in range(wide // HD):
            lanes = slice(h * HD, (h + 1) * HD)
            scores = lax.dot_general(
                q_buf[j * rows:(j + 1) * rows, lanes],
                k_buf[j * rows:j * rows + keys, lanes],
                (((1,), (1,)), ((), ())),
                preferred_element_type=jnp.float32,
            ) * (1.0 / math.sqrt(HD))
            scores = jnp.where(admitted, scores, -jnp.inf)
            peak = jnp.max(scores, axis=-1, keepdims=True)
            exps = jnp.exp(scores - peak)
            attention = (exps / jnp.sum(exps, axis=-1, keepdims=True)).astype(jnp.bfloat16)
            out_ref[j, :, lanes] = jnp.dot(
                attention,
                v_buf[j * rows:j * rows + keys, lanes],
                preferred_element_type=jnp.float32,
            ).astype(out_ref.dtype)


def predict_kernel(slot_ref, lat_ref, own_ref, e0, e1, l0, l1, out_ref):
    core, _, _, m = places()
    wide = lat_ref.shape[2]
    lent = ((e0, e1), (l0, l1))
    total = None
    for side in range(2):
        predicted = None
        for t in range(2):
            for x in range(2):
                if side == 0:
                    source = lat_ref[2 * t + x]
                    weight = own_ref[(2 * x + t) * wide:(2 * x + t + 1) * wide, :]
                else:
                    source = lat_ref[2 * t + (core if x == 0 else 1 - core)]
                    weight = lent[t][x][...]
                term = jnp.dot(source, weight, preferred_element_type=jnp.float32)
                predicted = term if predicted is None else predicted + term
        for t in range(2):
            target = lat_ref[4 + 2 * t + (m if side == 0 else 1 - m)].astype(jnp.float32)
            residue = predicted[:, t * wide:(t + 1) * wide] - target
            for i in range(wide // 128):
                piece = residue[:, i * 128:(i + 1) * 128]
                total = piece * piece if total is None else total + piece * piece
    row_errors = jnp.sum(total, axis=1, keepdims=True)
    rows, slots = total.shape[0], out_ref.shape[2]
    chosen = slot_ref[...] == lax.broadcasted_iota(jnp.int32, (rows, slots), 1)
    routed = jnp.sum(jnp.where(chosen, row_errors, 0.0), axis=0, keepdims=True)
    for i in range(out_ref.shape[0]):
        out_ref[i] = routed


def local_lines(signal, mask_token, keep, target_shard, enc_weight, pred_weight):
    core = lax.axis_index("grp")
    s = lax.axis_index("seq")
    m = lax.axis_index("mdl")
    z, y = s // 2, s % 2
    sequences, length, half = signal.shape
    per_range = keep.shape[1]
    block_len = length // per_range
    depth = enc_weight.shape[2]
    wide = half // 2

    vmem = pl.BlockSpec(memory_space=pltpu.VMEM)
    anywhere = pl.BlockSpec(memory_space=pl.ANY)

    def to_near(c, z, y, m):
        return (1 - z // 2, z % 2 + 2 * c, y, m)

    def to_far(c, z, y, m):
        return (z // 2, 1 - z % 2 + 2 * c, y, m)

    def across_z(c, z, y, m):
        if z // 2 == c:
            return (c, (z + 2) % 4, y, m)
        return (1 - c, z + 1 - 2 * (z % 2), y, m)

    def across_zy(c, z, y, m):
        c, z, y, m = across_z(c, z, y, m)
        return (c, z, 1 - y, m)

    def flip_y(c, z, y, m):
        return (c, z, 1 - y, m)

    def flip_core(c, z, y, m):
        return (1 - c, z, y, m)

    def flip_x(c, z, y, m):
        return (c, z, y, 1 - m)

    def second_hop(c, z, y, m):
        if z // 2 == c:
            return (c, z, 1 - y, m)
        return (c, z + 1 - 2 * (z % 2), y, m)

    cut = half // 2
    mine, given, mine_own, given_own = pl.pallas_call(
        mask_kernel,
        out_shape=[jax.ShapeDtypeStruct((length, half), jnp.bfloat16)] * 4,
        in_specs=[vmem] * 3,
        out_specs=[vmem] * 4,
    )(signal, mask_token, keep)
    near, far, rest, early, late = pl.pallas_call(
        slice_kernel,
        out_shape=[jax.ShapeDtypeStruct(shape, jnp.bfloat16) for shape in (
            (3, depth, wide), (3, depth // 2, wide), (3, depth // 2, wide),
            (cut, half), (cut, half),
        )],
        in_specs=[anywhere] * 3,
        out_specs=[vmem] * 5,
        scratch_shapes=[pltpu.SemaphoreType.DMA((5,))],
    )(mine, enc_weight, pred_weight)
    first, second = move(mine, across_z), move(given, across_zy)
    small = jnp.stack([keep, target_shard])
    small, _ = lax.optimization_barrier((small, mine))
    routing = move(small, lambda c, z, y, m: ((2 * z + y) // 4, (2 * z + y) % 4, c, m))
    near, routing = lax.optimization_barrier((near, routing))
    x_own = jnp.stack([first, second])
    near_w = move(near, to_near)
    weight_early = move(early, flip_x)
    far, x_own = lax.optimization_barrier((far, x_own))
    far_w = move(far, to_far)
    home = core == z // 2
    sent = jnp.where(home, jnp.stack([mine_own, given_own]), x_own)
    come = move(sent, second_hop)
    kept_home = (jnp.arange(2) == 0)[:, None, None] & home
    x_near = jnp.where(kept_home, mine_own[None], come)
    x_across = move(x_own, flip_x)
    x_near, x_across = lax.optimization_barrier((x_near, x_across))
    x_near_across = move(x_near, flip_x)
    near_y = move(near_w, flip_y)
    rest, far_w, near_w = lax.optimization_barrier((rest, far_w, near_w))
    rest_w = move(rest, to_far)
    far_y = move(far_w, flip_y)
    rest_y_source, near_y, weight_early = lax.optimization_barrier((rest_w, near_y, weight_early))
    rest_y = move(rest_y_source, flip_y)
    weight_early_c = move(weight_early, flip_core)
    late, _ = lax.optimization_barrier((late, x_near_across))
    weight_late = move(late, flip_x)
    weight_late_c = move(weight_late, flip_core)
    hidden = lax.dynamic_index_in_dim(routing[0], y, 0, keepdims=False) == 0
    shard_of = routing[1].reshape(-1)
    blocks = shard_of.shape[0]
    capacity = max(2, 2 * blocks // 8)
    order_ids = jnp.arange(blocks)
    earlier = (shard_of[:, None] == shard_of[None, :]) & (order_ids[:, None] < order_ids[None, :])
    slot = shard_of * capacity + jnp.sum(earlier.astype(jnp.int32), axis=0)
    slot = lax.dynamic_index_in_dim(slot.reshape(sequences, -1), y, 0, keepdims=False)
    slot = jnp.where(hidden, slot, -1)
    slot = lax.dynamic_slice_in_dim(slot, m * (per_range // 2), per_range // 2)
    slot = jnp.repeat(slot, block_len)[:, None]

    def edge(own, near):
        found = jnp.where(jnp.where(home, 1 - z % 2, z % 2) == 1 - core, own, near)
        part = jnp.where(core == 0, 1 - y, y)
        first = jnp.where(core == 0, length - WIN, 0)
        return lax.dynamic_slice(found, (part, first, 0), (1, WIN, half))[0]

    halo = move(jnp.stack([edge(x_own, x_near), edge(x_across, x_near_across)]), flip_core)
    rest_yc_source, halo = lax.optimization_barrier((rest_y, halo))
    pieces = []
    for piece in (near_w, near_y, far_w, far_y, rest_w):
        pieces += [piece, move(piece, flip_core)]
    pieces += [rest_y, move(rest_yc_source, flip_core)]
    span = 4 * length + 2 * WIN

    latent = pl.pallas_call(
        encode_kernel,
        out_shape=jax.ShapeDtypeStruct((4, length, wide), jnp.bfloat16),
        in_specs=[anywhere] * (5 + PIECES),
        out_specs=vmem,
        scratch_shapes=[
            pltpu.VMEM((span, 2 * half), jnp.bfloat16),
            pltpu.VMEM((3, 2 * half, wide), jnp.bfloat16),
            pltpu.VMEM((4 * length, wide), jnp.bfloat16),
            pltpu.VMEM((span, wide), jnp.bfloat16),
            pltpu.VMEM((span, wide), jnp.bfloat16),
            pltpu.SemaphoreType.DMA((10 + PIECES,)),
        ],
        compiler_params=pltpu.CompilerParams(vmem_limit_bytes=60 * 2**20),
    )(x_own, x_across, x_near, x_near_across, halo, *pieces)
    lines = [[4 * i + 2 * j + k for i in range(4) for k in range(2)] for j in range(2)]
    latents = lax.all_to_all(
        latent.reshape(8, length // 2, wide), ("seq", "mdl"),
        split_axis=0, concat_axis=0, tiled=True, axis_index_groups=lines,
    )
    routed = pl.pallas_call(
        predict_kernel,
        out_shape=jax.ShapeDtypeStruct((16, 1, 8 * capacity), jnp.float32),
        in_specs=[vmem] * 7,
        out_specs=vmem,
        compiler_params=pltpu.CompilerParams(vmem_limit_bytes=24 * 2**20),
    )(
        slot, latents, pred_weight,
        weight_early, weight_early_c, weight_late, weight_late_c,
    )
    arrived = lax.all_to_all(routed, ("seq", "mdl"), split_axis=0, concat_axis=0, tiled=True)
    mine = lax.dynamic_slice_in_dim(arrived[:, 0], capacity * s, capacity, 1)
    summed = jnp.sum(mine.reshape(4, 4, capacity), axis=1)
    return summed.reshape(1, -1) / float(block_len * 2 * half)


def solution(mesh):
    placed = (
        P(None, "seq", "mdl"),
        P("mdl"),
        P(None, "seq"),
        P(None, "seq"),
        P("grp", None, "seq", "mdl"),
        P(None, "mdl"),
    )
    plan = local_lines if mesh.shape["seq"] == 8 else local
    return jax.shard_map(
        plan, mesh=mesh, in_specs=placed, out_specs=P("seq", "grp"), check_vma=False
    )
```

```python
import functools
import math

import jax
import jax.numpy as jnp
from jax import lax
from jax.experimental import pallas as pl
from jax.experimental.pallas import tpu as pltpu
from jax.sharding import PartitionSpec as P

HD = 128
WIN = 64
AXES = ("grp", "seq", "mdl")
PIECES = 12


def padded(x, sides, width):
    for axis, dim in sides:
        count, length = (lax.axis_size(axis), x.shape[dim])
        up = [(i, (i + 1) % count) for i in range(count - 1)]
        down = [(j, i) for i, j in up]
        last = lax.slice_in_dim(x, length - width, length, axis=dim)
        leading = lax.slice_in_dim(x, 0, width, axis=dim)
        before = lax.ppermute(last, axis, up)
        after = lax.ppermute(leading, axis, down)
        x = jnp.concatenate([before, x, after], axis=dim)
    return x


def predict(context, target, live_flags, pred_weight, divisor):
    flat_rows = context.reshape(-1, context.shape[-1])
    wide_rows = lax.all_gather(flat_rows, "mdl", axis=1, tiled=True)
    predicted = jnp.dot(wide_rows, pred_weight, preferred_element_type=jnp.float32)
    residue = predicted - target.reshape(flat_rows.shape).astype(jnp.float32)
    partial_sums = jnp.sum((residue * residue).reshape(live_flags.shape[0], -1), axis=1)
    summed = lax.psum(partial_sums, "mdl")
    return summed / divisor * live_flags


def local(signal, mask_token, keep, target_shard, enc_weight, pred_weight):
    group_index = lax.axis_index("grp")
    seq_index = lax.axis_index("seq")
    shards = lax.axis_size("seq")
    sequences, length, half_width = signal.shape
    per_range = keep.shape[1]
    block_len = length // per_range
    kept_rows = jnp.repeat(keep, block_len, axis=1)[:, :, None]
    masked_in = jnp.where(kept_rows == 1, signal, mask_token[None, None, :])
    source = jnp.where(group_index == 0, masked_in, signal)
    wide_in = lax.all_gather(source, "mdl", axis=2, tiled=True)
    full_width = wide_in.shape[2]
    flat_in = wide_in.reshape(-1, full_width)
    span = length + 2 * WIN
    weight_all = lax.all_gather(enc_weight, "seq", axis=2, tiled=True)[0]
    queries = jnp.dot(flat_in, weight_all[0], preferred_element_type=jnp.float32).astype(
        jnp.bfloat16
    )
    pair_made = jnp.einsum(
        "nd,cde->cne", flat_in, weight_all[1:], preferred_element_type=jnp.float32
    ).astype(jnp.bfloat16)
    own_pairs = pair_made.reshape(2, sequences, length, half_width)
    pair_rows = padded(own_pairs, (("seq", 2),), WIN)
    head_count = half_width // HD
    query_heads = queries.reshape(sequences, length, head_count, HD)
    key_heads = pair_rows[0].reshape(sequences, span, head_count, HD)
    value_heads = pair_rows[1].reshape(sequences, span, head_count, HD)
    query_pos = seq_index * length + jnp.arange(length)
    key_pos = seq_index * length - WIN + jnp.arange(span)
    total_len = length * shards
    in_window = (
        (jnp.abs(query_pos[:, None] - key_pos[None, :]) <= WIN)
        & (key_pos[None, :] >= 0)
        & (key_pos[None, :] < total_len)
    )
    scores = jnp.einsum(
        "sahd,sbhd->shab", query_heads, key_heads, preferred_element_type=jnp.float32
    ) * (1.0 / math.sqrt(HD))
    scores = jnp.where(in_window[None, None], scores, -jnp.inf)
    row_peak = jnp.max(scores, axis=-1, keepdims=True)
    exp_scores = jnp.exp(scores - row_peak)
    attention = (exp_scores / jnp.sum(exp_scores, axis=-1, keepdims=True)).astype(jnp.bfloat16)
    attended = jnp.einsum(
        "shab,sbhd->sahd", attention, value_heads, preferred_element_type=jnp.float32
    ).astype(jnp.bfloat16)
    latent = attended.reshape(sequences * per_range, block_len, half_width)
    blocks_here = latent.shape[0]
    capacity = max(2, 2 * blocks_here // shards)
    slot_count = shards * capacity
    shard_of = target_shard.reshape(-1)
    masked_flag = (keep.reshape(-1) == 0).astype(jnp.float32)
    order_ids = jnp.arange(blocks_here)
    earlier = (shard_of[:, None] == shard_of[None, :]) & (order_ids[:, None] < order_ids[None, :])
    slot_rank = jnp.sum(earlier.astype(jnp.int32), axis=0)
    slot_index = shard_of * capacity + slot_rank
    onehot = slot_index[None, :] == jnp.arange(slot_count)[:, None]
    divisor = float(block_len * full_width)
    halves = lax.all_to_all(latent[None], "grp", split_axis=1, concat_axis=0, tiled=True)
    half_count = blocks_here // 2
    first_block = group_index * half_count
    own_flags = lax.dynamic_slice_in_dim(masked_flag, first_block, half_count)
    losses = predict(halves[0], halves[1], own_flags, pred_weight, divisor)
    spread = lax.dynamic_update_slice_in_dim(
        jnp.zeros((blocks_here,), jnp.float32), losses, first_block, 0
    )
    slotted = jnp.sum(jnp.where(onehot, spread[None, :], 0.0), axis=1).reshape(shards, capacity)
    arrived = lax.all_to_all(slotted, "seq", split_axis=0, concat_axis=0, tiled=True)
    result = lax.psum_scatter(arrived, "grp", scatter_dimension=0, tiled=True)
    return result.reshape(1, -1)


def move(x, target):
    pairs = []
    for c in range(2):
        for s in range(8):
            for m in range(2):
                c2, z2, y2, m2 = target(c, s // 2, s % 2, m)
                pairs.append(((c * 8 + s) * 2 + m, (c2 * 8 + 2 * z2 + y2) * 2 + m2))
    return lax.ppermute(x, AXES, pairs)


def places():
    s = lax.axis_index("seq")
    return lax.axis_index("grp"), s // 2, lax.rem(s, 2), lax.axis_index("mdl")


def mask_kernel(
    signal_ref, token_ref, keep_ref, mine_ref, given_ref, mine_own_ref, given_own_ref
):
    core, _, y, _ = places()
    length = signal_ref.shape[1]
    blocks = keep_ref.shape[1]
    block_len = length // blocks
    row = lax.broadcasted_iota(jnp.int32, (length, blocks), 0)
    first = lax.broadcasted_iota(jnp.int32, (length, blocks), 1) * block_len
    covers = (row >= first) & (row < first + block_len)
    token = token_ref[...].astype(jnp.float32).reshape(1, -1)
    for other, own, chosen in ((mine_ref, mine_own_ref, y), (given_ref, given_own_ref, 1 - y)):
        kept = jnp.where(covers, keep_ref[pl.ds(chosen, 1), :], 0)
        kept = jnp.sum(kept, axis=1, keepdims=True)
        rows = signal_ref[chosen].astype(jnp.float32)
        other[...] = jnp.where(kept + 1 - core > 0, rows, token).astype(other.dtype)
        own[...] = jnp.where(kept + core > 0, rows, token).astype(own.dtype)


def slice_kernel(
    after_ref, weight_ref, pred_ref, near_ref, far_ref, rest_ref, early_ref, late_ref, sems
):
    core, z, _, _ = places()
    wide = near_ref.shape[2]
    cut = early_ref.shape[0]
    t = lax.rem(z, 2)
    copies = []
    cut_rows = far_ref.shape[1]
    for target, chosen, skipped in ((near_ref, t, 0), (far_ref, 1 - t, 0), (rest_ref, 1 - t, cut_rows)):
        lanes = pl.ds(pl.multiple_of(chosen * wide, 128), wide)
        rows = pl.ds(skipped, target.shape[1])
        copies.append((weight_ref.at[0, :, rows, lanes], target))
    for index, target in enumerate((early_ref, late_ref)):
        first = pl.multiple_of((2 * core + index) * cut, 128)
        copies.append((pred_ref.at[pl.ds(first, cut), :], target))
    copies = [
        pltpu.make_async_copy(source, target, sems.at[index])
        for index, (source, target) in enumerate(copies)
    ]
    for copy in copies:
        copy.start()
    for copy in copies:
        copy.wait()


def encode_kernel(x_own, x_across, x_near, x_near_across, halo_ref, *refs):
    pieces = refs[:PIECES]
    out_ref, x_buf, w_buf, q_buf, k_buf, v_buf, sems = refs[PIECES:]
    core, z, y, m = places()
    half = x_own.shape[-1]
    rows = x_own.shape[1]
    depth = pieces[0].shape[1]
    wide = pieces[0].shape[2]
    own_rows = 4 * rows
    copies = []
    side = jnp.where(core == z // 2, 1 - lax.rem(z, 2), lax.rem(z, 2))
    for piece, near, across in (
        (x_own, 0, 0), (x_across, 0, 1), (x_near, 1, 0), (x_near_across, 1, 1)
    ):
        first = WIN + 2 * rows * (side if near == 0 else 1 - side)
        lane = half * (m if across == 0 else 1 - m)
        for part in range(2):
            copies.append((
                piece.at[part],
                x_buf.at[
                    pl.ds(pl.multiple_of(first + (y if part == 0 else 1 - y) * rows, 64), rows),
                    pl.ds(pl.multiple_of(lane, 128), half),
                ],
            ))
    halo_first = pl.multiple_of((1 - core) * (WIN + own_rows), 64)
    empty_first = pl.multiple_of(core * (WIN + own_rows), 64)
    for across in range(2):
        lane = half * (m if across == 0 else 1 - m)
        copies.append((
            halo_ref.at[across],
            x_buf.at[pl.ds(halo_first, WIN), pl.ds(pl.multiple_of(lane, 128), half)],
        ))
    t = lax.rem(z, 2)
    for index, piece in enumerate(pieces):
        crossed, other = (index // 2) % 2, index % 2
        low = core if (other == 0) == (index >= 4) else 1 - core
        pos_z = 2 * low + (t if index < 4 else 1 - t)
        pos = 2 * pos_z + (y if crossed == 0 else 1 - y)
        count = piece.shape[1]
        first = pos * depth + (count if index >= 8 else 0)
        copies.append((piece, w_buf.at[:, pl.ds(pl.multiple_of(first, 32), count), :]))
    started = []
    for index, (source, target) in enumerate(copies):
        copy = pltpu.make_async_copy(source, target, sems.at[index])
        copy.start()
        started.append(copy)
    x_buf[pl.ds(empty_first, WIN), :] = jnp.zeros((WIN, 2 * half), x_buf.dtype)
    for copy in started:
        copy.wait()
    x = x_buf[...]
    q_buf[...] = jnp.dot(
        x[WIN:WIN + own_rows], w_buf[0], preferred_element_type=jnp.float32
    ).astype(q_buf.dtype)
    k_buf[...] = jnp.dot(x, w_buf[1], preferred_element_type=jnp.float32).astype(k_buf.dtype)
    v_buf[...] = jnp.dot(x, w_buf[2], preferred_element_type=jnp.float32).astype(v_buf.dtype)
    keys = rows + 2 * WIN
    a = lax.broadcasted_iota(jnp.int32, (rows, keys), 0)
    b = lax.broadcasted_iota(jnp.int32, (rows, keys), 1)
    band = (b >= a) & (b <= a + 2 * WIN)
    for j in range(4):
        admitted = band
        if j == 0:
            admitted = admitted & (b >= WIN * (1 - core))
        if j == 3:
            admitted = admitted & (b < keys - WIN * core)
        for h in range(wide // HD):
            lanes = slice(h * HD, (h + 1) * HD)
            scores = lax.dot_general(
                q_buf[j * rows:(j + 1) * rows, lanes],
                k_buf[j * rows:j * rows + keys, lanes],
                (((1,), (1,)), ((), ())),
                preferred_element_type=jnp.float32,
            ) * (1.0 / math.sqrt(HD))
            scores = jnp.where(admitted, scores, -jnp.inf)
            peak = jnp.max(scores, axis=-1, keepdims=True)
            exps = jnp.exp(scores - peak)
            attention = (exps / jnp.sum(exps, axis=-1, keepdims=True)).astype(jnp.bfloat16)
            out_ref[j, :, lanes] = jnp.dot(
                attention,
                v_buf[j * rows:j * rows + keys, lanes],
                preferred_element_type=jnp.float32,
            ).astype(out_ref.dtype)


def predict_kernel(slot_ref, lat_ref, own_ref, e0, e1, l0, l1, out_ref):
    core, _, _, m = places()
    wide = lat_ref.shape[2]
    lent = ((e0, e1), (l0, l1))
    total = None
    for side in range(2):
        predicted = None
        for t in range(2):
            for x in range(2):
                if side == 0:
                    source = lat_ref[2 * t + x]
                    weight = own_ref[(2 * x + t) * wide:(2 * x + t + 1) * wide, :]
                else:
                    source = lat_ref[2 * t + (core if x == 0 else 1 - core)]
                    weight = lent[t][x][...]
                term = jnp.dot(source, weight, preferred_element_type=jnp.float32)
                predicted = term if predicted is None else predicted + term
        for t in range(2):
            target = lat_ref[4 + 2 * t + (m if side == 0 else 1 - m)].astype(jnp.float32)
            residue = predicted[:, t * wide:(t + 1) * wide] - target
            for i in range(wide // 128):
                piece = residue[:, i * 128:(i + 1) * 128]
                total = piece * piece if total is None else total + piece * piece
    row_errors = jnp.sum(total, axis=1, keepdims=True)
    rows, slots = total.shape[0], out_ref.shape[2]
    chosen = slot_ref[...] == lax.broadcasted_iota(jnp.int32, (rows, slots), 1)
    routed = jnp.sum(jnp.where(chosen, row_errors, 0.0), axis=0, keepdims=True)
    for i in range(out_ref.shape[0]):
        out_ref[i] = routed


def local_lines(signal, mask_token, keep, target_shard, enc_weight, pred_weight):
    core = lax.axis_index("grp")
    s = lax.axis_index("seq")
    m = lax.axis_index("mdl")
    z, y = s // 2, s % 2
    sequences, length, half = signal.shape
    per_range = keep.shape[1]
    block_len = length // per_range
    depth = enc_weight.shape[2]
    wide = half // 2

    vmem = pl.BlockSpec(memory_space=pltpu.VMEM)
    anywhere = pl.BlockSpec(memory_space=pl.ANY)

    def to_near(c, z, y, m):
        return (1 - z // 2, z % 2 + 2 * c, y, m)

    def to_far(c, z, y, m):
        return (z // 2, 1 - z % 2 + 2 * c, y, m)

    def across_z(c, z, y, m):
        if z // 2 == c:
            return (c, (z + 2) % 4, y, m)
        return (1 - c, z + 1 - 2 * (z % 2), y, m)

    def across_zy(c, z, y, m):
        c, z, y, m = across_z(c, z, y, m)
        return (c, z, 1 - y, m)

    def flip_y(c, z, y, m):
        return (c, z, 1 - y, m)

    def flip_core(c, z, y, m):
        return (1 - c, z, y, m)

    def flip_x(c, z, y, m):
        return (c, z, y, 1 - m)

    def second_hop(c, z, y, m):
        if z // 2 == c:
            return (c, z, 1 - y, m)
        return (c, z + 1 - 2 * (z % 2), y, m)

    cut = half // 2
    mine, given, mine_own, given_own = pl.pallas_call(
        mask_kernel,
        out_shape=[jax.ShapeDtypeStruct((length, half), jnp.bfloat16)] * 4,
        in_specs=[vmem] * 3,
        out_specs=[vmem] * 4,
    )(signal, mask_token, keep)
    near, far, rest, early, late = pl.pallas_call(
        slice_kernel,
        out_shape=[jax.ShapeDtypeStruct(shape, jnp.bfloat16) for shape in (
            (3, depth, wide), (3, depth // 2, wide), (3, depth // 2, wide),
            (cut, half), (cut, half),
        )],
        in_specs=[anywhere] * 3,
        out_specs=[vmem] * 5,
        scratch_shapes=[pltpu.SemaphoreType.DMA((5,))],
    )(mine, enc_weight, pred_weight)
    first, second = move(mine, across_z), move(given, across_zy)
    small = jnp.stack([keep, target_shard])
    small, _ = lax.optimization_barrier((small, mine))
    routing = move(small, lambda c, z, y, m: ((2 * z + y) // 4, (2 * z + y) % 4, c, m))
    x_own = jnp.stack([first, second])
    near_w = move(near, to_near)
    weight_early = move(early, flip_x)
    far, x_own, routing = lax.optimization_barrier((far, x_own, routing))
    far_w = move(far, to_far)
    home = core == z // 2
    sent = jnp.where(home, jnp.stack([mine_own, given_own]), x_own)
    come = move(sent, second_hop)
    come, weight_early = lax.optimization_barrier((come, weight_early))
    kept_home = (jnp.arange(2) == 0)[:, None, None] & home
    x_near = jnp.where(kept_home, mine_own[None], come)
    x_across = move(x_own, flip_x)
    x_near, x_across, weight_early = lax.optimization_barrier((x_near, x_across, weight_early))
    x_near_across = move(x_near, flip_x)
    near_y = move(near_w, flip_y)
    rest, far_w, near_w = lax.optimization_barrier((rest, far_w, near_w))
    rest_w = move(rest, to_far)
    far_y = move(far_w, flip_y)
    rest_y_source, near_y = lax.optimization_barrier((rest_w, near_y))
    rest_y = move(rest_y_source, flip_y)
    weight_early_c = move(weight_early, flip_core)
    late, _ = lax.optimization_barrier((late, x_near_across))
    weight_late = move(late, flip_x)
    weight_late_c = move(weight_late, flip_core)
    hidden = lax.dynamic_index_in_dim(routing[0], y, 0, keepdims=False) == 0
    shard_of = routing[1].reshape(-1)
    blocks = shard_of.shape[0]
    capacity = max(2, 2 * blocks // 8)
    order_ids = jnp.arange(blocks)
    earlier = (shard_of[:, None] == shard_of[None, :]) & (order_ids[:, None] < order_ids[None, :])
    slot = shard_of * capacity + jnp.sum(earlier.astype(jnp.int32), axis=0)
    slot = lax.dynamic_index_in_dim(slot.reshape(sequences, -1), y, 0, keepdims=False)
    slot = jnp.where(hidden, slot, -1)
    slot = lax.dynamic_slice_in_dim(slot, m * (per_range // 2), per_range // 2)
    slot = jnp.repeat(slot, block_len)[:, None]

    def edge(own, near):
        found = jnp.where(jnp.where(home, 1 - z % 2, z % 2) == 1 - core, own, near)
        part = jnp.where(core == 0, 1 - y, y)
        first = jnp.where(core == 0, length - WIN, 0)
        return lax.dynamic_slice(found, (part, first, 0), (1, WIN, half))[0]

    halo = move(jnp.stack([edge(x_own, x_near), edge(x_across, x_near_across)]), flip_core)
    rest_yc_source, halo = lax.optimization_barrier((rest_y, halo))
    pieces = []
    for piece in (near_w, near_y, far_w, far_y, rest_w):
        pieces += [piece, move(piece, flip_core)]
    pieces += [rest_y, move(rest_yc_source, flip_core)]
    span = 4 * length + 2 * WIN

    latent = pl.pallas_call(
        encode_kernel,
        out_shape=jax.ShapeDtypeStruct((4, length, wide), jnp.bfloat16),
        in_specs=[anywhere] * (5 + PIECES),
        out_specs=vmem,
        scratch_shapes=[
            pltpu.VMEM((span, 2 * half), jnp.bfloat16),
            pltpu.VMEM((3, 2 * half, wide), jnp.bfloat16),
            pltpu.VMEM((4 * length, wide), jnp.bfloat16),
            pltpu.VMEM((span, wide), jnp.bfloat16),
            pltpu.VMEM((span, wide), jnp.bfloat16),
            pltpu.SemaphoreType.DMA((10 + PIECES,)),
        ],
        compiler_params=pltpu.CompilerParams(vmem_limit_bytes=60 * 2**20),
    )(x_own, x_across, x_near, x_near_across, halo, *pieces)
    lines = [[4 * i + 2 * j + k for i in range(4) for k in range(2)] for j in range(2)]
    latents = lax.all_to_all(
        latent.reshape(8, length // 2, wide), ("seq", "mdl"),
        split_axis=0, concat_axis=0, tiled=True, axis_index_groups=lines,
    )
    routed = pl.pallas_call(
        predict_kernel,
        out_shape=jax.ShapeDtypeStruct((16, 1, 8 * capacity), jnp.float32),
        in_specs=[vmem] * 7,
        out_specs=vmem,
        compiler_params=pltpu.CompilerParams(vmem_limit_bytes=24 * 2**20),
    )(
        slot, latents, pred_weight,
        weight_early, weight_early_c, weight_late, weight_late_c,
    )
    arrived = lax.all_to_all(routed, ("seq", "mdl"), split_axis=0, concat_axis=0, tiled=True)
    mine = lax.dynamic_slice_in_dim(arrived[:, 0], capacity * s, capacity, 1)
    summed = jnp.sum(mine.reshape(4, 4, capacity), axis=1)
    return summed.reshape(1, -1) / float(block_len * 2 * half)


def solution(mesh):
    placed = (
        P(None, "seq", "mdl"),
        P("mdl"),
        P(None, "seq"),
        P(None, "seq"),
        P("grp", None, "seq", "mdl"),
        P(None, "mdl"),
    )
    plan = local_lines if mesh.shape["seq"] == 8 else local
    return jax.shard_map(
        plan, mesh=mesh, in_specs=placed, out_specs=P("seq", "grp"), check_vma=False
    )
```

```python
import functools
import math

import jax
import jax.numpy as jnp
from jax import lax
from jax.experimental import pallas as pl
from jax.experimental.pallas import tpu as pltpu
from jax.sharding import PartitionSpec as P

HD = 128
WIN = 64
AXES = ("grp", "seq", "mdl")
PIECES = 8


def padded(x, sides, width):
    for axis, dim in sides:
        count, length = (lax.axis_size(axis), x.shape[dim])
        up = [(i, (i + 1) % count) for i in range(count - 1)]
        down = [(j, i) for i, j in up]
        last = lax.slice_in_dim(x, length - width, length, axis=dim)
        leading = lax.slice_in_dim(x, 0, width, axis=dim)
        before = lax.ppermute(last, axis, up)
        after = lax.ppermute(leading, axis, down)
        x = jnp.concatenate([before, x, after], axis=dim)
    return x


def predict(context, target, live_flags, pred_weight, divisor):
    flat_rows = context.reshape(-1, context.shape[-1])
    wide_rows = lax.all_gather(flat_rows, "mdl", axis=1, tiled=True)
    predicted = jnp.dot(wide_rows, pred_weight, preferred_element_type=jnp.float32)
    residue = predicted - target.reshape(flat_rows.shape).astype(jnp.float32)
    partial_sums = jnp.sum((residue * residue).reshape(live_flags.shape[0], -1), axis=1)
    summed = lax.psum(partial_sums, "mdl")
    return summed / divisor * live_flags


def local(signal, mask_token, keep, target_shard, enc_weight, pred_weight):
    group_index = lax.axis_index("grp")
    seq_index = lax.axis_index("seq")
    shards = lax.axis_size("seq")
    sequences, length, half_width = signal.shape
    per_range = keep.shape[1]
    block_len = length // per_range
    kept_rows = jnp.repeat(keep, block_len, axis=1)[:, :, None]
    masked_in = jnp.where(kept_rows == 1, signal, mask_token[None, None, :])
    source = jnp.where(group_index == 0, masked_in, signal)
    wide_in = lax.all_gather(source, "mdl", axis=2, tiled=True)
    full_width = wide_in.shape[2]
    flat_in = wide_in.reshape(-1, full_width)
    span = length + 2 * WIN
    weight_all = lax.all_gather(enc_weight, "seq", axis=2, tiled=True)[0]
    queries = jnp.dot(flat_in, weight_all[0], preferred_element_type=jnp.float32).astype(
        jnp.bfloat16
    )
    pair_made = jnp.einsum(
        "nd,cde->cne", flat_in, weight_all[1:], preferred_element_type=jnp.float32
    ).astype(jnp.bfloat16)
    own_pairs = pair_made.reshape(2, sequences, length, half_width)
    pair_rows = padded(own_pairs, (("seq", 2),), WIN)
    head_count = half_width // HD
    query_heads = queries.reshape(sequences, length, head_count, HD)
    key_heads = pair_rows[0].reshape(sequences, span, head_count, HD)
    value_heads = pair_rows[1].reshape(sequences, span, head_count, HD)
    query_pos = seq_index * length + jnp.arange(length)
    key_pos = seq_index * length - WIN + jnp.arange(span)
    total_len = length * shards
    in_window = (
        (jnp.abs(query_pos[:, None] - key_pos[None, :]) <= WIN)
        & (key_pos[None, :] >= 0)
        & (key_pos[None, :] < total_len)
    )
    scores = jnp.einsum(
        "sahd,sbhd->shab", query_heads, key_heads, preferred_element_type=jnp.float32
    ) * (1.0 / math.sqrt(HD))
    scores = jnp.where(in_window[None, None], scores, -jnp.inf)
    row_peak = jnp.max(scores, axis=-1, keepdims=True)
    exp_scores = jnp.exp(scores - row_peak)
    attention = (exp_scores / jnp.sum(exp_scores, axis=-1, keepdims=True)).astype(jnp.bfloat16)
    attended = jnp.einsum(
        "shab,sbhd->sahd", attention, value_heads, preferred_element_type=jnp.float32
    ).astype(jnp.bfloat16)
    latent = attended.reshape(sequences * per_range, block_len, half_width)
    blocks_here = latent.shape[0]
    capacity = max(2, 2 * blocks_here // shards)
    slot_count = shards * capacity
    shard_of = target_shard.reshape(-1)
    masked_flag = (keep.reshape(-1) == 0).astype(jnp.float32)
    order_ids = jnp.arange(blocks_here)
    earlier = (shard_of[:, None] == shard_of[None, :]) & (order_ids[:, None] < order_ids[None, :])
    slot_rank = jnp.sum(earlier.astype(jnp.int32), axis=0)
    slot_index = shard_of * capacity + slot_rank
    onehot = slot_index[None, :] == jnp.arange(slot_count)[:, None]
    divisor = float(block_len * full_width)
    halves = lax.all_to_all(latent[None], "grp", split_axis=1, concat_axis=0, tiled=True)
    half_count = blocks_here // 2
    first_block = group_index * half_count
    own_flags = lax.dynamic_slice_in_dim(masked_flag, first_block, half_count)
    losses = predict(halves[0], halves[1], own_flags, pred_weight, divisor)
    spread = lax.dynamic_update_slice_in_dim(
        jnp.zeros((blocks_here,), jnp.float32), losses, first_block, 0
    )
    slotted = jnp.sum(jnp.where(onehot, spread[None, :], 0.0), axis=1).reshape(shards, capacity)
    arrived = lax.all_to_all(slotted, "seq", split_axis=0, concat_axis=0, tiled=True)
    result = lax.psum_scatter(arrived, "grp", scatter_dimension=0, tiled=True)
    return result.reshape(1, -1)


def move(x, target):
    pairs = []
    for c in range(2):
        for s in range(8):
            for m in range(2):
                c2, z2, y2, m2 = target(c, s // 2, s % 2, m)
                pairs.append(((c * 8 + s) * 2 + m, (c2 * 8 + 2 * z2 + y2) * 2 + m2))
    return lax.ppermute(x, AXES, pairs)


def places():
    s = lax.axis_index("seq")
    return lax.axis_index("grp"), s // 2, lax.rem(s, 2), lax.axis_index("mdl")


def mask_kernel(
    signal_ref, token_ref, keep_ref, mine_ref, given_ref, mine_own_ref, given_own_ref
):
    core, _, y, _ = places()
    length = signal_ref.shape[1]
    blocks = keep_ref.shape[1]
    block_len = length // blocks
    row = lax.broadcasted_iota(jnp.int32, (length, blocks), 0)
    first = lax.broadcasted_iota(jnp.int32, (length, blocks), 1) * block_len
    covers = (row >= first) & (row < first + block_len)
    token = token_ref[...].astype(jnp.float32).reshape(1, -1)
    for other, own, chosen in ((mine_ref, mine_own_ref, y), (given_ref, given_own_ref, 1 - y)):
        kept = jnp.where(covers, keep_ref[pl.ds(chosen, 1), :], 0)
        kept = jnp.sum(kept, axis=1, keepdims=True)
        rows = signal_ref[chosen].astype(jnp.float32)
        other[...] = jnp.where(kept + 1 - core > 0, rows, token).astype(other.dtype)
        own[...] = jnp.where(kept + core > 0, rows, token).astype(own.dtype)


def slice_kernel(after_ref, weight_ref, pred_ref, near_ref, far_ref, early_ref, late_ref, sems):
    core, z, _, _ = places()
    wide = near_ref.shape[2]
    cut = early_ref.shape[0]
    t = lax.rem(z, 2)
    copies = []
    for target, chosen in ((near_ref, t), (far_ref, 1 - t)):
        lanes = pl.ds(pl.multiple_of(chosen * wide, 128), wide)
        copies.append((weight_ref.at[0, :, :, lanes], target))
    for index, target in enumerate((early_ref, late_ref)):
        first = pl.multiple_of((2 * core + index) * cut, 128)
        copies.append((pred_ref.at[pl.ds(first, cut), :], target))
    copies = [
        pltpu.make_async_copy(source, target, sems.at[index])
        for index, (source, target) in enumerate(copies)
    ]
    for copy in copies:
        copy.start()
    for copy in copies:
        copy.wait()


def encode_kernel(x_own, x_across, x_near, x_near_across, halo_ref, *refs):
    pieces = refs[:PIECES]
    out_ref, x_buf, w_buf, made_buf, sems = refs[PIECES:]
    core, z, y, m = places()
    half = x_own.shape[-1]
    rows = x_own.shape[1]
    depth = pieces[0].shape[1]
    wide = pieces[0].shape[2]
    own_rows = 4 * rows
    copies = []
    side = jnp.where(core == z // 2, 1 - lax.rem(z, 2), lax.rem(z, 2))
    for piece, near, across in (
        (x_own, 0, 0), (x_across, 0, 1), (x_near, 1, 0), (x_near_across, 1, 1)
    ):
        first = WIN + 2 * rows * (side if near == 0 else 1 - side)
        lane = half * (m if across == 0 else 1 - m)
        for part in range(2):
            copies.append((
                piece.at[part],
                x_buf.at[
                    pl.ds(pl.multiple_of(first + (y if part == 0 else 1 - y) * rows, 64), rows),
                    pl.ds(pl.multiple_of(lane, 128), half),
                ],
            ))
    halo_first = pl.multiple_of((1 - core) * (WIN + own_rows), 64)
    empty_first = pl.multiple_of(core * (WIN + own_rows), 64)
    for across in range(2):
        lane = half * (m if across == 0 else 1 - m)
        copies.append((
            halo_ref.at[across],
            x_buf.at[pl.ds(halo_first, WIN), pl.ds(pl.multiple_of(lane, 128), half)],
        ))
    t = lax.rem(z, 2)
    for index, piece in enumerate(pieces):
        crossed, other = (index // 2) % 2, index % 2
        low = core if (other == 0) == (index >= 4) else 1 - core
        pos_z = 2 * low + (t if index < 4 else 1 - t)
        pos = 2 * pos_z + (y if crossed == 0 else 1 - y)
        for kind in range(3):
            copies.append((
                piece.at[kind],
                w_buf.at[
                    pl.ds(pl.multiple_of(pos * depth, 64), depth),
                    kind * wide:(kind + 1) * wide,
                ],
            ))
    started = []
    for index, (source, target) in enumerate(copies):
        copy = pltpu.make_async_copy(source, target, sems.at[index])
        copy.start()
        started.append(copy)
    x_buf[pl.ds(empty_first, WIN), :] = jnp.zeros((WIN, 2 * half), x_buf.dtype)
    for copy in started:
        copy.wait()
    made_buf[...] = jnp.dot(
        x_buf[...], w_buf[...], preferred_element_type=jnp.float32
    ).astype(made_buf.dtype)
    keys = rows + 2 * WIN
    a = lax.broadcasted_iota(jnp.int32, (rows, keys), 0)
    b = lax.broadcasted_iota(jnp.int32, (rows, keys), 1)
    band = (b >= a) & (b <= a + 2 * WIN)
    for j in range(4):
        admitted = band
        if j == 0:
            admitted = admitted & (b >= WIN * (1 - core))
        if j == 3:
            admitted = admitted & (b < keys - WIN * core)
        for h in range(wide // HD):
            query, key, value = (
                slice(kind * wide + h * HD, kind * wide + (h + 1) * HD) for kind in range(3)
            )
            scores = lax.dot_general(
                made_buf[WIN + j * rows:WIN + (j + 1) * rows, query],
                made_buf[j * rows:j * rows + keys, key],
                (((1,), (1,)), ((), ())),
                preferred_element_type=jnp.float32,
            ) * (1.0 / math.sqrt(HD))
            scores = jnp.where(admitted, scores, -jnp.inf)
            peak = jnp.max(scores, axis=-1, keepdims=True)
            exps = jnp.exp(scores - peak)
            attention = (exps / jnp.sum(exps, axis=-1, keepdims=True)).astype(jnp.bfloat16)
            out_ref[j, :, h * HD:(h + 1) * HD] = jnp.dot(
                attention,
                made_buf[j * rows:j * rows + keys, value],
                preferred_element_type=jnp.float32,
            ).astype(out_ref.dtype)


def predict_kernel(slot_ref, lat_ref, own_ref, e0, e1, l0, l1, out_ref):
    core, _, _, m = places()
    wide = lat_ref.shape[2]
    lent = ((e0, e1), (l0, l1))
    total = None
    for side in range(2):
        predicted = None
        for t in range(2):
            for x in range(2):
                if side == 0:
                    source = lat_ref[2 * t + x]
                    weight = own_ref[(2 * x + t) * wide:(2 * x + t + 1) * wide, :]
                else:
                    source = lat_ref[2 * t + (core if x == 0 else 1 - core)]
                    weight = lent[t][x][...]
                term = jnp.dot(source, weight, preferred_element_type=jnp.float32)
                predicted = term if predicted is None else predicted + term
        for t in range(2):
            target = lat_ref[4 + 2 * t + (m if side == 0 else 1 - m)].astype(jnp.float32)
            residue = predicted[:, t * wide:(t + 1) * wide] - target
            for i in range(wide // 128):
                piece = residue[:, i * 128:(i + 1) * 128]
                total = piece * piece if total is None else total + piece * piece
    row_errors = jnp.sum(total, axis=1, keepdims=True)
    rows, slots = total.shape[0], out_ref.shape[2]
    chosen = slot_ref[...] == lax.broadcasted_iota(jnp.int32, (rows, slots), 1)
    routed = jnp.sum(jnp.where(chosen, row_errors, 0.0), axis=0, keepdims=True)
    for i in range(out_ref.shape[0]):
        out_ref[i] = routed


def local_lines(signal, mask_token, keep, target_shard, enc_weight, pred_weight):
    core = lax.axis_index("grp")
    s = lax.axis_index("seq")
    m = lax.axis_index("mdl")
    z, y = s // 2, s % 2
    sequences, length, half = signal.shape
    per_range = keep.shape[1]
    block_len = length // per_range
    depth = enc_weight.shape[2]
    wide = half // 2

    vmem = pl.BlockSpec(memory_space=pltpu.VMEM)
    anywhere = pl.BlockSpec(memory_space=pl.ANY)

    def to_near(c, z, y, m):
        return (1 - z // 2, z % 2 + 2 * c, y, m)

    def to_far(c, z, y, m):
        return (z // 2, 1 - z % 2 + 2 * c, y, m)

    def across_z(c, z, y, m):
        if z // 2 == c:
            return (c, (z + 2) % 4, y, m)
        return (1 - c, z + 1 - 2 * (z % 2), y, m)

    def across_zy(c, z, y, m):
        c, z, y, m = across_z(c, z, y, m)
        return (c, z, 1 - y, m)

    def flip_y(c, z, y, m):
        return (c, z, 1 - y, m)

    def flip_core(c, z, y, m):
        return (1 - c, z, y, m)

    def flip_x(c, z, y, m):
        return (c, z, y, 1 - m)

    def second_hop(c, z, y, m):
        if z // 2 == c:
            return (c, z, 1 - y, m)
        return (c, z + 1 - 2 * (z % 2), y, m)

    cut = half // 2
    mine, given, mine_own, given_own = pl.pallas_call(
        mask_kernel,
        out_shape=[jax.ShapeDtypeStruct((length, half), jnp.bfloat16)] * 4,
        in_specs=[vmem] * 3,
        out_specs=[vmem] * 4,
    )(signal, mask_token, keep)
    near, far, early, late = pl.pallas_call(
        slice_kernel,
        out_shape=[jax.ShapeDtypeStruct(shape, jnp.bfloat16) for shape in (
            (3, depth, wide), (3, depth, wide), (cut, half), (cut, half),
        )],
        in_specs=[anywhere] * 3,
        out_specs=[vmem] * 4,
        scratch_shapes=[pltpu.SemaphoreType.DMA((4,))],
    )(mine, enc_weight, pred_weight)
    first, second = move(mine, across_z), move(given, across_zy)
    small = jnp.stack([keep, target_shard])
    small, _ = lax.optimization_barrier((small, mine))
    routing = move(small, lambda c, z, y, m: ((2 * z + y) // 4, (2 * z + y) % 4, c, m))
    near, routing, first, second = lax.optimization_barrier((near, routing, first, second))
    x_own = jnp.stack([first, second])
    near_w = move(near, to_near)
    weight_early = move(early, flip_x)
    far, x_own = lax.optimization_barrier((far, x_own))
    far_w = move(far, to_far)
    home = core == z // 2
    sent = jnp.where(home, jnp.stack([mine_own, given_own]), x_own)
    come = move(sent, second_hop)
    kept_home = (jnp.arange(2) == 0)[:, None, None] & home
    x_near = jnp.where(kept_home, mine_own[None], come)
    x_across = move(x_own, flip_x)
    near_y_source, weight_early = lax.optimization_barrier((near_w, weight_early))
    near_y = move(near_y_source, flip_y)
    far_y_source, near_y = lax.optimization_barrier((far_w, near_y))
    far_y = move(far_y_source, flip_y)
    weight_early_c = move(weight_early, flip_core)
    x_near, x_across = lax.optimization_barrier((x_near, x_across))
    x_near_across = move(x_near, flip_x)
    late, _ = lax.optimization_barrier((late, x_near_across))
    weight_late = move(late, flip_x)
    weight_late_c = move(weight_late, flip_core)
    hidden = lax.dynamic_index_in_dim(routing[0], y, 0, keepdims=False) == 0
    shard_of = routing[1].reshape(-1)
    blocks = shard_of.shape[0]
    capacity = max(2, 2 * blocks // 8)
    order_ids = jnp.arange(blocks)
    earlier = (shard_of[:, None] == shard_of[None, :]) & (order_ids[:, None] < order_ids[None, :])
    slot = shard_of * capacity + jnp.sum(earlier.astype(jnp.int32), axis=0)
    slot = lax.dynamic_index_in_dim(slot.reshape(sequences, -1), y, 0, keepdims=False)
    slot = jnp.where(hidden, slot, -1)
    slot = lax.dynamic_slice_in_dim(slot, m * (per_range // 2), per_range // 2)
    slot = jnp.repeat(slot, block_len)[:, None]

    def edge(own, near):
        found = jnp.where(jnp.where(home, 1 - z % 2, z % 2) == 1 - core, own, near)
        part = jnp.where(core == 0, 1 - y, y)
        first = jnp.where(core == 0, length - WIN, 0)
        return lax.dynamic_slice(found, (part, first, 0), (1, WIN, half))[0]

    halo = move(jnp.stack([edge(x_own, x_near), edge(x_across, x_near_across)]), flip_core)
    far_yc_source, halo = lax.optimization_barrier((far_y, halo))
    pieces = [
        near_w, move(near_w, flip_core), near_y, move(near_y, flip_core),
        far_w, move(far_w, flip_core), far_y, move(far_yc_source, flip_core),
    ]
    span = 4 * length + 2 * WIN

    latent = pl.pallas_call(
        encode_kernel,
        out_shape=jax.ShapeDtypeStruct((4, length, wide), jnp.bfloat16),
        in_specs=[anywhere] * (5 + PIECES),
        out_specs=vmem,
        scratch_shapes=[
            pltpu.VMEM((span, 2 * half), jnp.bfloat16),
            pltpu.VMEM((2 * half, 3 * wide), jnp.bfloat16),
            pltpu.VMEM((span, 3 * wide), jnp.bfloat16),
            pltpu.SemaphoreType.DMA((10 + 3 * PIECES,)),
        ],
        compiler_params=pltpu.CompilerParams(vmem_limit_bytes=60 * 2**20),
    )(x_own, x_across, x_near, x_near_across, halo, *pieces)
    lines = [[4 * i + 2 * j + k for i in range(4) for k in range(2)] for j in range(2)]
    latents = lax.all_to_all(
        latent.reshape(8, length // 2, wide), ("seq", "mdl"),
        split_axis=0, concat_axis=0, tiled=True, axis_index_groups=lines,
    )
    routed = pl.pallas_call(
        predict_kernel,
        out_shape=jax.ShapeDtypeStruct((16, 1, 8 * capacity), jnp.float32),
        in_specs=[vmem] * 7,
        out_specs=vmem,
        compiler_params=pltpu.CompilerParams(vmem_limit_bytes=24 * 2**20),
    )(
        slot, latents, pred_weight,
        weight_early, weight_early_c, weight_late, weight_late_c,
    )
    arrived = lax.all_to_all(routed, ("seq", "mdl"), split_axis=0, concat_axis=0, tiled=True)
    mine = lax.dynamic_slice_in_dim(arrived[:, 0], capacity * s, capacity, 1)
    summed = jnp.sum(mine.reshape(4, 4, capacity), axis=1)
    return summed.reshape(1, -1) / float(block_len * 2 * half)


def solution(mesh):
    placed = (
        P(None, "seq", "mdl"),
        P("mdl"),
        P(None, "seq"),
        P(None, "seq"),
        P("grp", None, "seq", "mdl"),
        P(None, "mdl"),
    )
    plan = local_lines if mesh.shape["seq"] == 8 else local
    return jax.shard_map(
        plan, mesh=mesh, in_specs=placed, out_specs=P("seq", "grp"), check_vma=False
    )
```

```python
import functools
import math

import jax
import jax.numpy as jnp
from jax import lax
from jax.experimental import pallas as pl
from jax.experimental.pallas import tpu as pltpu
from jax.sharding import PartitionSpec as P

HD = 128
WIN = 64
AXES = ("grp", "seq", "mdl")
PIECES = 8


def padded(x, sides, width):
    for axis, dim in sides:
        count, length = (lax.axis_size(axis), x.shape[dim])
        up = [(i, (i + 1) % count) for i in range(count - 1)]
        down = [(j, i) for i, j in up]
        last = lax.slice_in_dim(x, length - width, length, axis=dim)
        leading = lax.slice_in_dim(x, 0, width, axis=dim)
        before = lax.ppermute(last, axis, up)
        after = lax.ppermute(leading, axis, down)
        x = jnp.concatenate([before, x, after], axis=dim)
    return x


def predict(context, target, live_flags, pred_weight, divisor):
    flat_rows = context.reshape(-1, context.shape[-1])
    wide_rows = lax.all_gather(flat_rows, "mdl", axis=1, tiled=True)
    predicted = jnp.dot(wide_rows, pred_weight, preferred_element_type=jnp.float32)
    residue = predicted - target.reshape(flat_rows.shape).astype(jnp.float32)
    partial_sums = jnp.sum((residue * residue).reshape(live_flags.shape[0], -1), axis=1)
    summed = lax.psum(partial_sums, "mdl")
    return summed / divisor * live_flags


def local(signal, mask_token, keep, target_shard, enc_weight, pred_weight):
    group_index = lax.axis_index("grp")
    seq_index = lax.axis_index("seq")
    shards = lax.axis_size("seq")
    sequences, length, half_width = signal.shape
    per_range = keep.shape[1]
    block_len = length // per_range
    kept_rows = jnp.repeat(keep, block_len, axis=1)[:, :, None]
    masked_in = jnp.where(kept_rows == 1, signal, mask_token[None, None, :])
    source = jnp.where(group_index == 0, masked_in, signal)
    wide_in = lax.all_gather(source, "mdl", axis=2, tiled=True)
    full_width = wide_in.shape[2]
    flat_in = wide_in.reshape(-1, full_width)
    span = length + 2 * WIN
    weight_all = lax.all_gather(enc_weight, "seq", axis=2, tiled=True)[0]
    queries = jnp.dot(flat_in, weight_all[0], preferred_element_type=jnp.float32).astype(
        jnp.bfloat16
    )
    pair_made = jnp.einsum(
        "nd,cde->cne", flat_in, weight_all[1:], preferred_element_type=jnp.float32
    ).astype(jnp.bfloat16)
    own_pairs = pair_made.reshape(2, sequences, length, half_width)
    pair_rows = padded(own_pairs, (("seq", 2),), WIN)
    head_count = half_width // HD
    query_heads = queries.reshape(sequences, length, head_count, HD)
    key_heads = pair_rows[0].reshape(sequences, span, head_count, HD)
    value_heads = pair_rows[1].reshape(sequences, span, head_count, HD)
    query_pos = seq_index * length + jnp.arange(length)
    key_pos = seq_index * length - WIN + jnp.arange(span)
    total_len = length * shards
    in_window = (
        (jnp.abs(query_pos[:, None] - key_pos[None, :]) <= WIN)
        & (key_pos[None, :] >= 0)
        & (key_pos[None, :] < total_len)
    )
    scores = jnp.einsum(
        "sahd,sbhd->shab", query_heads, key_heads, preferred_element_type=jnp.float32
    ) * (1.0 / math.sqrt(HD))
    scores = jnp.where(in_window[None, None], scores, -jnp.inf)
    row_peak = jnp.max(scores, axis=-1, keepdims=True)
    exp_scores = jnp.exp(scores - row_peak)
    attention = (exp_scores / jnp.sum(exp_scores, axis=-1, keepdims=True)).astype(jnp.bfloat16)
    attended = jnp.einsum(
        "shab,sbhd->sahd", attention, value_heads, preferred_element_type=jnp.float32
    ).astype(jnp.bfloat16)
    latent = attended.reshape(sequences * per_range, block_len, half_width)
    blocks_here = latent.shape[0]
    capacity = max(2, 2 * blocks_here // shards)
    slot_count = shards * capacity
    shard_of = target_shard.reshape(-1)
    masked_flag = (keep.reshape(-1) == 0).astype(jnp.float32)
    order_ids = jnp.arange(blocks_here)
    earlier = (shard_of[:, None] == shard_of[None, :]) & (order_ids[:, None] < order_ids[None, :])
    slot_rank = jnp.sum(earlier.astype(jnp.int32), axis=0)
    slot_index = shard_of * capacity + slot_rank
    onehot = slot_index[None, :] == jnp.arange(slot_count)[:, None]
    divisor = float(block_len * full_width)
    halves = lax.all_to_all(latent[None], "grp", split_axis=1, concat_axis=0, tiled=True)
    half_count = blocks_here // 2
    first_block = group_index * half_count
    own_flags = lax.dynamic_slice_in_dim(masked_flag, first_block, half_count)
    losses = predict(halves[0], halves[1], own_flags, pred_weight, divisor)
    spread = lax.dynamic_update_slice_in_dim(
        jnp.zeros((blocks_here,), jnp.float32), losses, first_block, 0
    )
    slotted = jnp.sum(jnp.where(onehot, spread[None, :], 0.0), axis=1).reshape(shards, capacity)
    arrived = lax.all_to_all(slotted, "seq", split_axis=0, concat_axis=0, tiled=True)
    result = lax.psum_scatter(arrived, "grp", scatter_dimension=0, tiled=True)
    return result.reshape(1, -1)


def move(x, target):
    pairs = []
    for c in range(2):
        for s in range(8):
            for m in range(2):
                c2, z2, y2, m2 = target(c, s // 2, s % 2, m)
                pairs.append(((c * 8 + s) * 2 + m, (c2 * 8 + 2 * z2 + y2) * 2 + m2))
    return lax.ppermute(x, AXES, pairs)


def places():
    s = lax.axis_index("seq")
    return lax.axis_index("grp"), s // 2, lax.rem(s, 2), lax.axis_index("mdl")


def mask_kernel(
    signal_ref, token_ref, keep_ref, mine_ref, given_ref, mine_own_ref, given_own_ref
):
    core, _, y, _ = places()
    length = signal_ref.shape[1]
    blocks = keep_ref.shape[1]
    block_len = length // blocks
    row = lax.broadcasted_iota(jnp.int32, (length, blocks), 0)
    first = lax.broadcasted_iota(jnp.int32, (length, blocks), 1) * block_len
    covers = (row >= first) & (row < first + block_len)
    token = token_ref[...].astype(jnp.float32).reshape(1, -1)
    for other, own, chosen in ((mine_ref, mine_own_ref, y), (given_ref, given_own_ref, 1 - y)):
        kept = jnp.where(covers, keep_ref[pl.ds(chosen, 1), :], 0)
        kept = jnp.sum(kept, axis=1, keepdims=True)
        rows = signal_ref[chosen].astype(jnp.float32)
        other[...] = jnp.where(kept + 1 - core > 0, rows, token).astype(other.dtype)
        own[...] = jnp.where(kept + core > 0, rows, token).astype(own.dtype)


def slice_kernel(after_ref, weight_ref, pred_ref, near_ref, far_ref, early_ref, late_ref, sems):
    core, z, _, _ = places()
    wide = near_ref.shape[2]
    cut = early_ref.shape[0]
    t = lax.rem(z, 2)
    copies = []
    for target, chosen in ((near_ref, t), (far_ref, 1 - t)):
        lanes = pl.ds(pl.multiple_of(chosen * wide, 128), wide)
        copies.append((weight_ref.at[0, :, :, lanes], target))
    for index, target in enumerate((early_ref, late_ref)):
        first = pl.multiple_of((2 * core + index) * cut, 128)
        copies.append((pred_ref.at[pl.ds(first, cut), :], target))
    copies = [
        pltpu.make_async_copy(source, target, sems.at[index])
        for index, (source, target) in enumerate(copies)
    ]
    for copy in copies:
        copy.start()
    for copy in copies:
        copy.wait()


def encode_kernel(x_own, x_across, x_near, x_near_across, halo_ref, *refs):
    pieces = refs[:PIECES]
    out_ref, x_buf, w_buf, q_buf, k_buf, v_buf, sems = refs[PIECES:]
    core, z, y, m = places()
    half = x_own.shape[-1]
    rows = x_own.shape[1]
    depth = pieces[0].shape[1]
    wide = pieces[0].shape[2]
    own_rows = 4 * rows
    copies = []
    side = jnp.where(core == z // 2, 1 - lax.rem(z, 2), lax.rem(z, 2))
    for piece, near, across in (
        (x_own, 0, 0), (x_across, 0, 1), (x_near, 1, 0), (x_near_across, 1, 1)
    ):
        first = WIN + 2 * rows * (side if near == 0 else 1 - side)
        for part in range(2):
            row = pl.multiple_of(first + (y if part == 0 else 1 - y) * rows, 64)
            copies.append((
                piece.at[part], x_buf.at[m if across == 0 else 1 - m, pl.ds(row, rows), :]
            ))
    halo_first = pl.multiple_of((1 - core) * (WIN + own_rows), 64)
    empty_first = pl.multiple_of(core * (WIN + own_rows), 64)
    for across in range(2):
        copies.append((
            halo_ref.at[across],
            x_buf.at[m if across == 0 else 1 - m, pl.ds(halo_first, WIN), :],
        ))
    t = lax.rem(z, 2)
    for index, piece in enumerate(pieces):
        crossed, other = (index // 2) % 2, index % 2
        low = core if (other == 0) == (index >= 4) else 1 - core
        pos_z = 2 * low + (t if index < 4 else 1 - t)
        pos = 2 * pos_z + (y if crossed == 0 else 1 - y)
        copies.append((
            piece, w_buf.at[:, pl.ds(pl.multiple_of(pos * depth, 64), depth), :]
        ))
    started = []
    for index, (source, target) in enumerate(copies):
        copy = pltpu.make_async_copy(source, target, sems.at[index])
        copy.start()
        started.append(copy)
    x_buf[:, pl.ds(empty_first, WIN), :] = jnp.zeros((2, WIN, half), x_buf.dtype)
    for copy in started:
        copy.wait()

    def project(kind, first, count):
        total = None
        for i in range(2):
            term = jnp.dot(
                x_buf[i, first:first + count, :],
                w_buf[kind, i * half:(i + 1) * half, :],
                preferred_element_type=jnp.float32,
            )
            total = term if total is None else total + term
        return total.astype(q_buf.dtype)

    q_buf[...] = project(0, WIN, own_rows)
    k_buf[...] = project(1, 0, own_rows + 2 * WIN)
    v_buf[...] = project(2, 0, own_rows + 2 * WIN)
    keys = rows + 2 * WIN
    a = lax.broadcasted_iota(jnp.int32, (rows, keys), 0)
    b = lax.broadcasted_iota(jnp.int32, (rows, keys), 1)
    band = (b >= a) & (b <= a + 2 * WIN)
    for j in range(4):
        admitted = band
        if j == 0:
            admitted = admitted & (b >= WIN * (1 - core))
        if j == 3:
            admitted = admitted & (b < keys - WIN * core)
        for h in range(wide // HD):
            lanes = slice(h * HD, (h + 1) * HD)
            scores = lax.dot_general(
                q_buf[j * rows:(j + 1) * rows, lanes],
                k_buf[j * rows:j * rows + keys, lanes],
                (((1,), (1,)), ((), ())),
                preferred_element_type=jnp.float32,
            ) * (1.0 / math.sqrt(HD))
            scores = jnp.where(admitted, scores, -jnp.inf)
            peak = jnp.max(scores, axis=-1, keepdims=True)
            exps = jnp.exp(scores - peak)
            attention = (exps / jnp.sum(exps, axis=-1, keepdims=True)).astype(jnp.bfloat16)
            out_ref[j, :, lanes] = jnp.dot(
                attention,
                v_buf[j * rows:j * rows + keys, lanes],
                preferred_element_type=jnp.float32,
            ).astype(out_ref.dtype)


def predict_kernel(slot_ref, lat_ref, own_ref, e0, e1, l0, l1, out_ref):
    core, _, _, m = places()
    wide = lat_ref.shape[2]
    lent = ((e0, e1), (l0, l1))
    total = None
    for side in range(2):
        predicted = None
        for t in range(2):
            for x in range(2):
                if side == 0:
                    source = lat_ref[2 * t + x]
                    weight = own_ref[(2 * x + t) * wide:(2 * x + t + 1) * wide, :]
                else:
                    source = lat_ref[2 * t + (core if x == 0 else 1 - core)]
                    weight = lent[t][x][...]
                term = jnp.dot(source, weight, preferred_element_type=jnp.float32)
                predicted = term if predicted is None else predicted + term
        for t in range(2):
            target = lat_ref[4 + 2 * t + (m if side == 0 else 1 - m)].astype(jnp.float32)
            residue = predicted[:, t * wide:(t + 1) * wide] - target
            for i in range(wide // 128):
                piece = residue[:, i * 128:(i + 1) * 128]
                total = piece * piece if total is None else total + piece * piece
    row_errors = jnp.sum(total, axis=1, keepdims=True)
    rows, slots = total.shape[0], out_ref.shape[2]
    chosen = slot_ref[...] == lax.broadcasted_iota(jnp.int32, (rows, slots), 1)
    routed = jnp.sum(jnp.where(chosen, row_errors, 0.0), axis=0, keepdims=True)
    for i in range(out_ref.shape[0]):
        out_ref[i] = routed


def local_lines(signal, mask_token, keep, target_shard, enc_weight, pred_weight):
    core = lax.axis_index("grp")
    s = lax.axis_index("seq")
    m = lax.axis_index("mdl")
    z, y = s // 2, s % 2
    sequences, length, half = signal.shape
    per_range = keep.shape[1]
    block_len = length // per_range
    depth = enc_weight.shape[2]
    wide = half // 2

    vmem = pl.BlockSpec(memory_space=pltpu.VMEM)
    anywhere = pl.BlockSpec(memory_space=pl.ANY)

    def to_near(c, z, y, m):
        return (1 - z // 2, z % 2 + 2 * c, y, m)

    def to_far(c, z, y, m):
        return (z // 2, 1 - z % 2 + 2 * c, y, m)

    def across_z(c, z, y, m):
        if z // 2 == c:
            return (c, (z + 2) % 4, y, m)
        return (1 - c, z + 1 - 2 * (z % 2), y, m)

    def across_zy(c, z, y, m):
        c, z, y, m = across_z(c, z, y, m)
        return (c, z, 1 - y, m)

    def flip_y(c, z, y, m):
        return (c, z, 1 - y, m)

    def flip_core(c, z, y, m):
        return (1 - c, z, y, m)

    def flip_x(c, z, y, m):
        return (c, z, y, 1 - m)

    def second_hop(c, z, y, m):
        if z // 2 == c:
            return (c, z, 1 - y, m)
        return (c, z + 1 - 2 * (z % 2), y, m)

    cut = half // 2
    mine, given, mine_own, given_own = pl.pallas_call(
        mask_kernel,
        out_shape=[jax.ShapeDtypeStruct((length, half), jnp.bfloat16)] * 4,
        in_specs=[vmem] * 3,
        out_specs=[vmem] * 4,
    )(signal, mask_token, keep)
    near, far, early, late = pl.pallas_call(
        slice_kernel,
        out_shape=[jax.ShapeDtypeStruct(shape, jnp.bfloat16) for shape in (
            (3, depth, wide), (3, depth, wide), (cut, half), (cut, half),
        )],
        in_specs=[anywhere] * 3,
        out_specs=[vmem] * 4,
        scratch_shapes=[pltpu.SemaphoreType.DMA((4,))],
    )(mine, enc_weight, pred_weight)
    first, second = move(mine, across_z), move(given, across_zy)
    small = jnp.stack([keep, target_shard])
    small, _ = lax.optimization_barrier((small, mine))
    routing = move(small, lambda c, z, y, m: ((2 * z + y) // 4, (2 * z + y) % 4, c, m))
    near, routing, first, second = lax.optimization_barrier((near, routing, first, second))
    x_own = jnp.stack([first, second])
    near_w = move(near, to_near)
    weight_early = move(early, flip_x)
    far, x_own = lax.optimization_barrier((far, x_own))
    far_w = move(far, to_far)
    home = core == z // 2
    sent = jnp.where(home, jnp.stack([mine_own, given_own]), x_own)
    come = move(sent, second_hop)
    kept_home = (jnp.arange(2) == 0)[:, None, None] & home
    x_near = jnp.where(kept_home, mine_own[None], come)
    x_across = move(x_own, flip_x)
    near_y_source, weight_early = lax.optimization_barrier((near_w, weight_early))
    near_y = move(near_y_source, flip_y)
    far_y_source, near_y = lax.optimization_barrier((far_w, near_y))
    far_y = move(far_y_source, flip_y)
    weight_early_c = move(weight_early, flip_core)
    x_near, x_across = lax.optimization_barrier((x_near, x_across))
    x_near_across = move(x_near, flip_x)
    late, _ = lax.optimization_barrier((late, x_near_across))
    weight_late = move(late, flip_x)
    weight_late_c = move(weight_late, flip_core)
    hidden = lax.dynamic_index_in_dim(routing[0], y, 0, keepdims=False) == 0
    shard_of = routing[1].reshape(-1)
    blocks = shard_of.shape[0]
    capacity = max(2, 2 * blocks // 8)
    order_ids = jnp.arange(blocks)
    earlier = (shard_of[:, None] == shard_of[None, :]) & (order_ids[:, None] < order_ids[None, :])
    slot = shard_of * capacity + jnp.sum(earlier.astype(jnp.int32), axis=0)
    slot = lax.dynamic_index_in_dim(slot.reshape(sequences, -1), y, 0, keepdims=False)
    slot = jnp.where(hidden, slot, -1)
    slot = lax.dynamic_slice_in_dim(slot, m * (per_range // 2), per_range // 2)
    slot = jnp.repeat(slot, block_len)[:, None]

    def edge(own, near):
        found = jnp.where(jnp.where(home, 1 - z % 2, z % 2) == 1 - core, own, near)
        part = jnp.where(core == 0, 1 - y, y)
        first = jnp.where(core == 0, length - WIN, 0)
        return lax.dynamic_slice(found, (part, first, 0), (1, WIN, half))[0]

    halo = move(jnp.stack([edge(x_own, x_near), edge(x_across, x_near_across)]), flip_core)
    far_yc_source, halo = lax.optimization_barrier((far_y, halo))
    pieces = [
        near_w, move(near_w, flip_core), near_y, move(near_y, flip_core),
        far_w, move(far_w, flip_core), far_y, move(far_yc_source, flip_core),
    ]
    span = 4 * length + 2 * WIN

    latent = pl.pallas_call(
        encode_kernel,
        out_shape=jax.ShapeDtypeStruct((4, length, wide), jnp.bfloat16),
        in_specs=[anywhere] * (5 + PIECES),
        out_specs=vmem,
        scratch_shapes=[
            pltpu.VMEM((2, span, half), jnp.bfloat16),
            pltpu.VMEM((3, 2 * half, wide), jnp.bfloat16),
            pltpu.VMEM((4 * length, wide), jnp.bfloat16),
            pltpu.VMEM((span, wide), jnp.bfloat16),
            pltpu.VMEM((span, wide), jnp.bfloat16),
            pltpu.SemaphoreType.DMA((10 + PIECES,)),
        ],
        compiler_params=pltpu.CompilerParams(vmem_limit_bytes=60 * 2**20),
    )(x_own, x_across, x_near, x_near_across, halo, *pieces)
    lines = [[4 * i + 2 * j + k for i in range(4) for k in range(2)] for j in range(2)]
    latents = lax.all_to_all(
        latent.reshape(8, length // 2, wide), ("seq", "mdl"),
        split_axis=0, concat_axis=0, tiled=True, axis_index_groups=lines,
    )
    routed = pl.pallas_call(
        predict_kernel,
        out_shape=jax.ShapeDtypeStruct((16, 1, 8 * capacity), jnp.float32),
        in_specs=[vmem] * 7,
        out_specs=vmem,
        compiler_params=pltpu.CompilerParams(vmem_limit_bytes=24 * 2**20),
    )(
        slot, latents, pred_weight,
        weight_early, weight_early_c, weight_late, weight_late_c,
    )
    arrived = lax.all_to_all(routed, ("seq", "mdl"), split_axis=0, concat_axis=0, tiled=True)
    mine = lax.dynamic_slice_in_dim(arrived[:, 0], capacity * s, capacity, 1)
    summed = jnp.sum(mine.reshape(4, 4, capacity), axis=1)
    return summed.reshape(1, -1) / float(block_len * 2 * half)


def solution(mesh):
    placed = (
        P(None, "seq", "mdl"),
        P("mdl"),
        P(None, "seq"),
        P(None, "seq"),
        P("grp", None, "seq", "mdl"),
        P(None, "mdl"),
    )
    plan = local_lines if mesh.shape["seq"] == 8 else local
    return jax.shard_map(
        plan, mesh=mesh, in_specs=placed, out_specs=P("seq", "grp"), check_vma=False
    )
```

```python
import functools
import math

import jax
import jax.numpy as jnp
from jax import lax
from jax.experimental import pallas as pl
from jax.experimental.pallas import tpu as pltpu
from jax.sharding import PartitionSpec as P

HD = 128
WIN = 64
AXES = ("grp", "seq", "mdl")


def padded(x, sides, width):
    for axis, dim in sides:
        count, length = (lax.axis_size(axis), x.shape[dim])
        up = [(i, (i + 1) % count) for i in range(count - 1)]
        down = [(j, i) for i, j in up]
        last = lax.slice_in_dim(x, length - width, length, axis=dim)
        leading = lax.slice_in_dim(x, 0, width, axis=dim)
        before = lax.ppermute(last, axis, up)
        after = lax.ppermute(leading, axis, down)
        x = jnp.concatenate([before, x, after], axis=dim)
    return x


def predict(context, target, live_flags, pred_weight, divisor):
    flat_rows = context.reshape(-1, context.shape[-1])
    wide_rows = lax.all_gather(flat_rows, "mdl", axis=1, tiled=True)
    predicted = jnp.dot(wide_rows, pred_weight, preferred_element_type=jnp.float32)
    residue = predicted - target.reshape(flat_rows.shape).astype(jnp.float32)
    partial_sums = jnp.sum((residue * residue).reshape(live_flags.shape[0], -1), axis=1)
    summed = lax.psum(partial_sums, "mdl")
    return summed / divisor * live_flags


def local(signal, mask_token, keep, target_shard, enc_weight, pred_weight):
    group_index = lax.axis_index("grp")
    seq_index = lax.axis_index("seq")
    shards = lax.axis_size("seq")
    sequences, length, half_width = signal.shape
    per_range = keep.shape[1]
    block_len = length // per_range
    kept_rows = jnp.repeat(keep, block_len, axis=1)[:, :, None]
    masked_in = jnp.where(kept_rows == 1, signal, mask_token[None, None, :])
    source = jnp.where(group_index == 0, masked_in, signal)
    wide_in = lax.all_gather(source, "mdl", axis=2, tiled=True)
    full_width = wide_in.shape[2]
    flat_in = wide_in.reshape(-1, full_width)
    span = length + 2 * WIN
    weight_all = lax.all_gather(enc_weight, "seq", axis=2, tiled=True)[0]
    queries = jnp.dot(flat_in, weight_all[0], preferred_element_type=jnp.float32).astype(
        jnp.bfloat16
    )
    pair_made = jnp.einsum(
        "nd,cde->cne", flat_in, weight_all[1:], preferred_element_type=jnp.float32
    ).astype(jnp.bfloat16)
    own_pairs = pair_made.reshape(2, sequences, length, half_width)
    pair_rows = padded(own_pairs, (("seq", 2),), WIN)
    head_count = half_width // HD
    query_heads = queries.reshape(sequences, length, head_count, HD)
    key_heads = pair_rows[0].reshape(sequences, span, head_count, HD)
    value_heads = pair_rows[1].reshape(sequences, span, head_count, HD)
    query_pos = seq_index * length + jnp.arange(length)
    key_pos = seq_index * length - WIN + jnp.arange(span)
    total_len = length * shards
    in_window = (
        (jnp.abs(query_pos[:, None] - key_pos[None, :]) <= WIN)
        & (key_pos[None, :] >= 0)
        & (key_pos[None, :] < total_len)
    )
    scores = jnp.einsum(
        "sahd,sbhd->shab", query_heads, key_heads, preferred_element_type=jnp.float32
    ) * (1.0 / math.sqrt(HD))
    scores = jnp.where(in_window[None, None], scores, -jnp.inf)
    row_peak = jnp.max(scores, axis=-1, keepdims=True)
    exp_scores = jnp.exp(scores - row_peak)
    attention = (exp_scores / jnp.sum(exp_scores, axis=-1, keepdims=True)).astype(jnp.bfloat16)
    attended = jnp.einsum(
        "shab,sbhd->sahd", attention, value_heads, preferred_element_type=jnp.float32
    ).astype(jnp.bfloat16)
    latent = attended.reshape(sequences * per_range, block_len, half_width)
    blocks_here = latent.shape[0]
    capacity = max(2, 2 * blocks_here // shards)
    slot_count = shards * capacity
    shard_of = target_shard.reshape(-1)
    masked_flag = (keep.reshape(-1) == 0).astype(jnp.float32)
    order_ids = jnp.arange(blocks_here)
    earlier = (shard_of[:, None] == shard_of[None, :]) & (order_ids[:, None] < order_ids[None, :])
    slot_rank = jnp.sum(earlier.astype(jnp.int32), axis=0)
    slot_index = shard_of * capacity + slot_rank
    onehot = slot_index[None, :] == jnp.arange(slot_count)[:, None]
    divisor = float(block_len * full_width)
    halves = lax.all_to_all(latent[None], "grp", split_axis=1, concat_axis=0, tiled=True)
    half_count = blocks_here // 2
    first_block = group_index * half_count
    own_flags = lax.dynamic_slice_in_dim(masked_flag, first_block, half_count)
    losses = predict(halves[0], halves[1], own_flags, pred_weight, divisor)
    spread = lax.dynamic_update_slice_in_dim(
        jnp.zeros((blocks_here,), jnp.float32), losses, first_block, 0
    )
    slotted = jnp.sum(jnp.where(onehot, spread[None, :], 0.0), axis=1).reshape(shards, capacity)
    arrived = lax.all_to_all(slotted, "seq", split_axis=0, concat_axis=0, tiled=True)
    result = lax.psum_scatter(arrived, "grp", scatter_dimension=0, tiled=True)
    return result.reshape(1, -1)


def move(x, target):
    pairs = []
    for c in range(2):
        for s in range(8):
            for m in range(2):
                c2, z2, y2, m2 = target(c, s // 2, s % 2, m)
                pairs.append(((c * 8 + s) * 2 + m, (c2 * 8 + 2 * z2 + y2) * 2 + m2))
    return lax.ppermute(x, AXES, pairs)


def places():
    s = lax.axis_index("seq")
    return lax.axis_index("grp"), s // 2, lax.rem(s, 2), lax.axis_index("mdl")


def mask_kernel(
    signal_ref, token_ref, keep_ref, mine_ref, given_ref, mine_own_ref, given_own_ref
):
    core, _, y, _ = places()
    length = signal_ref.shape[1]
    blocks = keep_ref.shape[1]
    block_len = length // blocks
    row = lax.broadcasted_iota(jnp.int32, (length, blocks), 0)
    first = lax.broadcasted_iota(jnp.int32, (length, blocks), 1) * block_len
    covers = (row >= first) & (row < first + block_len)
    token = token_ref[...].astype(jnp.float32).reshape(1, -1)
    for other, own, chosen in ((mine_ref, mine_own_ref, y), (given_ref, given_own_ref, 1 - y)):
        kept = jnp.where(covers, keep_ref[pl.ds(chosen, 1), :], 0)
        kept = jnp.sum(kept, axis=1, keepdims=True)
        rows = signal_ref[chosen].astype(jnp.float32)
        other[...] = jnp.where(kept + 1 - core > 0, rows, token).astype(other.dtype)
        own[...] = jnp.where(kept + core > 0, rows, token).astype(own.dtype)


def slice_kernel(after_ref, weight_ref, pred_ref, near_ref, far_ref, early_ref, late_ref, sems):
    core, z, _, _ = places()
    wide = near_ref.shape[2]
    cut = early_ref.shape[0]
    t = lax.rem(z, 2)
    copies = []
    for target, chosen in ((near_ref, t), (far_ref, 1 - t)):
        lanes = pl.ds(pl.multiple_of(chosen * wide, 128), wide)
        copies.append((weight_ref.at[0, :, :, lanes], target))
    for index, target in enumerate((early_ref, late_ref)):
        first = pl.multiple_of((2 * core + index) * cut, 128)
        copies.append((pred_ref.at[pl.ds(first, cut), :], target))
    copies = [
        pltpu.make_async_copy(source, target, sems.at[index])
        for index, (source, target) in enumerate(copies)
    ]
    for copy in copies:
        copy.start()
    for copy in copies:
        copy.wait()


def start_all(pairs, sems):
    copies = [
        pltpu.make_async_copy(source, target, sems.at[index])
        for index, (source, target) in enumerate(pairs)
    ]
    for copy in copies:
        copy.start()
    return copies


def weight_rows(index, y, core, depth):
    crossed, other = (index // 2) % 2, index % 2
    low = core if (other == 0) == (index >= 4) else 1 - core
    return low, pl.ds(pl.multiple_of((y if crossed == 0 else 1 - y) * depth, 64), depth)


def partial_kernel(x_own, x_across, x_near, x_near_across, halo_ref, w0, w1, w2, w3, *refs):
    made_ref, rest_ref, x_buf, w_buf, sems = refs
    core, z, y, m = places()
    half = x_own.shape[-1]
    rows = x_own.shape[1]
    depth = w0.shape[1]
    own_rows = 4 * rows
    pairs = []
    side = jnp.where(core == z // 2, 1 - lax.rem(z, 2), lax.rem(z, 2))
    for piece, near, across in (
        (x_own, 0, 0), (x_across, 0, 1), (x_near, 1, 0), (x_near_across, 1, 1)
    ):
        first = WIN + 2 * rows * (side if near == 0 else 1 - side)
        for part in range(2):
            row = pl.multiple_of(first + (y if part == 0 else 1 - y) * rows, 64)
            pairs.append((
                piece.at[part], x_buf.at[m if across == 0 else 1 - m, pl.ds(row, rows), :]
            ))
    halo_first = pl.multiple_of((1 - core) * (WIN + own_rows), 64)
    empty_first = pl.multiple_of(core * (WIN + own_rows), 64)
    for across in range(2):
        pairs.append((
            halo_ref.at[across],
            x_buf.at[m if across == 0 else 1 - m, pl.ds(halo_first, WIN), :],
        ))
    for index, piece in enumerate((w0, w1, w2, w3)):
        low, span = weight_rows(index, y, core, depth)
        pairs.append((piece, w_buf.at[:, low, span, :]))
    copies = start_all(pairs, sems)
    x_buf[:, pl.ds(empty_first, WIN), :] = jnp.zeros((2, WIN, half), x_buf.dtype)
    for copy in copies:
        copy.wait()
    t = lax.rem(z, 2)
    width = half // 2
    here = pl.ds(pl.multiple_of(t * width, 128), width)
    there = pl.ds(pl.multiple_of((1 - t) * width, 128), width)
    for i in range(2):
        rest_ref[i] = x_buf[i, :, there]
    for kind in range(3):
        made_ref[kind] = jnp.dot(
            x_buf[0, :, here], w_buf[kind, 0], preferred_element_type=jnp.float32
        ) + jnp.dot(x_buf[1, :, here], w_buf[kind, 1], preferred_element_type=jnp.float32)


def encode_kernel(made_hbm, rest_hbm, w4, w5, w6, w7, out_ref, *refs):
    made_buf, rest_buf, w_buf, q_buf, k_buf, v_buf, sems = refs
    core, z, y, m = places()
    depth = w4.shape[1]
    wide = w4.shape[2]
    rows = out_ref.shape[1]
    own_rows = 4 * rows
    pairs = [(made_hbm, made_buf), (rest_hbm, rest_buf)]
    for index, piece in enumerate((w4, w5, w6, w7)):
        low, span = weight_rows(4 + index, y, core, depth)
        pairs.append((piece, w_buf.at[:, low, span, :]))
    for copy in start_all(pairs, sems):
        copy.wait()

    def project(kind, first, count):
        total = made_buf[kind, first:first + count, :]
        for i in range(2):
            total = total + jnp.dot(
                rest_buf[i, first:first + count, :],
                w_buf[kind, i],
                preferred_element_type=jnp.float32,
            )
        return total.astype(q_buf.dtype)

    q_buf[...] = project(0, WIN, own_rows)
    k_buf[...] = project(1, 0, own_rows + 2 * WIN)
    v_buf[...] = project(2, 0, own_rows + 2 * WIN)
    keys = rows + 2 * WIN
    a = lax.broadcasted_iota(jnp.int32, (rows, keys), 0)
    b = lax.broadcasted_iota(jnp.int32, (rows, keys), 1)
    band = (b >= a) & (b <= a + 2 * WIN)
    for j in range(4):
        admitted = band
        if j == 0:
            admitted = admitted & (b >= WIN * (1 - core))
        if j == 3:
            admitted = admitted & (b < keys - WIN * core)
        for h in range(wide // HD):
            lanes = slice(h * HD, (h + 1) * HD)
            scores = lax.dot_general(
                q_buf[j * rows:(j + 1) * rows, lanes],
                k_buf[j * rows:j * rows + keys, lanes],
                (((1,), (1,)), ((), ())),
                preferred_element_type=jnp.float32,
            ) * (1.0 / math.sqrt(HD))
            scores = jnp.where(admitted, scores, -jnp.inf)
            peak = jnp.max(scores, axis=-1, keepdims=True)
            exps = jnp.exp(scores - peak)
            attention = (exps / jnp.sum(exps, axis=-1, keepdims=True)).astype(jnp.bfloat16)
            out_ref[j, :, lanes] = jnp.dot(
                attention,
                v_buf[j * rows:j * rows + keys, lanes],
                preferred_element_type=jnp.float32,
            ).astype(out_ref.dtype)


def predict_kernel(slot_ref, lat_ref, own_ref, e0, e1, l0, l1, out_ref):
    core, _, _, m = places()
    wide = lat_ref.shape[2]
    lent = ((e0, e1), (l0, l1))
    total = None
    for side in range(2):
        predicted = None
        for t in range(2):
            for x in range(2):
                if side == 0:
                    source = lat_ref[2 * t + x]
                    weight = own_ref[(2 * x + t) * wide:(2 * x + t + 1) * wide, :]
                else:
                    source = lat_ref[2 * t + (core if x == 0 else 1 - core)]
                    weight = lent[t][x][...]
                term = jnp.dot(source, weight, preferred_element_type=jnp.float32)
                predicted = term if predicted is None else predicted + term
        for t in range(2):
            target = lat_ref[4 + 2 * t + (m if side == 0 else 1 - m)].astype(jnp.float32)
            residue = predicted[:, t * wide:(t + 1) * wide] - target
            for i in range(wide // 128):
                piece = residue[:, i * 128:(i + 1) * 128]
                total = piece * piece if total is None else total + piece * piece
    row_errors = jnp.sum(total, axis=1, keepdims=True)
    rows, slots = total.shape[0], out_ref.shape[2]
    chosen = slot_ref[...] == lax.broadcasted_iota(jnp.int32, (rows, slots), 1)
    routed = jnp.sum(jnp.where(chosen, row_errors, 0.0), axis=0, keepdims=True)
    for i in range(out_ref.shape[0]):
        out_ref[i] = routed


def local_lines(signal, mask_token, keep, target_shard, enc_weight, pred_weight):
    core = lax.axis_index("grp")
    s = lax.axis_index("seq")
    m = lax.axis_index("mdl")
    z, y = s // 2, s % 2
    sequences, length, half = signal.shape
    per_range = keep.shape[1]
    block_len = length // per_range
    depth = enc_weight.shape[2]
    wide = half // 2

    vmem = pl.BlockSpec(memory_space=pltpu.VMEM)
    anywhere = pl.BlockSpec(memory_space=pl.ANY)

    def to_near(c, z, y, m):
        return (1 - z // 2, z % 2 + 2 * c, y, m)

    def to_far(c, z, y, m):
        return (z // 2, 1 - z % 2 + 2 * c, y, m)

    def across_z(c, z, y, m):
        if z // 2 == c:
            return (c, (z + 2) % 4, y, m)
        return (1 - c, z + 1 - 2 * (z % 2), y, m)

    def across_zy(c, z, y, m):
        c, z, y, m = across_z(c, z, y, m)
        return (c, z, 1 - y, m)

    def flip_y(c, z, y, m):
        return (c, z, 1 - y, m)

    def flip_core(c, z, y, m):
        return (1 - c, z, y, m)

    def flip_x(c, z, y, m):
        return (c, z, y, 1 - m)

    def second_hop(c, z, y, m):
        if z // 2 == c:
            return (c, z, 1 - y, m)
        return (c, z + 1 - 2 * (z % 2), y, m)

    cut = half // 2
    mine, given, mine_own, given_own = pl.pallas_call(
        mask_kernel,
        out_shape=[jax.ShapeDtypeStruct((length, half), jnp.bfloat16)] * 4,
        in_specs=[vmem] * 3,
        out_specs=[vmem] * 4,
    )(signal, mask_token, keep)
    near, far, early, late = pl.pallas_call(
        slice_kernel,
        out_shape=[jax.ShapeDtypeStruct(shape, jnp.bfloat16) for shape in (
            (3, depth, wide), (3, depth, wide), (cut, half), (cut, half),
        )],
        in_specs=[anywhere] * 3,
        out_specs=[vmem] * 4,
        scratch_shapes=[pltpu.SemaphoreType.DMA((4,))],
    )(mine, enc_weight, pred_weight)
    first, second = move(mine, across_z), move(given, across_zy)
    small = jnp.stack([keep, target_shard])
    small, _ = lax.optimization_barrier((small, mine))
    routing = move(small, lambda c, z, y, m: ((2 * z + y) // 4, (2 * z + y) % 4, c, m))
    near, routing, first, second = lax.optimization_barrier((near, routing, first, second))
    x_own = jnp.stack([first, second])
    near_w = move(near, to_near)
    weight_early = move(early, flip_x)
    far, x_own = lax.optimization_barrier((far, x_own))
    far_w = move(far, to_far)
    home = core == z // 2
    sent = jnp.where(home, jnp.stack([mine_own, given_own]), x_own)
    come = move(sent, second_hop)
    kept_home = (jnp.arange(2) == 0)[:, None, None] & home
    x_near = jnp.where(kept_home, mine_own[None], come)
    x_across = move(x_own, flip_x)
    near_y_source, weight_early = lax.optimization_barrier((near_w, weight_early))
    near_y = move(near_y_source, flip_y)
    far_y_source, near_y = lax.optimization_barrier((far_w, near_y))
    far_y = move(far_y_source, flip_y)
    weight_early_c = move(weight_early, flip_core)
    x_near, x_across = lax.optimization_barrier((x_near, x_across))
    x_near_across = move(x_near, flip_x)
    late, _ = lax.optimization_barrier((late, x_near_across))
    weight_late = move(late, flip_x)
    weight_late_c = move(weight_late, flip_core)
    hidden = lax.dynamic_index_in_dim(routing[0], y, 0, keepdims=False) == 0
    shard_of = routing[1].reshape(-1)
    blocks = shard_of.shape[0]
    capacity = max(2, 2 * blocks // 8)
    order_ids = jnp.arange(blocks)
    earlier = (shard_of[:, None] == shard_of[None, :]) & (order_ids[:, None] < order_ids[None, :])
    slot = shard_of * capacity + jnp.sum(earlier.astype(jnp.int32), axis=0)
    slot = lax.dynamic_index_in_dim(slot.reshape(sequences, -1), y, 0, keepdims=False)
    slot = jnp.where(hidden, slot, -1)
    slot = lax.dynamic_slice_in_dim(slot, m * (per_range // 2), per_range // 2)
    slot = jnp.repeat(slot, block_len)[:, None]

    def edge(own, near):
        found = jnp.where(jnp.where(home, 1 - z % 2, z % 2) == 1 - core, own, near)
        part = jnp.where(core == 0, 1 - y, y)
        first = jnp.where(core == 0, length - WIN, 0)
        return lax.dynamic_slice(found, (part, first, 0), (1, WIN, half))[0]

    halo = move(jnp.stack([edge(x_own, x_near), edge(x_across, x_near_across)]), flip_core)
    span = 4 * length + 2 * WIN

    large = pltpu.CompilerParams(vmem_limit_bytes=60 * 2**20)
    made, rest = pl.pallas_call(
        partial_kernel,
        out_shape=[
            jax.ShapeDtypeStruct((3, span, wide), jnp.float32),
            jax.ShapeDtypeStruct((2, span, half // 2), jnp.bfloat16),
        ],
        in_specs=[anywhere] * 9,
        out_specs=[vmem] * 2,
        scratch_shapes=[
            pltpu.VMEM((2, span, half), jnp.bfloat16),
            pltpu.VMEM((3, 2, half // 2, wide), jnp.bfloat16),
            pltpu.SemaphoreType.DMA((14,)),
        ],
        compiler_params=large,
    )(
        x_own, x_across, x_near, x_near_across, halo,
        near_w, move(near_w, flip_core), near_y, move(near_y, flip_core),
    )
    far_yc_source, made = lax.optimization_barrier((far_y, made))
    latent = pl.pallas_call(
        encode_kernel,
        out_shape=jax.ShapeDtypeStruct((4, length, wide), jnp.bfloat16),
        in_specs=[anywhere] * 6,
        out_specs=vmem,
        scratch_shapes=[
            pltpu.VMEM((3, span, wide), jnp.float32),
            pltpu.VMEM((2, span, half // 2), jnp.bfloat16),
            pltpu.VMEM((3, 2, half // 2, wide), jnp.bfloat16),
            pltpu.VMEM((4 * length, wide), jnp.bfloat16),
            pltpu.VMEM((span, wide), jnp.bfloat16),
            pltpu.VMEM((span, wide), jnp.bfloat16),
            pltpu.SemaphoreType.DMA((6,)),
        ],
        compiler_params=large,
    )(made, rest, far_w, move(far_w, flip_core), far_y, move(far_yc_source, flip_core))
    lines = [[4 * i + 2 * j + k for i in range(4) for k in range(2)] for j in range(2)]
    latents = lax.all_to_all(
        latent.reshape(8, length // 2, wide), ("seq", "mdl"),
        split_axis=0, concat_axis=0, tiled=True, axis_index_groups=lines,
    )
    routed = pl.pallas_call(
        predict_kernel,
        out_shape=jax.ShapeDtypeStruct((16, 1, 8 * capacity), jnp.float32),
        in_specs=[vmem] * 7,
        out_specs=vmem,
        compiler_params=pltpu.CompilerParams(vmem_limit_bytes=24 * 2**20),
    )(
        slot, latents, pred_weight,
        weight_early, weight_early_c, weight_late, weight_late_c,
    )
    arrived = lax.all_to_all(routed, ("seq", "mdl"), split_axis=0, concat_axis=0, tiled=True)
    mine = lax.dynamic_slice_in_dim(arrived[:, 0], capacity * s, capacity, 1)
    summed = jnp.sum(mine.reshape(4, 4, capacity), axis=1)
    return summed.reshape(1, -1) / float(block_len * 2 * half)


def solution(mesh):
    placed = (
        P(None, "seq", "mdl"),
        P("mdl"),
        P(None, "seq"),
        P(None, "seq"),
        P("grp", None, "seq", "mdl"),
        P(None, "mdl"),
    )
    plan = local_lines if mesh.shape["seq"] == 8 else local
    return jax.shard_map(
        plan, mesh=mesh, in_specs=placed, out_specs=P("seq", "grp"), check_vma=False
    )
```

```python
import functools
import math

import jax
import jax.numpy as jnp
from jax import lax
from jax.experimental import pallas as pl
from jax.experimental.pallas import tpu as pltpu
from jax.sharding import PartitionSpec as P

HD = 128
WIN = 64
AXES = ("grp", "seq", "mdl")
PIECES = 8


def padded(x, sides, width):
    for axis, dim in sides:
        count, length = (lax.axis_size(axis), x.shape[dim])
        up = [(i, (i + 1) % count) for i in range(count - 1)]
        down = [(j, i) for i, j in up]
        last = lax.slice_in_dim(x, length - width, length, axis=dim)
        leading = lax.slice_in_dim(x, 0, width, axis=dim)
        before = lax.ppermute(last, axis, up)
        after = lax.ppermute(leading, axis, down)
        x = jnp.concatenate([before, x, after], axis=dim)
    return x


def predict(context, target, live_flags, pred_weight, divisor):
    flat_rows = context.reshape(-1, context.shape[-1])
    wide_rows = lax.all_gather(flat_rows, "mdl", axis=1, tiled=True)
    predicted = jnp.dot(wide_rows, pred_weight, preferred_element_type=jnp.float32)
    residue = predicted - target.reshape(flat_rows.shape).astype(jnp.float32)
    partial_sums = jnp.sum((residue * residue).reshape(live_flags.shape[0], -1), axis=1)
    summed = lax.psum(partial_sums, "mdl")
    return summed / divisor * live_flags


def local(signal, mask_token, keep, target_shard, enc_weight, pred_weight):
    group_index = lax.axis_index("grp")
    seq_index = lax.axis_index("seq")
    shards = lax.axis_size("seq")
    sequences, length, half_width = signal.shape
    per_range = keep.shape[1]
    block_len = length // per_range
    kept_rows = jnp.repeat(keep, block_len, axis=1)[:, :, None]
    masked_in = jnp.where(kept_rows == 1, signal, mask_token[None, None, :])
    source = jnp.where(group_index == 0, masked_in, signal)
    wide_in = lax.all_gather(source, "mdl", axis=2, tiled=True)
    full_width = wide_in.shape[2]
    flat_in = wide_in.reshape(-1, full_width)
    span = length + 2 * WIN
    weight_all = lax.all_gather(enc_weight, "seq", axis=2, tiled=True)[0]
    queries = jnp.dot(flat_in, weight_all[0], preferred_element_type=jnp.float32).astype(
        jnp.bfloat16
    )
    pair_made = jnp.einsum(
        "nd,cde->cne", flat_in, weight_all[1:], preferred_element_type=jnp.float32
    ).astype(jnp.bfloat16)
    own_pairs = pair_made.reshape(2, sequences, length, half_width)
    pair_rows = padded(own_pairs, (("seq", 2),), WIN)
    head_count = half_width // HD
    query_heads = queries.reshape(sequences, length, head_count, HD)
    key_heads = pair_rows[0].reshape(sequences, span, head_count, HD)
    value_heads = pair_rows[1].reshape(sequences, span, head_count, HD)
    query_pos = seq_index * length + jnp.arange(length)
    key_pos = seq_index * length - WIN + jnp.arange(span)
    total_len = length * shards
    in_window = (
        (jnp.abs(query_pos[:, None] - key_pos[None, :]) <= WIN)
        & (key_pos[None, :] >= 0)
        & (key_pos[None, :] < total_len)
    )
    scores = jnp.einsum(
        "sahd,sbhd->shab", query_heads, key_heads, preferred_element_type=jnp.float32
    ) * (1.0 / math.sqrt(HD))
    scores = jnp.where(in_window[None, None], scores, -jnp.inf)
    row_peak = jnp.max(scores, axis=-1, keepdims=True)
    exp_scores = jnp.exp(scores - row_peak)
    attention = (exp_scores / jnp.sum(exp_scores, axis=-1, keepdims=True)).astype(jnp.bfloat16)
    attended = jnp.einsum(
        "shab,sbhd->sahd", attention, value_heads, preferred_element_type=jnp.float32
    ).astype(jnp.bfloat16)
    latent = attended.reshape(sequences * per_range, block_len, half_width)
    blocks_here = latent.shape[0]
    capacity = max(2, 2 * blocks_here // shards)
    slot_count = shards * capacity
    shard_of = target_shard.reshape(-1)
    masked_flag = (keep.reshape(-1) == 0).astype(jnp.float32)
    order_ids = jnp.arange(blocks_here)
    earlier = (shard_of[:, None] == shard_of[None, :]) & (order_ids[:, None] < order_ids[None, :])
    slot_rank = jnp.sum(earlier.astype(jnp.int32), axis=0)
    slot_index = shard_of * capacity + slot_rank
    onehot = slot_index[None, :] == jnp.arange(slot_count)[:, None]
    divisor = float(block_len * full_width)
    halves = lax.all_to_all(latent[None], "grp", split_axis=1, concat_axis=0, tiled=True)
    half_count = blocks_here // 2
    first_block = group_index * half_count
    own_flags = lax.dynamic_slice_in_dim(masked_flag, first_block, half_count)
    losses = predict(halves[0], halves[1], own_flags, pred_weight, divisor)
    spread = lax.dynamic_update_slice_in_dim(
        jnp.zeros((blocks_here,), jnp.float32), losses, first_block, 0
    )
    slotted = jnp.sum(jnp.where(onehot, spread[None, :], 0.0), axis=1).reshape(shards, capacity)
    arrived = lax.all_to_all(slotted, "seq", split_axis=0, concat_axis=0, tiled=True)
    result = lax.psum_scatter(arrived, "grp", scatter_dimension=0, tiled=True)
    return result.reshape(1, -1)


def move(x, target):
    pairs = []
    for c in range(2):
        for s in range(8):
            for m in range(2):
                c2, z2, y2, m2 = target(c, s // 2, s % 2, m)
                pairs.append(((c * 8 + s) * 2 + m, (c2 * 8 + 2 * z2 + y2) * 2 + m2))
    return lax.ppermute(x, AXES, pairs)


def places():
    s = lax.axis_index("seq")
    return lax.axis_index("grp"), s // 2, lax.rem(s, 2), lax.axis_index("mdl")


def mask_kernel(
    signal_ref, token_ref, keep_ref, mine_ref, given_ref, mine_own_ref, given_own_ref
):
    core, _, y, _ = places()
    length = signal_ref.shape[1]
    blocks = keep_ref.shape[1]
    block_len = length // blocks
    row = lax.broadcasted_iota(jnp.int32, (length, blocks), 0)
    first = lax.broadcasted_iota(jnp.int32, (length, blocks), 1) * block_len
    covers = (row >= first) & (row < first + block_len)
    token = token_ref[...].astype(jnp.float32).reshape(1, -1)
    for other, own, chosen in ((mine_ref, mine_own_ref, y), (given_ref, given_own_ref, 1 - y)):
        kept = jnp.where(covers, keep_ref[pl.ds(chosen, 1), :], 0)
        kept = jnp.sum(kept, axis=1, keepdims=True)
        rows = signal_ref[chosen].astype(jnp.float32)
        other[...] = jnp.where(kept + 1 - core > 0, rows, token).astype(other.dtype)
        own[...] = jnp.where(kept + core > 0, rows, token).astype(own.dtype)


def slice_kernel(after_ref, weight_ref, pred_ref, near_ref, far_ref, early_ref, late_ref, sems):
    core, z, _, _ = places()
    wide = near_ref.shape[2]
    cut = early_ref.shape[0]
    t = lax.rem(z, 2)
    copies = []
    for target, chosen in ((near_ref, t), (far_ref, 1 - t)):
        lanes = pl.ds(pl.multiple_of(chosen * wide, 128), wide)
        copies.append((weight_ref.at[0, :, :, lanes], target))
    for index, target in enumerate((early_ref, late_ref)):
        first = pl.multiple_of((2 * core + index) * cut, 128)
        copies.append((pred_ref.at[pl.ds(first, cut), :], target))
    copies = [
        pltpu.make_async_copy(source, target, sems.at[index])
        for index, (source, target) in enumerate(copies)
    ]
    for copy in copies:
        copy.start()
    for copy in copies:
        copy.wait()


def encode_kernel(x_own, x_across, x_near, x_near_across, halo_ref, *refs):
    pieces = refs[:PIECES]
    out_ref, x_buf, w_buf, q_buf, k_buf, v_buf, sems = refs[PIECES:]
    core, z, y, m = places()
    half = x_own.shape[-1]
    rows = x_own.shape[1]
    depth = pieces[0].shape[1]
    wide = pieces[0].shape[2]
    own_rows = 4 * rows
    copies = []
    side = jnp.where(core == z // 2, 1 - lax.rem(z, 2), lax.rem(z, 2))
    for piece, near, across in (
        (x_own, 0, 0), (x_across, 0, 1), (x_near, 1, 0), (x_near_across, 1, 1)
    ):
        first = WIN + 2 * rows * (side if near == 0 else 1 - side)
        for part in range(2):
            row = pl.multiple_of(first + (y if part == 0 else 1 - y) * rows, 64)
            copies.append((
                piece.at[part], x_buf.at[m if across == 0 else 1 - m, pl.ds(row, rows), :]
            ))
    halo_first = pl.multiple_of((1 - core) * (WIN + own_rows), 64)
    empty_first = pl.multiple_of(core * (WIN + own_rows), 64)
    for across in range(2):
        copies.append((
            halo_ref.at[across],
            x_buf.at[m if across == 0 else 1 - m, pl.ds(halo_first, WIN), :],
        ))
    t = lax.rem(z, 2)
    for index, piece in enumerate(pieces):
        crossed, other = (index // 2) % 2, index % 2
        low = core if (other == 0) == (index >= 4) else 1 - core
        pos_z = 2 * low + (t if index < 4 else 1 - t)
        pos = 2 * pos_z + (y if crossed == 0 else 1 - y)
        copies.append((
            piece, w_buf.at[:, pl.ds(pl.multiple_of(pos * depth, 64), depth), :]
        ))
    started = []
    for index, (source, target) in enumerate(copies):
        copy = pltpu.make_async_copy(source, target, sems.at[index])
        copy.start()
        started.append(copy)
    x_buf[:, pl.ds(empty_first, WIN), :] = jnp.zeros((2, WIN, half), x_buf.dtype)
    for copy in started:
        copy.wait()

    def project(kind, first, count):
        total = None
        for i in range(2):
            term = jnp.dot(
                x_buf[i, first:first + count, :],
                w_buf[kind, i * half:(i + 1) * half, :],
                preferred_element_type=jnp.float32,
            )
            total = term if total is None else total + term
        return total.astype(q_buf.dtype)

    q_buf[...] = project(0, WIN, own_rows)
    k_buf[...] = project(1, 0, own_rows + 2 * WIN)
    v_buf[...] = project(2, 0, own_rows + 2 * WIN)
    keys = rows + 2 * WIN
    a = lax.broadcasted_iota(jnp.int32, (rows, keys), 0)
    b = lax.broadcasted_iota(jnp.int32, (rows, keys), 1)
    band = (b >= a) & (b <= a + 2 * WIN)
    for j in range(4):
        admitted = band
        if j == 0:
            admitted = admitted & (b >= WIN * (1 - core))
        if j == 3:
            admitted = admitted & (b < keys - WIN * core)
        for h in range(wide // HD):
            lanes = slice(h * HD, (h + 1) * HD)
            scores = lax.dot_general(
                q_buf[j * rows:(j + 1) * rows, lanes],
                k_buf[j * rows:j * rows + keys, lanes],
                (((1,), (1,)), ((), ())),
                preferred_element_type=jnp.float32,
            ) * (1.0 / math.sqrt(HD))
            scores = jnp.where(admitted, scores, -jnp.inf)
            peak = jnp.max(scores, axis=-1, keepdims=True)
            exps = jnp.exp(scores - peak)
            attention = (exps / jnp.sum(exps, axis=-1, keepdims=True)).astype(jnp.bfloat16)
            out_ref[j, :, lanes] = jnp.dot(
                attention,
                v_buf[j * rows:j * rows + keys, lanes],
                preferred_element_type=jnp.float32,
            ).astype(out_ref.dtype)


def predict_kernel(slot_ref, lat_ref, own_ref, e0, e1, l0, l1, out_ref):
    core, _, _, m = places()
    wide = lat_ref.shape[2]
    lent = ((e0, e1), (l0, l1))
    total = None
    for side in range(2):
        predicted = None
        for t in range(2):
            for x in range(2):
                if side == 0:
                    source = lat_ref[2 * t + x]
                    weight = own_ref[(2 * x + t) * wide:(2 * x + t + 1) * wide, :]
                else:
                    source = lat_ref[2 * t + (core if x == 0 else 1 - core)]
                    weight = lent[t][x][...]
                term = jnp.dot(source, weight, preferred_element_type=jnp.float32)
                predicted = term if predicted is None else predicted + term
        for t in range(2):
            target = lat_ref[4 + 2 * t + (m if side == 0 else 1 - m)].astype(jnp.float32)
            residue = predicted[:, t * wide:(t + 1) * wide] - target
            for i in range(wide // 128):
                piece = residue[:, i * 128:(i + 1) * 128]
                total = piece * piece if total is None else total + piece * piece
    row_errors = jnp.sum(total, axis=1, keepdims=True)
    rows, slots = total.shape[0], out_ref.shape[2]
    chosen = slot_ref[...] == lax.broadcasted_iota(jnp.int32, (rows, slots), 1)
    routed = jnp.sum(jnp.where(chosen, row_errors, 0.0), axis=0, keepdims=True)
    for i in range(out_ref.shape[0]):
        out_ref[i] = routed


def local_lines(signal, mask_token, keep, target_shard, enc_weight, pred_weight):
    core = lax.axis_index("grp")
    s = lax.axis_index("seq")
    m = lax.axis_index("mdl")
    z, y = s // 2, s % 2
    sequences, length, half = signal.shape
    per_range = keep.shape[1]
    block_len = length // per_range
    depth = enc_weight.shape[2]
    wide = half // 2

    vmem = pl.BlockSpec(memory_space=pltpu.VMEM)
    anywhere = pl.BlockSpec(memory_space=pl.ANY)

    def to_near(c, z, y, m):
        return (1 - z // 2, z % 2 + 2 * c, y, m)

    def to_far(c, z, y, m):
        return (z // 2, 1 - z % 2 + 2 * c, y, m)

    def across_z(c, z, y, m):
        if z // 2 == c:
            return (c, (z + 2) % 4, y, m)
        return (1 - c, z + 1 - 2 * (z % 2), y, m)

    def across_zy(c, z, y, m):
        c, z, y, m = across_z(c, z, y, m)
        return (c, z, 1 - y, m)

    def flip_y(c, z, y, m):
        return (c, z, 1 - y, m)

    def flip_core(c, z, y, m):
        return (1 - c, z, y, m)

    def flip_x(c, z, y, m):
        return (c, z, y, 1 - m)

    def second_hop(c, z, y, m):
        if z // 2 == c:
            return (c, z, 1 - y, m)
        return (c, z + 1 - 2 * (z % 2), y, m)

    cut = half // 2
    mine, given, mine_own, given_own = pl.pallas_call(
        mask_kernel,
        out_shape=[jax.ShapeDtypeStruct((length, half), jnp.bfloat16)] * 4,
        in_specs=[vmem] * 3,
        out_specs=[vmem] * 4,
    )(signal, mask_token, keep)
    near, far, early, late = pl.pallas_call(
        slice_kernel,
        out_shape=[jax.ShapeDtypeStruct(shape, jnp.bfloat16) for shape in (
            (3, depth, wide), (3, depth, wide), (cut, half), (cut, half),
        )],
        in_specs=[anywhere] * 3,
        out_specs=[vmem] * 4,
        scratch_shapes=[pltpu.SemaphoreType.DMA((4,))],
    )(mine, enc_weight, pred_weight)
    first, second = move(mine, across_z), move(given, across_zy)
    small = jnp.stack([keep, target_shard])
    small, _ = lax.optimization_barrier((small, mine))
    routing = move(small, lambda c, z, y, m: ((2 * z + y) // 4, (2 * z + y) % 4, c, m))
    near, routing, first, second = lax.optimization_barrier((near, routing, first, second))
    x_own = jnp.stack([first, second])
    near_w = move(near, to_near)
    weight_early = move(early, flip_x)
    far, x_own = lax.optimization_barrier((far, x_own))
    far_w = move(far, to_far)
    home = core == z // 2
    sent = jnp.where(home, jnp.stack([mine_own, given_own]), x_own)
    come = move(sent, second_hop)
    kept_home = (jnp.arange(2) == 0)[:, None, None] & home
    x_near = jnp.where(kept_home, mine_own[None], come)
    x_across = move(x_own, flip_x)
    near_y_source, weight_early = lax.optimization_barrier((near_w, weight_early))
    near_y = move(near_y_source, flip_y)
    far_y_source, near_y = lax.optimization_barrier((far_w, near_y))
    far_y = move(far_y_source, flip_y)
    weight_early_c = move(weight_early, flip_core)
    x_near_across = move(x_near, flip_x)
    late, _ = lax.optimization_barrier((late, x_near_across))
    weight_late = move(late, flip_x)
    weight_late_c = move(weight_late, flip_core)
    hidden = lax.dynamic_index_in_dim(routing[0], y, 0, keepdims=False) == 0
    shard_of = routing[1].reshape(-1)
    blocks = shard_of.shape[0]
    capacity = max(2, 2 * blocks // 8)
    order_ids = jnp.arange(blocks)
    earlier = (shard_of[:, None] == shard_of[None, :]) & (order_ids[:, None] < order_ids[None, :])
    slot = shard_of * capacity + jnp.sum(earlier.astype(jnp.int32), axis=0)
    slot = lax.dynamic_index_in_dim(slot.reshape(sequences, -1), y, 0, keepdims=False)
    slot = jnp.where(hidden, slot, -1)
    slot = lax.dynamic_slice_in_dim(slot, m * (per_range // 2), per_range // 2)
    slot = jnp.repeat(slot, block_len)[:, None]

    def edge(own, near):
        found = jnp.where(jnp.where(home, 1 - z % 2, z % 2) == 1 - core, own, near)
        part = jnp.where(core == 0, 1 - y, y)
        first = jnp.where(core == 0, length - WIN, 0)
        return lax.dynamic_slice(found, (part, first, 0), (1, WIN, half))[0]

    halo = move(jnp.stack([edge(x_own, x_near), edge(x_across, x_near_across)]), flip_core)
    far_yc_source, halo = lax.optimization_barrier((far_y, halo))
    pieces = [
        near_w, move(near_w, flip_core), near_y, move(near_y, flip_core),
        far_w, move(far_w, flip_core), far_y, move(far_yc_source, flip_core),
    ]
    span = 4 * length + 2 * WIN

    latent = pl.pallas_call(
        encode_kernel,
        out_shape=jax.ShapeDtypeStruct((4, length, wide), jnp.bfloat16),
        in_specs=[anywhere] * (5 + PIECES),
        out_specs=vmem,
        scratch_shapes=[
            pltpu.VMEM((2, span, half), jnp.bfloat16),
            pltpu.VMEM((3, 2 * half, wide), jnp.bfloat16),
            pltpu.VMEM((4 * length, wide), jnp.bfloat16),
            pltpu.VMEM((span, wide), jnp.bfloat16),
            pltpu.VMEM((span, wide), jnp.bfloat16),
            pltpu.SemaphoreType.DMA((10 + PIECES,)),
        ],
        compiler_params=pltpu.CompilerParams(vmem_limit_bytes=60 * 2**20),
    )(x_own, x_across, x_near, x_near_across, halo, *pieces)
    lines = [[4 * i + 2 * j + k for i in range(4) for k in range(2)] for j in range(2)]
    latents = lax.all_to_all(
        latent.reshape(8, length // 2, wide), ("seq", "mdl"),
        split_axis=0, concat_axis=0, tiled=True, axis_index_groups=lines,
    )
    routed = pl.pallas_call(
        predict_kernel,
        out_shape=jax.ShapeDtypeStruct((16, 1, 8 * capacity), jnp.float32),
        in_specs=[vmem] * 7,
        out_specs=vmem,
        compiler_params=pltpu.CompilerParams(vmem_limit_bytes=24 * 2**20),
    )(
        slot, latents, pred_weight,
        weight_early, weight_early_c, weight_late, weight_late_c,
    )
    arrived = lax.all_to_all(routed, ("seq", "mdl"), split_axis=0, concat_axis=0, tiled=True)
    mine = lax.dynamic_slice_in_dim(arrived[:, 0], capacity * s, capacity, 1)
    summed = jnp.sum(mine.reshape(4, 4, capacity), axis=1)
    return summed.reshape(1, -1) / float(block_len * 2 * half)


def solution(mesh):
    placed = (
        P(None, "seq", "mdl"),
        P("mdl"),
        P(None, "seq"),
        P(None, "seq"),
        P("grp", None, "seq", "mdl"),
        P(None, "mdl"),
    )
    plan = local_lines if mesh.shape["seq"] == 8 else local
    return jax.shard_map(
        plan, mesh=mesh, in_specs=placed, out_specs=P("seq", "grp"), check_vma=False
    )
```

```python
import functools
import math

import jax
import jax.numpy as jnp
from jax import lax
from jax.experimental import pallas as pl
from jax.experimental.pallas import tpu as pltpu
from jax.sharding import PartitionSpec as P

HD = 128
WIN = 64
AXES = ("grp", "seq", "mdl")
PIECES = 8


def padded(x, sides, width):
    for axis, dim in sides:
        count, length = (lax.axis_size(axis), x.shape[dim])
        up = [(i, (i + 1) % count) for i in range(count - 1)]
        down = [(j, i) for i, j in up]
        last = lax.slice_in_dim(x, length - width, length, axis=dim)
        leading = lax.slice_in_dim(x, 0, width, axis=dim)
        before = lax.ppermute(last, axis, up)
        after = lax.ppermute(leading, axis, down)
        x = jnp.concatenate([before, x, after], axis=dim)
    return x


def predict(context, target, live_flags, pred_weight, divisor):
    flat_rows = context.reshape(-1, context.shape[-1])
    wide_rows = lax.all_gather(flat_rows, "mdl", axis=1, tiled=True)
    predicted = jnp.dot(wide_rows, pred_weight, preferred_element_type=jnp.float32)
    residue = predicted - target.reshape(flat_rows.shape).astype(jnp.float32)
    partial_sums = jnp.sum((residue * residue).reshape(live_flags.shape[0], -1), axis=1)
    summed = lax.psum(partial_sums, "mdl")
    return summed / divisor * live_flags


def local(signal, mask_token, keep, target_shard, enc_weight, pred_weight):
    group_index = lax.axis_index("grp")
    seq_index = lax.axis_index("seq")
    shards = lax.axis_size("seq")
    sequences, length, half_width = signal.shape
    per_range = keep.shape[1]
    block_len = length // per_range
    kept_rows = jnp.repeat(keep, block_len, axis=1)[:, :, None]
    masked_in = jnp.where(kept_rows == 1, signal, mask_token[None, None, :])
    source = jnp.where(group_index == 0, masked_in, signal)
    wide_in = lax.all_gather(source, "mdl", axis=2, tiled=True)
    full_width = wide_in.shape[2]
    flat_in = wide_in.reshape(-1, full_width)
    span = length + 2 * WIN
    weight_all = lax.all_gather(enc_weight, "seq", axis=2, tiled=True)[0]
    queries = jnp.dot(flat_in, weight_all[0], preferred_element_type=jnp.float32).astype(
        jnp.bfloat16
    )
    pair_made = jnp.einsum(
        "nd,cde->cne", flat_in, weight_all[1:], preferred_element_type=jnp.float32
    ).astype(jnp.bfloat16)
    own_pairs = pair_made.reshape(2, sequences, length, half_width)
    pair_rows = padded(own_pairs, (("seq", 2),), WIN)
    head_count = half_width // HD
    query_heads = queries.reshape(sequences, length, head_count, HD)
    key_heads = pair_rows[0].reshape(sequences, span, head_count, HD)
    value_heads = pair_rows[1].reshape(sequences, span, head_count, HD)
    query_pos = seq_index * length + jnp.arange(length)
    key_pos = seq_index * length - WIN + jnp.arange(span)
    total_len = length * shards
    in_window = (
        (jnp.abs(query_pos[:, None] - key_pos[None, :]) <= WIN)
        & (key_pos[None, :] >= 0)
        & (key_pos[None, :] < total_len)
    )
    scores = jnp.einsum(
        "sahd,sbhd->shab", query_heads, key_heads, preferred_element_type=jnp.float32
    ) * (1.0 / math.sqrt(HD))
    scores = jnp.where(in_window[None, None], scores, -jnp.inf)
    row_peak = jnp.max(scores, axis=-1, keepdims=True)
    exp_scores = jnp.exp(scores - row_peak)
    attention = (exp_scores / jnp.sum(exp_scores, axis=-1, keepdims=True)).astype(jnp.bfloat16)
    attended = jnp.einsum(
        "shab,sbhd->sahd", attention, value_heads, preferred_element_type=jnp.float32
    ).astype(jnp.bfloat16)
    latent = attended.reshape(sequences * per_range, block_len, half_width)
    blocks_here = latent.shape[0]
    capacity = max(2, 2 * blocks_here // shards)
    slot_count = shards * capacity
    shard_of = target_shard.reshape(-1)
    masked_flag = (keep.reshape(-1) == 0).astype(jnp.float32)
    order_ids = jnp.arange(blocks_here)
    earlier = (shard_of[:, None] == shard_of[None, :]) & (order_ids[:, None] < order_ids[None, :])
    slot_rank = jnp.sum(earlier.astype(jnp.int32), axis=0)
    slot_index = shard_of * capacity + slot_rank
    onehot = slot_index[None, :] == jnp.arange(slot_count)[:, None]
    divisor = float(block_len * full_width)
    halves = lax.all_to_all(latent[None], "grp", split_axis=1, concat_axis=0, tiled=True)
    half_count = blocks_here // 2
    first_block = group_index * half_count
    own_flags = lax.dynamic_slice_in_dim(masked_flag, first_block, half_count)
    losses = predict(halves[0], halves[1], own_flags, pred_weight, divisor)
    spread = lax.dynamic_update_slice_in_dim(
        jnp.zeros((blocks_here,), jnp.float32), losses, first_block, 0
    )
    slotted = jnp.sum(jnp.where(onehot, spread[None, :], 0.0), axis=1).reshape(shards, capacity)
    arrived = lax.all_to_all(slotted, "seq", split_axis=0, concat_axis=0, tiled=True)
    result = lax.psum_scatter(arrived, "grp", scatter_dimension=0, tiled=True)
    return result.reshape(1, -1)


def move(x, target):
    pairs = []
    for c in range(2):
        for s in range(8):
            for m in range(2):
                c2, z2, y2, m2 = target(c, s // 2, s % 2, m)
                pairs.append(((c * 8 + s) * 2 + m, (c2 * 8 + 2 * z2 + y2) * 2 + m2))
    return lax.ppermute(x, AXES, pairs)


def places():
    s = lax.axis_index("seq")
    return lax.axis_index("grp"), s // 2, lax.rem(s, 2), lax.axis_index("mdl")


def mask_kernel(
    signal_ref, token_ref, keep_ref, mine_ref, given_ref, mine_own_ref, given_own_ref
):
    core, _, y, _ = places()
    length = signal_ref.shape[1]
    blocks = keep_ref.shape[1]
    block_len = length // blocks
    row = lax.broadcasted_iota(jnp.int32, (length, blocks), 0)
    first = lax.broadcasted_iota(jnp.int32, (length, blocks), 1) * block_len
    covers = (row >= first) & (row < first + block_len)
    token = token_ref[...].astype(jnp.float32).reshape(1, -1)
    for other, own, chosen in ((mine_ref, mine_own_ref, y), (given_ref, given_own_ref, 1 - y)):
        kept = jnp.where(covers, keep_ref[pl.ds(chosen, 1), :], 0)
        kept = jnp.sum(kept, axis=1, keepdims=True)
        rows = signal_ref[chosen].astype(jnp.float32)
        other[...] = jnp.where(kept + 1 - core > 0, rows, token).astype(other.dtype)
        own[...] = jnp.where(kept + core > 0, rows, token).astype(own.dtype)


def slice_kernel(after_ref, weight_ref, pred_ref, near_ref, far_ref, early_ref, late_ref, sems):
    core, z, _, _ = places()
    wide = near_ref.shape[2]
    t = lax.rem(z, 2)
    copies = []
    for target, chosen in ((near_ref, t), (far_ref, 1 - t)):
        lanes = pl.ds(pl.multiple_of(chosen * wide, 128), wide)
        copies.append((weight_ref.at[0, :, :, lanes], target))
    count = early_ref.shape[0] + late_ref.shape[0]
    for target, skipped in ((early_ref, 0), (late_ref, early_ref.shape[0])):
        first = pl.multiple_of(core * count + skipped, 128)
        copies.append((pred_ref.at[pl.ds(first, target.shape[0]), :], target))
    copies = [
        pltpu.make_async_copy(source, target, sems.at[index])
        for index, (source, target) in enumerate(copies)
    ]
    for copy in copies:
        copy.start()
    for copy in copies:
        copy.wait()


def encode_kernel(x_own, x_across, x_near, x_near_across, halo_ref, *refs):
    pieces = refs[:PIECES]
    out_ref, x_buf, w_buf, q_buf, k_buf, v_buf, sems = refs[PIECES:]
    core, z, y, m = places()
    half = x_own.shape[-1]
    rows = x_own.shape[1]
    depth = pieces[0].shape[1]
    wide = pieces[0].shape[2]
    own_rows = 4 * rows
    copies = []
    side = jnp.where(core == z // 2, 1 - lax.rem(z, 2), lax.rem(z, 2))
    for piece, near, across in (
        (x_own, 0, 0), (x_across, 0, 1), (x_near, 1, 0), (x_near_across, 1, 1)
    ):
        first = WIN + 2 * rows * (side if near == 0 else 1 - side)
        for part in range(2):
            row = pl.multiple_of(first + (y if part == 0 else 1 - y) * rows, 64)
            copies.append((
                piece.at[part], x_buf.at[m if across == 0 else 1 - m, pl.ds(row, rows), :]
            ))
    halo_first = pl.multiple_of((1 - core) * (WIN + own_rows), 64)
    empty_first = pl.multiple_of(core * (WIN + own_rows), 64)
    for across in range(2):
        copies.append((
            halo_ref.at[across],
            x_buf.at[m if across == 0 else 1 - m, pl.ds(halo_first, WIN), :],
        ))
    t = lax.rem(z, 2)
    for index, piece in enumerate(pieces):
        crossed, other = (index // 2) % 2, index % 2
        low = core if (other == 0) == (index >= 4) else 1 - core
        pos_z = 2 * low + (t if index < 4 else 1 - t)
        pos = 2 * pos_z + (y if crossed == 0 else 1 - y)
        copies.append((
            piece, w_buf.at[:, pl.ds(pl.multiple_of(pos * depth, 64), depth), :]
        ))
    started = []
    for index, (source, target) in enumerate(copies):
        copy = pltpu.make_async_copy(source, target, sems.at[index])
        copy.start()
        started.append(copy)
    x_buf[:, pl.ds(empty_first, WIN), :] = jnp.zeros((2, WIN, half), x_buf.dtype)
    for copy in started:
        copy.wait()

    def project(kind, first, count):
        total = None
        for i in range(2):
            term = jnp.dot(
                x_buf[i, first:first + count, :],
                w_buf[kind, i * half:(i + 1) * half, :],
                preferred_element_type=jnp.float32,
            )
            total = term if total is None else total + term
        return total.astype(q_buf.dtype)

    q_buf[...] = project(0, WIN, own_rows)
    k_buf[...] = project(1, 0, own_rows + 2 * WIN)
    v_buf[...] = project(2, 0, own_rows + 2 * WIN)
    keys = rows + 2 * WIN
    a = lax.broadcasted_iota(jnp.int32, (rows, keys), 0)
    b = lax.broadcasted_iota(jnp.int32, (rows, keys), 1)
    band = (b >= a) & (b <= a + 2 * WIN)
    for j in range(4):
        admitted = band
        if j == 0:
            admitted = admitted & (b >= WIN * (1 - core))
        if j == 3:
            admitted = admitted & (b < keys - WIN * core)
        for h in range(wide // HD):
            lanes = slice(h * HD, (h + 1) * HD)
            scores = lax.dot_general(
                q_buf[j * rows:(j + 1) * rows, lanes],
                k_buf[j * rows:j * rows + keys, lanes],
                (((1,), (1,)), ((), ())),
                preferred_element_type=jnp.float32,
            ) * (1.0 / math.sqrt(HD))
            scores = jnp.where(admitted, scores, -jnp.inf)
            peak = jnp.max(scores, axis=-1, keepdims=True)
            exps = jnp.exp(scores - peak)
            attention = (exps / jnp.sum(exps, axis=-1, keepdims=True)).astype(jnp.bfloat16)
            out_ref[j, :, lanes] = jnp.dot(
                attention,
                v_buf[j * rows:j * rows + keys, lanes],
                preferred_element_type=jnp.float32,
            ).astype(out_ref.dtype)


def predict_kernel(slot_ref, lat_ref, own_ref, *refs):
    lent, out_ref = (refs[:3], refs[3:6]), refs[6]
    core, _, _, m = places()
    wide = lat_ref.shape[2]
    cut = lent[0][0].shape[0]
    total = None
    for side in range(2):
        terms = []
        for t in range(2):
            for x in range(2):
                if side == 0:
                    source = lat_ref[2 * t + x]
                    terms.append((source, own_ref[(2 * x + t) * wide:(2 * x + t + 1) * wide, :]))
                    continue
                source = lat_ref[2 * t + (core if x == 0 else 1 - core)]
                first, second, third = lent[x]
                if t == 0:
                    terms.append((source[:, :cut], first[...]))
                    terms.append((source[:, cut:], second[:wide - cut, :]))
                else:
                    terms.append((source[:, :wide - cut], second[wide - cut:, :]))
                    terms.append((source[:, wide - cut:], third[...]))
        predicted = None
        for source, weight in terms:
            term = jnp.dot(source, weight, preferred_element_type=jnp.float32)
            predicted = term if predicted is None else predicted + term
        for t in range(2):
            target = lat_ref[4 + 2 * t + (m if side == 0 else 1 - m)].astype(jnp.float32)
            residue = predicted[:, t * wide:(t + 1) * wide] - target
            for i in range(wide // 128):
                piece = residue[:, i * 128:(i + 1) * 128]
                total = piece * piece if total is None else total + piece * piece
    row_errors = jnp.sum(total, axis=1, keepdims=True)
    rows, slots = total.shape[0], out_ref.shape[2]
    chosen = slot_ref[...] == lax.broadcasted_iota(jnp.int32, (rows, slots), 1)
    routed = jnp.sum(jnp.where(chosen, row_errors, 0.0), axis=0, keepdims=True)
    for i in range(out_ref.shape[0]):
        out_ref[i] = routed


def local_lines(signal, mask_token, keep, target_shard, enc_weight, pred_weight):
    core = lax.axis_index("grp")
    s = lax.axis_index("seq")
    m = lax.axis_index("mdl")
    z, y = s // 2, s % 2
    sequences, length, half = signal.shape
    per_range = keep.shape[1]
    block_len = length // per_range
    depth = enc_weight.shape[2]
    wide = half // 2

    vmem = pl.BlockSpec(memory_space=pltpu.VMEM)
    anywhere = pl.BlockSpec(memory_space=pl.ANY)

    def to_near(c, z, y, m):
        return (1 - z // 2, z % 2 + 2 * c, y, m)

    def to_far(c, z, y, m):
        return (z // 2, 1 - z % 2 + 2 * c, y, m)

    def across_z(c, z, y, m):
        if z // 2 == c:
            return (c, (z + 2) % 4, y, m)
        return (1 - c, z + 1 - 2 * (z % 2), y, m)

    def across_zy(c, z, y, m):
        c, z, y, m = across_z(c, z, y, m)
        return (c, z, 1 - y, m)

    def flip_y(c, z, y, m):
        return (c, z, 1 - y, m)

    def flip_core(c, z, y, m):
        return (1 - c, z, y, m)

    def flip_x(c, z, y, m):
        return (c, z, y, 1 - m)

    def second_hop(c, z, y, m):
        if z // 2 == c:
            return (c, z, 1 - y, m)
        return (c, z + 1 - 2 * (z % 2), y, m)

    cut = half // 3
    mine, given, mine_own, given_own = pl.pallas_call(
        mask_kernel,
        out_shape=[jax.ShapeDtypeStruct((length, half), jnp.bfloat16)] * 4,
        in_specs=[vmem] * 3,
        out_specs=[vmem] * 4,
    )(signal, mask_token, keep)
    near, far, early, late = pl.pallas_call(
        slice_kernel,
        out_shape=[jax.ShapeDtypeStruct(shape, jnp.bfloat16) for shape in (
            (3, depth, wide), (3, depth, wide), (cut, half), (half - cut, half),
        )],
        in_specs=[anywhere] * 3,
        out_specs=[vmem] * 4,
        scratch_shapes=[pltpu.SemaphoreType.DMA((4,))],
    )(mine, enc_weight, pred_weight)
    first, second = move(mine, across_z), move(given, across_zy)
    small = jnp.stack([keep, target_shard])
    small, _ = lax.optimization_barrier((small, mine))
    routing = move(small, lambda c, z, y, m: ((2 * z + y) // 4, (2 * z + y) % 4, c, m))
    near, routing, first, second = lax.optimization_barrier((near, routing, first, second))
    x_own = jnp.stack([first, second])
    near_w = move(near, to_near)
    weight_early = move(early, flip_x)
    far, x_own = lax.optimization_barrier((far, x_own))
    far_w = move(far, to_far)
    home = core == z // 2
    sent = jnp.where(home, jnp.stack([mine_own, given_own]), x_own)
    come = move(sent, second_hop)
    kept_home = (jnp.arange(2) == 0)[:, None, None] & home
    x_near = jnp.where(kept_home, mine_own[None], come)
    x_across = move(x_own, flip_x)
    near_y_source, weight_early = lax.optimization_barrier((near_w, weight_early))
    near_y = move(near_y_source, flip_y)
    far_y_source, near_y = lax.optimization_barrier((far_w, near_y))
    far_y = move(far_y_source, flip_y)
    x_near_across = move(x_near, flip_x)
    late, _ = lax.optimization_barrier((late, x_near_across))
    columns = [weight_early, move(late[:cut], flip_x), move(late[cut:], flip_x)]
    columns += [move(piece, flip_core) for piece in columns]
    hidden = lax.dynamic_index_in_dim(routing[0], y, 0, keepdims=False) == 0
    shard_of = routing[1].reshape(-1)
    blocks = shard_of.shape[0]
    capacity = max(2, 2 * blocks // 8)
    order_ids = jnp.arange(blocks)
    earlier = (shard_of[:, None] == shard_of[None, :]) & (order_ids[:, None] < order_ids[None, :])
    slot = shard_of * capacity + jnp.sum(earlier.astype(jnp.int32), axis=0)
    slot = lax.dynamic_index_in_dim(slot.reshape(sequences, -1), y, 0, keepdims=False)
    slot = jnp.where(hidden, slot, -1)
    slot = lax.dynamic_slice_in_dim(slot, m * (per_range // 2), per_range // 2)
    slot = jnp.repeat(slot, block_len)[:, None]

    def edge(own, near):
        found = jnp.where(jnp.where(home, 1 - z % 2, z % 2) == 1 - core, own, near)
        part = jnp.where(core == 0, 1 - y, y)
        first = jnp.where(core == 0, length - WIN, 0)
        return lax.dynamic_slice(found, (part, first, 0), (1, WIN, half))[0]

    halo = move(jnp.stack([edge(x_own, x_near), edge(x_across, x_near_across)]), flip_core)
    far_yc_source, halo = lax.optimization_barrier((far_y, halo))
    pieces = [
        near_w, move(near_w, flip_core), near_y, move(near_y, flip_core),
        far_w, move(far_w, flip_core), far_y, move(far_yc_source, flip_core),
    ]
    span = 4 * length + 2 * WIN

    latent = pl.pallas_call(
        encode_kernel,
        out_shape=jax.ShapeDtypeStruct((4, length, wide), jnp.bfloat16),
        in_specs=[anywhere] * (5 + PIECES),
        out_specs=vmem,
        scratch_shapes=[
            pltpu.VMEM((2, span, half), jnp.bfloat16),
            pltpu.VMEM((3, 2 * half, wide), jnp.bfloat16),
            pltpu.VMEM((4 * length, wide), jnp.bfloat16),
            pltpu.VMEM((span, wide), jnp.bfloat16),
            pltpu.VMEM((span, wide), jnp.bfloat16),
            pltpu.SemaphoreType.DMA((10 + PIECES,)),
        ],
        compiler_params=pltpu.CompilerParams(vmem_limit_bytes=60 * 2**20),
    )(x_own, x_across, x_near, x_near_across, halo, *pieces)
    lines = [[4 * i + 2 * j + k for i in range(4) for k in range(2)] for j in range(2)]
    latents = lax.all_to_all(
        latent.reshape(8, length // 2, wide), ("seq", "mdl"),
        split_axis=0, concat_axis=0, tiled=True, axis_index_groups=lines,
    )
    routed = pl.pallas_call(
        predict_kernel,
        out_shape=jax.ShapeDtypeStruct((16, 1, 8 * capacity), jnp.float32),
        in_specs=[vmem] * 9,
        out_specs=vmem,
        compiler_params=pltpu.CompilerParams(vmem_limit_bytes=24 * 2**20),
    )(
        slot, latents, pred_weight,
        *columns,
    )
    arrived = lax.all_to_all(routed, ("seq", "mdl"), split_axis=0, concat_axis=0, tiled=True)
    mine = lax.dynamic_slice_in_dim(arrived[:, 0], capacity * s, capacity, 1)
    summed = jnp.sum(mine.reshape(4, 4, capacity), axis=1)
    return summed.reshape(1, -1) / float(block_len * 2 * half)


def solution(mesh):
    placed = (
        P(None, "seq", "mdl"),
        P("mdl"),
        P(None, "seq"),
        P(None, "seq"),
        P("grp", None, "seq", "mdl"),
        P(None, "mdl"),
    )
    plan = local_lines if mesh.shape["seq"] == 8 else local
    return jax.shard_map(
        plan, mesh=mesh, in_specs=placed, out_specs=P("seq", "grp"), check_vma=False
    )
```

```python
import functools
import math

import jax
import jax.numpy as jnp
from jax import lax
from jax.experimental import pallas as pl
from jax.experimental.pallas import tpu as pltpu
from jax.sharding import PartitionSpec as P

HD = 128
WIN = 64
AXES = ("grp", "seq", "mdl")
PIECES = 8


def padded(x, sides, width):
    for axis, dim in sides:
        count, length = (lax.axis_size(axis), x.shape[dim])
        up = [(i, (i + 1) % count) for i in range(count - 1)]
        down = [(j, i) for i, j in up]
        last = lax.slice_in_dim(x, length - width, length, axis=dim)
        leading = lax.slice_in_dim(x, 0, width, axis=dim)
        before = lax.ppermute(last, axis, up)
        after = lax.ppermute(leading, axis, down)
        x = jnp.concatenate([before, x, after], axis=dim)
    return x


def predict(context, target, live_flags, pred_weight, divisor):
    flat_rows = context.reshape(-1, context.shape[-1])
    wide_rows = lax.all_gather(flat_rows, "mdl", axis=1, tiled=True)
    predicted = jnp.dot(wide_rows, pred_weight, preferred_element_type=jnp.float32)
    residue = predicted - target.reshape(flat_rows.shape).astype(jnp.float32)
    partial_sums = jnp.sum((residue * residue).reshape(live_flags.shape[0], -1), axis=1)
    summed = lax.psum(partial_sums, "mdl")
    return summed / divisor * live_flags


def local(signal, mask_token, keep, target_shard, enc_weight, pred_weight):
    group_index = lax.axis_index("grp")
    seq_index = lax.axis_index("seq")
    shards = lax.axis_size("seq")
    sequences, length, half_width = signal.shape
    per_range = keep.shape[1]
    block_len = length // per_range
    kept_rows = jnp.repeat(keep, block_len, axis=1)[:, :, None]
    masked_in = jnp.where(kept_rows == 1, signal, mask_token[None, None, :])
    source = jnp.where(group_index == 0, masked_in, signal)
    wide_in = lax.all_gather(source, "mdl", axis=2, tiled=True)
    full_width = wide_in.shape[2]
    flat_in = wide_in.reshape(-1, full_width)
    span = length + 2 * WIN
    weight_all = lax.all_gather(enc_weight, "seq", axis=2, tiled=True)[0]
    queries = jnp.dot(flat_in, weight_all[0], preferred_element_type=jnp.float32).astype(
        jnp.bfloat16
    )
    pair_made = jnp.einsum(
        "nd,cde->cne", flat_in, weight_all[1:], preferred_element_type=jnp.float32
    ).astype(jnp.bfloat16)
    own_pairs = pair_made.reshape(2, sequences, length, half_width)
    pair_rows = padded(own_pairs, (("seq", 2),), WIN)
    head_count = half_width // HD
    query_heads = queries.reshape(sequences, length, head_count, HD)
    key_heads = pair_rows[0].reshape(sequences, span, head_count, HD)
    value_heads = pair_rows[1].reshape(sequences, span, head_count, HD)
    query_pos = seq_index * length + jnp.arange(length)
    key_pos = seq_index * length - WIN + jnp.arange(span)
    total_len = length * shards
    in_window = (
        (jnp.abs(query_pos[:, None] - key_pos[None, :]) <= WIN)
        & (key_pos[None, :] >= 0)
        & (key_pos[None, :] < total_len)
    )
    scores = jnp.einsum(
        "sahd,sbhd->shab", query_heads, key_heads, preferred_element_type=jnp.float32
    ) * (1.0 / math.sqrt(HD))
    scores = jnp.where(in_window[None, None], scores, -jnp.inf)
    row_peak = jnp.max(scores, axis=-1, keepdims=True)
    exp_scores = jnp.exp(scores - row_peak)
    attention = (exp_scores / jnp.sum(exp_scores, axis=-1, keepdims=True)).astype(jnp.bfloat16)
    attended = jnp.einsum(
        "shab,sbhd->sahd", attention, value_heads, preferred_element_type=jnp.float32
    ).astype(jnp.bfloat16)
    latent = attended.reshape(sequences * per_range, block_len, half_width)
    blocks_here = latent.shape[0]
    capacity = max(2, 2 * blocks_here // shards)
    slot_count = shards * capacity
    shard_of = target_shard.reshape(-1)
    masked_flag = (keep.reshape(-1) == 0).astype(jnp.float32)
    order_ids = jnp.arange(blocks_here)
    earlier = (shard_of[:, None] == shard_of[None, :]) & (order_ids[:, None] < order_ids[None, :])
    slot_rank = jnp.sum(earlier.astype(jnp.int32), axis=0)
    slot_index = shard_of * capacity + slot_rank
    onehot = slot_index[None, :] == jnp.arange(slot_count)[:, None]
    divisor = float(block_len * full_width)
    halves = lax.all_to_all(latent[None], "grp", split_axis=1, concat_axis=0, tiled=True)
    half_count = blocks_here // 2
    first_block = group_index * half_count
    own_flags = lax.dynamic_slice_in_dim(masked_flag, first_block, half_count)
    losses = predict(halves[0], halves[1], own_flags, pred_weight, divisor)
    spread = lax.dynamic_update_slice_in_dim(
        jnp.zeros((blocks_here,), jnp.float32), losses, first_block, 0
    )
    slotted = jnp.sum(jnp.where(onehot, spread[None, :], 0.0), axis=1).reshape(shards, capacity)
    arrived = lax.all_to_all(slotted, "seq", split_axis=0, concat_axis=0, tiled=True)
    result = lax.psum_scatter(arrived, "grp", scatter_dimension=0, tiled=True)
    return result.reshape(1, -1)


def move(x, target):
    pairs = []
    for c in range(2):
        for s in range(8):
            for m in range(2):
                c2, z2, y2, m2 = target(c, s // 2, s % 2, m)
                pairs.append(((c * 8 + s) * 2 + m, (c2 * 8 + 2 * z2 + y2) * 2 + m2))
    return lax.ppermute(x, AXES, pairs)


def places():
    s = lax.axis_index("seq")
    return lax.axis_index("grp"), s // 2, lax.rem(s, 2), lax.axis_index("mdl")


def mask_kernel(
    signal_ref, token_ref, keep_ref, mine_ref, given_ref, mine_own_ref, given_own_ref
):
    core, _, y, _ = places()
    length = signal_ref.shape[1]
    blocks = keep_ref.shape[1]
    block_len = length // blocks
    row = lax.broadcasted_iota(jnp.int32, (length, blocks), 0)
    first = lax.broadcasted_iota(jnp.int32, (length, blocks), 1) * block_len
    covers = (row >= first) & (row < first + block_len)
    token = token_ref[...].astype(jnp.float32).reshape(1, -1)
    for other, own, chosen in ((mine_ref, mine_own_ref, y), (given_ref, given_own_ref, 1 - y)):
        kept = jnp.where(covers, keep_ref[pl.ds(chosen, 1), :], 0)
        kept = jnp.sum(kept, axis=1, keepdims=True)
        rows = signal_ref[chosen].astype(jnp.float32)
        other[...] = jnp.where(kept + 1 - core > 0, rows, token).astype(other.dtype)
        own[...] = jnp.where(kept + core > 0, rows, token).astype(own.dtype)


def slice_kernel(after_ref, weight_ref, pred_ref, near_ref, far_ref, early_ref, late_ref, sems):
    core, z, _, _ = places()
    wide = near_ref.shape[2]
    cut = early_ref.shape[0]
    t = lax.rem(z, 2)
    copies = []
    for target, chosen in ((near_ref, t), (far_ref, 1 - t)):
        lanes = pl.ds(pl.multiple_of(chosen * wide, 128), wide)
        copies.append((weight_ref.at[0, :, :, lanes], target))
    for index, target in enumerate((early_ref, late_ref)):
        first = pl.multiple_of((2 * core + index) * cut, 128)
        copies.append((pred_ref.at[pl.ds(first, cut), :], target))
    copies = [
        pltpu.make_async_copy(source, target, sems.at[index])
        for index, (source, target) in enumerate(copies)
    ]
    for copy in copies:
        copy.start()
    for copy in copies:
        copy.wait()


def encode_kernel(x_own, x_across, x_near, x_near_across, halo_ref, *refs):
    pieces = refs[:PIECES]
    out_ref, x_buf, w_buf, q_buf, k_buf, v_buf, sems = refs[PIECES:]
    core, z, y, m = places()
    half = x_own.shape[-1]
    rows = x_own.shape[1]
    depth = pieces[0].shape[1]
    wide = pieces[0].shape[2]
    own_rows = 4 * rows
    copies = []
    side = jnp.where(core == z // 2, 1 - lax.rem(z, 2), lax.rem(z, 2))
    for piece, near, across in (
        (x_own, 0, 0), (x_across, 0, 1), (x_near, 1, 0), (x_near_across, 1, 1)
    ):
        first = WIN + 2 * rows * (side if near == 0 else 1 - side)
        for part in range(2):
            row = pl.multiple_of(first + (y if part == 0 else 1 - y) * rows, 64)
            copies.append((
                piece.at[part], x_buf.at[m if across == 0 else 1 - m, pl.ds(row, rows), :]
            ))
    halo_first = pl.multiple_of((1 - core) * (WIN + own_rows), 64)
    empty_first = pl.multiple_of(core * (WIN + own_rows), 64)
    for across in range(2):
        copies.append((
            halo_ref.at[across],
            x_buf.at[m if across == 0 else 1 - m, pl.ds(halo_first, WIN), :],
        ))
    t = lax.rem(z, 2)
    for index, piece in enumerate(pieces):
        crossed, other = (index // 2) % 2, index % 2
        low = core if (other == 0) == (index >= 4) else 1 - core
        pos_z = 2 * low + (t if index < 4 else 1 - t)
        pos = 2 * pos_z + (y if crossed == 0 else 1 - y)
        copies.append((
            piece, w_buf.at[:, pl.ds(pl.multiple_of(pos * depth, 64), depth), :]
        ))
    started = []
    for index, (source, target) in enumerate(copies):
        copy = pltpu.make_async_copy(source, target, sems.at[index])
        copy.start()
        started.append(copy)
    x_buf[:, pl.ds(empty_first, WIN), :] = jnp.zeros((2, WIN, half), x_buf.dtype)
    for copy in started:
        copy.wait()

    def project(kind, first, count):
        total = None
        for i in range(2):
            term = jnp.dot(
                x_buf[i, first:first + count, :],
                w_buf[kind, i * half:(i + 1) * half, :],
                preferred_element_type=jnp.float32,
            )
            total = term if total is None else total + term
        return total.astype(q_buf.dtype)

    q_buf[...] = project(0, WIN, own_rows)
    k_buf[...] = project(1, 0, own_rows + 2 * WIN)
    v_buf[...] = project(2, 0, own_rows + 2 * WIN)
    keys = rows + 2 * WIN
    a = lax.broadcasted_iota(jnp.int32, (rows, keys), 0)
    b = lax.broadcasted_iota(jnp.int32, (rows, keys), 1)
    band = (b >= a) & (b <= a + 2 * WIN)
    for j in range(4):
        admitted = band
        if j == 0:
            admitted = admitted & (b >= WIN * (1 - core))
        if j == 3:
            admitted = admitted & (b < keys - WIN * core)
        for h in range(wide // HD):
            lanes = slice(h * HD, (h + 1) * HD)
            scores = lax.dot_general(
                q_buf[j * rows:(j + 1) * rows, lanes],
                k_buf[j * rows:j * rows + keys, lanes],
                (((1,), (1,)), ((), ())),
                preferred_element_type=jnp.float32,
            ) * (1.0 / math.sqrt(HD))
            scores = jnp.where(admitted, scores, -jnp.inf)
            peak = jnp.max(scores, axis=-1, keepdims=True)
            exps = jnp.exp(scores - peak)
            attention = (exps / jnp.sum(exps, axis=-1, keepdims=True)).astype(jnp.bfloat16)
            out_ref[j, :, lanes] = jnp.dot(
                attention,
                v_buf[j * rows:j * rows + keys, lanes],
                preferred_element_type=jnp.float32,
            ).astype(out_ref.dtype)


def predict_kernel(slot_ref, lat_ref, own_ref, e0, e1, l0, l1, out_ref):
    core, _, _, m = places()
    wide = lat_ref.shape[2]
    lent = ((e0, e1), (l0, l1))
    total = None
    for side in range(2):
        predicted = None
        for t in range(2):
            for x in range(2):
                if side == 0:
                    source = lat_ref[2 * t + x]
                    weight = own_ref[(2 * x + t) * wide:(2 * x + t + 1) * wide, :]
                else:
                    source = lat_ref[2 * t + (core if x == 0 else 1 - core)]
                    weight = lent[t][x][...]
                term = jnp.dot(source, weight, preferred_element_type=jnp.float32)
                predicted = term if predicted is None else predicted + term
        for t in range(2):
            target = lat_ref[4 + 2 * t + (m if side == 0 else 1 - m)].astype(jnp.float32)
            residue = predicted[:, t * wide:(t + 1) * wide] - target
            for i in range(wide // 128):
                piece = residue[:, i * 128:(i + 1) * 128]
                total = piece * piece if total is None else total + piece * piece
    row_errors = jnp.sum(total, axis=1, keepdims=True)
    rows, slots = total.shape[0], out_ref.shape[2]
    chosen = slot_ref[...] == lax.broadcasted_iota(jnp.int32, (rows, slots), 1)
    routed = jnp.sum(jnp.where(chosen, row_errors, 0.0), axis=0, keepdims=True)
    for i in range(out_ref.shape[0]):
        out_ref[i] = routed


def local_lines(signal, mask_token, keep, target_shard, enc_weight, pred_weight):
    core = lax.axis_index("grp")
    s = lax.axis_index("seq")
    m = lax.axis_index("mdl")
    z, y = s // 2, s % 2
    sequences, length, half = signal.shape
    per_range = keep.shape[1]
    block_len = length // per_range
    depth = enc_weight.shape[2]
    wide = half // 2

    vmem = pl.BlockSpec(memory_space=pltpu.VMEM)
    anywhere = pl.BlockSpec(memory_space=pl.ANY)

    def to_near(c, z, y, m):
        return (1 - z // 2, z % 2 + 2 * c, y, m)

    def to_far(c, z, y, m):
        return (z // 2, 1 - z % 2 + 2 * c, y, m)

    def across_z(c, z, y, m):
        if z // 2 == c:
            return (c, (z + 2) % 4, y, m)
        return (1 - c, z + 1 - 2 * (z % 2), y, m)

    def across_zy(c, z, y, m):
        c, z, y, m = across_z(c, z, y, m)
        return (c, z, 1 - y, m)

    def flip_y(c, z, y, m):
        return (c, z, 1 - y, m)

    def flip_core(c, z, y, m):
        return (1 - c, z, y, m)

    def flip_x(c, z, y, m):
        return (c, z, y, 1 - m)

    def second_hop(c, z, y, m):
        if z // 2 == c:
            return (c, z, 1 - y, m)
        return (c, z + 1 - 2 * (z % 2), y, m)

    cut = half // 2
    mine, given, mine_own, given_own = pl.pallas_call(
        mask_kernel,
        out_shape=[jax.ShapeDtypeStruct((length, half), jnp.bfloat16)] * 4,
        in_specs=[vmem] * 3,
        out_specs=[vmem] * 4,
    )(signal, mask_token, keep)
    near, far, early, late = pl.pallas_call(
        slice_kernel,
        out_shape=[jax.ShapeDtypeStruct(shape, jnp.bfloat16) for shape in (
            (3, depth, wide), (3, depth, wide), (cut, half), (cut, half),
        )],
        in_specs=[anywhere] * 3,
        out_specs=[vmem] * 4,
        scratch_shapes=[pltpu.SemaphoreType.DMA((4,))],
    )(mine, enc_weight, pred_weight)
    first, second = move(mine, across_z), move(given, across_zy)
    small = jnp.stack([keep, target_shard])
    small, early = lax.optimization_barrier((small, early))
    routing = move(small, lambda c, z, y, m: ((2 * z + y) // 4, (2 * z + y) % 4, c, m))
    near, first, second = lax.optimization_barrier((near, first, second))
    x_own = jnp.stack([first, second])
    near_w = move(near, to_near)
    weight_early = move(early, flip_x)
    far, x_own, routing = lax.optimization_barrier((far, x_own, routing))
    far_w = move(far, to_far)
    home = core == z // 2
    sent = jnp.where(home, jnp.stack([mine_own, given_own]), x_own)
    come = move(sent, second_hop)
    kept_home = (jnp.arange(2) == 0)[:, None, None] & home
    x_near = jnp.where(kept_home, mine_own[None], come)
    x_across = move(x_own, flip_x)
    near_y_source, weight_early = lax.optimization_barrier((near_w, weight_early))
    near_y = move(near_y_source, flip_y)
    far_y_source, near_y = lax.optimization_barrier((far_w, near_y))
    far_y = move(far_y_source, flip_y)
    weight_early_c = move(weight_early, flip_core)
    x_near_across = move(x_near, flip_x)
    late, _ = lax.optimization_barrier((late, x_near_across))
    weight_late = move(late, flip_x)
    weight_late_c = move(weight_late, flip_core)
    hidden = lax.dynamic_index_in_dim(routing[0], y, 0, keepdims=False) == 0
    shard_of = routing[1].reshape(-1)
    blocks = shard_of.shape[0]
    capacity = max(2, 2 * blocks // 8)
    order_ids = jnp.arange(blocks)
    earlier = (shard_of[:, None] == shard_of[None, :]) & (order_ids[:, None] < order_ids[None, :])
    slot = shard_of * capacity + jnp.sum(earlier.astype(jnp.int32), axis=0)
    slot = lax.dynamic_index_in_dim(slot.reshape(sequences, -1), y, 0, keepdims=False)
    slot = jnp.where(hidden, slot, -1)
    slot = lax.dynamic_slice_in_dim(slot, m * (per_range // 2), per_range // 2)
    slot = jnp.repeat(slot, block_len)[:, None]

    def edge(own, near):
        found = jnp.where(jnp.where(home, 1 - z % 2, z % 2) == 1 - core, own, near)
        part = jnp.where(core == 0, 1 - y, y)
        first = jnp.where(core == 0, length - WIN, 0)
        return lax.dynamic_slice(found, (part, first, 0), (1, WIN, half))[0]

    halo = move(jnp.stack([edge(x_own, x_near), edge(x_across, x_near_across)]), flip_core)
    far_yc_source, halo = lax.optimization_barrier((far_y, halo))
    pieces = [
        near_w, move(near_w, flip_core), near_y, move(near_y, flip_core),
        far_w, move(far_w, flip_core), far_y, move(far_yc_source, flip_core),
    ]
    span = 4 * length + 2 * WIN

    latent = pl.pallas_call(
        encode_kernel,
        out_shape=jax.ShapeDtypeStruct((4, length, wide), jnp.bfloat16),
        in_specs=[anywhere] * (5 + PIECES),
        out_specs=vmem,
        scratch_shapes=[
            pltpu.VMEM((2, span, half), jnp.bfloat16),
            pltpu.VMEM((3, 2 * half, wide), jnp.bfloat16),
            pltpu.VMEM((4 * length, wide), jnp.bfloat16),
            pltpu.VMEM((span, wide), jnp.bfloat16),
            pltpu.VMEM((span, wide), jnp.bfloat16),
            pltpu.SemaphoreType.DMA((10 + PIECES,)),
        ],
        compiler_params=pltpu.CompilerParams(vmem_limit_bytes=60 * 2**20),
    )(x_own, x_across, x_near, x_near_across, halo, *pieces)
    lines = [[4 * i + 2 * j + k for i in range(4) for k in range(2)] for j in range(2)]
    latents = lax.all_to_all(
        latent.reshape(8, length // 2, wide), ("seq", "mdl"),
        split_axis=0, concat_axis=0, tiled=True, axis_index_groups=lines,
    )
    routed = pl.pallas_call(
        predict_kernel,
        out_shape=jax.ShapeDtypeStruct((16, 1, 8 * capacity), jnp.float32),
        in_specs=[vmem] * 7,
        out_specs=vmem,
        compiler_params=pltpu.CompilerParams(vmem_limit_bytes=24 * 2**20),
    )(
        slot, latents, pred_weight,
        weight_early, weight_early_c, weight_late, weight_late_c,
    )
    arrived = lax.all_to_all(routed, ("seq", "mdl"), split_axis=0, concat_axis=0, tiled=True)
    mine = lax.dynamic_slice_in_dim(arrived[:, 0], capacity * s, capacity, 1)
    summed = jnp.sum(mine.reshape(4, 4, capacity), axis=1)
    return summed.reshape(1, -1) / float(block_len * 2 * half)


def solution(mesh):
    placed = (
        P(None, "seq", "mdl"),
        P("mdl"),
        P(None, "seq"),
        P(None, "seq"),
        P("grp", None, "seq", "mdl"),
        P(None, "mdl"),
    )
    plan = local_lines if mesh.shape["seq"] == 8 else local
    return jax.shard_map(
        plan, mesh=mesh, in_specs=placed, out_specs=P("seq", "grp"), check_vma=False
    )
```

```python
import functools
import math

import jax
import jax.numpy as jnp
from jax import lax
from jax.experimental import pallas as pl
from jax.experimental.pallas import tpu as pltpu
from jax.sharding import PartitionSpec as P

HD = 128
WIN = 64
AXES = ("grp", "seq", "mdl")
PIECES = 8


def padded(x, sides, width):
    for axis, dim in sides:
        count, length = (lax.axis_size(axis), x.shape[dim])
        up = [(i, (i + 1) % count) for i in range(count - 1)]
        down = [(j, i) for i, j in up]
        last = lax.slice_in_dim(x, length - width, length, axis=dim)
        leading = lax.slice_in_dim(x, 0, width, axis=dim)
        before = lax.ppermute(last, axis, up)
        after = lax.ppermute(leading, axis, down)
        x = jnp.concatenate([before, x, after], axis=dim)
    return x


def predict(context, target, live_flags, pred_weight, divisor):
    flat_rows = context.reshape(-1, context.shape[-1])
    wide_rows = lax.all_gather(flat_rows, "mdl", axis=1, tiled=True)
    predicted = jnp.dot(wide_rows, pred_weight, preferred_element_type=jnp.float32)
    residue = predicted - target.reshape(flat_rows.shape).astype(jnp.float32)
    partial_sums = jnp.sum((residue * residue).reshape(live_flags.shape[0], -1), axis=1)
    summed = lax.psum(partial_sums, "mdl")
    return summed / divisor * live_flags


def local(signal, mask_token, keep, target_shard, enc_weight, pred_weight):
    group_index = lax.axis_index("grp")
    seq_index = lax.axis_index("seq")
    shards = lax.axis_size("seq")
    sequences, length, half_width = signal.shape
    per_range = keep.shape[1]
    block_len = length // per_range
    kept_rows = jnp.repeat(keep, block_len, axis=1)[:, :, None]
    masked_in = jnp.where(kept_rows == 1, signal, mask_token[None, None, :])
    source = jnp.where(group_index == 0, masked_in, signal)
    wide_in = lax.all_gather(source, "mdl", axis=2, tiled=True)
    full_width = wide_in.shape[2]
    flat_in = wide_in.reshape(-1, full_width)
    span = length + 2 * WIN
    weight_all = lax.all_gather(enc_weight, "seq", axis=2, tiled=True)[0]
    queries = jnp.dot(flat_in, weight_all[0], preferred_element_type=jnp.float32).astype(
        jnp.bfloat16
    )
    pair_made = jnp.einsum(
        "nd,cde->cne", flat_in, weight_all[1:], preferred_element_type=jnp.float32
    ).astype(jnp.bfloat16)
    own_pairs = pair_made.reshape(2, sequences, length, half_width)
    pair_rows = padded(own_pairs, (("seq", 2),), WIN)
    head_count = half_width // HD
    query_heads = queries.reshape(sequences, length, head_count, HD)
    key_heads = pair_rows[0].reshape(sequences, span, head_count, HD)
    value_heads = pair_rows[1].reshape(sequences, span, head_count, HD)
    query_pos = seq_index * length + jnp.arange(length)
    key_pos = seq_index * length - WIN + jnp.arange(span)
    total_len = length * shards
    in_window = (
        (jnp.abs(query_pos[:, None] - key_pos[None, :]) <= WIN)
        & (key_pos[None, :] >= 0)
        & (key_pos[None, :] < total_len)
    )
    scores = jnp.einsum(
        "sahd,sbhd->shab", query_heads, key_heads, preferred_element_type=jnp.float32
    ) * (1.0 / math.sqrt(HD))
    scores = jnp.where(in_window[None, None], scores, -jnp.inf)
    row_peak = jnp.max(scores, axis=-1, keepdims=True)
    exp_scores = jnp.exp(scores - row_peak)
    attention = (exp_scores / jnp.sum(exp_scores, axis=-1, keepdims=True)).astype(jnp.bfloat16)
    attended = jnp.einsum(
        "shab,sbhd->sahd", attention, value_heads, preferred_element_type=jnp.float32
    ).astype(jnp.bfloat16)
    latent = attended.reshape(sequences * per_range, block_len, half_width)
    blocks_here = latent.shape[0]
    capacity = max(2, 2 * blocks_here // shards)
    slot_count = shards * capacity
    shard_of = target_shard.reshape(-1)
    masked_flag = (keep.reshape(-1) == 0).astype(jnp.float32)
    order_ids = jnp.arange(blocks_here)
    earlier = (shard_of[:, None] == shard_of[None, :]) & (order_ids[:, None] < order_ids[None, :])
    slot_rank = jnp.sum(earlier.astype(jnp.int32), axis=0)
    slot_index = shard_of * capacity + slot_rank
    onehot = slot_index[None, :] == jnp.arange(slot_count)[:, None]
    divisor = float(block_len * full_width)
    halves = lax.all_to_all(latent[None], "grp", split_axis=1, concat_axis=0, tiled=True)
    half_count = blocks_here // 2
    first_block = group_index * half_count
    own_flags = lax.dynamic_slice_in_dim(masked_flag, first_block, half_count)
    losses = predict(halves[0], halves[1], own_flags, pred_weight, divisor)
    spread = lax.dynamic_update_slice_in_dim(
        jnp.zeros((blocks_here,), jnp.float32), losses, first_block, 0
    )
    slotted = jnp.sum(jnp.where(onehot, spread[None, :], 0.0), axis=1).reshape(shards, capacity)
    arrived = lax.all_to_all(slotted, "seq", split_axis=0, concat_axis=0, tiled=True)
    result = lax.psum_scatter(arrived, "grp", scatter_dimension=0, tiled=True)
    return result.reshape(1, -1)


def move(x, target):
    pairs = []
    for c in range(2):
        for s in range(8):
            for m in range(2):
                c2, z2, y2, m2 = target(c, s // 2, s % 2, m)
                pairs.append(((c * 8 + s) * 2 + m, (c2 * 8 + 2 * z2 + y2) * 2 + m2))
    return lax.ppermute(x, AXES, pairs)


def places():
    s = lax.axis_index("seq")
    return lax.axis_index("grp"), s // 2, lax.rem(s, 2), lax.axis_index("mdl")


def mask_kernel(
    signal_ref, token_ref, keep_ref, mine_ref, given_ref, mine_own_ref, given_own_ref
):
    core, _, y, _ = places()
    length = signal_ref.shape[1]
    blocks = keep_ref.shape[1]
    block_len = length // blocks
    row = lax.broadcasted_iota(jnp.int32, (length, blocks), 0)
    first = lax.broadcasted_iota(jnp.int32, (length, blocks), 1) * block_len
    covers = (row >= first) & (row < first + block_len)
    token = token_ref[...].astype(jnp.float32).reshape(1, -1)
    for other, own, chosen in ((mine_ref, mine_own_ref, y), (given_ref, given_own_ref, 1 - y)):
        kept = jnp.where(covers, keep_ref[pl.ds(chosen, 1), :], 0)
        kept = jnp.sum(kept, axis=1, keepdims=True)
        rows = signal_ref[chosen].astype(jnp.float32)
        other[...] = jnp.where(kept + 1 - core > 0, rows, token).astype(other.dtype)
        own[...] = jnp.where(kept + core > 0, rows, token).astype(own.dtype)


def slice_kernel(after_ref, weight_ref, pred_ref, near_ref, far_ref, early_ref, late_ref, sems):
    core, z, _, _ = places()
    wide = near_ref.shape[2]
    cut = early_ref.shape[0]
    t = lax.rem(z, 2)
    copies = []
    for target, chosen in ((near_ref, t), (far_ref, 1 - t)):
        lanes = pl.ds(pl.multiple_of(chosen * wide, 128), wide)
        copies.append((weight_ref.at[0, :, :, lanes], target))
    for index, target in enumerate((early_ref, late_ref)):
        first = pl.multiple_of((2 * core + index) * cut, 128)
        copies.append((pred_ref.at[pl.ds(first, cut), :], target))
    copies = [
        pltpu.make_async_copy(source, target, sems.at[index])
        for index, (source, target) in enumerate(copies)
    ]
    for copy in copies:
        copy.start()
    for copy in copies:
        copy.wait()


def encode_kernel(x_own, x_across, x_near, x_near_across, halo_ref, *refs):
    pieces = refs[:PIECES]
    out_ref, x_buf, w_buf, q_buf, k_buf, v_buf, sems = refs[PIECES:]
    core, z, y, m = places()
    half = x_own.shape[-1]
    rows = x_own.shape[1]
    depth = pieces[0].shape[1]
    wide = pieces[0].shape[2]
    own_rows = 4 * rows
    copies = []
    side = jnp.where(core == z // 2, 1 - lax.rem(z, 2), lax.rem(z, 2))
    for piece, near, across in (
        (x_own, 0, 0), (x_across, 0, 1), (x_near, 1, 0), (x_near_across, 1, 1)
    ):
        first = WIN + 2 * rows * (side if near == 0 else 1 - side)
        for part in range(2):
            row = pl.multiple_of(first + (y if part == 0 else 1 - y) * rows, 64)
            copies.append((
                piece.at[part], x_buf.at[m if across == 0 else 1 - m, pl.ds(row, rows), :]
            ))
    halo_first = pl.multiple_of((1 - core) * (WIN + own_rows), 64)
    empty_first = pl.multiple_of(core * (WIN + own_rows), 64)
    for across in range(2):
        copies.append((
            halo_ref.at[across],
            x_buf.at[m if across == 0 else 1 - m, pl.ds(halo_first, WIN), :],
        ))
    t = lax.rem(z, 2)
    for index, piece in enumerate(pieces):
        crossed, other = (index // 2) % 2, index % 2
        low = core if (other == 0) == (index >= 4) else 1 - core
        pos_z = 2 * low + (t if index < 4 else 1 - t)
        pos = 2 * pos_z + (y if crossed == 0 else 1 - y)
        copies.append((
            piece, w_buf.at[:, pl.ds(pl.multiple_of(pos * depth, 64), depth), :]
        ))
    started = []
    for index, (source, target) in enumerate(copies):
        copy = pltpu.make_async_copy(source, target, sems.at[index])
        copy.start()
        started.append(copy)
    x_buf[:, pl.ds(empty_first, WIN), :] = jnp.zeros((2, WIN, half), x_buf.dtype)
    for copy in started:
        copy.wait()

    def project(kind, first, count):
        total = None
        for i in range(2):
            term = jnp.dot(
                x_buf[i, first:first + count, :],
                w_buf[kind, i * half:(i + 1) * half, :],
                preferred_element_type=jnp.float32,
            )
            total = term if total is None else total + term
        return total.astype(q_buf.dtype)

    q_buf[...] = project(0, WIN, own_rows)
    k_buf[...] = project(1, 0, own_rows + 2 * WIN)
    v_buf[...] = project(2, 0, own_rows + 2 * WIN)
    keys = rows + 2 * WIN
    a = lax.broadcasted_iota(jnp.int32, (rows, keys), 0)
    b = lax.broadcasted_iota(jnp.int32, (rows, keys), 1)
    band = (b >= a) & (b <= a + 2 * WIN)
    for j in range(4):
        admitted = band
        if j == 0:
            admitted = admitted & (b >= WIN * (1 - core))
        if j == 3:
            admitted = admitted & (b < keys - WIN * core)
        for h in range(wide // HD):
            lanes = slice(h * HD, (h + 1) * HD)
            scores = lax.dot_general(
                q_buf[j * rows:(j + 1) * rows, lanes],
                k_buf[j * rows:j * rows + keys, lanes],
                (((1,), (1,)), ((), ())),
                preferred_element_type=jnp.float32,
            ) * (1.0 / math.sqrt(HD))
            scores = jnp.where(admitted, scores, -jnp.inf)
            peak = jnp.max(scores, axis=-1, keepdims=True)
            exps = jnp.exp(scores - peak)
            attention = (exps / jnp.sum(exps, axis=-1, keepdims=True)).astype(jnp.bfloat16)
            out_ref[j, :, lanes] = jnp.dot(
                attention,
                v_buf[j * rows:j * rows + keys, lanes],
                preferred_element_type=jnp.float32,
            ).astype(out_ref.dtype)


def predict_kernel(slot_ref, lat_ref, own_ref, e0, e1, l0, l1, out_ref):
    core, _, _, m = places()
    wide = lat_ref.shape[2]
    lent = ((e0, e1), (l0, l1))
    total = None
    for side in range(2):
        predicted = None
        for t in range(2):
            for x in range(2):
                if side == 0:
                    source = lat_ref[2 * t + x]
                    weight = own_ref[(2 * x + t) * wide:(2 * x + t + 1) * wide, :]
                else:
                    source = lat_ref[2 * t + (core if x == 0 else 1 - core)]
                    weight = lent[t][x][...]
                term = jnp.dot(source, weight, preferred_element_type=jnp.float32)
                predicted = term if predicted is None else predicted + term
        for t in range(2):
            target = lat_ref[4 + 2 * t + (m if side == 0 else 1 - m)].astype(jnp.float32)
            residue = predicted[:, t * wide:(t + 1) * wide] - target
            for i in range(wide // 128):
                piece = residue[:, i * 128:(i + 1) * 128]
                total = piece * piece if total is None else total + piece * piece
    row_errors = jnp.sum(total, axis=1, keepdims=True)
    rows, slots = total.shape[0], out_ref.shape[2]
    chosen = slot_ref[...] == lax.broadcasted_iota(jnp.int32, (rows, slots), 1)
    routed = jnp.sum(jnp.where(chosen, row_errors, 0.0), axis=0, keepdims=True)
    for i in range(out_ref.shape[0]):
        out_ref[i] = routed


def local_lines(signal, mask_token, keep, target_shard, enc_weight, pred_weight):
    core = lax.axis_index("grp")
    s = lax.axis_index("seq")
    m = lax.axis_index("mdl")
    z, y = s // 2, s % 2
    sequences, length, half = signal.shape
    per_range = keep.shape[1]
    block_len = length // per_range
    depth = enc_weight.shape[2]
    wide = half // 2

    vmem = pl.BlockSpec(memory_space=pltpu.VMEM)
    anywhere = pl.BlockSpec(memory_space=pl.ANY)

    def to_near(c, z, y, m):
        return (1 - z // 2, z % 2 + 2 * c, y, m)

    def to_far(c, z, y, m):
        return (z // 2, 1 - z % 2 + 2 * c, y, m)

    def across_z(c, z, y, m):
        if z // 2 == c:
            return (c, (z + 2) % 4, y, m)
        return (1 - c, z + 1 - 2 * (z % 2), y, m)

    def across_zy(c, z, y, m):
        c, z, y, m = across_z(c, z, y, m)
        return (c, z, 1 - y, m)

    def flip_y(c, z, y, m):
        return (c, z, 1 - y, m)

    def flip_core(c, z, y, m):
        return (1 - c, z, y, m)

    def flip_x(c, z, y, m):
        return (c, z, y, 1 - m)

    def second_hop(c, z, y, m):
        if z // 2 == c:
            return (c, z, 1 - y, m)
        return (c, z + 1 - 2 * (z % 2), y, m)

    cut = half // 2
    mine, given, mine_own, given_own = pl.pallas_call(
        mask_kernel,
        out_shape=[jax.ShapeDtypeStruct((length, half), jnp.bfloat16)] * 4,
        in_specs=[vmem] * 3,
        out_specs=[vmem] * 4,
    )(signal, mask_token, keep)
    near, far, early, late = pl.pallas_call(
        slice_kernel,
        out_shape=[jax.ShapeDtypeStruct(shape, jnp.bfloat16) for shape in (
            (3, depth, wide), (3, depth, wide), (cut, half), (cut, half),
        )],
        in_specs=[anywhere] * 3,
        out_specs=[vmem] * 4,
        scratch_shapes=[pltpu.SemaphoreType.DMA((4,))],
    )(mine, enc_weight, pred_weight)
    first, second = move(mine, across_z), move(given, across_zy)
    small = jnp.stack([keep, target_shard])
    small, _ = lax.optimization_barrier((small, mine))
    routing = move(small, lambda c, z, y, m: ((2 * z + y) // 4, (2 * z + y) % 4, c, m))
    near, routing, first, second = lax.optimization_barrier((near, routing, first, second))
    x_own = jnp.stack([first, second])
    near_w = move(near, to_near)
    weight_early = move(early, flip_x)
    far, x_own = lax.optimization_barrier((far, x_own))
    far_w = move(far, to_far)
    home = core == z // 2
    sent = jnp.where(home, jnp.stack([mine_own, given_own]), x_own)
    come = move(sent, second_hop)
    kept_home = (jnp.arange(2) == 0)[:, None, None] & home
    x_near = jnp.where(kept_home, mine_own[None], come)
    x_across = move(x_own, flip_x)
    near_y_source, weight_early = lax.optimization_barrier((near_w, weight_early))
    near_y = move(near_y_source, flip_y)
    far_y_source, near_y = lax.optimization_barrier((far_w, near_y))
    far_y = move(far_y_source, flip_y)
    weight_early_c = move(weight_early, flip_core)
    x_near_across = move(x_near, flip_x)
    late, _ = lax.optimization_barrier((late, x_near_across))
    weight_late = move(late, flip_x)
    weight_late_c = move(weight_late, flip_core)
    hidden = lax.dynamic_index_in_dim(routing[0], y, 0, keepdims=False) == 0
    shard_of = routing[1].reshape(-1)
    blocks = shard_of.shape[0]
    capacity = max(2, 2 * blocks // 8)
    order_ids = jnp.arange(blocks)
    earlier = (shard_of[:, None] == shard_of[None, :]) & (order_ids[:, None] < order_ids[None, :])
    slot = shard_of * capacity + jnp.sum(earlier.astype(jnp.int32), axis=0)
    slot = lax.dynamic_index_in_dim(slot.reshape(sequences, -1), y, 0, keepdims=False)
    slot = jnp.where(hidden, slot, -1)
    slot = lax.dynamic_slice_in_dim(slot, m * (per_range // 2), per_range // 2)
    slot = jnp.repeat(slot, block_len)[:, None]

    def edge(own, near):
        found = jnp.where(jnp.where(home, 1 - z % 2, z % 2) == 1 - core, own, near)
        part = jnp.where(core == 0, 1 - y, y)
        first = jnp.where(core == 0, length - WIN, 0)
        return lax.dynamic_slice(found, (part, first, 0), (1, WIN, half))[0]

    near_c, near_yc = move(near_w, flip_core), move(near_y, flip_core)
    edges = jnp.stack([edge(x_own, x_near), edge(x_across, x_near_across)])
    edges, near_c, near_yc = lax.optimization_barrier((edges, near_c, near_yc))
    halo = move(edges, flip_core)
    far_yc_source, halo = lax.optimization_barrier((far_y, halo))
    pieces = [
        near_w, near_c, near_y, near_yc,
        far_w, move(far_w, flip_core), far_y, move(far_yc_source, flip_core),
    ]
    span = 4 * length + 2 * WIN

    latent = pl.pallas_call(
        encode_kernel,
        out_shape=jax.ShapeDtypeStruct((4, length, wide), jnp.bfloat16),
        in_specs=[anywhere] * (5 + PIECES),
        out_specs=vmem,
        scratch_shapes=[
            pltpu.VMEM((2, span, half), jnp.bfloat16),
            pltpu.VMEM((3, 2 * half, wide), jnp.bfloat16),
            pltpu.VMEM((4 * length, wide), jnp.bfloat16),
            pltpu.VMEM((span, wide), jnp.bfloat16),
            pltpu.VMEM((span, wide), jnp.bfloat16),
            pltpu.SemaphoreType.DMA((10 + PIECES,)),
        ],
        compiler_params=pltpu.CompilerParams(vmem_limit_bytes=60 * 2**20),
    )(x_own, x_across, x_near, x_near_across, halo, *pieces)
    lines = [[4 * i + 2 * j + k for i in range(4) for k in range(2)] for j in range(2)]
    latents = lax.all_to_all(
        latent.reshape(8, length // 2, wide), ("seq", "mdl"),
        split_axis=0, concat_axis=0, tiled=True, axis_index_groups=lines,
    )
    routed = pl.pallas_call(
        predict_kernel,
        out_shape=jax.ShapeDtypeStruct((16, 1, 8 * capacity), jnp.float32),
        in_specs=[vmem] * 7,
        out_specs=vmem,
        compiler_params=pltpu.CompilerParams(vmem_limit_bytes=24 * 2**20),
    )(
        slot, latents, pred_weight,
        weight_early, weight_early_c, weight_late, weight_late_c,
    )
    arrived = lax.all_to_all(routed, ("seq", "mdl"), split_axis=0, concat_axis=0, tiled=True)
    mine = lax.dynamic_slice_in_dim(arrived[:, 0], capacity * s, capacity, 1)
    summed = jnp.sum(mine.reshape(4, 4, capacity), axis=1)
    return summed.reshape(1, -1) / float(block_len * 2 * half)


def solution(mesh):
    placed = (
        P(None, "seq", "mdl"),
        P("mdl"),
        P(None, "seq"),
        P(None, "seq"),
        P("grp", None, "seq", "mdl"),
        P(None, "mdl"),
    )
    plan = local_lines if mesh.shape["seq"] == 8 else local
    return jax.shard_map(
        plan, mesh=mesh, in_specs=placed, out_specs=P("seq", "grp"), check_vma=False
    )
```

```python
import functools
import math

import jax
import jax.numpy as jnp
from jax import lax
from jax.experimental import pallas as pl
from jax.experimental.pallas import tpu as pltpu
from jax.sharding import PartitionSpec as P

HD = 128
WIN = 64
AXES = ("grp", "seq", "mdl")
PIECES = 7


def padded(x, sides, width):
    for axis, dim in sides:
        count, length = (lax.axis_size(axis), x.shape[dim])
        up = [(i, (i + 1) % count) for i in range(count - 1)]
        down = [(j, i) for i, j in up]
        last = lax.slice_in_dim(x, length - width, length, axis=dim)
        leading = lax.slice_in_dim(x, 0, width, axis=dim)
        before = lax.ppermute(last, axis, up)
        after = lax.ppermute(leading, axis, down)
        x = jnp.concatenate([before, x, after], axis=dim)
    return x


def predict(context, target, live_flags, pred_weight, divisor):
    flat_rows = context.reshape(-1, context.shape[-1])
    wide_rows = lax.all_gather(flat_rows, "mdl", axis=1, tiled=True)
    predicted = jnp.dot(wide_rows, pred_weight, preferred_element_type=jnp.float32)
    residue = predicted - target.reshape(flat_rows.shape).astype(jnp.float32)
    partial_sums = jnp.sum((residue * residue).reshape(live_flags.shape[0], -1), axis=1)
    summed = lax.psum(partial_sums, "mdl")
    return summed / divisor * live_flags


def local(signal, mask_token, keep, target_shard, enc_weight, pred_weight):
    group_index = lax.axis_index("grp")
    seq_index = lax.axis_index("seq")
    shards = lax.axis_size("seq")
    sequences, length, half_width = signal.shape
    per_range = keep.shape[1]
    block_len = length // per_range
    kept_rows = jnp.repeat(keep, block_len, axis=1)[:, :, None]
    masked_in = jnp.where(kept_rows == 1, signal, mask_token[None, None, :])
    source = jnp.where(group_index == 0, masked_in, signal)
    wide_in = lax.all_gather(source, "mdl", axis=2, tiled=True)
    full_width = wide_in.shape[2]
    flat_in = wide_in.reshape(-1, full_width)
    span = length + 2 * WIN
    weight_all = lax.all_gather(enc_weight, "seq", axis=2, tiled=True)[0]
    queries = jnp.dot(flat_in, weight_all[0], preferred_element_type=jnp.float32).astype(
        jnp.bfloat16
    )
    pair_made = jnp.einsum(
        "nd,cde->cne", flat_in, weight_all[1:], preferred_element_type=jnp.float32
    ).astype(jnp.bfloat16)
    own_pairs = pair_made.reshape(2, sequences, length, half_width)
    pair_rows = padded(own_pairs, (("seq", 2),), WIN)
    head_count = half_width // HD
    query_heads = queries.reshape(sequences, length, head_count, HD)
    key_heads = pair_rows[0].reshape(sequences, span, head_count, HD)
    value_heads = pair_rows[1].reshape(sequences, span, head_count, HD)
    query_pos = seq_index * length + jnp.arange(length)
    key_pos = seq_index * length - WIN + jnp.arange(span)
    total_len = length * shards
    in_window = (
        (jnp.abs(query_pos[:, None] - key_pos[None, :]) <= WIN)
        & (key_pos[None, :] >= 0)
        & (key_pos[None, :] < total_len)
    )
    scores = jnp.einsum(
        "sahd,sbhd->shab", query_heads, key_heads, preferred_element_type=jnp.float32
    ) * (1.0 / math.sqrt(HD))
    scores = jnp.where(in_window[None, None], scores, -jnp.inf)
    row_peak = jnp.max(scores, axis=-1, keepdims=True)
    exp_scores = jnp.exp(scores - row_peak)
    attention = (exp_scores / jnp.sum(exp_scores, axis=-1, keepdims=True)).astype(jnp.bfloat16)
    attended = jnp.einsum(
        "shab,sbhd->sahd", attention, value_heads, preferred_element_type=jnp.float32
    ).astype(jnp.bfloat16)
    latent = attended.reshape(sequences * per_range, block_len, half_width)
    blocks_here = latent.shape[0]
    capacity = max(2, 2 * blocks_here // shards)
    slot_count = shards * capacity
    shard_of = target_shard.reshape(-1)
    masked_flag = (keep.reshape(-1) == 0).astype(jnp.float32)
    order_ids = jnp.arange(blocks_here)
    earlier = (shard_of[:, None] == shard_of[None, :]) & (order_ids[:, None] < order_ids[None, :])
    slot_rank = jnp.sum(earlier.astype(jnp.int32), axis=0)
    slot_index = shard_of * capacity + slot_rank
    onehot = slot_index[None, :] == jnp.arange(slot_count)[:, None]
    divisor = float(block_len * full_width)
    halves = lax.all_to_all(latent[None], "grp", split_axis=1, concat_axis=0, tiled=True)
    half_count = blocks_here // 2
    first_block = group_index * half_count
    own_flags = lax.dynamic_slice_in_dim(masked_flag, first_block, half_count)
    losses = predict(halves[0], halves[1], own_flags, pred_weight, divisor)
    spread = lax.dynamic_update_slice_in_dim(
        jnp.zeros((blocks_here,), jnp.float32), losses, first_block, 0
    )
    slotted = jnp.sum(jnp.where(onehot, spread[None, :], 0.0), axis=1).reshape(shards, capacity)
    arrived = lax.all_to_all(slotted, "seq", split_axis=0, concat_axis=0, tiled=True)
    result = lax.psum_scatter(arrived, "grp", scatter_dimension=0, tiled=True)
    return result.reshape(1, -1)


def move(x, target):
    pairs = []
    for c in range(2):
        for s in range(8):
            for m in range(2):
                c2, z2, y2, m2 = target(c, s // 2, s % 2, m)
                pairs.append(((c * 8 + s) * 2 + m, (c2 * 8 + 2 * z2 + y2) * 2 + m2))
    return lax.ppermute(x, AXES, pairs)


def places():
    s = lax.axis_index("seq")
    return lax.axis_index("grp"), s // 2, lax.rem(s, 2), lax.axis_index("mdl")


def mask_kernel(
    signal_ref, token_ref, keep_ref, mine_ref, given_ref, mine_own_ref, given_own_ref
):
    core, _, y, _ = places()
    length = signal_ref.shape[1]
    blocks = keep_ref.shape[1]
    block_len = length // blocks
    row = lax.broadcasted_iota(jnp.int32, (length, blocks), 0)
    first = lax.broadcasted_iota(jnp.int32, (length, blocks), 1) * block_len
    covers = (row >= first) & (row < first + block_len)
    token = token_ref[...].astype(jnp.float32).reshape(1, -1)
    for other, own, chosen in ((mine_ref, mine_own_ref, y), (given_ref, given_own_ref, 1 - y)):
        kept = jnp.where(covers, keep_ref[pl.ds(chosen, 1), :], 0)
        kept = jnp.sum(kept, axis=1, keepdims=True)
        rows = signal_ref[chosen].astype(jnp.float32)
        other[...] = jnp.where(kept + 1 - core > 0, rows, token).astype(other.dtype)
        own[...] = jnp.where(kept + core > 0, rows, token).astype(own.dtype)


def slice_kernel(after_ref, weight_ref, pred_ref, near_ref, far_ref, early_ref, late_ref, sems):
    core, z, _, _ = places()
    wide = near_ref.shape[2]
    cut = early_ref.shape[0]
    t = lax.rem(z, 2)
    copies = []
    for target, chosen in ((near_ref, t), (far_ref, 1 - t)):
        lanes = pl.ds(pl.multiple_of(chosen * wide, 128), wide)
        copies.append((weight_ref.at[0, :, :, lanes], target))
    for index, target in enumerate((early_ref, late_ref)):
        first = pl.multiple_of((2 * core + index) * cut, 128)
        copies.append((pred_ref.at[pl.ds(first, cut), :], target))
    copies = [
        pltpu.make_async_copy(source, target, sems.at[index])
        for index, (source, target) in enumerate(copies)
    ]
    for copy in copies:
        copy.start()
    for copy in copies:
        copy.wait()


def encode_kernel(x_own, x_across, x_near, x_near_across, halo_ref, *refs):
    near_w, near_y, pair_c = refs[:3]
    pieces = [near_w, pair_c.at[0], near_y, pair_c.at[1], *refs[3:PIECES]]
    out_ref, x_buf, w_buf, q_buf, k_buf, v_buf, sems = refs[PIECES:]
    core, z, y, m = places()
    half = x_own.shape[-1]
    rows = x_own.shape[1]
    depth = pieces[0].shape[1]
    wide = pieces[0].shape[2]
    own_rows = 4 * rows
    copies = []
    side = jnp.where(core == z // 2, 1 - lax.rem(z, 2), lax.rem(z, 2))
    for piece, near, across in (
        (x_own, 0, 0), (x_across, 0, 1), (x_near, 1, 0), (x_near_across, 1, 1)
    ):
        first = WIN + 2 * rows * (side if near == 0 else 1 - side)
        for part in range(2):
            row = pl.multiple_of(first + (y if part == 0 else 1 - y) * rows, 64)
            copies.append((
                piece.at[part], x_buf.at[m if across == 0 else 1 - m, pl.ds(row, rows), :]
            ))
    halo_first = pl.multiple_of((1 - core) * (WIN + own_rows), 64)
    empty_first = pl.multiple_of(core * (WIN + own_rows), 64)
    for across in range(2):
        copies.append((
            halo_ref.at[across],
            x_buf.at[m if across == 0 else 1 - m, pl.ds(halo_first, WIN), :],
        ))
    t = lax.rem(z, 2)
    for index, piece in enumerate(pieces):
        crossed, other = (index // 2) % 2, index % 2
        low = core if (other == 0) == (index >= 4) else 1 - core
        pos_z = 2 * low + (t if index < 4 else 1 - t)
        pos = 2 * pos_z + (y if crossed == 0 else 1 - y)
        copies.append((
            piece, w_buf.at[:, pl.ds(pl.multiple_of(pos * depth, 64), depth), :]
        ))
    started = []
    for index, (source, target) in enumerate(copies):
        copy = pltpu.make_async_copy(source, target, sems.at[index])
        copy.start()
        started.append(copy)
    x_buf[:, pl.ds(empty_first, WIN), :] = jnp.zeros((2, WIN, half), x_buf.dtype)
    for copy in started:
        copy.wait()

    def project(kind, first, count):
        total = None
        for i in range(2):
            term = jnp.dot(
                x_buf[i, first:first + count, :],
                w_buf[kind, i * half:(i + 1) * half, :],
                preferred_element_type=jnp.float32,
            )
            total = term if total is None else total + term
        return total.astype(q_buf.dtype)

    q_buf[...] = project(0, WIN, own_rows)
    k_buf[...] = project(1, 0, own_rows + 2 * WIN)
    v_buf[...] = project(2, 0, own_rows + 2 * WIN)
    keys = rows + 2 * WIN
    a = lax.broadcasted_iota(jnp.int32, (rows, keys), 0)
    b = lax.broadcasted_iota(jnp.int32, (rows, keys), 1)
    band = (b >= a) & (b <= a + 2 * WIN)
    for j in range(4):
        admitted = band
        if j == 0:
            admitted = admitted & (b >= WIN * (1 - core))
        if j == 3:
            admitted = admitted & (b < keys - WIN * core)
        for h in range(wide // HD):
            lanes = slice(h * HD, (h + 1) * HD)
            scores = lax.dot_general(
                q_buf[j * rows:(j + 1) * rows, lanes],
                k_buf[j * rows:j * rows + keys, lanes],
                (((1,), (1,)), ((), ())),
                preferred_element_type=jnp.float32,
            ) * (1.0 / math.sqrt(HD))
            scores = jnp.where(admitted, scores, -jnp.inf)
            peak = jnp.max(scores, axis=-1, keepdims=True)
            exps = jnp.exp(scores - peak)
            attention = (exps / jnp.sum(exps, axis=-1, keepdims=True)).astype(jnp.bfloat16)
            out_ref[j, :, lanes] = jnp.dot(
                attention,
                v_buf[j * rows:j * rows + keys, lanes],
                preferred_element_type=jnp.float32,
            ).astype(out_ref.dtype)


def predict_kernel(slot_ref, lat_ref, own_ref, e0, e1, l0, l1, out_ref):
    core, _, _, m = places()
    wide = lat_ref.shape[2]
    lent = ((e0, e1), (l0, l1))
    total = None
    for side in range(2):
        predicted = None
        for t in range(2):
            for x in range(2):
                if side == 0:
                    source = lat_ref[2 * t + x]
                    weight = own_ref[(2 * x + t) * wide:(2 * x + t + 1) * wide, :]
                else:
                    source = lat_ref[2 * t + (core if x == 0 else 1 - core)]
                    weight = lent[t][x][...]
                term = jnp.dot(source, weight, preferred_element_type=jnp.float32)
                predicted = term if predicted is None else predicted + term
        for t in range(2):
            target = lat_ref[4 + 2 * t + (m if side == 0 else 1 - m)].astype(jnp.float32)
            residue = predicted[:, t * wide:(t + 1) * wide] - target
            for i in range(wide // 128):
                piece = residue[:, i * 128:(i + 1) * 128]
                total = piece * piece if total is None else total + piece * piece
    row_errors = jnp.sum(total, axis=1, keepdims=True)
    rows, slots = total.shape[0], out_ref.shape[2]
    chosen = slot_ref[...] == lax.broadcasted_iota(jnp.int32, (rows, slots), 1)
    routed = jnp.sum(jnp.where(chosen, row_errors, 0.0), axis=0, keepdims=True)
    for i in range(out_ref.shape[0]):
        out_ref[i] = routed


def local_lines(signal, mask_token, keep, target_shard, enc_weight, pred_weight):
    core = lax.axis_index("grp")
    s = lax.axis_index("seq")
    m = lax.axis_index("mdl")
    z, y = s // 2, s % 2
    sequences, length, half = signal.shape
    per_range = keep.shape[1]
    block_len = length // per_range
    depth = enc_weight.shape[2]
    wide = half // 2

    vmem = pl.BlockSpec(memory_space=pltpu.VMEM)
    anywhere = pl.BlockSpec(memory_space=pl.ANY)

    def to_near(c, z, y, m):
        return (1 - z // 2, z % 2 + 2 * c, y, m)

    def to_far(c, z, y, m):
        return (z // 2, 1 - z % 2 + 2 * c, y, m)

    def across_z(c, z, y, m):
        if z // 2 == c:
            return (c, (z + 2) % 4, y, m)
        return (1 - c, z + 1 - 2 * (z % 2), y, m)

    def across_zy(c, z, y, m):
        c, z, y, m = across_z(c, z, y, m)
        return (c, z, 1 - y, m)

    def flip_y(c, z, y, m):
        return (c, z, 1 - y, m)

    def flip_core(c, z, y, m):
        return (1 - c, z, y, m)

    def flip_x(c, z, y, m):
        return (c, z, y, 1 - m)

    def second_hop(c, z, y, m):
        if z // 2 == c:
            return (c, z, 1 - y, m)
        return (c, z + 1 - 2 * (z % 2), y, m)

    cut = half // 2
    mine, given, mine_own, given_own = pl.pallas_call(
        mask_kernel,
        out_shape=[jax.ShapeDtypeStruct((length, half), jnp.bfloat16)] * 4,
        in_specs=[vmem] * 3,
        out_specs=[vmem] * 4,
    )(signal, mask_token, keep)
    near, far, early, late = pl.pallas_call(
        slice_kernel,
        out_shape=[jax.ShapeDtypeStruct(shape, jnp.bfloat16) for shape in (
            (3, depth, wide), (3, depth, wide), (cut, half), (cut, half),
        )],
        in_specs=[anywhere] * 3,
        out_specs=[vmem] * 4,
        scratch_shapes=[pltpu.SemaphoreType.DMA((4,))],
    )(mine, enc_weight, pred_weight)
    first, second = move(mine, across_z), move(given, across_zy)
    small = jnp.stack([keep, target_shard])
    small, _ = lax.optimization_barrier((small, mine))
    routing = move(small, lambda c, z, y, m: ((2 * z + y) // 4, (2 * z + y) % 4, c, m))
    near, routing, first, second = lax.optimization_barrier((near, routing, first, second))
    x_own = jnp.stack([first, second])
    near_w = move(near, to_near)
    weight_early = move(early, flip_x)
    far, x_own = lax.optimization_barrier((far, x_own))
    far_w = move(far, to_far)
    home = core == z // 2
    sent = jnp.where(home, jnp.stack([mine_own, given_own]), x_own)
    come = move(sent, second_hop)
    kept_home = (jnp.arange(2) == 0)[:, None, None] & home
    x_near = jnp.where(kept_home, mine_own[None], come)
    x_across = move(x_own, flip_x)
    near_y_source, weight_early = lax.optimization_barrier((near_w, weight_early))
    near_y = move(near_y_source, flip_y)
    far_y_source, near_y = lax.optimization_barrier((far_w, near_y))
    far_y = move(far_y_source, flip_y)
    weight_early_c = move(weight_early, flip_core)
    x_near, x_across = lax.optimization_barrier((x_near, x_across))
    x_near_across = move(x_near, flip_x)
    late, _ = lax.optimization_barrier((late, x_near_across))
    weight_late = move(late, flip_x)
    weight_late_c = move(weight_late, flip_core)
    hidden = lax.dynamic_index_in_dim(routing[0], y, 0, keepdims=False) == 0
    shard_of = routing[1].reshape(-1)
    blocks = shard_of.shape[0]
    capacity = max(2, 2 * blocks // 8)
    order_ids = jnp.arange(blocks)
    earlier = (shard_of[:, None] == shard_of[None, :]) & (order_ids[:, None] < order_ids[None, :])
    slot = shard_of * capacity + jnp.sum(earlier.astype(jnp.int32), axis=0)
    slot = lax.dynamic_index_in_dim(slot.reshape(sequences, -1), y, 0, keepdims=False)
    slot = jnp.where(hidden, slot, -1)
    slot = lax.dynamic_slice_in_dim(slot, m * (per_range // 2), per_range // 2)
    slot = jnp.repeat(slot, block_len)[:, None]

    def edge(own, near):
        found = jnp.where(jnp.where(home, 1 - z % 2, z % 2) == 1 - core, own, near)
        part = jnp.where(core == 0, 1 - y, y)
        first = jnp.where(core == 0, length - WIN, 0)
        return lax.dynamic_slice(found, (part, first, 0), (1, WIN, half))[0]

    halo = move(jnp.stack([edge(x_own, x_near), edge(x_across, x_near_across)]), flip_core)
    far_yc_source, halo = lax.optimization_barrier((far_y, halo))
    pieces = [
        near_w, near_y, move(jnp.stack([near_w, near_y]), flip_core),
        far_w, move(far_w, flip_core), far_y, move(far_yc_source, flip_core),
    ]
    span = 4 * length + 2 * WIN

    latent = pl.pallas_call(
        encode_kernel,
        out_shape=jax.ShapeDtypeStruct((4, length, wide), jnp.bfloat16),
        in_specs=[anywhere] * (5 + PIECES),
        out_specs=vmem,
        scratch_shapes=[
            pltpu.VMEM((2, span, half), jnp.bfloat16),
            pltpu.VMEM((3, 2 * half, wide), jnp.bfloat16),
            pltpu.VMEM((4 * length, wide), jnp.bfloat16),
            pltpu.VMEM((span, wide), jnp.bfloat16),
            pltpu.VMEM((span, wide), jnp.bfloat16),
            pltpu.SemaphoreType.DMA((11 + PIECES,)),
        ],
        compiler_params=pltpu.CompilerParams(vmem_limit_bytes=60 * 2**20),
    )(x_own, x_across, x_near, x_near_across, halo, *pieces)
    lines = [[4 * i + 2 * j + k for i in range(4) for k in range(2)] for j in range(2)]
    latents = lax.all_to_all(
        latent.reshape(8, length // 2, wide), ("seq", "mdl"),
        split_axis=0, concat_axis=0, tiled=True, axis_index_groups=lines,
    )
    routed = pl.pallas_call(
        predict_kernel,
        out_shape=jax.ShapeDtypeStruct((16, 1, 8 * capacity), jnp.float32),
        in_specs=[vmem] * 7,
        out_specs=vmem,
        compiler_params=pltpu.CompilerParams(vmem_limit_bytes=24 * 2**20),
    )(
        slot, latents, pred_weight,
        weight_early, weight_early_c, weight_late, weight_late_c,
    )
    arrived = lax.all_to_all(routed, ("seq", "mdl"), split_axis=0, concat_axis=0, tiled=True)
    mine = lax.dynamic_slice_in_dim(arrived[:, 0], capacity * s, capacity, 1)
    summed = jnp.sum(mine.reshape(4, 4, capacity), axis=1)
    return summed.reshape(1, -1) / float(block_len * 2 * half)


def solution(mesh):
    placed = (
        P(None, "seq", "mdl"),
        P("mdl"),
        P(None, "seq"),
        P(None, "seq"),
        P("grp", None, "seq", "mdl"),
        P(None, "mdl"),
    )
    plan = local_lines if mesh.shape["seq"] == 8 else local
    return jax.shard_map(
        plan, mesh=mesh, in_specs=placed, out_specs=P("seq", "grp"), check_vma=False
    )
```
